32 devices in a mesh: parts: 2 (over y), gx: 4 (over z), gy: 2 (over x), gz: 2 (over core).
Axes of the slice: x: 2, y: 2, z: 4, core: 2. Of those that a mesh axis runs over, the one named last changes fastest.
Arguments:
- embeds: bfloat16 [8192, 512], P(('parts', 'gx', 'gy', 'gz')), parts along dimension 0, may hold values from -6 to 6
- cluster: int32 [8192], P(('parts', 'gx', 'gy', 'gz')), parts along dimension 0, may hold values from 0 to 127, as said below
Outputs:
- nearest: float32 [8192], P(('parts', 'gx', 'gy', 'gz')), parts along dimension 0
The draws below stay inside these ranges and needn't reach their ends.
There are 2 independent parts, one for each index of `parts`. The reference program is written for one: setup_inputs(seed, part) draws one part's arguments, and reference() takes and returns one part's arrays. A program takes and returns all parts, laid end to end along the dimension named above; each array names one. Nothing has to cross between parts.
Inputs may be any that keep to these rules, and one draw needn't show every extreme that they name: `cluster`: cluster c belongs to owner c // 16. Among the 256 embeddings of one device, at most 64 lie in clusters of any one owner, and on every device some owner has exactly 64.
All inputs are finite; a program needn't handle non-finite values.
Results may differ from the reference program's by a relative error of at most 0.0018.
Values may be sent and summed in bfloat16 or wider, within the bound.
No kernel may reach another device: no remote copies, remote signals or barrier semaphores. Data moves between devices by JAX's collectives and lax.ppermute only.
A program may use at most 64 MiB of HBM per device.

```python
import jax
import jax.numpy as jnp
from jax import lax

D = 512
ROWS = 256
CLU_OWN = 16
OWNERS = 8
CAP = 64
ITEMS = 4096
N_GX = 4
N_GY = 2
N_GZ = 2


def draw_cluster(key, part):
    key = jax.random.fold_in(key, 7)
    devices = N_GX * N_GY * N_GZ
    owners = N_GX * N_GY
    slots = owners * CAP
    keys = jax.random.split(key, 5)
    column = jnp.arange(slots, dtype=jnp.int32)[None, :]
    scores = jax.random.randint(keys[0], (devices, slots), 0, 2 ** 19) * slots + column
    filled = jax.random.randint(keys[1], (devices, 1), 0, owners)
    scores = jnp.where(column // CAP == filled, -1 - column, scores)
    chosen = jnp.argsort(scores, axis=1, stable=True)[:, :ROWS]
    chosen = jax.random.permutation(keys[2], chosen, axis=1, independent=True)
    target = chosen // CAP
    local = jnp.minimum(jax.random.randint(keys[3], (devices, ROWS), 0, CLU_OWN), jax.random.randint(keys[4], (devices, ROWS), 0, CLU_OWN))
    return (target * CLU_OWN + local).reshape(-1).astype(jnp.int32)


def steps_of(stream_key, extent, shards, least, top_value):
    def one(dim, blocks):
        draws = jax.random.uniform(jax.random.fold_in(jax.random.fold_in(stream_key, 6), dim), (blocks,), jnp.float32, least / len(shards), top_value / len(shards))
        return jnp.repeat(jnp.exp(draws), extent[dim] // blocks).reshape((-1,) + (1,) * (len(extent) - dim - 1))

    level = one(*shards[0])
    for cut in shards[1:]:
        level = level * one(*cut)
    return level


def scatter_about(own_key, shape, deviation, limit, cuts=(), held_as=jnp.bfloat16):
    entries = deviation * jax.random.normal(own_key, shape, jnp.float32)
    if cuts:
        entries = entries * steps_of(own_key, shape, cuts, -0.22, 0.18)
    return jnp.clip(entries, -limit, limit).astype(held_as)


def setup_inputs(seed: int = 0, part: int = 0) -> dict:
    key_of = jax.random.split(jax.random.key(seed), 3)
    part_keys = jax.random.split(jax.random.fold_in(key_of[2], part), 3)
    embeds = scatter_about(part_keys[0], (ITEMS, D), 1.0, 6.0, ((0, 16),))
    cluster = draw_cluster(jax.random.fold_in(jax.random.fold_in(key_of[2], part), 71), part)
    return {"embeds": embeds, "cluster": cluster}


EPS = 1e-06

def reference(embeds, cluster):
    vecs = embeds.astype(jnp.float32)
    unit = (vecs * lax.rsqrt(lax.optimization_barrier(jnp.sum(vecs * vecs, axis=1, keepdims=True)) + EPS)).astype(jnp.bfloat16)
    unit_wide = unit.astype(jnp.float32)
    target = cluster // CLU_OWN
    slots = N_GX * N_GY * N_GZ * CAP

    def per_owner(which):
        index = jnp.nonzero(target == which, size=slots, fill_value=ITEMS)[0].astype(jnp.int32)
        valid = index < ITEMS
        safe = jnp.minimum(index, ITEMS - 1)
        member = unit_wide[safe]
        labels = jnp.where(valid, cluster[safe], -1)
        sims = jnp.dot(member, member.T, precision=lax.Precision.HIGHEST)
        keep = (labels[:, None] == labels[None, :]) & valid[:, None] & (index[:, None] != index[None, :])
        best = lax.optimization_barrier(jnp.max(jnp.where(keep, sims, -1.0), axis=1))
        return (index, best)
    index, best = lax.map(per_owner, jnp.arange(OWNERS, dtype=jnp.int32))
    nearest = jnp.full((ITEMS,), -1.0, jnp.float32)
    return nearest.at[index.reshape(-1)].set(best.reshape(-1), mode='drop')
```

```python
import jax
import jax.numpy as jnp
from jax import lax
from jax.experimental import pallas as pl
from jax.experimental.pallas import tpu as pltpu
from jax.sharding import PartitionSpec as P

CLU_OWN = 16


EPS = 1e-06

GROUP = ("gx", "gy", "gz")


def normalised(block):
    vecs = block.astype(jnp.float32)
    return (vecs * lax.rsqrt(jnp.sum(vecs * vecs, axis=1, keepdims=True) + EPS)).astype(
        jnp.bfloat16
    )


def as_column(labels):
    rows = labels.shape[1]
    return jnp.transpose(jnp.broadcast_to(labels, (128, rows)))


def best_of(queries, query_labels, keys, key_column, own=False):
    sims = lax.dot_general(
        keys, queries, (((1,), (1,)), ((), ())), preferred_element_type=jnp.float32
    )
    halves = []
    for start in range(0, sims.shape[1], 128):
        keep = key_column == query_labels[:, start : start + 128]
        if own:
            row = lax.broadcasted_iota(jnp.int32, keep.shape, 0)
            column = lax.broadcasted_iota(jnp.int32, keep.shape, 1) + start
            keep = keep & (row != column)
        halves.append(
            jnp.max(
                jnp.where(keep, sims[:, start : start + 128], -1.0), axis=0, keepdims=True
            )
        )
    return jnp.concatenate(halves, axis=1)


def near_kernel(blocks, labels, best_ref, unit_ref):
    query_labels = labels[0][...]
    best = None
    for at, (block, label) in enumerate(zip(blocks, labels)):
        unit_ref[at] = normalised(block[...])
        found = best_of(
            unit_ref[0], query_labels, unit_ref[at], as_column(label[...]), own=at == 0
        )
        best = found if best is None else jnp.maximum(best, found)
    best_ref[...] = best


def far_kernel(unit_ref, back, ahead, labels, near_ref, mine, sibling, to_back, to_ahead):
    own, other, prev, prev_other, succ, succ_other, l_back, l_ahead = [r[...] for r in labels]
    u_back = normalised(back[...])
    u_ahead = normalised(ahead[...])
    c_back = as_column(l_back)
    c_ahead = as_column(l_ahead)
    mine[...] = jnp.maximum(
        near_ref[...],
        jnp.maximum(
            best_of(unit_ref[0], own, u_back, c_back),
            best_of(unit_ref[0], own, u_ahead, c_ahead),
        ),
    )
    sibling[...] = jnp.maximum(
        best_of(unit_ref[1], other, u_back, c_back),
        best_of(unit_ref[1], other, u_ahead, c_ahead),
    )
    to_ahead[...] = jnp.maximum(
        best_of(u_ahead, l_ahead, u_back, c_back),
        jnp.maximum(
            best_of(u_ahead, l_ahead, unit_ref[2], as_column(prev)),
            best_of(u_ahead, l_ahead, unit_ref[3], as_column(prev_other)),
        ),
    )
    to_back[...] = jnp.maximum(
        best_of(u_back, l_back, u_ahead, c_ahead),
        jnp.maximum(
            best_of(u_back, l_back, unit_ref[4], as_column(succ)),
            best_of(u_back, l_back, unit_ref[5], as_column(succ_other)),
        ),
    )


def ring_perms(size_x, size_y, size_z):
    chips = size_x * size_y
    half = chips // 2

    def device(place, core):
        place = place % chips
        x, y = (place, 0) if place < size_x else (chips - 1 - place, 1)
        return (x * size_y + y) * size_z + core

    def perm(to):
        return [
            (device(p, k), device(*to(p, k))) for p in range(chips) for k in range(size_z)
        ]

    def swapped(place, core):
        return core if place % chips < half else 1 - core

    return {
        "sibling": perm(lambda p, k: (p, 1 - k)),
        "next": perm(lambda p, k: (p + 1, k)),
        "prev": perm(lambda p, k: (p - 1, k)),
        "next_sibling": perm(lambda p, k: (p + 1, 1 - k)),
        "prev_sibling": perm(lambda p, k: (p - 1, 1 - k)),
        "relay_next": perm(lambda p, k: (p + 1, swapped(p + 1, k))),
        "two_next": perm(lambda p, k: (p + 2, swapped(p + 2, k))),
        "two_prev": perm(lambda p, k: (p - 2, k)),
        "back_two_next": perm(lambda p, k: (p + 2, k)),
        "back_two_prev": perm(lambda p, k: (p - 2, swapped(p, k))),
    }


def on_ring(embeds, cluster):
    rows, width = embeds.shape
    perms = ring_perms(*(lax.axis_size(a) for a in GROUP))

    def send(value, name):
        return lax.ppermute(value, GROUP, perms[name])

    label = cluster.reshape(1, rows)
    prev = send(embeds, "next")
    succ = send(embeds, "prev")
    other = send(embeds, "sibling")
    labels = [label] + [
        send(label, name)
        for name in (
            "sibling",
            "next",
            "next_sibling",
            "prev",
            "prev_sibling",
            "two_next",
            "two_prev",
        )
    ]
    back = send(prev, "relay_next")
    ahead = send(succ, "prev")
    prev_other = send(prev, "sibling")
    succ_other = send(succ, "sibling")

    vmem = pl.BlockSpec(memory_space=pltpu.VMEM)
    line = jax.ShapeDtypeStruct((1, rows), jnp.float32)
    blocks = [embeds, other, prev, prev_other, succ, succ_other]
    near, units = pl.pallas_call(
        lambda *refs: near_kernel(refs[:6], refs[6:12], refs[12], refs[13]),
        out_shape=[line, jax.ShapeDtypeStruct((6, rows, width), jnp.bfloat16)],
        in_specs=[vmem] * 12,
        out_specs=[vmem] * 2,
        compiler_params=pltpu.CompilerParams(vmem_limit_bytes=32 * 2**20),
        cost_estimate=pl.CostEstimate(
            flops=12 * rows * rows * width, bytes_accessed=24 * rows * width, transcendentals=0
        ),
        name="near",
    )(*blocks, *labels[:6])
    mine, sibling, to_back, to_ahead = pl.pallas_call(
        lambda *refs: far_kernel(refs[0], refs[1], refs[2], refs[3:11], *refs[11:]),
        out_shape=[line] * 4,
        in_specs=[vmem] * 12,
        out_specs=[vmem] * 4,
        compiler_params=pltpu.CompilerParams(vmem_limit_bytes=32 * 2**20),
        cost_estimate=pl.CostEstimate(
            flops=20 * rows * rows * width, bytes_accessed=16 * rows * width, transcendentals=0
        ),
        name="far",
    )(units, back, ahead, *labels, near)
    best = jnp.maximum(
        jnp.maximum(mine, send(sibling, "sibling")),
        jnp.maximum(send(to_back, "back_two_prev"), send(to_ahead, "back_two_next")),
    )
    return best.reshape(rows)


def masked_sims(queries, query_labels, query_ids, keys, key_labels, key_ids):
    sims = jnp.einsum("qd,kd->qk", queries, keys, preferred_element_type=jnp.float32)
    keep = (
        (query_labels[:, None] == key_labels[None, :])
        & (query_labels[:, None] >= 0)
        & (query_ids[:, None] != key_ids[None, :])
    )
    return jnp.where(keep, sims, -1.0)


def by_owner(embeds, cluster):
    rows, width = embeds.shape
    size_x = lax.axis_size("gx")
    size_y = lax.axis_size("gy")
    owners = size_x * size_y
    cap = 2 * rows // owners
    total = owners * cap
    unit = normalised(embeds)
    target = cluster // CLU_OWN
    onehot = (target[:, None] == jnp.arange(owners, dtype=jnp.int32)[None, :]).astype(jnp.int32)
    before = jnp.cumsum(onehot, axis=0) - onehot
    slot = jnp.sum(before * onehot, axis=1)
    place = target * cap + slot
    outgoing = jnp.zeros((total, width), jnp.bfloat16).at[place].set(unit)
    out_labels = jnp.full((total,), -1, jnp.int32).at[place].set(cluster)
    got, got_labels = (
        lax.all_to_all(
            outgoing.reshape(owners, cap, width),
            ("gx", "gy"),
            split_axis=0,
            concat_axis=0,
            tiled=True,
        ),
        lax.all_to_all(
            out_labels.reshape(owners, cap), ("gx", "gy"), split_axis=0, concat_axis=0, tiled=True
        ),
    )
    members = got.reshape(total, width)
    labels = got_labels.reshape(total)
    core = lax.axis_index("gz")
    query_ids = core * total + jnp.arange(total, dtype=jnp.int32)
    keys = lax.all_gather(members, "gz", axis=0, tiled=True)
    key_labels = lax.all_gather(labels, "gz", axis=0, tiled=True)
    key_ids = jnp.arange(keys.shape[0], dtype=jnp.int32)
    best = jnp.maximum(
        jnp.full((total,), -1.0, jnp.float32),
        jnp.max(masked_sims(members, labels, query_ids, keys, key_labels, key_ids), axis=1),
    )
    back = lax.all_to_all(
        best.reshape(owners, cap), ("gx", "gy"), split_axis=0, concat_axis=0, tiled=True
    )
    return back.reshape(total)[place]


def solution(mesh):
    shape = mesh.shape
    ring = shape["gx"] * shape["gy"] == 8 and shape["gy"] == 2 and shape["gz"] == 2
    placed = (P(("parts", "gx", "gy", "gz"), None), P(("parts", "gx", "gy", "gz")))
    return jax.shard_map(
        on_ring if ring else by_owner,
        mesh=mesh,
        in_specs=placed,
        out_specs=P(("parts", "gx", "gy", "gz")),
        check_vma=False,
    )
```

```python
import jax
import jax.numpy as jnp
from jax import lax
from jax.experimental import pallas as pl
from jax.experimental.pallas import tpu as pltpu
from jax.sharding import PartitionSpec as P

CLU_OWN = 16


EPS = 1e-06

GROUP = ("gx", "gy", "gz")


def normalised(block):
    vecs = block.astype(jnp.float32)
    return (vecs * lax.rsqrt(jnp.sum(vecs * vecs, axis=1, keepdims=True) + EPS)).astype(
        jnp.bfloat16
    )


LABEL_ROWS = 16
CHUNKS = 4


def pack_kernel(embeds, label, packed, raw, line, sems):
    rows, width = embeds.shape
    step = rows // CHUNKS
    line_copy = pltpu.make_async_copy(label, line, sems.at[CHUNKS])
    line_copy.start()
    copies = []
    for i in range(CHUNKS):
        part = pl.ds(i * step, step)
        copies.append(pltpu.make_async_copy(embeds.at[part], raw.at[part], sems.at[i]))
        copies[-1].start()
    line_copy.wait()
    lines = jnp.broadcast_to(line[...].astype(jnp.float32), (LABEL_ROWS, rows))
    packed[rows:, :rows] = lines.astype(jnp.bfloat16)
    packed[rows:, rows:] = jnp.zeros((LABEL_ROWS, width - rows), jnp.bfloat16)
    for i in range(CHUNKS):
        part = pl.ds(i * step, step)
        copies[i].wait()
        packed[part, :] = normalised(raw[part, :])


class Block:
    def __init__(self, ref):
        self.rows = ref.shape[0] - LABEL_ROWS
        self.unit = ref[: self.rows, :]
        self.label = ref[self.rows :, : self.rows].astype(jnp.float32)[:1]

    def column(self):
        return jnp.transpose(jnp.broadcast_to(self.label, (128, self.rows)))


def best_of(queries, keys, key_column, own=False):
    sims = lax.dot_general(
        keys.unit, queries.unit, (((1,), (1,)), ((), ())), preferred_element_type=jnp.float32
    )
    halves = []
    for start in range(0, sims.shape[1], 128):
        keep = key_column == queries.label[:, start : start + 128]
        if own:
            row = lax.broadcasted_iota(jnp.int32, keep.shape, 0)
            column = lax.broadcasted_iota(jnp.int32, keep.shape, 1) + start
            keep = keep & (row != column)
        halves.append(
            jnp.max(
                jnp.where(keep, sims[:, start : start + 128], -1.0), axis=0, keepdims=True
            )
        )
    return jnp.concatenate(halves, axis=1)


def near_kernel(*refs):
    *blocks, best_ref = refs
    mine = Block(blocks[0])
    best = best_of(mine, mine, mine.column(), own=True)
    for ref in blocks[1:]:
        keys = Block(ref)
        best = jnp.maximum(best, best_of(mine, keys, keys.column()))
    best_ref[...] = best


def far_kernel(
    own, prev, prev_other, succ, succ_other, back, ahead, near, mine, to_back, to_ahead
):
    own, back, ahead = Block(own), Block(back), Block(ahead)
    c_own, c_back, c_ahead = own.column(), back.column(), ahead.column()
    mine[...] = jnp.maximum(
        near[...], jnp.maximum(best_of(own, back, c_back), best_of(own, ahead, c_ahead))
    )
    found = jnp.maximum(best_of(ahead, back, c_back), best_of(ahead, own, c_own))
    for ref in (prev, prev_other):
        keys = Block(ref)
        found = jnp.maximum(found, best_of(ahead, keys, keys.column()))
    to_ahead[...] = found
    found = jnp.maximum(best_of(back, ahead, c_ahead), best_of(back, own, c_own))
    for ref in (succ, succ_other):
        keys = Block(ref)
        found = jnp.maximum(found, best_of(back, keys, keys.column()))
    to_back[...] = found


def ring_perms(size_x, size_y, size_z):
    chips = size_x * size_y

    def device(place, core):
        place = place % chips
        x, y = (place, 0) if place < size_x else (chips - 1 - place, 1)
        return (x * size_y + y) * size_z + core

    def perm(to):
        return [
            (device(p, k), device(*to(p, k))) for p in range(chips) for k in range(size_z)
        ]

    def from_back(place, core):
        return core ^ (place % chips in (0, 1))

    def from_ahead(place, core):
        return core ^ (place % chips not in (chips - 2, chips - 1))

    return {
        "sibling": perm(lambda p, k: (p, 1 - k)),
        "next": perm(lambda p, k: (p + 1, k)),
        "prev": perm(lambda p, k: (p - 1, k)),
        "on_next": perm(lambda p, k: (p + 1, from_back(p + 1, k))),
        "on_prev": perm(lambda p, k: (p - 1, from_ahead(p - 1, k))),
        "home_back": perm(lambda p, k: (p - 2, from_back(p, k))),
        "home_ahead": perm(lambda p, k: (p + 2, from_ahead(p, k))),
    }


def on_ring(embeds, cluster):
    rows, width = embeds.shape
    perms = ring_perms(*(lax.axis_size(a) for a in GROUP))

    def send(value, name):
        return lax.ppermute(value, GROUP, perms[name])

    vmem = pl.BlockSpec(memory_space=pltpu.VMEM)
    line = jax.ShapeDtypeStruct((1, rows), jnp.float32)
    own = pl.pallas_call(
        pack_kernel,
        out_shape=jax.ShapeDtypeStruct((rows + LABEL_ROWS, width), jnp.bfloat16),
        in_specs=[pl.BlockSpec(memory_space=pl.ANY)] * 2,
        out_specs=vmem,
        scratch_shapes=[
            pltpu.VMEM((rows, width), jnp.bfloat16),
            pltpu.VMEM((1, rows), jnp.int32),
            pltpu.SemaphoreType.DMA((CHUNKS + 1,)),
        ],
        compiler_params=pltpu.CompilerParams(vmem_limit_bytes=60 * 2**20),
        name="pack",
    )(embeds, cluster.reshape(1, rows))
    prev = send(own, "next")
    succ = send(own, "prev")
    other = send(own, "sibling")
    back = send(prev, "on_next")
    ahead = send(succ, "on_prev")
    prev_other = send(prev, "sibling")
    succ_other = send(succ, "sibling")
    params = pltpu.CompilerParams(vmem_limit_bytes=32 * 2**20)
    near = pl.pallas_call(
        near_kernel,
        out_shape=line,
        in_specs=[vmem] * 6,
        out_specs=vmem,
        compiler_params=params,
        cost_estimate=pl.CostEstimate(
            flops=12 * rows * rows * width, bytes_accessed=12 * rows * width, transcendentals=0
        ),
        name="near",
    )(own, other, prev, prev_other, succ, succ_other)
    mine, to_back, to_ahead = pl.pallas_call(
        far_kernel,
        out_shape=[line] * 3,
        in_specs=[vmem] * 8,
        out_specs=[vmem] * 3,
        compiler_params=params,
        cost_estimate=pl.CostEstimate(
            flops=20 * rows * rows * width, bytes_accessed=14 * rows * width, transcendentals=0
        ),
        name="far",
    )(own, prev, prev_other, succ, succ_other, back, ahead, near)
    best = jnp.maximum(
        mine, jnp.maximum(send(to_back, "home_back"), send(to_ahead, "home_ahead"))
    )
    return best.reshape(rows)


def masked_sims(queries, query_labels, query_ids, keys, key_labels, key_ids):
    sims = jnp.einsum("qd,kd->qk", queries, keys, preferred_element_type=jnp.float32)
    keep = (
        (query_labels[:, None] == key_labels[None, :])
        & (query_labels[:, None] >= 0)
        & (query_ids[:, None] != key_ids[None, :])
    )
    return jnp.where(keep, sims, -1.0)


def by_owner(embeds, cluster):
    rows, width = embeds.shape
    size_x = lax.axis_size("gx")
    size_y = lax.axis_size("gy")
    owners = size_x * size_y
    cap = 2 * rows // owners
    total = owners * cap
    unit = normalised(embeds)
    target = cluster // CLU_OWN
    onehot = (target[:, None] == jnp.arange(owners, dtype=jnp.int32)[None, :]).astype(jnp.int32)
    before = jnp.cumsum(onehot, axis=0) - onehot
    slot = jnp.sum(before * onehot, axis=1)
    place = target * cap + slot
    outgoing = jnp.zeros((total, width), jnp.bfloat16).at[place].set(unit)
    out_labels = jnp.full((total,), -1, jnp.int32).at[place].set(cluster)
    got, got_labels = (
        lax.all_to_all(
            outgoing.reshape(owners, cap, width),
            ("gx", "gy"),
            split_axis=0,
            concat_axis=0,
            tiled=True,
        ),
        lax.all_to_all(
            out_labels.reshape(owners, cap), ("gx", "gy"), split_axis=0, concat_axis=0, tiled=True
        ),
    )
    members = got.reshape(total, width)
    labels = got_labels.reshape(total)
    core = lax.axis_index("gz")
    query_ids = core * total + jnp.arange(total, dtype=jnp.int32)
    keys = lax.all_gather(members, "gz", axis=0, tiled=True)
    key_labels = lax.all_gather(labels, "gz", axis=0, tiled=True)
    key_ids = jnp.arange(keys.shape[0], dtype=jnp.int32)
    best = jnp.maximum(
        jnp.full((total,), -1.0, jnp.float32),
        jnp.max(masked_sims(members, labels, query_ids, keys, key_labels, key_ids), axis=1),
    )
    back = lax.all_to_all(
        best.reshape(owners, cap), ("gx", "gy"), split_axis=0, concat_axis=0, tiled=True
    )
    return back.reshape(total)[place]


def solution(mesh):
    shape = mesh.shape
    ring = shape["gx"] * shape["gy"] == 8 and shape["gy"] == 2 and shape["gz"] == 2
    placed = (P(("parts", "gx", "gy", "gz"), None), P(("parts", "gx", "gy", "gz")))
    return jax.shard_map(
        on_ring if ring else by_owner,
        mesh=mesh,
        in_specs=placed,
        out_specs=P(("parts", "gx", "gy", "gz")),
        check_vma=False,
    )
```

```python
import jax
import jax.numpy as jnp
from jax import lax
from jax.experimental import pallas as pl
from jax.experimental.pallas import tpu as pltpu
from jax.sharding import PartitionSpec as P

CLU_OWN = 16


EPS = 1e-06

GROUP = ("gx", "gy", "gz")


def normalised(block):
    vecs = block.astype(jnp.float32)
    return (vecs * lax.rsqrt(jnp.sum(vecs * vecs, axis=1, keepdims=True) + EPS)).astype(
        jnp.bfloat16
    )


LABEL_ROWS = 16
VMEM_BYTES = 32 * 2**20
NEAR_COST = 6
FIRST_COST = 5
SECOND_COST = 6


def pack_first_kernel(embeds, label, first, raw, line, sems):
    rows, width = embeds.shape
    half = rows // 2
    copies = [
        pltpu.make_async_copy(label, line, sems.at[0]),
        pltpu.make_async_copy(embeds.at[pl.ds(0, half)], raw, sems.at[1]),
    ]
    for copy in copies:
        copy.start()
    copies[0].wait()
    lines = jnp.broadcast_to(line[...].astype(jnp.float32), (LABEL_ROWS, rows))
    first[half:, :rows] = lines.astype(jnp.bfloat16)
    first[half:, rows:] = jnp.zeros((LABEL_ROWS, width - rows), jnp.bfloat16)
    copies[1].wait()
    first[:half, :] = normalised(raw[...])


def pack_second_kernel(embeds, first, second, both, raw, sem):
    half = second.shape[0]
    copy = pltpu.make_async_copy(embeds.at[pl.ds(half, half)], raw, sem)
    copy.start()
    both[:half, :] = first[:half, :]
    both[2 * half :, :] = first[half:, :]
    copy.wait()
    unit = normalised(raw[...])
    second[...] = unit
    both[half : 2 * half, :] = unit


class Block:
    def __init__(self, unit, label):
        self.unit = unit
        self.label = label
        self.rows = unit.shape[0]
        self.along_rows = None

    def column(self):
        if self.along_rows is None:
            self.along_rows = jnp.transpose(jnp.broadcast_to(self.label, (128, self.rows)))
        return self.along_rows


def labels_in(first):
    half = first.shape[0] - LABEL_ROWS
    return first[half:, : 2 * half].astype(jnp.float32)[:1]


def packed(ref):
    rows = ref.shape[0] - LABEL_ROWS
    return Block(ref[:rows, :], ref[rows:, :rows].astype(jnp.float32)[:1])


def whole(first, second):
    half = second.shape[0]
    return Block(jnp.concatenate([first[:half, :], second[...]], axis=0), labels_in(first))


def first_half(first):
    half = first.shape[0] - LABEL_ROWS
    return Block(first[:half, :], labels_in(first)[:, :half])


def second_half(first, second):
    half = second.shape[0]
    return Block(second[...], labels_in(first)[:, half:])


def best_of(queries, *all_keys):
    best = None
    for keys in all_keys:
        sims = lax.dot_general(
            keys.unit, queries.unit, (((1,), (1,)), ((), ())), preferred_element_type=jnp.float32
        )
        pieces = []
        for start in range(0, queries.rows, 128):
            keep = keys.column() == queries.label[:, start : start + 128]
            if keys is queries:
                row = lax.broadcasted_iota(jnp.int32, keep.shape, 0)
                column = lax.broadcasted_iota(jnp.int32, keep.shape, 1) + start
                keep = keep & (row != column)
            found = jnp.where(keep, sims[:, start : start + 128], -1.0)
            pieces.append(jnp.max(found, axis=0, keepdims=True))
        found = jnp.concatenate(pieces, axis=1)
        best = found if best is None else jnp.maximum(best, found)
    return best


def near_kernel(
    own, prev_a, prev_b, succ_a, succ_b, mine, to_prev, to_succ
):
    own = packed(own)
    prev, succ = whole(prev_a, prev_b), whole(succ_a, succ_b)
    mine[...] = best_of(own, own, prev, succ)
    to_prev[...] = best_of(prev, own)
    to_succ[...] = best_of(succ, own)


def other_kernel(own, other, mine, mine_out):
    mine_out[...] = jnp.maximum(mine[...], best_of(packed(own), packed(other)))


def far_first_kernel(
    own, prev_a, prev_b, succ_a, succ_b, back_a, ahead_a, *refs
):
    mine, to_prev, to_succ, mine_out, to_prev_out, to_succ_out, to_back, to_ahead = refs
    own = packed(own)
    prev, succ = whole(prev_a, prev_b), whole(succ_a, succ_b)
    back, ahead = first_half(back_a), first_half(ahead_a)
    mine_out[...] = jnp.maximum(mine[...], best_of(own, back, ahead))
    to_prev_out[...] = jnp.maximum(to_prev[...], best_of(prev, ahead))
    to_succ_out[...] = jnp.maximum(to_succ[...], best_of(succ, back))
    to_back[...] = best_of(back, own, succ, ahead)
    to_ahead[...] = best_of(ahead, own, prev, back)


def far_second_kernel(
    own, prev_a, prev_b, succ_a, succ_b, back_a, ahead_a, back_b, ahead_b, *refs
):
    mine, to_prev, to_succ, back_first, ahead_first, *out = refs
    mine_out, to_prev_out, to_succ_out, to_back, to_ahead = out
    own = packed(own)
    prev, succ = whole(prev_a, prev_b), whole(succ_a, succ_b)
    half = back_b.shape[0]
    back, ahead = first_half(back_a), first_half(ahead_a)
    back_rest, ahead_rest = second_half(back_a, back_b), second_half(ahead_a, ahead_b)
    mine_out[...] = jnp.maximum(mine[...], best_of(own, back_rest, ahead_rest))
    to_prev_out[...] = jnp.maximum(to_prev[...], best_of(prev, ahead_rest))
    to_succ_out[...] = jnp.maximum(to_succ[...], best_of(succ, back_rest))
    to_back[:, :half] = jnp.maximum(back_first[...], best_of(back, ahead_rest))
    to_back[:, half:] = best_of(back_rest, own, succ, ahead, ahead_rest)
    to_ahead[:, :half] = jnp.maximum(ahead_first[...], best_of(ahead, back_rest))
    to_ahead[:, half:] = best_of(ahead_rest, own, prev, back, back_rest)


ONE_BACK = (0, 0, 0, 1, 1, 0, 0, 1)
TWO_BACK = (1, 1, 0, 0, 0, 0, 0, 0)


def ring_perms(size_x, size_y, size_z):
    chips = size_x * size_y

    def device(place, core):
        place = place % chips
        x, y = (place, 0) if place < size_x else (chips - 1 - place, 1)
        return (x * size_y + y) * size_z + core

    def changed(place, step):
        place = place % chips
        if step == 0:
            return 0
        if step < 0:
            return 1 - changed(place - step, -step)
        return (ONE_BACK if step == 1 else TWO_BACK)[place]

    def perm(held, step):
        pairs = []
        for place in range(chips):
            for core in range(size_z):
                source = core ^ changed(place, held)
                target = source ^ changed(place + step, held + step)
                pairs.append((device(place, core), device(place + step, target)))
        return pairs

    return {
        "sibling": [(d, d ^ 1) for d in range(chips * size_z)],
        "next": perm(0, 1),
        "prev": perm(0, -1),
        "on_next": perm(1, 1),
        "on_prev": perm(-1, -1),
        "home_prev": perm(1, -1),
        "home_succ": perm(-1, 1),
        "home_back": perm(2, -2),
        "home_ahead": perm(-2, 2),
    }


def kernel_call(kernel, inputs, outputs, matmuls):
    vmem = pl.BlockSpec(memory_space=pltpu.VMEM)
    return pl.pallas_call(
        kernel,
        out_shape=outputs,
        in_specs=[vmem] * len(inputs),
        out_specs=[vmem] * len(outputs),
        compiler_params=pltpu.CompilerParams(vmem_limit_bytes=VMEM_BYTES),
        cost_estimate=pl.CostEstimate(
            flops=matmuls * 2**26, bytes_accessed=2**20, transcendentals=0
        ),
        name=kernel.__name__,
    )(*inputs)


def on_ring(embeds, cluster):
    rows, width = embeds.shape
    half = rows // 2
    perms = ring_perms(*(lax.axis_size(a) for a in GROUP))

    def send(value, name):
        return lax.ppermute(value, GROUP, perms[name])

    line = jax.ShapeDtypeStruct((1, rows), jnp.float32)
    half_line = jax.ShapeDtypeStruct((1, half), jnp.float32)
    anywhere = pl.BlockSpec(memory_space=pl.ANY)
    vmem = pl.BlockSpec(memory_space=pltpu.VMEM)
    params = pltpu.CompilerParams(vmem_limit_bytes=VMEM_BYTES)
    own_a = pl.pallas_call(
        pack_first_kernel,
        out_shape=jax.ShapeDtypeStruct((half + LABEL_ROWS, width), jnp.bfloat16),
        in_specs=[anywhere] * 2,
        out_specs=vmem,
        scratch_shapes=[
            pltpu.VMEM((half, width), jnp.bfloat16),
            pltpu.VMEM((1, rows), jnp.int32),
            pltpu.SemaphoreType.DMA((2,)),
        ],
        compiler_params=params,
        name="pack_first",
    )(embeds, cluster.reshape(1, rows))
    own_b, own = pl.pallas_call(
        pack_second_kernel,
        out_shape=[
            jax.ShapeDtypeStruct((half, width), jnp.bfloat16),
            jax.ShapeDtypeStruct((rows + LABEL_ROWS, width), jnp.bfloat16),
        ],
        in_specs=[anywhere, vmem],
        out_specs=[vmem] * 2,
        scratch_shapes=[pltpu.VMEM((half, width), jnp.bfloat16), pltpu.SemaphoreType.DMA],
        compiler_params=params,
        name="pack_second",
    )(embeds, own_a)
    prev_a, succ_a = send(own_a, "next"), send(own_a, "prev")
    prev_b, succ_b = send(own_b, "next"), send(own_b, "prev")
    other = send(own, "sibling")
    back_a, ahead_a = send(prev_a, "on_next"), send(succ_a, "on_prev")
    back_b, ahead_b = send(prev_b, "on_next"), send(succ_b, "on_prev")
    blocks = [own, prev_a, prev_b, succ_a, succ_b]
    near = kernel_call(near_kernel, blocks, [line] * 3, NEAR_COST)
    parts = kernel_call(
        far_first_kernel,
        [*blocks, back_a, ahead_a, *near],
        [line] * 3 + [half_line] * 2,
        FIRST_COST,
    )
    mine, *found = kernel_call(
        far_second_kernel,
        [*blocks, back_a, ahead_a, back_b, ahead_b, *parts],
        [line] * 5,
        SECOND_COST,
    )
    (mine,) = kernel_call(other_kernel, [own, other, mine], [line], 1)
    homes = ("home_prev", "home_succ", "home_back", "home_ahead")
    for value, home in zip(found[::-1], homes[::-1]):
        mine = jnp.maximum(mine, send(value, home))
    return mine.reshape(rows)


def masked_sims(queries, query_labels, query_ids, keys, key_labels, key_ids):
    sims = jnp.einsum("qd,kd->qk", queries, keys, preferred_element_type=jnp.float32)
    keep = (
        (query_labels[:, None] == key_labels[None, :])
        & (query_labels[:, None] >= 0)
        & (query_ids[:, None] != key_ids[None, :])
    )
    return jnp.where(keep, sims, -1.0)


def by_owner(embeds, cluster):
    rows, width = embeds.shape
    size_x = lax.axis_size("gx")
    size_y = lax.axis_size("gy")
    owners = size_x * size_y
    cap = 2 * rows // owners
    total = owners * cap
    unit = normalised(embeds)
    target = cluster // CLU_OWN
    onehot = (target[:, None] == jnp.arange(owners, dtype=jnp.int32)[None, :]).astype(jnp.int32)
    before = jnp.cumsum(onehot, axis=0) - onehot
    slot = jnp.sum(before * onehot, axis=1)
    place = target * cap + slot
    outgoing = jnp.zeros((total, width), jnp.bfloat16).at[place].set(unit)
    out_labels = jnp.full((total,), -1, jnp.int32).at[place].set(cluster)
    got, got_labels = (
        lax.all_to_all(
            outgoing.reshape(owners, cap, width),
            ("gx", "gy"),
            split_axis=0,
            concat_axis=0,
            tiled=True,
        ),
        lax.all_to_all(
            out_labels.reshape(owners, cap), ("gx", "gy"), split_axis=0, concat_axis=0, tiled=True
        ),
    )
    members = got.reshape(total, width)
    labels = got_labels.reshape(total)
    core = lax.axis_index("gz")
    query_ids = core * total + jnp.arange(total, dtype=jnp.int32)
    keys = lax.all_gather(members, "gz", axis=0, tiled=True)
    key_labels = lax.all_gather(labels, "gz", axis=0, tiled=True)
    key_ids = jnp.arange(keys.shape[0], dtype=jnp.int32)
    best = jnp.maximum(
        jnp.full((total,), -1.0, jnp.float32),
        jnp.max(masked_sims(members, labels, query_ids, keys, key_labels, key_ids), axis=1),
    )
    back = lax.all_to_all(
        best.reshape(owners, cap), ("gx", "gy"), split_axis=0, concat_axis=0, tiled=True
    )
    return back.reshape(total)[place]


def solution(mesh):
    shape = mesh.shape
    ring = shape["gx"] * shape["gy"] == 8 and shape["gy"] == 2 and shape["gz"] == 2
    placed = (P(("parts", "gx", "gy", "gz"), None), P(("parts", "gx", "gy", "gz")))
    return jax.shard_map(
        on_ring if ring else by_owner,
        mesh=mesh,
        in_specs=placed,
        out_specs=P(("parts", "gx", "gy", "gz")),
        check_vma=False,
    )
```

```python
import jax
import jax.numpy as jnp
from jax import lax
from jax.experimental import pallas as pl
from jax.experimental.pallas import tpu as pltpu
from jax.sharding import PartitionSpec as P

CLU_OWN = 16


EPS = 1e-06

GROUP = ("gx", "gy", "gz")


def normalised(block):
    vecs = block.astype(jnp.float32)
    return (vecs * lax.rsqrt(jnp.sum(vecs * vecs, axis=1, keepdims=True) + EPS)).astype(
        jnp.bfloat16
    )


LABEL_ROWS = 16
VMEM_BYTES = 32 * 2**20
PACK_BYTES = 32 * 2**20
NEAR_COST = 1
FIRST_COST = 5
SECOND_COST = 200


def pack_first_kernel(embeds, label, first, raw, line, sems):
    rows, width = embeds.shape
    half = rows // 2
    copies = [
        pltpu.make_async_copy(label, line, sems.at[0]),
        pltpu.make_async_copy(embeds.at[pl.ds(0, half)], raw, sems.at[1]),
    ]
    for copy in copies:
        copy.start()
    copies[0].wait()
    lines = jnp.broadcast_to(line[...].astype(jnp.float32), (LABEL_ROWS, rows))
    first[half:, :rows] = lines.astype(jnp.bfloat16)
    first[half:, rows:] = jnp.zeros((LABEL_ROWS, width - rows), jnp.bfloat16)
    copies[1].wait()
    first[:half, :] = normalised(raw[...])


def pack_second_kernel(embeds, first, second, both, raw, sem):
    half = second.shape[0]
    copy = pltpu.make_async_copy(embeds.at[pl.ds(half, half)], raw, sem)
    copy.start()
    both[:half, :] = first[:half, :]
    both[2 * half :, :] = first[half:, :]
    copy.wait()
    unit = normalised(raw[...])
    second[...] = unit
    both[half : 2 * half, :] = unit


class Block:
    def __init__(self, unit, label):
        self.unit = unit
        self.label = label
        self.rows = unit.shape[0]
        self.along_rows = None

    def column(self):
        if self.along_rows is None:
            self.along_rows = jnp.transpose(jnp.broadcast_to(self.label, (128, self.rows)))
        return self.along_rows


def labels_in(first):
    half = first.shape[0] - LABEL_ROWS
    return first[half:, : 2 * half].astype(jnp.float32)[:1]


def packed(ref):
    rows = ref.shape[0] - LABEL_ROWS
    return Block(ref[:rows, :], ref[rows:, :rows].astype(jnp.float32)[:1])


def whole(first, second):
    half = second.shape[0]
    return Block(jnp.concatenate([first[:half, :], second[...]], axis=0), labels_in(first))


def first_half(first):
    half = first.shape[0] - LABEL_ROWS
    return Block(first[:half, :], labels_in(first)[:, :half])


def second_half(first, second):
    half = second.shape[0]
    return Block(second[...], labels_in(first)[:, half:])


def best_of(queries, *all_keys):
    best = None
    for keys in all_keys:
        sims = lax.dot_general(
            keys.unit, queries.unit, (((1,), (1,)), ((), ())), preferred_element_type=jnp.float32
        )
        pieces = []
        for start in range(0, queries.rows, 128):
            keep = keys.column() == queries.label[:, start : start + 128]
            if keys is queries:
                row = lax.broadcasted_iota(jnp.int32, keep.shape, 0)
                column = lax.broadcasted_iota(jnp.int32, keep.shape, 1) + start
                keep = keep & (row != column)
            found = jnp.where(keep, sims[:, start : start + 128], -1.0)
            pieces.append(jnp.max(found, axis=0, keepdims=True))
        found = jnp.concatenate(pieces, axis=1)
        best = found if best is None else jnp.maximum(best, found)
    return best


def near_kernel(own, prev_a, prev_b, succ_a, succ_b, mine, bundle):
    half = prev_b.shape[0]
    for at, (first, second) in enumerate(((prev_a, prev_b), (succ_a, succ_b))):
        bundle[at, :half, :] = first[:half, :]
        bundle[at, half : 2 * half, :] = second[...]
        bundle[at, 2 * half :, :] = first[half:, :]
    bundle[2] = own[...]
    own = packed(own)
    mine[...] = best_of(own, own, whole(prev_a, prev_b), whole(succ_a, succ_b))


def far_first_kernel(own, bundle, back_a, ahead_a, near, mine, to_back, to_ahead):
    own, prev, succ = packed(own), packed(bundle.at[0]), packed(bundle.at[1])
    back, ahead = first_half(back_a), first_half(ahead_a)
    mine[...] = jnp.maximum(near[...], best_of(own, back, ahead))
    to_back[...] = best_of(back, own, succ, ahead)
    to_ahead[...] = best_of(ahead, own, prev, back)


def far_second_kernel(own, bundle, back_a, ahead_a, back_b, ahead_b, *refs):
    near, back_first, ahead_first, mine, to_back, to_ahead = refs
    own, prev, succ = packed(own), packed(bundle.at[0]), packed(bundle.at[1])
    half = back_b.shape[0]
    back, ahead = first_half(back_a), first_half(ahead_a)
    back_rest, ahead_rest = second_half(back_a, back_b), second_half(ahead_a, ahead_b)
    mine[...] = jnp.maximum(near[...], best_of(own, back_rest, ahead_rest))
    to_back[:, :half] = jnp.maximum(back_first[...], best_of(back, ahead_rest))
    to_back[:, half:] = best_of(back_rest, own, succ, ahead, ahead_rest)
    to_ahead[:, :half] = jnp.maximum(ahead_first[...], best_of(ahead, back_rest))
    to_ahead[:, half:] = best_of(ahead_rest, own, prev, back, back_rest)


def far_other_kernel(others, back_a, ahead_a, back_b, ahead_b, *refs):
    back_found, ahead_found, to_back, to_ahead = refs
    back, ahead = whole(back_a, back_b), whole(ahead_a, ahead_b)
    to_back[...] = jnp.maximum(back_found[...], best_of(back, packed(others.at[1])))
    to_ahead[...] = jnp.maximum(ahead_found[...], best_of(ahead, packed(others.at[0])))


def other_kernel(own, others, found, mine):
    keys = (packed(others.at[at]) for at in range(3))
    mine[...] = jnp.maximum(found[...], best_of(packed(own), *keys))


def ring_perms(size_x, size_y, size_z):
    chips = size_x * size_y

    def device(place, core):
        place = place % chips
        x, y = (place, 0) if place < size_x else (chips - 1 - place, 1)
        return (x * size_y + y) * size_z + core

    def perm(to):
        return [
            (device(p, k), device(*to(p, k))) for p in range(chips) for k in range(size_z)
        ]

    def from_back(place, core):
        return core ^ (place % chips in (0, 1))

    def from_ahead(place, core):
        return core ^ (place % chips not in (chips - 2, chips - 1))

    return {
        "sibling": perm(lambda p, k: (p, 1 - k)),
        "next": perm(lambda p, k: (p + 1, k)),
        "prev": perm(lambda p, k: (p - 1, k)),
        "on_next": perm(lambda p, k: (p + 1, from_back(p + 1, k))),
        "on_prev": perm(lambda p, k: (p - 1, from_ahead(p - 1, k))),
        "home_back": perm(lambda p, k: (p - 2, from_back(p, k))),
        "home_ahead": perm(lambda p, k: (p + 2, from_ahead(p, k))),
    }


def kernel_call(kernel, inputs, outputs, matmuls):
    vmem = pl.BlockSpec(memory_space=pltpu.VMEM)
    return pl.pallas_call(
        kernel,
        out_shape=outputs,
        in_specs=[vmem] * len(inputs),
        out_specs=[vmem] * len(outputs),
        compiler_params=pltpu.CompilerParams(vmem_limit_bytes=VMEM_BYTES),
        cost_estimate=pl.CostEstimate(
            flops=matmuls * 2**26, bytes_accessed=2**20, transcendentals=0
        ),
        name=kernel.__name__,
    )(*inputs)


def on_ring(embeds, cluster):
    rows, width = embeds.shape
    half = rows // 2
    perms = ring_perms(*(lax.axis_size(a) for a in GROUP))

    def send(value, name):
        return lax.ppermute(value, GROUP, perms[name])

    line = jax.ShapeDtypeStruct((1, rows), jnp.float32)
    half_line = jax.ShapeDtypeStruct((1, half), jnp.float32)
    anywhere = pl.BlockSpec(memory_space=pl.ANY)
    vmem = pl.BlockSpec(memory_space=pltpu.VMEM)
    params = pltpu.CompilerParams(vmem_limit_bytes=PACK_BYTES)
    own_a = pl.pallas_call(
        pack_first_kernel,
        out_shape=jax.ShapeDtypeStruct((half + LABEL_ROWS, width), jnp.bfloat16),
        in_specs=[anywhere] * 2,
        out_specs=vmem,
        scratch_shapes=[
            pltpu.VMEM((half, width), jnp.bfloat16),
            pltpu.VMEM((1, rows), jnp.int32),
            pltpu.SemaphoreType.DMA((2,)),
        ],
        compiler_params=params,
        name="pack_first",
    )(embeds, cluster.reshape(1, rows))
    own_b, own = pl.pallas_call(
        pack_second_kernel,
        out_shape=[
            jax.ShapeDtypeStruct((half, width), jnp.bfloat16),
            jax.ShapeDtypeStruct((rows + LABEL_ROWS, width), jnp.bfloat16),
        ],
        in_specs=[anywhere, vmem],
        out_specs=[vmem] * 2,
        scratch_shapes=[pltpu.VMEM((half, width), jnp.bfloat16), pltpu.SemaphoreType.DMA],
        compiler_params=params,
        name="pack_second",
    )(embeds, own_a)
    prev_a, succ_a = send(own_a, "next"), send(own_a, "prev")
    prev_b, succ_b = send(own_b, "next"), send(own_b, "prev")
    back_a, ahead_a = send(prev_a, "on_next"), send(succ_a, "on_prev")
    back_b, ahead_b = send(prev_b, "on_next"), send(succ_b, "on_prev")
    mine, bundle = kernel_call(
        near_kernel,
        [own, prev_a, prev_b, succ_a, succ_b],
        [line, jax.ShapeDtypeStruct((3, rows + LABEL_ROWS, width), jnp.bfloat16)],
        NEAR_COST,
    )
    others = send(bundle, "sibling")
    parts = kernel_call(
        far_first_kernel,
        [own, bundle, back_a, ahead_a, mine],
        [line, half_line, half_line],
        FIRST_COST,
    )
    mine, to_back, to_ahead = kernel_call(
        far_second_kernel,
        [own, bundle, back_a, ahead_a, back_b, ahead_b, *parts],
        [line] * 3,
        SECOND_COST,
    )
    to_back, to_ahead = kernel_call(
        far_other_kernel,
        [others, back_a, ahead_a, back_b, ahead_b, to_back, to_ahead],
        [line] * 2,
        2,
    )
    (mine,) = kernel_call(other_kernel, [own, others, mine], [line], 3)
    best = jnp.maximum(
        mine, jnp.maximum(send(to_back, "home_back"), send(to_ahead, "home_ahead"))
    )
    return best.reshape(rows)


def masked_sims(queries, query_labels, query_ids, keys, key_labels, key_ids):
    sims = jnp.einsum("qd,kd->qk", queries, keys, preferred_element_type=jnp.float32)
    keep = (
        (query_labels[:, None] == key_labels[None, :])
        & (query_labels[:, None] >= 0)
        & (query_ids[:, None] != key_ids[None, :])
    )
    return jnp.where(keep, sims, -1.0)


def by_owner(embeds, cluster):
    rows, width = embeds.shape
    size_x = lax.axis_size("gx")
    size_y = lax.axis_size("gy")
    owners = size_x * size_y
    cap = 2 * rows // owners
    total = owners * cap
    unit = normalised(embeds)
    target = cluster // CLU_OWN
    onehot = (target[:, None] == jnp.arange(owners, dtype=jnp.int32)[None, :]).astype(jnp.int32)
    before = jnp.cumsum(onehot, axis=0) - onehot
    slot = jnp.sum(before * onehot, axis=1)
    place = target * cap + slot
    outgoing = jnp.zeros((total, width), jnp.bfloat16).at[place].set(unit)
    out_labels = jnp.full((total,), -1, jnp.int32).at[place].set(cluster)
    got, got_labels = (
        lax.all_to_all(
            outgoing.reshape(owners, cap, width),
            ("gx", "gy"),
            split_axis=0,
            concat_axis=0,
            tiled=True,
        ),
        lax.all_to_all(
            out_labels.reshape(owners, cap), ("gx", "gy"), split_axis=0, concat_axis=0, tiled=True
        ),
    )
    members = got.reshape(total, width)
    labels = got_labels.reshape(total)
    core = lax.axis_index("gz")
    query_ids = core * total + jnp.arange(total, dtype=jnp.int32)
    keys = lax.all_gather(members, "gz", axis=0, tiled=True)
    key_labels = lax.all_gather(labels, "gz", axis=0, tiled=True)
    key_ids = jnp.arange(keys.shape[0], dtype=jnp.int32)
    best = jnp.maximum(
        jnp.full((total,), -1.0, jnp.float32),
        jnp.max(masked_sims(members, labels, query_ids, keys, key_labels, key_ids), axis=1),
    )
    back = lax.all_to_all(
        best.reshape(owners, cap), ("gx", "gy"), split_axis=0, concat_axis=0, tiled=True
    )
    return back.reshape(total)[place]


def solution(mesh):
    shape = mesh.shape
    ring = shape["gx"] * shape["gy"] == 8 and shape["gy"] == 2 and shape["gz"] == 2
    placed = (P(("parts", "gx", "gy", "gz"), None), P(("parts", "gx", "gy", "gz")))
    return jax.shard_map(
        on_ring if ring else by_owner,
        mesh=mesh,
        in_specs=placed,
        out_specs=P(("parts", "gx", "gy", "gz")),
        check_vma=False,
    )
```

```python
import jax
import jax.numpy as jnp
from jax import lax
from jax.experimental import pallas as pl
from jax.experimental.pallas import tpu as pltpu
from jax.sharding import PartitionSpec as P

CLU_OWN = 16


EPS = 1e-06

GROUP = ("gx", "gy", "gz")


def normalised(block):
    vecs = block.astype(jnp.float32)
    return (vecs * lax.rsqrt(jnp.sum(vecs * vecs, axis=1, keepdims=True) + EPS)).astype(
        jnp.bfloat16
    )


LABEL_ROWS = 16
VMEM_BYTES = 32 * 2**20
NEAR_COST = 1
FIRST_COST = 5
SECOND_COST = 200


def pack_first_kernel(embeds, label, first, raw, line, sems):
    rows, width = embeds.shape
    half = rows // 2
    copies = [
        pltpu.make_async_copy(label, line, sems.at[0]),
        pltpu.make_async_copy(embeds.at[pl.ds(0, half)], raw, sems.at[1]),
    ]
    for copy in copies:
        copy.start()
    copies[0].wait()
    lines = jnp.broadcast_to(line[...].astype(jnp.float32), (LABEL_ROWS, rows))
    first[half:, :rows] = lines.astype(jnp.bfloat16)
    first[half:, rows:] = jnp.zeros((LABEL_ROWS, width - rows), jnp.bfloat16)
    copies[1].wait()
    first[:half, :] = normalised(raw[...])


def pack_second_kernel(embeds, first, second, both, raw, sem):
    half = second.shape[0]
    copy = pltpu.make_async_copy(embeds.at[pl.ds(half, half)], raw, sem)
    copy.start()
    both[:half, :] = first[:half, :]
    both[2 * half :, :] = first[half:, :]
    copy.wait()
    unit = normalised(raw[...])
    second[...] = unit
    both[half : 2 * half, :] = unit


class Block:
    def __init__(self, unit, label):
        self.unit = unit
        self.label = label
        self.rows = unit.shape[0]
        self.along_rows = None

    def column(self):
        if self.along_rows is None:
            self.along_rows = jnp.transpose(jnp.broadcast_to(self.label, (128, self.rows)))
        return self.along_rows


def labels_in(first):
    half = first.shape[0] - LABEL_ROWS
    return first[half:, : 2 * half].astype(jnp.float32)[:1]


def packed(ref):
    rows = ref.shape[0] - LABEL_ROWS
    return Block(ref[:rows, :], ref[rows:, :rows].astype(jnp.float32)[:1])


def whole(first, second):
    half = second.shape[0]
    return Block(jnp.concatenate([first[:half, :], second[...]], axis=0), labels_in(first))


def first_half(first):
    half = first.shape[0] - LABEL_ROWS
    return Block(first[:half, :], labels_in(first)[:, :half])


def second_half(first, second):
    half = second.shape[0]
    return Block(second[...], labels_in(first)[:, half:])


def joined(*blocks):
    return Block(
        jnp.concatenate([block.unit for block in blocks], axis=0),
        jnp.concatenate([block.label for block in blocks], axis=1),
    )


def best_of(queries, *all_keys):
    best = None
    for keys in all_keys:
        sims = lax.dot_general(
            keys.unit, queries.unit, (((1,), (1,)), ((), ())), preferred_element_type=jnp.float32
        )
        pieces = []
        for start in range(0, queries.rows, 128):
            keep = keys.column() == queries.label[:, start : start + 128]
            if keys is queries:
                row = lax.broadcasted_iota(jnp.int32, keep.shape, 0)
                column = lax.broadcasted_iota(jnp.int32, keep.shape, 1) + start
                keep = keep & (row != column)
            found = jnp.where(keep, sims[:, start : start + 128], -1.0)
            pieces.append(jnp.max(found, axis=0, keepdims=True))
        found = jnp.concatenate(pieces, axis=1)
        best = found if best is None else jnp.maximum(best, found)
    return best


def near_kernel(own, prev_a, prev_b, succ_a, succ_b, mine, bundle):
    half = prev_b.shape[0]
    for at, (first, second) in enumerate(((prev_a, prev_b), (succ_a, succ_b))):
        bundle[at, :half, :] = first[:half, :]
        bundle[at, half : 2 * half, :] = second[...]
        bundle[at, 2 * half :, :] = first[half:, :]
    bundle[2] = own[...]
    own = packed(own)
    mine[...] = best_of(own, own, whole(prev_a, prev_b), whole(succ_a, succ_b))


def far_first_kernel(own, prev_a, prev_b, succ_a, succ_b, back_a, ahead_a, found):
    near = packed(own), whole(prev_a, prev_b), whole(succ_a, succ_b)
    rows = joined(first_half(back_a), first_half(ahead_a))
    found[...] = best_of(rows, rows, *near)


def far_second_kernel(
    own, prev_a, prev_b, succ_a, succ_b, back_a, ahead_a, back_b, ahead_b, *refs
):
    first_found, to_back, to_ahead = refs
    near = packed(own), whole(prev_a, prev_b), whole(succ_a, succ_b)
    half = back_b.shape[0]
    first = joined(first_half(back_a), first_half(ahead_a))
    second = joined(second_half(back_a, back_b), second_half(ahead_a, ahead_b))
    found = jnp.maximum(first_found[...], best_of(first, second))
    found_second = best_of(second, second, first, *near)
    to_back[:, :half] = found[:, :half]
    to_back[:, half:] = found_second[:, :half]
    to_ahead[:, :half] = found[:, half:]
    to_ahead[:, half:] = found_second[:, half:]


def far_other_kernel(others, back_a, ahead_a, back_b, ahead_b, *refs):
    back_found, ahead_found, to_back, to_ahead = refs
    back, ahead = whole(back_a, back_b), whole(ahead_a, ahead_b)
    to_back[...] = jnp.maximum(back_found[...], best_of(back, packed(others.at[1])))
    to_ahead[...] = jnp.maximum(ahead_found[...], best_of(ahead, packed(others.at[0])))


def own_kernel(own, others, back_a, ahead_a, back_b, ahead_b, near, mine):
    keys = [packed(others.at[at]) for at in range(3)]
    keys += [whole(back_a, back_b), whole(ahead_a, ahead_b)]
    mine[...] = jnp.maximum(near[...], best_of(packed(own), *keys))


def ring_perms(size_x, size_y, size_z):
    chips = size_x * size_y

    def device(place, core):
        place = place % chips
        x, y = (place, 0) if place < size_x else (chips - 1 - place, 1)
        return (x * size_y + y) * size_z + core

    def perm(to):
        return [
            (device(p, k), device(*to(p, k))) for p in range(chips) for k in range(size_z)
        ]

    def from_prev(place, core):
        return core ^ (place % chips in (0, 1))

    def from_next(place, core):
        return core ^ (place % chips not in (0, 1))

    return {
        "sibling": perm(lambda p, k: (p, 1 - k)),
        "next": perm(lambda p, k: (p + 1, from_prev(p + 1, k))),
        "prev": perm(lambda p, k: (p - 1, from_next(p - 1, k))),
        "on_next": perm(lambda p, k: (p + 1, k)),
        "on_prev": perm(lambda p, k: (p - 1, k)),
        "home_back": perm(lambda p, k: (p - 2, from_prev(p - 1, k))),
        "home_ahead": perm(lambda p, k: (p + 2, from_next(p + 1, k))),
    }


def kernel_call(kernel, inputs, outputs, matmuls):
    vmem = pl.BlockSpec(memory_space=pltpu.VMEM)
    return pl.pallas_call(
        kernel,
        out_shape=outputs,
        in_specs=[vmem] * len(inputs),
        out_specs=[vmem] * len(outputs),
        compiler_params=pltpu.CompilerParams(vmem_limit_bytes=VMEM_BYTES),
        cost_estimate=pl.CostEstimate(
            flops=matmuls * 2**26, bytes_accessed=2**20, transcendentals=0
        ),
        name=kernel.__name__,
    )(*inputs)


def on_ring(embeds, cluster):
    rows, width = embeds.shape
    half = rows // 2
    perms = ring_perms(*(lax.axis_size(a) for a in GROUP))

    def send(value, name):
        return lax.ppermute(value, GROUP, perms[name])

    line = jax.ShapeDtypeStruct((1, rows), jnp.float32)
    anywhere = pl.BlockSpec(memory_space=pl.ANY)
    vmem = pl.BlockSpec(memory_space=pltpu.VMEM)
    params = pltpu.CompilerParams(vmem_limit_bytes=VMEM_BYTES)
    embeds = pltpu.with_memory_space_constraint(embeds, pltpu.HBM)
    label = pltpu.with_memory_space_constraint(cluster.reshape(1, rows), pltpu.HBM)
    own_a = pl.pallas_call(
        pack_first_kernel,
        out_shape=jax.ShapeDtypeStruct((half + LABEL_ROWS, width), jnp.bfloat16),
        in_specs=[anywhere] * 2,
        out_specs=vmem,
        scratch_shapes=[
            pltpu.VMEM((half, width), jnp.bfloat16),
            pltpu.VMEM((1, rows), jnp.int32),
            pltpu.SemaphoreType.DMA((2,)),
        ],
        compiler_params=params,
        name="pack_first",
    )(embeds, label)
    own_b, own = pl.pallas_call(
        pack_second_kernel,
        out_shape=[
            jax.ShapeDtypeStruct((half, width), jnp.bfloat16),
            jax.ShapeDtypeStruct((rows + LABEL_ROWS, width), jnp.bfloat16),
        ],
        in_specs=[anywhere, vmem],
        out_specs=[vmem] * 2,
        scratch_shapes=[pltpu.VMEM((half, width), jnp.bfloat16), pltpu.SemaphoreType.DMA],
        compiler_params=params,
        name="pack_second",
    )(embeds, own_a)
    prev_a, succ_a = send(own_a, "next"), send(own_a, "prev")
    prev_b, succ_b = send(own_b, "next"), send(own_b, "prev")
    back_a, ahead_a = send(prev_a, "on_next"), send(succ_a, "on_prev")
    back_b, ahead_b = send(prev_b, "on_next"), send(succ_b, "on_prev")
    mine, bundle = kernel_call(
        near_kernel,
        [own, prev_a, prev_b, succ_a, succ_b],
        [line, jax.ShapeDtypeStruct((3, rows + LABEL_ROWS, width), jnp.bfloat16)],
        NEAR_COST,
    )
    others = send(bundle, "sibling")
    blocks = [own, prev_a, prev_b, succ_a, succ_b]
    far = [back_a, ahead_a, back_b, ahead_b]
    (first_found,) = kernel_call(
        far_first_kernel, [*blocks, back_a, ahead_a], [line], FIRST_COST
    )
    to_back, to_ahead = kernel_call(
        far_second_kernel, [*blocks, *far, first_found], [line] * 2, SECOND_COST
    )
    to_back, to_ahead = kernel_call(
        far_other_kernel, [others, *far, to_back, to_ahead], [line] * 2, 2
    )
    (mine,) = kernel_call(own_kernel, [own, others, *far, mine], [line], 5)
    best = jnp.maximum(
        mine, jnp.maximum(send(to_back, "home_back"), send(to_ahead, "home_ahead"))
    )
    return best.reshape(rows)


def masked_sims(queries, query_labels, query_ids, keys, key_labels, key_ids):
    sims = jnp.einsum("qd,kd->qk", queries, keys, preferred_element_type=jnp.float32)
    keep = (
        (query_labels[:, None] == key_labels[None, :])
        & (query_labels[:, None] >= 0)
        & (query_ids[:, None] != key_ids[None, :])
    )
    return jnp.where(keep, sims, -1.0)


def by_owner(embeds, cluster):
    rows, width = embeds.shape
    size_x = lax.axis_size("gx")
    size_y = lax.axis_size("gy")
    owners = size_x * size_y
    cap = 2 * rows // owners
    total = owners * cap
    unit = normalised(embeds)
    target = cluster // CLU_OWN
    onehot = (target[:, None] == jnp.arange(owners, dtype=jnp.int32)[None, :]).astype(jnp.int32)
    before = jnp.cumsum(onehot, axis=0) - onehot
    slot = jnp.sum(before * onehot, axis=1)
    place = target * cap + slot
    outgoing = jnp.zeros((total, width), jnp.bfloat16).at[place].set(unit)
    out_labels = jnp.full((total,), -1, jnp.int32).at[place].set(cluster)
    got, got_labels = (
        lax.all_to_all(
            outgoing.reshape(owners, cap, width),
            ("gx", "gy"),
            split_axis=0,
            concat_axis=0,
            tiled=True,
        ),
        lax.all_to_all(
            out_labels.reshape(owners, cap), ("gx", "gy"), split_axis=0, concat_axis=0, tiled=True
        ),
    )
    members = got.reshape(total, width)
    labels = got_labels.reshape(total)
    core = lax.axis_index("gz")
    query_ids = core * total + jnp.arange(total, dtype=jnp.int32)
    keys = lax.all_gather(members, "gz", axis=0, tiled=True)
    key_labels = lax.all_gather(labels, "gz", axis=0, tiled=True)
    key_ids = jnp.arange(keys.shape[0], dtype=jnp.int32)
    best = jnp.maximum(
        jnp.full((total,), -1.0, jnp.float32),
        jnp.max(masked_sims(members, labels, query_ids, keys, key_labels, key_ids), axis=1),
    )
    back = lax.all_to_all(
        best.reshape(owners, cap), ("gx", "gy"), split_axis=0, concat_axis=0, tiled=True
    )
    return back.reshape(total)[place]


def solution(mesh):
    shape = mesh.shape
    ring = shape["gx"] * shape["gy"] == 8 and shape["gy"] == 2 and shape["gz"] == 2
    placed = (P(("parts", "gx", "gy", "gz"), None), P(("parts", "gx", "gy", "gz")))
    return jax.shard_map(
        on_ring if ring else by_owner,
        mesh=mesh,
        in_specs=placed,
        out_specs=P(("parts", "gx", "gy", "gz")),
        check_vma=False,
    )
```

```python
import jax
import jax.numpy as jnp
from jax import lax
from jax.experimental import pallas as pl
from jax.experimental.pallas import tpu as pltpu
from jax.sharding import PartitionSpec as P

CLU_OWN = 16


EPS = 1e-06

GROUP = ("gx", "gy", "gz")


def normalised(block):
    vecs = block.astype(jnp.float32)
    return (vecs * lax.rsqrt(jnp.sum(vecs * vecs, axis=1, keepdims=True) + EPS)).astype(
        jnp.bfloat16
    )


LABEL_ROWS = 16
VMEM_BYTES = 32 * 2**20
OWN_COST = 100
FIRST_COST = 5
SECOND_COST = 5


def pack_kernel(embeds, label, packed, raw, line, sems):
    rows, width = embeds.shape
    half = rows // 2
    copies = [pltpu.make_async_copy(label, line, sems.at[0])]
    for i in range(2):
        part = pl.ds(i * half, half)
        copies.append(pltpu.make_async_copy(embeds.at[part], raw.at[part], sems.at[1 + i]))
    for copy in copies:
        copy.start()
    copies[0].wait()
    lines = jnp.broadcast_to(line[...].astype(jnp.float32), (LABEL_ROWS, rows))
    packed[rows:, :rows] = lines.astype(jnp.bfloat16)
    packed[rows:, rows:] = jnp.zeros((LABEL_ROWS, width - rows), jnp.bfloat16)
    for i in range(2):
        part = pl.ds(i * half, half)
        copies[1 + i].wait()
        packed[part, :] = normalised(raw[part, :])


class Block:
    def __init__(self, unit, label):
        self.unit = unit
        self.label = label
        self.rows = unit.shape[0]
        self.along_rows = None

    def column(self):
        if self.along_rows is None:
            self.along_rows = jnp.transpose(jnp.broadcast_to(self.label, (128, self.rows)))
        return self.along_rows


def unpacked(ref):
    rows = ref.shape[0] - LABEL_ROWS
    return Block(ref[:rows, :], ref[rows:, :rows].astype(jnp.float32)[:1])


def best_of(queries, *all_keys):
    best = None
    for keys in all_keys:
        sims = lax.dot_general(
            keys.unit, queries.unit, (((1,), (1,)), ((), ())), preferred_element_type=jnp.float32
        )
        pieces = []
        for start in range(0, queries.rows, 128):
            keep = keys.column() == queries.label[:, start : start + 128]
            if keys is queries:
                row = lax.broadcasted_iota(jnp.int32, keep.shape, 0)
                column = lax.broadcasted_iota(jnp.int32, keep.shape, 1) + start
                keep = keep & (row != column)
            found = jnp.where(keep, sims[:, start : start + 128], -1.0)
            pieces.append(jnp.max(found, axis=0, keepdims=True))
        found = jnp.concatenate(pieces, axis=1)
        best = found if best is None else jnp.maximum(best, found)
    return best


def rows_kernel(rows, *refs):
    *keys, best = refs
    best[...] = best_of(unpacked(rows), *(unpacked(key) for key in keys))


def last_kernel(rows, *refs):
    *keys, _, best = refs
    best[...] = best_of(unpacked(rows), *(unpacked(key) for key in keys))


def own_kernel(rows, *refs):
    *keys, best = refs
    rows = unpacked(rows)
    best[...] = best_of(rows, rows, *(unpacked(key) for key in keys))


def ring_perms(size_x, size_y, size_z):
    chips = size_x * size_y

    def device(place, core):
        place = place % chips
        x, y = (place, 0) if place < size_x else (chips - 1 - place, 1)
        return (x * size_y + y) * size_z + core

    def perm(to):
        return [
            (device(p, k), device(*to(p, k))) for p in range(chips) for k in range(size_z)
        ]

    step = (1, -1)
    return {
        "sibling": perm(lambda p, k: (p, 1 - k)),
        "lane": perm(lambda p, k: (p + step[k], k)),
        "other_lane": perm(lambda p, k: (p + step[1 - k], 1 - k)),
        "home": perm(lambda p, k: (p - 2 * step[k], k)),
        "home_other": perm(lambda p, k: (p - 2 * step[k], 1 - k)),
    }


def kernel_call(kernel, blocks, cost, name):
    vmem = pl.BlockSpec(memory_space=pltpu.VMEM)
    rows = blocks[0].shape[0] - LABEL_ROWS
    return pl.pallas_call(
        kernel,
        out_shape=jax.ShapeDtypeStruct((1, rows), jnp.float32),
        in_specs=[vmem] * len(blocks),
        out_specs=vmem,
        compiler_params=pltpu.CompilerParams(vmem_limit_bytes=VMEM_BYTES),
        cost_estimate=pl.CostEstimate(
            flops=cost * 2**26, bytes_accessed=2**20, transcendentals=0
        ),
        name=name,
    )(*blocks)


def on_ring(embeds, cluster):
    rows, width = embeds.shape
    perms = ring_perms(*(lax.axis_size(a) for a in GROUP))

    def send(value, name):
        return lax.ppermute(value, GROUP, perms[name])

    anywhere = pl.BlockSpec(memory_space=pl.ANY)
    own = pl.pallas_call(
        pack_kernel,
        out_shape=jax.ShapeDtypeStruct((rows + LABEL_ROWS, width), jnp.bfloat16),
        in_specs=[anywhere] * 2,
        out_specs=pl.BlockSpec(memory_space=pltpu.VMEM),
        scratch_shapes=[
            pltpu.VMEM((rows, width), jnp.bfloat16),
            pltpu.VMEM((1, rows), jnp.int32),
            pltpu.SemaphoreType.DMA((3,)),
        ],
        compiler_params=pltpu.CompilerParams(vmem_limit_bytes=VMEM_BYTES),
        name="pack",
    )(
        pltpu.with_memory_space_constraint(embeds, pltpu.HBM),
        pltpu.with_memory_space_constraint(cluster.reshape(1, rows), pltpu.HBM),
    )
    one_first, one_second = send(own, "lane"), send(own, "other_lane")
    two_first, two_second = send(one_first, "lane"), send(one_second, "lane")
    other = send(own, "sibling")
    beyond = [send(block, "sibling") for block in (one_first, one_second, two_first)]
    chip = [own, other]
    found_first = kernel_call(rows_kernel, [two_first, *chip, *beyond], FIRST_COST, "first")
    mine = kernel_call(
        own_kernel, [own, other, one_first, one_second, *beyond[:2]], OWN_COST, "own"
    )
    found_second = kernel_call(
        last_kernel, [two_second, *chip, *beyond, mine], SECOND_COST, "second"
    )
    best = jnp.maximum(
        mine, jnp.maximum(send(found_first, "home"), send(found_second, "home_other"))
    )
    return best.reshape(rows)


def masked_sims(queries, query_labels, query_ids, keys, key_labels, key_ids):
    sims = jnp.einsum("qd,kd->qk", queries, keys, preferred_element_type=jnp.float32)
    keep = (
        (query_labels[:, None] == key_labels[None, :])
        & (query_labels[:, None] >= 0)
        & (query_ids[:, None] != key_ids[None, :])
    )
    return jnp.where(keep, sims, -1.0)


def by_owner(embeds, cluster):
    rows, width = embeds.shape
    size_x = lax.axis_size("gx")
    size_y = lax.axis_size("gy")
    owners = size_x * size_y
    cap = 2 * rows // owners
    total = owners * cap
    unit = normalised(embeds)
    target = cluster // CLU_OWN
    onehot = (target[:, None] == jnp.arange(owners, dtype=jnp.int32)[None, :]).astype(jnp.int32)
    before = jnp.cumsum(onehot, axis=0) - onehot
    slot = jnp.sum(before * onehot, axis=1)
    place = target * cap + slot
    outgoing = jnp.zeros((total, width), jnp.bfloat16).at[place].set(unit)
    out_labels = jnp.full((total,), -1, jnp.int32).at[place].set(cluster)
    got, got_labels = (
        lax.all_to_all(
            outgoing.reshape(owners, cap, width),
            ("gx", "gy"),
            split_axis=0,
            concat_axis=0,
            tiled=True,
        ),
        lax.all_to_all(
            out_labels.reshape(owners, cap), ("gx", "gy"), split_axis=0, concat_axis=0, tiled=True
        ),
    )
    members = got.reshape(total, width)
    labels = got_labels.reshape(total)
    core = lax.axis_index("gz")
    query_ids = core * total + jnp.arange(total, dtype=jnp.int32)
    keys = lax.all_gather(members, "gz", axis=0, tiled=True)
    key_labels = lax.all_gather(labels, "gz", axis=0, tiled=True)
    key_ids = jnp.arange(keys.shape[0], dtype=jnp.int32)
    best = jnp.maximum(
        jnp.full((total,), -1.0, jnp.float32),
        jnp.max(masked_sims(members, labels, query_ids, keys, key_labels, key_ids), axis=1),
    )
    back = lax.all_to_all(
        best.reshape(owners, cap), ("gx", "gy"), split_axis=0, concat_axis=0, tiled=True
    )
    return back.reshape(total)[place]


def solution(mesh):
    shape = mesh.shape
    ring = shape["gx"] * shape["gy"] == 8 and shape["gy"] == 2 and shape["gz"] == 2
    placed = (P(("parts", "gx", "gy", "gz"), None), P(("parts", "gx", "gy", "gz")))
    return jax.shard_map(
        on_ring if ring else by_owner,
        mesh=mesh,
        in_specs=placed,
        out_specs=P(("parts", "gx", "gy", "gz")),
        check_vma=False,
    )
```

```python
import jax
import jax.numpy as jnp
from jax import lax
from jax.experimental import pallas as pl
from jax.experimental.pallas import tpu as pltpu
from jax.sharding import PartitionSpec as P

CLU_OWN = 16


EPS = 1e-06

GROUP = ("gx", "gy", "gz")


def normalised(block):
    vecs = block.astype(jnp.float32)
    return (vecs * lax.rsqrt(jnp.sum(vecs * vecs, axis=1, keepdims=True) + EPS)).astype(
        jnp.bfloat16
    )


LABEL_ROWS = 16
LANES = 128
VMEM_BYTES = 32 * 2**20
NEAR_COST = 2
OWN_COST = 100
FIRST_COST = 5
SECOND_COST = 5


def pack_kernel(embeds, label, packed, raw, line, sems):
    rows, width = embeds.shape
    half = rows // 2
    copies = [pltpu.make_async_copy(label, line, sems.at[0])]
    for i in range(2):
        part = pl.ds(i * half, half)
        copies.append(pltpu.make_async_copy(embeds.at[part], raw.at[part], sems.at[1 + i]))
    for copy in copies:
        copy.start()
    copies[0].wait()
    row = lax.broadcasted_iota(jnp.int32, (LABEL_ROWS, LANES), 0)
    lines = jnp.zeros((LABEL_ROWS, LANES), jnp.float32)
    for i in range(rows // LANES):
        piece = line[:, i * LANES : (i + 1) * LANES].astype(jnp.float32)
        lines = jnp.where(row == i, piece, lines)
    packed[rows * width // LANES :, :] = lines.astype(jnp.bfloat16)
    for i in range(2):
        copies[1 + i].wait()
        unit = normalised(raw[pl.ds(i * half, half), :])
        for j in range(width // LANES):
            packed[pl.ds(j * rows + i * half, half), :] = unit[:, j * LANES : (j + 1) * LANES]


class Block:
    def __init__(self, packed, rows):
        labels_at = packed.shape[0] - LABEL_ROWS
        columns = [packed[at : at + rows, :] for at in range(0, labels_at, rows)]
        self.unit = jnp.concatenate(columns, axis=1)
        lines = packed[labels_at:, :].astype(jnp.float32)
        self.label = jnp.concatenate([lines[i : i + 1] for i in range(rows // LANES)], axis=1)
        self.rows = rows
        self.along_rows = None

    def column(self):
        if self.along_rows is None:
            self.along_rows = jnp.transpose(jnp.broadcast_to(self.label, (LANES, self.rows)))
        return self.along_rows


def best_of(queries, *all_keys):
    best = None
    for keys in all_keys:
        sims = lax.dot_general(
            keys.unit, queries.unit, (((1,), (1,)), ((), ())), preferred_element_type=jnp.float32
        )
        pieces = []
        for start in range(0, queries.rows, LANES):
            keep = keys.column() == queries.label[:, start : start + LANES]
            if keys is queries:
                row = lax.broadcasted_iota(jnp.int32, keep.shape, 0)
                column = lax.broadcasted_iota(jnp.int32, keep.shape, 1) + start
                keep = keep & (row != column)
            found = jnp.where(keep, sims[:, start : start + LANES], -1.0)
            pieces.append(jnp.max(found, axis=0, keepdims=True))
        found = jnp.concatenate(pieces, axis=1)
        best = found if best is None else jnp.maximum(best, found)
    return best


def near_kernel(rows, other, best):
    size = best.shape[1]
    rows = Block(rows, size)
    best[...] = best_of(rows, rows, Block(other, size))


def rows_kernel(rows, *refs):
    *keys, best = refs
    size = best.shape[1]
    best[...] = best_of(Block(rows, size), *(Block(key, size) for key in keys))


def last_kernel(rows, *refs):
    *keys, _, best = refs
    rows_kernel(rows, *keys, best)


def more_kernel(rows, *refs):
    *keys, found, best = refs
    rows_kernel(rows, *keys, best)
    best[...] = jnp.maximum(best[...], found[...])


def ring_perms(size_x, size_y, size_z):
    chips = size_x * size_y

    def device(place, core):
        place = place % chips
        x, y = (place, 0) if place < size_x else (chips - 1 - place, 1)
        return (x * size_y + y) * size_z + core

    def perm(to):
        return [
            (device(p, k), device(*to(p, k))) for p in range(chips) for k in range(size_z)
        ]

    step = (1, -1)
    return {
        "sibling": perm(lambda p, k: (p, 1 - k)),
        "lane": perm(lambda p, k: (p + step[k], k)),
        "other_lane": perm(lambda p, k: (p + step[1 - k], 1 - k)),
        "home": perm(lambda p, k: (p - 2 * step[k], k)),
        "home_other": perm(lambda p, k: (p - 2 * step[k], 1 - k)),
    }


def kernel_call(kernel, rows, blocks, cost, name):
    vmem = pl.BlockSpec(memory_space=pltpu.VMEM)
    return pl.pallas_call(
        kernel,
        out_shape=jax.ShapeDtypeStruct((1, rows), jnp.float32),
        in_specs=[vmem] * len(blocks),
        out_specs=vmem,
        compiler_params=pltpu.CompilerParams(vmem_limit_bytes=VMEM_BYTES),
        cost_estimate=pl.CostEstimate(
            flops=cost * 2**26, bytes_accessed=2**20, transcendentals=0
        ),
        name=name,
    )(*blocks)


def on_ring(embeds, cluster):
    rows, width = embeds.shape
    perms = ring_perms(*(lax.axis_size(a) for a in GROUP))

    def send(value, name):
        return lax.ppermute(value, GROUP, perms[name])

    anywhere = pl.BlockSpec(memory_space=pl.ANY)
    own = pl.pallas_call(
        pack_kernel,
        out_shape=jax.ShapeDtypeStruct((rows * width // LANES + LABEL_ROWS, LANES), jnp.bfloat16),
        in_specs=[anywhere] * 2,
        out_specs=pl.BlockSpec(memory_space=pltpu.VMEM),
        scratch_shapes=[
            pltpu.VMEM((rows, width), jnp.bfloat16),
            pltpu.VMEM((1, rows), jnp.int32),
            pltpu.SemaphoreType.DMA((3,)),
        ],
        compiler_params=pltpu.CompilerParams(vmem_limit_bytes=VMEM_BYTES),
        name="pack",
    )(
        pltpu.with_memory_space_constraint(embeds, pltpu.HBM),
        pltpu.with_memory_space_constraint(cluster.reshape(1, rows), pltpu.HBM),
    )
    other = send(own, "sibling")
    near = kernel_call(near_kernel, rows, [own, other], NEAR_COST, "near")
    own_again, near = lax.optimization_barrier((own, near))
    one_first, one_second = send(own, "lane"), send(own_again, "other_lane")
    two_first, two_second = send(one_first, "lane"), send(one_second, "lane")
    beyond = [send(block, "sibling") for block in (one_first, one_second, two_first)]
    keys = [own, other, *beyond]
    mine = kernel_call(
        more_kernel, rows, [own, one_first, one_second, *beyond[:2], near], OWN_COST, "own"
    )
    found_first = kernel_call(
        last_kernel, rows, [two_first, *keys, mine], FIRST_COST, "first"
    )
    found_second = kernel_call(
        last_kernel, rows, [two_second, *keys, found_first], SECOND_COST, "second"
    )
    best = jnp.maximum(
        mine, jnp.maximum(send(found_first, "home"), send(found_second, "home_other"))
    )
    return best.reshape(rows)


def masked_sims(queries, query_labels, query_ids, keys, key_labels, key_ids):
    sims = jnp.einsum("qd,kd->qk", queries, keys, preferred_element_type=jnp.float32)
    keep = (
        (query_labels[:, None] == key_labels[None, :])
        & (query_labels[:, None] >= 0)
        & (query_ids[:, None] != key_ids[None, :])
    )
    return jnp.where(keep, sims, -1.0)


def by_owner(embeds, cluster):
    rows, width = embeds.shape
    size_x = lax.axis_size("gx")
    size_y = lax.axis_size("gy")
    owners = size_x * size_y
    cap = 2 * rows // owners
    total = owners * cap
    unit = normalised(embeds)
    target = cluster // CLU_OWN
    onehot = (target[:, None] == jnp.arange(owners, dtype=jnp.int32)[None, :]).astype(jnp.int32)
    before = jnp.cumsum(onehot, axis=0) - onehot
    slot = jnp.sum(before * onehot, axis=1)
    place = target * cap + slot
    outgoing = jnp.zeros((total, width), jnp.bfloat16).at[place].set(unit)
    out_labels = jnp.full((total,), -1, jnp.int32).at[place].set(cluster)
    got, got_labels = (
        lax.all_to_all(
            outgoing.reshape(owners, cap, width),
            ("gx", "gy"),
            split_axis=0,
            concat_axis=0,
            tiled=True,
        ),
        lax.all_to_all(
            out_labels.reshape(owners, cap), ("gx", "gy"), split_axis=0, concat_axis=0, tiled=True
        ),
    )
    members = got.reshape(total, width)
    labels = got_labels.reshape(total)
    core = lax.axis_index("gz")
    query_ids = core * total + jnp.arange(total, dtype=jnp.int32)
    keys = lax.all_gather(members, "gz", axis=0, tiled=True)
    key_labels = lax.all_gather(labels, "gz", axis=0, tiled=True)
    key_ids = jnp.arange(keys.shape[0], dtype=jnp.int32)
    best = jnp.maximum(
        jnp.full((total,), -1.0, jnp.float32),
        jnp.max(masked_sims(members, labels, query_ids, keys, key_labels, key_ids), axis=1),
    )
    back = lax.all_to_all(
        best.reshape(owners, cap), ("gx", "gy"), split_axis=0, concat_axis=0, tiled=True
    )
    return back.reshape(total)[place]


def solution(mesh):
    shape = mesh.shape
    ring = shape["gx"] * shape["gy"] == 8 and shape["gy"] == 2 and shape["gz"] == 2
    placed = (P(("parts", "gx", "gy", "gz"), None), P(("parts", "gx", "gy", "gz")))
    return jax.shard_map(
        on_ring if ring else by_owner,
        mesh=mesh,
        in_specs=placed,
        out_specs=P(("parts", "gx", "gy", "gz")),
        check_vma=False,
    )
```

```python
import jax
import jax.numpy as jnp
from jax import lax
from jax.experimental import pallas as pl
from jax.experimental.pallas import tpu as pltpu
from jax.sharding import PartitionSpec as P

CLU_OWN = 16


EPS = 1e-06

GROUP = ("gx", "gy", "gz")


def normalised(block):
    vecs = block.astype(jnp.float32)
    return (vecs * lax.rsqrt(jnp.sum(vecs * vecs, axis=1, keepdims=True) + EPS)).astype(
        jnp.bfloat16
    )


LANES = 128
LABEL_ROWS = 16
VMEM_BYTES = 32 * 2**20
NEAR_COST = 1
FIRST_COST = 5
BACK_COST = 2
SECOND_COST = 200


def put_unit(unit, chunk, at, size):
    count, width = unit.shape
    for j in range(width // LANES):
        chunk[j * size + at : j * size + at + count, :] = unit[:, j * LANES : (j + 1) * LANES]


def pack_first_kernel(embeds, label, first, raw, line, sems):
    rows, width = embeds.shape
    half = rows // 2
    copies = [
        pltpu.make_async_copy(label, line, sems.at[0]),
        pltpu.make_async_copy(embeds.at[pl.ds(0, half)], raw, sems.at[1]),
    ]
    for copy in copies:
        copy.start()
    copies[0].wait()
    row = lax.broadcasted_iota(jnp.int32, (LABEL_ROWS, LANES), 0)
    lines = jnp.zeros((LABEL_ROWS, LANES), jnp.float32)
    for i in range(rows // LANES):
        piece = line[:, i * LANES : (i + 1) * LANES].astype(jnp.float32)
        lines = jnp.where(row == i, piece, lines)
    first[half * width // LANES :, :] = lines.astype(jnp.bfloat16)
    copies[1].wait()
    put_unit(normalised(raw[...]), first, 0, half)


def pack_second_kernel(embeds, first, second, both):
    rows, width = embeds.shape
    half = rows // 2
    unit = normalised(embeds[half:, :])
    put_unit(unit, second, 0, half)
    put_chunks(first, second, both, rows)


def put_chunks(first, second, both, rows):
    size = second.shape[0]
    half = rows // 2
    for at in range(0, size, half):
        both[2 * at : 2 * at + half, :] = first[at : at + half, :]
        both[2 * at + half : 2 * (at + half), :] = second[at : at + half, :]
    both[2 * size :, :] = first[size:, :]


class Block:
    def __init__(self, unit, label):
        self.unit = unit
        self.label = label
        self.rows = unit.shape[0]
        self.along_rows = None

    def column(self):
        if self.along_rows is None:
            self.along_rows = jnp.transpose(jnp.broadcast_to(self.label, (LANES, self.rows)))
        return self.along_rows


def unit_in(chunk, rows, end):
    return jnp.concatenate([chunk[at : at + rows, :] for at in range(0, end, rows)], axis=1)


def labels_in(first, rows):
    lines = first[first.shape[0] - LABEL_ROWS :, :].astype(jnp.float32)
    return jnp.concatenate([lines[i : i + 1] for i in range(rows // LANES)], axis=1)


def packed(both, rows):
    return Block(unit_in(both, rows, both.shape[0] - LABEL_ROWS), labels_in(both, rows))


def first_half(first, rows):
    half = rows // 2
    unit = unit_in(first, half, first.shape[0] - LABEL_ROWS)
    return Block(unit, labels_in(first, rows)[:, :half])


def second_half(first, second, rows):
    half = rows // 2
    return Block(unit_in(second, half, second.shape[0]), labels_in(first, rows)[:, half:])


def whole(first, second, rows):
    return joined(first_half(first, rows), second_half(first, second, rows))


def joined(*blocks):
    return Block(
        jnp.concatenate([block.unit for block in blocks], axis=0),
        jnp.concatenate([block.label for block in blocks], axis=1),
    )


def best_of(queries, *all_keys):
    best = None
    for keys in all_keys:
        sims = lax.dot_general(
            keys.unit, queries.unit, (((1,), (1,)), ((), ())), preferred_element_type=jnp.float32
        )
        pieces = []
        for start in range(0, queries.rows, LANES):
            keep = keys.column() == queries.label[:, start : start + LANES]
            if keys is queries:
                row = lax.broadcasted_iota(jnp.int32, keep.shape, 0)
                column = lax.broadcasted_iota(jnp.int32, keep.shape, 1) + start
                keep = keep & (row != column)
            found = jnp.where(keep, sims[:, start : start + LANES], -1.0)
            pieces.append(jnp.max(found, axis=0, keepdims=True))
        found = jnp.concatenate(pieces, axis=1)
        best = found if best is None else jnp.maximum(best, found)
    return best


def near_kernel(own, prev_a, prev_b, succ_a, succ_b, mine, bundle):
    rows = mine.shape[1]
    put_chunks(prev_a, prev_b, bundle.at[0], rows)
    put_chunks(succ_a, succ_b, bundle.at[1], rows)
    bundle[2] = own[...]
    own = packed(own, rows)
    mine[...] = best_of(own, own, whole(prev_a, prev_b, rows), whole(succ_a, succ_b, rows))


def far_first_kernel(own, prev_a, prev_b, succ_a, succ_b, back_a, ahead_a, found):
    rows = found.shape[1]
    near = packed(own, rows), whole(prev_a, prev_b, rows), whole(succ_a, succ_b, rows)
    queries = joined(first_half(back_a, rows), first_half(ahead_a, rows))
    found[...] = best_of(queries, queries, *near)


def far_back_kernel(own, succ_a, succ_b, back_a, ahead_a, back_b, found, back, ahead):
    rows = found.shape[1]
    half = rows // 2
    rest, first = second_half(back_a, back_b, rows), first_half(ahead_a, rows)
    back[:, :half] = found[:, :half]
    back[:, half:] = best_of(rest, packed(own, rows), whole(succ_a, succ_b, rows), first)
    ahead[...] = jnp.maximum(found[:, half:], best_of(first, rest))


def far_second_kernel(own, prev_a, prev_b, back_a, ahead_a, back_b, ahead_b, *refs):
    back_found, ahead_found, to_back, to_ahead = refs
    rows = to_back.shape[1]
    half = rows // 2
    back, rest = whole(back_a, back_b, rows), second_half(ahead_a, ahead_b, rows)
    to_back[...] = jnp.maximum(back_found[...], best_of(back, rest))
    to_ahead[:, :half] = ahead_found[...]
    to_ahead[:, half:] = best_of(rest, packed(own, rows), whole(prev_a, prev_b, rows), back)


def far_other_kernel(others, back_a, ahead_a, back_b, ahead_b, *refs):
    back_found, ahead_found, to_back, to_ahead = refs
    rows = to_back.shape[1]
    back, ahead = whole(back_a, back_b, rows), whole(ahead_a, ahead_b, rows)
    prev, succ = packed(others.at[0], rows), packed(others.at[1], rows)
    to_back[...] = jnp.maximum(back_found[...], best_of(back, succ))
    to_ahead[...] = jnp.maximum(ahead_found[...], best_of(ahead, prev))


def own_kernel(own, others, back_a, ahead_a, back_b, ahead_b, near, mine):
    rows = mine.shape[1]
    keys = [packed(others.at[at], rows) for at in range(3)]
    keys += [whole(back_a, back_b, rows), whole(ahead_a, ahead_b, rows)]
    mine[...] = jnp.maximum(near[...], best_of(packed(own, rows), *keys))


def ring_perms(size_x, size_y, size_z):
    chips = size_x * size_y

    def device(place, core):
        place = place % chips
        x, y = (place, 0) if place < size_x else (chips - 1 - place, 1)
        return (x * size_y + y) * size_z + core

    def perm(to):
        return [
            (device(p, k), device(*to(p, k))) for p in range(chips) for k in range(size_z)
        ]

    def from_prev(place, core):
        return core ^ (place % chips in (0, 1))

    def from_next(place, core):
        return core ^ (place % chips not in (0, 1))

    return {
        "sibling": perm(lambda p, k: (p, 1 - k)),
        "next": perm(lambda p, k: (p + 1, from_prev(p + 1, k))),
        "prev": perm(lambda p, k: (p - 1, from_next(p - 1, k))),
        "on_next": perm(lambda p, k: (p + 1, k)),
        "on_prev": perm(lambda p, k: (p - 1, k)),
        "home_back": perm(lambda p, k: (p - 2, from_prev(p - 1, k))),
        "home_ahead": perm(lambda p, k: (p + 2, from_next(p + 1, k))),
    }


def kernel_call(kernel, inputs, outputs, matmuls):
    vmem = pl.BlockSpec(memory_space=pltpu.VMEM)
    return pl.pallas_call(
        kernel,
        out_shape=outputs,
        in_specs=[vmem] * len(inputs),
        out_specs=[vmem] * len(outputs),
        compiler_params=pltpu.CompilerParams(vmem_limit_bytes=VMEM_BYTES),
        cost_estimate=pl.CostEstimate(
            flops=matmuls * 2**26, bytes_accessed=2**20, transcendentals=0
        ),
        name=kernel.__name__,
    )(*inputs)


def on_ring(embeds, cluster):
    rows, width = embeds.shape
    half = rows // 2
    perms = ring_perms(*(lax.axis_size(a) for a in GROUP))

    def send(value, name):
        return lax.ppermute(value, GROUP, perms[name])

    line = jax.ShapeDtypeStruct((1, rows), jnp.float32)
    half_line = jax.ShapeDtypeStruct((1, half), jnp.float32)

    def chunk(count, labels):
        size = count * width // LANES + labels * LABEL_ROWS
        return jax.ShapeDtypeStruct((size, LANES), jnp.bfloat16)

    anywhere = pl.BlockSpec(memory_space=pl.ANY)
    vmem = pl.BlockSpec(memory_space=pltpu.VMEM)
    own_a = pl.pallas_call(
        pack_first_kernel,
        out_shape=chunk(half, True),
        in_specs=[anywhere] * 2,
        out_specs=vmem,
        scratch_shapes=[
            pltpu.VMEM((half, width), jnp.bfloat16),
            pltpu.VMEM((1, rows), jnp.int32),
            pltpu.SemaphoreType.DMA((2,)),
        ],
        compiler_params=pltpu.CompilerParams(vmem_limit_bytes=VMEM_BYTES),
        name="pack_first",
    )(
        pltpu.with_memory_space_constraint(embeds, pltpu.HBM),
        pltpu.with_memory_space_constraint(cluster.reshape(1, rows), pltpu.HBM),
    )
    own_b, own = kernel_call(
        pack_second_kernel, [embeds, own_a], [chunk(half, False), chunk(rows, True)], 1
    )
    prev_a, succ_a = send(own_a, "next"), send(own_a, "prev")
    prev_b, succ_b = send(own_b, "next"), send(own_b, "prev")
    back_a, ahead_a = send(prev_a, "on_next"), send(succ_a, "on_prev")
    back_b, ahead_b = send(prev_b, "on_next"), send(succ_b, "on_prev")
    prev, succ, far = [prev_a, prev_b], [succ_a, succ_b], [back_a, ahead_a, back_b, ahead_b]
    bundle_shape = jax.ShapeDtypeStruct((3, *chunk(rows, True).shape), jnp.bfloat16)
    mine, bundle = kernel_call(near_kernel, [own, *prev, *succ], [line, bundle_shape], NEAR_COST)
    others = send(bundle, "sibling")
    (found,) = kernel_call(
        far_first_kernel, [own, *prev, *succ, back_a, ahead_a], [line], FIRST_COST
    )
    found = kernel_call(
        far_back_kernel, [own, *succ, back_a, ahead_a, back_b, found], [line, half_line], BACK_COST
    )
    found = kernel_call(far_second_kernel, [own, *prev, *far, *found], [line] * 2, SECOND_COST)
    to_back, to_ahead = kernel_call(far_other_kernel, [others, *far, *found], [line] * 2, 2)
    (mine,) = kernel_call(own_kernel, [own, others, *far, mine], [line], 5)
    best = jnp.maximum(
        mine, jnp.maximum(send(to_back, "home_back"), send(to_ahead, "home_ahead"))
    )
    return best.reshape(rows)


def masked_sims(queries, query_labels, query_ids, keys, key_labels, key_ids):
    sims = jnp.einsum("qd,kd->qk", queries, keys, preferred_element_type=jnp.float32)
    keep = (
        (query_labels[:, None] == key_labels[None, :])
        & (query_labels[:, None] >= 0)
        & (query_ids[:, None] != key_ids[None, :])
    )
    return jnp.where(keep, sims, -1.0)


def by_owner(embeds, cluster):
    rows, width = embeds.shape
    size_x = lax.axis_size("gx")
    size_y = lax.axis_size("gy")
    owners = size_x * size_y
    cap = 2 * rows // owners
    total = owners * cap
    unit = normalised(embeds)
    target = cluster // CLU_OWN
    onehot = (target[:, None] == jnp.arange(owners, dtype=jnp.int32)[None, :]).astype(jnp.int32)
    before = jnp.cumsum(onehot, axis=0) - onehot
    slot = jnp.sum(before * onehot, axis=1)
    place = target * cap + slot
    outgoing = jnp.zeros((total, width), jnp.bfloat16).at[place].set(unit)
    out_labels = jnp.full((total,), -1, jnp.int32).at[place].set(cluster)
    got, got_labels = (
        lax.all_to_all(
            outgoing.reshape(owners, cap, width),
            ("gx", "gy"),
            split_axis=0,
            concat_axis=0,
            tiled=True,
        ),
        lax.all_to_all(
            out_labels.reshape(owners, cap), ("gx", "gy"), split_axis=0, concat_axis=0, tiled=True
        ),
    )
    members = got.reshape(total, width)
    labels = got_labels.reshape(total)
    core = lax.axis_index("gz")
    query_ids = core * total + jnp.arange(total, dtype=jnp.int32)
    keys = lax.all_gather(members, "gz", axis=0, tiled=True)
    key_labels = lax.all_gather(labels, "gz", axis=0, tiled=True)
    key_ids = jnp.arange(keys.shape[0], dtype=jnp.int32)
    best = jnp.maximum(
        jnp.full((total,), -1.0, jnp.float32),
        jnp.max(masked_sims(members, labels, query_ids, keys, key_labels, key_ids), axis=1),
    )
    back = lax.all_to_all(
        best.reshape(owners, cap), ("gx", "gy"), split_axis=0, concat_axis=0, tiled=True
    )
    return back.reshape(total)[place]


def solution(mesh):
    shape = mesh.shape
    ring = shape["gx"] * shape["gy"] == 8 and shape["gy"] == 2 and shape["gz"] == 2
    placed = (P(("parts", "gx", "gy", "gz"), None), P(("parts", "gx", "gy", "gz")))
    return jax.shard_map(
        on_ring if ring else by_owner,
        mesh=mesh,
        in_specs=placed,
        out_specs=P(("parts", "gx", "gy", "gz")),
        check_vma=False,
    )
```

```python
import jax
import jax.numpy as jnp
from jax import lax
from jax.experimental import pallas as pl
from jax.experimental.pallas import tpu as pltpu
from jax.sharding import PartitionSpec as P

CLU_OWN = 16


EPS = 1e-06

GROUP = ("gx", "gy", "gz")


def normalised(block):
    vecs = block.astype(jnp.float32)
    return (vecs * lax.rsqrt(jnp.sum(vecs * vecs, axis=1, keepdims=True) + EPS)).astype(
        jnp.bfloat16
    )


LANES = 128
LABEL_ROWS = 16
VMEM_BYTES = 32 * 2**20
NEAR_COST = 1
FIRST_COST = 200
BACK_COST = 2
LAST_COST = 5


def put_unit(unit, chunk, at, size):
    count, width = unit.shape
    for j in range(width // LANES):
        chunk[j * size + at : j * size + at + count, :] = unit[:, j * LANES : (j + 1) * LANES]


def pack_first_kernel(embeds, label, first, raw, line, sems):
    rows, width = embeds.shape
    half = rows // 2
    copies = [
        pltpu.make_async_copy(label, line, sems.at[0]),
        pltpu.make_async_copy(embeds.at[pl.ds(0, half)], raw, sems.at[1]),
    ]
    for copy in copies:
        copy.start()
    copies[0].wait()
    row = lax.broadcasted_iota(jnp.int32, (LABEL_ROWS, LANES), 0)
    lines = jnp.zeros((LABEL_ROWS, LANES), jnp.float32)
    for i in range(rows // LANES):
        piece = line[:, i * LANES : (i + 1) * LANES].astype(jnp.float32)
        lines = jnp.where(row == i, piece, lines)
    first[half * width // LANES :, :] = lines.astype(jnp.bfloat16)
    copies[1].wait()
    put_unit(normalised(raw[...]), first, 0, half)


def pack_second_kernel(embeds, first, second, both):
    rows, width = embeds.shape
    half = rows // 2
    unit = normalised(embeds[half:, :])
    put_unit(unit, second, 0, half)
    put_chunks(first, second, both, rows)


def put_chunks(first, second, both, rows):
    size = second.shape[0]
    half = rows // 2
    for at in range(0, size, half):
        both[2 * at : 2 * at + half, :] = first[at : at + half, :]
        both[2 * at + half : 2 * (at + half), :] = second[at : at + half, :]
    both[2 * size :, :] = first[size:, :]


class Block:
    def __init__(self, unit, label):
        self.unit = unit
        self.label = label
        self.rows = unit.shape[0]
        self.along_rows = None

    def column(self):
        if self.along_rows is None:
            self.along_rows = jnp.transpose(jnp.broadcast_to(self.label, (LANES, self.rows)))
        return self.along_rows


def unit_in(chunk, rows, end):
    return jnp.concatenate([chunk[at : at + rows, :] for at in range(0, end, rows)], axis=1)


def labels_in(first, rows):
    lines = first[first.shape[0] - LABEL_ROWS :, :].astype(jnp.float32)
    return jnp.concatenate([lines[i : i + 1] for i in range(rows // LANES)], axis=1)


def packed(both, rows):
    return Block(unit_in(both, rows, both.shape[0] - LABEL_ROWS), labels_in(both, rows))


def first_half(first, rows):
    half = rows // 2
    unit = unit_in(first, half, first.shape[0] - LABEL_ROWS)
    return Block(unit, labels_in(first, rows)[:, :half])


def second_half(first, second, rows):
    half = rows // 2
    return Block(unit_in(second, half, second.shape[0]), labels_in(first, rows)[:, half:])


def whole(first, second, rows):
    return joined(first_half(first, rows), second_half(first, second, rows))


def joined(*blocks):
    return Block(
        jnp.concatenate([block.unit for block in blocks], axis=0),
        jnp.concatenate([block.label for block in blocks], axis=1),
    )


def best_of(queries, *all_keys):
    best = None
    for keys in all_keys:
        sims = lax.dot_general(
            keys.unit, queries.unit, (((1,), (1,)), ((), ())), preferred_element_type=jnp.float32
        )
        pieces = []
        for start in range(0, queries.rows, LANES):
            keep = keys.column() == queries.label[:, start : start + LANES]
            if keys is queries:
                row = lax.broadcasted_iota(jnp.int32, keep.shape, 0)
                column = lax.broadcasted_iota(jnp.int32, keep.shape, 1) + start
                keep = keep & (row != column)
            found = jnp.where(keep, sims[:, start : start + LANES], -1.0)
            pieces.append(jnp.max(found, axis=0, keepdims=True))
        found = jnp.concatenate(pieces, axis=1)
        best = found if best is None else jnp.maximum(best, found)
    return best


def near_kernel(own, prev_a, prev_b, succ_a, succ_b, mine, bundle):
    rows = mine.shape[1]
    put_chunks(prev_a, prev_b, bundle.at[0], rows)
    put_chunks(succ_a, succ_b, bundle.at[1], rows)
    bundle[2] = own[...]
    own = packed(own, rows)
    mine[...] = best_of(own, own, whole(prev_a, prev_b, rows), whole(succ_a, succ_b, rows))


def far_first_kernel(own, prev_a, prev_b, succ_a, succ_b, back_a, ahead_a, found):
    rows = found.shape[1]
    near = packed(own, rows), whole(prev_a, prev_b, rows), whole(succ_a, succ_b, rows)
    queries = joined(first_half(back_a, rows), first_half(ahead_a, rows))
    found[...] = best_of(queries, queries, *near)


def far_back_kernel(own, others, succ_a, succ_b, back_a, ahead_a, back_b, found, back, ahead):
    rows = found.shape[1]
    half = rows // 2
    prev_other, succ_other = packed(others.at[0], rows), packed(others.at[1], rows)
    first, rest = first_half(back_a, rows), second_half(back_a, back_b, rows)
    first_ahead = first_half(ahead_a, rows)
    keys = packed(own, rows), whole(succ_a, succ_b, rows), first_ahead
    both = best_of(joined(first, rest), succ_other)
    back[:, :half] = jnp.maximum(found[:, :half], both[:, :half])
    back[:, half:] = jnp.maximum(best_of(rest, *keys), both[:, half:])
    ahead[...] = jnp.maximum(found[:, half:], best_of(first_ahead, rest, prev_other))


def far_last_kernel(own, others, prev_a, prev_b, back_a, ahead_a, back_b, ahead_b, *refs):
    back_found, ahead_found, to_back, to_ahead = refs
    rows = to_back.shape[1]
    half = rows // 2
    back, rest = whole(back_a, back_b, rows), second_half(ahead_a, ahead_b, rows)
    keys = packed(own, rows), whole(prev_a, prev_b, rows), packed(others.at[0], rows), back
    to_back[...] = jnp.maximum(back_found[...], best_of(back, rest))
    to_ahead[:, :half] = ahead_found[...]
    to_ahead[:, half:] = best_of(rest, *keys)


def own_kernel(own, others, back_a, ahead_a, back_b, ahead_b, near, mine):
    rows = mine.shape[1]
    keys = [packed(others.at[at], rows) for at in range(3)]
    keys += [whole(back_a, back_b, rows), whole(ahead_a, ahead_b, rows)]
    mine[...] = jnp.maximum(near[...], best_of(packed(own, rows), *keys))


def ring_perms(size_x, size_y, size_z):
    chips = size_x * size_y

    def device(place, core):
        place = place % chips
        x, y = (place, 0) if place < size_x else (chips - 1 - place, 1)
        return (x * size_y + y) * size_z + core

    def perm(to):
        return [
            (device(p, k), device(*to(p, k))) for p in range(chips) for k in range(size_z)
        ]

    def from_prev(place, core):
        return core ^ (place % chips in (0, 1))

    def from_next(place, core):
        return core ^ (place % chips not in (0, 1))

    return {
        "sibling": perm(lambda p, k: (p, 1 - k)),
        "next": perm(lambda p, k: (p + 1, from_prev(p + 1, k))),
        "prev": perm(lambda p, k: (p - 1, from_next(p - 1, k))),
        "on_next": perm(lambda p, k: (p + 1, k)),
        "on_prev": perm(lambda p, k: (p - 1, k)),
        "home_back": perm(lambda p, k: (p - 2, from_prev(p - 1, k))),
        "home_ahead": perm(lambda p, k: (p + 2, from_next(p + 1, k))),
    }


def kernel_call(kernel, inputs, outputs, matmuls):
    vmem = pl.BlockSpec(memory_space=pltpu.VMEM)
    return pl.pallas_call(
        kernel,
        out_shape=outputs,
        in_specs=[vmem] * len(inputs),
        out_specs=[vmem] * len(outputs),
        compiler_params=pltpu.CompilerParams(vmem_limit_bytes=VMEM_BYTES),
        cost_estimate=pl.CostEstimate(
            flops=matmuls * 2**26, bytes_accessed=2**20, transcendentals=0
        ),
        name=kernel.__name__,
    )(*inputs)


def on_ring(embeds, cluster):
    rows, width = embeds.shape
    half = rows // 2
    perms = ring_perms(*(lax.axis_size(a) for a in GROUP))

    def send(value, name):
        return lax.ppermute(value, GROUP, perms[name])

    line = jax.ShapeDtypeStruct((1, rows), jnp.float32)
    half_line = jax.ShapeDtypeStruct((1, half), jnp.float32)

    def chunk(count, labels):
        size = count * width // LANES + labels * LABEL_ROWS
        return jax.ShapeDtypeStruct((size, LANES), jnp.bfloat16)

    anywhere = pl.BlockSpec(memory_space=pl.ANY)
    vmem = pl.BlockSpec(memory_space=pltpu.VMEM)
    own_a = pl.pallas_call(
        pack_first_kernel,
        out_shape=chunk(half, True),
        in_specs=[anywhere] * 2,
        out_specs=vmem,
        scratch_shapes=[
            pltpu.VMEM((half, width), jnp.bfloat16),
            pltpu.VMEM((1, rows), jnp.int32),
            pltpu.SemaphoreType.DMA((2,)),
        ],
        compiler_params=pltpu.CompilerParams(vmem_limit_bytes=VMEM_BYTES),
        name="pack_first",
    )(
        pltpu.with_memory_space_constraint(embeds, pltpu.HBM),
        pltpu.with_memory_space_constraint(cluster.reshape(1, rows), pltpu.HBM),
    )
    own_b, own = kernel_call(
        pack_second_kernel, [embeds, own_a], [chunk(half, False), chunk(rows, True)], 1
    )
    prev_a, succ_a = send(own_a, "next"), send(own_a, "prev")
    prev_b, succ_b = send(own_b, "next"), send(own_b, "prev")
    back_a, ahead_a = send(prev_a, "on_next"), send(succ_a, "on_prev")
    back_b, ahead_b = send(prev_b, "on_next"), send(succ_b, "on_prev")
    prev, succ, far = [prev_a, prev_b], [succ_a, succ_b], [back_a, ahead_a, back_b, ahead_b]
    bundle_shape = jax.ShapeDtypeStruct((3, *chunk(rows, True).shape), jnp.bfloat16)
    mine, bundle = kernel_call(near_kernel, [own, *prev, *succ], [line, bundle_shape], NEAR_COST)
    others = send(bundle, "sibling")
    (found,) = kernel_call(
        far_first_kernel, [own, *prev, *succ, back_a, ahead_a], [line], FIRST_COST
    )
    found = kernel_call(
        far_back_kernel,
        [own, others, *succ, back_a, ahead_a, back_b, found],
        [line, half_line],
        BACK_COST,
    )
    to_back, to_ahead = kernel_call(
        far_last_kernel, [own, others, *prev, *far, *found], [line] * 2, LAST_COST
    )
    (mine,) = kernel_call(own_kernel, [own, others, *far, mine], [line], 5)
    best = jnp.maximum(
        mine, jnp.maximum(send(to_back, "home_back"), send(to_ahead, "home_ahead"))
    )
    return best.reshape(rows)


def masked_sims(queries, query_labels, query_ids, keys, key_labels, key_ids):
    sims = jnp.einsum("qd,kd->qk", queries, keys, preferred_element_type=jnp.float32)
    keep = (
        (query_labels[:, None] == key_labels[None, :])
        & (query_labels[:, None] >= 0)
        & (query_ids[:, None] != key_ids[None, :])
    )
    return jnp.where(keep, sims, -1.0)


def by_owner(embeds, cluster):
    rows, width = embeds.shape
    size_x = lax.axis_size("gx")
    size_y = lax.axis_size("gy")
    owners = size_x * size_y
    cap = 2 * rows // owners
    total = owners * cap
    unit = normalised(embeds)
    target = cluster // CLU_OWN
    onehot = (target[:, None] == jnp.arange(owners, dtype=jnp.int32)[None, :]).astype(jnp.int32)
    before = jnp.cumsum(onehot, axis=0) - onehot
    slot = jnp.sum(before * onehot, axis=1)
    place = target * cap + slot
    outgoing = jnp.zeros((total, width), jnp.bfloat16).at[place].set(unit)
    out_labels = jnp.full((total,), -1, jnp.int32).at[place].set(cluster)
    got, got_labels = (
        lax.all_to_all(
            outgoing.reshape(owners, cap, width),
            ("gx", "gy"),
            split_axis=0,
            concat_axis=0,
            tiled=True,
        ),
        lax.all_to_all(
            out_labels.reshape(owners, cap), ("gx", "gy"), split_axis=0, concat_axis=0, tiled=True
        ),
    )
    members = got.reshape(total, width)
    labels = got_labels.reshape(total)
    core = lax.axis_index("gz")
    query_ids = core * total + jnp.arange(total, dtype=jnp.int32)
    keys = lax.all_gather(members, "gz", axis=0, tiled=True)
    key_labels = lax.all_gather(labels, "gz", axis=0, tiled=True)
    key_ids = jnp.arange(keys.shape[0], dtype=jnp.int32)
    best = jnp.maximum(
        jnp.full((total,), -1.0, jnp.float32),
        jnp.max(masked_sims(members, labels, query_ids, keys, key_labels, key_ids), axis=1),
    )
    back = lax.all_to_all(
        best.reshape(owners, cap), ("gx", "gy"), split_axis=0, concat_axis=0, tiled=True
    )
    return back.reshape(total)[place]


def solution(mesh):
    shape = mesh.shape
    ring = shape["gx"] * shape["gy"] == 8 and shape["gy"] == 2 and shape["gz"] == 2
    placed = (P(("parts", "gx", "gy", "gz"), None), P(("parts", "gx", "gy", "gz")))
    return jax.shard_map(
        on_ring if ring else by_owner,
        mesh=mesh,
        in_specs=placed,
        out_specs=P(("parts", "gx", "gy", "gz")),
        check_vma=False,
    )
```

```python
import jax
import jax.numpy as jnp
from jax import lax
from jax.experimental import pallas as pl
from jax.experimental.pallas import tpu as pltpu
from jax.sharding import PartitionSpec as P

CLU_OWN = 16


EPS = 1e-06

GROUP = ("gx", "gy", "gz")


def normalised(block):
    vecs = block.astype(jnp.float32)
    return (vecs * lax.rsqrt(jnp.sum(vecs * vecs, axis=1, keepdims=True) + EPS)).astype(
        jnp.bfloat16
    )


LANES = 128
LABEL_ROWS = 16
PARTS = 4
VMEM_BYTES = 32 * 2**20
NEAR_COST = 1
FIRST_COST = 200
BACK_COST = 2
LAST_COST = 5


def put_unit(unit, chunk, at, size):
    count, width = unit.shape
    for j in range(width // LANES):
        chunk[j * size + at : j * size + at + count, :] = unit[:, j * LANES : (j + 1) * LANES]


def pack_first_kernel(embeds, label, first, raw, line, sems):
    rows, width = embeds.shape
    half = rows // 2
    step = half // PARTS
    copies = [pltpu.make_async_copy(label, line, sems.at[PARTS])]
    for i in range(PARTS):
        part = pl.ds(i * step, step)
        copies.append(pltpu.make_async_copy(embeds.at[part], raw.at[part], sems.at[i]))
    for copy in copies:
        copy.start()
    copies[0].wait()
    row = lax.broadcasted_iota(jnp.int32, (LABEL_ROWS, LANES), 0)
    lines = jnp.zeros((LABEL_ROWS, LANES), jnp.float32)
    for i in range(rows // LANES):
        piece = line[:, i * LANES : (i + 1) * LANES].astype(jnp.float32)
        lines = jnp.where(row == i, piece, lines)
    first[half * width // LANES :, :] = lines.astype(jnp.bfloat16)
    for i in range(PARTS):
        copies[1 + i].wait()
        put_unit(normalised(raw[i * step : (i + 1) * step, :]), first, i * step, half)


def pack_second_kernel(embeds, first, second, both):
    rows, width = embeds.shape
    half = rows // 2
    unit = normalised(embeds[half:, :])
    put_unit(unit, second, 0, half)
    put_chunks(first, second, both, rows)


def put_chunks(first, second, both, rows):
    size = second.shape[0]
    half = rows // 2
    for at in range(0, size, half):
        both[2 * at : 2 * at + half, :] = first[at : at + half, :]
        both[2 * at + half : 2 * (at + half), :] = second[at : at + half, :]
    both[2 * size :, :] = first[size:, :]


class Block:
    def __init__(self, unit, label):
        self.unit = unit
        self.label = label
        self.rows = unit.shape[0]
        self.along_rows = None

    def column(self):
        if self.along_rows is None:
            self.along_rows = jnp.transpose(jnp.broadcast_to(self.label, (LANES, self.rows)))
        return self.along_rows


def unit_in(chunk, rows, end):
    return jnp.concatenate([chunk[at : at + rows, :] for at in range(0, end, rows)], axis=1)


def labels_in(first, rows):
    lines = first[first.shape[0] - LABEL_ROWS :, :].astype(jnp.float32)
    return jnp.concatenate([lines[i : i + 1] for i in range(rows // LANES)], axis=1)


def packed(both, rows):
    return Block(unit_in(both, rows, both.shape[0] - LABEL_ROWS), labels_in(both, rows))


def first_half(first, rows):
    half = rows // 2
    unit = unit_in(first, half, first.shape[0] - LABEL_ROWS)
    return Block(unit, labels_in(first, rows)[:, :half])


def second_half(first, second, rows):
    half = rows // 2
    return Block(unit_in(second, half, second.shape[0]), labels_in(first, rows)[:, half:])


def whole(first, second, rows):
    return joined(first_half(first, rows), second_half(first, second, rows))


def joined(*blocks):
    return Block(
        jnp.concatenate([block.unit for block in blocks], axis=0),
        jnp.concatenate([block.label for block in blocks], axis=1),
    )


def best_of(queries, *all_keys):
    best = jnp.full((queries.rows, LANES), -1.0, jnp.float32)
    column = queries.column()
    for keys in all_keys:
        sims = lax.dot_general(
            queries.unit, keys.unit, (((1,), (1,)), ((), ())), preferred_element_type=jnp.float32
        )
        for start in range(0, keys.rows, LANES):
            keep = column == keys.label[:, start : start + LANES]
            if keys is queries:
                row = lax.broadcasted_iota(jnp.int32, keep.shape, 0)
                lane = lax.broadcasted_iota(jnp.int32, keep.shape, 1) + start
                keep = keep & (row != lane)
            found = jnp.where(keep, sims[:, start : start + LANES], -1.0)
            best = jnp.maximum(best, found)
    return jnp.max(jnp.transpose(best), axis=0, keepdims=True)


def best_of_each(queries, keys):
    sims = lax.dot_general(
        keys.unit, queries.unit, (((1,), (1,)), ((), ())), preferred_element_type=jnp.float32
    )
    pieces = []
    for start in range(0, queries.rows, LANES):
        keep = keys.column() == queries.label[:, start : start + LANES]
        found = jnp.where(keep, sims[:, start : start + LANES], -1.0)
        pieces.append(jnp.max(found, axis=0, keepdims=True))
    return jnp.concatenate(pieces, axis=1)


def near_kernel(own, prev_a, prev_b, succ_a, succ_b, mine, bundle):
    rows = mine.shape[1]
    put_chunks(prev_a, prev_b, bundle.at[0], rows)
    put_chunks(succ_a, succ_b, bundle.at[1], rows)
    bundle[2] = own[...]
    own = packed(own, rows)
    mine[...] = best_of(own, own, whole(prev_a, prev_b, rows), whole(succ_a, succ_b, rows))


def far_first_kernel(own, prev_a, prev_b, succ_a, succ_b, back_a, ahead_a, found):
    rows = found.shape[1]
    near = packed(own, rows), whole(prev_a, prev_b, rows), whole(succ_a, succ_b, rows)
    queries = joined(first_half(back_a, rows), first_half(ahead_a, rows))
    found[...] = best_of(queries, queries, *near)


def far_back_kernel(own, others, succ_a, succ_b, back_a, ahead_a, back_b, found, back, ahead):
    rows = found.shape[1]
    half = rows // 2
    prev_other, succ_other = packed(others.at[0], rows), packed(others.at[1], rows)
    first, rest = first_half(back_a, rows), second_half(back_a, back_b, rows)
    first_ahead = first_half(ahead_a, rows)
    keys = packed(own, rows), whole(succ_a, succ_b, rows), first_ahead
    both = best_of(joined(first, rest), succ_other)
    back[:, :half] = jnp.maximum(found[:, :half], both[:, :half])
    back[:, half:] = jnp.maximum(best_of(rest, *keys), both[:, half:])
    ahead[...] = jnp.maximum(found[:, half:], best_of(first_ahead, rest, prev_other))


def far_last_kernel(own, others, prev_a, prev_b, back_a, ahead_a, back_b, ahead_b, *refs):
    back_found, ahead_found, to_back, to_ahead = refs
    rows = to_back.shape[1]
    half = rows // 2
    back, rest = whole(back_a, back_b, rows), second_half(ahead_a, ahead_b, rows)
    keys = packed(own, rows), whole(prev_a, prev_b, rows), packed(others.at[0], rows), back
    to_back[...] = jnp.maximum(back_found[...], best_of_each(back, rest))
    to_ahead[:, :half] = ahead_found[...]
    to_ahead[:, half:] = best_of(rest, *keys)


def own_kernel(own, others, back_a, ahead_a, back_b, ahead_b, near, mine):
    rows = mine.shape[1]
    keys = [packed(others.at[at], rows) for at in range(3)]
    keys += [whole(back_a, back_b, rows), whole(ahead_a, ahead_b, rows)]
    mine[...] = jnp.maximum(near[...], best_of(packed(own, rows), *keys))


def ring_perms(size_x, size_y, size_z):
    chips = size_x * size_y

    def device(place, core):
        place = place % chips
        x, y = (place, 0) if place < size_x else (chips - 1 - place, 1)
        return (x * size_y + y) * size_z + core

    def perm(to):
        return [
            (device(p, k), device(*to(p, k))) for p in range(chips) for k in range(size_z)
        ]

    def from_prev(place, core):
        return core ^ (place % chips in (0, 1))

    def from_next(place, core):
        return core ^ (place % chips not in (0, 1))

    return {
        "sibling": perm(lambda p, k: (p, 1 - k)),
        "next": perm(lambda p, k: (p + 1, from_prev(p + 1, k))),
        "prev": perm(lambda p, k: (p - 1, from_next(p - 1, k))),
        "on_next": perm(lambda p, k: (p + 1, k)),
        "on_prev": perm(lambda p, k: (p - 1, k)),
        "home_back": perm(lambda p, k: (p - 2, from_prev(p - 1, k))),
        "home_ahead": perm(lambda p, k: (p + 2, from_next(p + 1, k))),
    }


def kernel_call(kernel, inputs, outputs, matmuls):
    vmem = pl.BlockSpec(memory_space=pltpu.VMEM)
    return pl.pallas_call(
        kernel,
        out_shape=outputs,
        in_specs=[vmem] * len(inputs),
        out_specs=[vmem] * len(outputs),
        compiler_params=pltpu.CompilerParams(vmem_limit_bytes=VMEM_BYTES),
        cost_estimate=pl.CostEstimate(
            flops=matmuls * 2**26, bytes_accessed=2**20, transcendentals=0
        ),
        name=kernel.__name__,
    )(*inputs)


def on_ring(embeds, cluster):
    rows, width = embeds.shape
    half = rows // 2
    perms = ring_perms(*(lax.axis_size(a) for a in GROUP))

    def send(value, name):
        return lax.ppermute(value, GROUP, perms[name])

    line = jax.ShapeDtypeStruct((1, rows), jnp.float32)
    half_line = jax.ShapeDtypeStruct((1, half), jnp.float32)

    def chunk(count, labels):
        size = count * width // LANES + labels * LABEL_ROWS
        return jax.ShapeDtypeStruct((size, LANES), jnp.bfloat16)

    anywhere = pl.BlockSpec(memory_space=pl.ANY)
    vmem = pl.BlockSpec(memory_space=pltpu.VMEM)
    own_a = pl.pallas_call(
        pack_first_kernel,
        out_shape=chunk(half, True),
        in_specs=[anywhere] * 2,
        out_specs=vmem,
        scratch_shapes=[
            pltpu.VMEM((half, width), jnp.bfloat16),
            pltpu.VMEM((1, rows), jnp.int32),
            pltpu.SemaphoreType.DMA((PARTS + 1,)),
        ],
        compiler_params=pltpu.CompilerParams(vmem_limit_bytes=VMEM_BYTES),
        name="pack_first",
    )(
        pltpu.with_memory_space_constraint(embeds, pltpu.HBM),
        pltpu.with_memory_space_constraint(cluster.reshape(1, rows), pltpu.HBM),
    )
    own_b, own = kernel_call(
        pack_second_kernel, [embeds, own_a], [chunk(half, False), chunk(rows, True)], 1
    )
    prev_a, succ_a = send(own_a, "next"), send(own_a, "prev")
    prev_b, succ_b = send(own_b, "next"), send(own_b, "prev")
    back_a, ahead_a = send(prev_a, "on_next"), send(succ_a, "on_prev")
    back_b, ahead_b = send(prev_b, "on_next"), send(succ_b, "on_prev")
    prev, succ, far = [prev_a, prev_b], [succ_a, succ_b], [back_a, ahead_a, back_b, ahead_b]
    bundle_shape = jax.ShapeDtypeStruct((3, *chunk(rows, True).shape), jnp.bfloat16)
    mine, bundle = kernel_call(near_kernel, [own, *prev, *succ], [line, bundle_shape], NEAR_COST)
    others = send(bundle, "sibling")
    (found,) = kernel_call(
        far_first_kernel, [own, *prev, *succ, back_a, ahead_a], [line], FIRST_COST
    )
    found = kernel_call(
        far_back_kernel,
        [own, others, *succ, back_a, ahead_a, back_b, found],
        [line, half_line],
        BACK_COST,
    )
    to_back, to_ahead = kernel_call(
        far_last_kernel, [own, others, *prev, *far, *found], [line] * 2, LAST_COST
    )
    (mine,) = kernel_call(own_kernel, [own, others, *far, mine], [line], 5)
    best = jnp.maximum(
        mine, jnp.maximum(send(to_back, "home_back"), send(to_ahead, "home_ahead"))
    )
    return best.reshape(rows)


def masked_sims(queries, query_labels, query_ids, keys, key_labels, key_ids):
    sims = jnp.einsum("qd,kd->qk", queries, keys, preferred_element_type=jnp.float32)
    keep = (
        (query_labels[:, None] == key_labels[None, :])
        & (query_labels[:, None] >= 0)
        & (query_ids[:, None] != key_ids[None, :])
    )
    return jnp.where(keep, sims, -1.0)


def by_owner(embeds, cluster):
    rows, width = embeds.shape
    size_x = lax.axis_size("gx")
    size_y = lax.axis_size("gy")
    owners = size_x * size_y
    cap = 2 * rows // owners
    total = owners * cap
    unit = normalised(embeds)
    target = cluster // CLU_OWN
    onehot = (target[:, None] == jnp.arange(owners, dtype=jnp.int32)[None, :]).astype(jnp.int32)
    before = jnp.cumsum(onehot, axis=0) - onehot
    slot = jnp.sum(before * onehot, axis=1)
    place = target * cap + slot
    outgoing = jnp.zeros((total, width), jnp.bfloat16).at[place].set(unit)
    out_labels = jnp.full((total,), -1, jnp.int32).at[place].set(cluster)
    got, got_labels = (
        lax.all_to_all(
            outgoing.reshape(owners, cap, width),
            ("gx", "gy"),
            split_axis=0,
            concat_axis=0,
            tiled=True,
        ),
        lax.all_to_all(
            out_labels.reshape(owners, cap), ("gx", "gy"), split_axis=0, concat_axis=0, tiled=True
        ),
    )
    members = got.reshape(total, width)
    labels = got_labels.reshape(total)
    core = lax.axis_index("gz")
    query_ids = core * total + jnp.arange(total, dtype=jnp.int32)
    keys = lax.all_gather(members, "gz", axis=0, tiled=True)
    key_labels = lax.all_gather(labels, "gz", axis=0, tiled=True)
    key_ids = jnp.arange(keys.shape[0], dtype=jnp.int32)
    best = jnp.maximum(
        jnp.full((total,), -1.0, jnp.float32),
        jnp.max(masked_sims(members, labels, query_ids, keys, key_labels, key_ids), axis=1),
    )
    back = lax.all_to_all(
        best.reshape(owners, cap), ("gx", "gy"), split_axis=0, concat_axis=0, tiled=True
    )
    return back.reshape(total)[place]


def solution(mesh):
    shape = mesh.shape
    ring = shape["gx"] * shape["gy"] == 8 and shape["gy"] == 2 and shape["gz"] == 2
    placed = (P(("parts", "gx", "gy", "gz"), None), P(("parts", "gx", "gy", "gz")))
    return jax.shard_map(
        on_ring if ring else by_owner,
        mesh=mesh,
        in_specs=placed,
        out_specs=P(("parts", "gx", "gy", "gz")),
        check_vma=False,
    )
```

```python
import jax
import jax.numpy as jnp
from jax import lax
from jax.experimental import pallas as pl
from jax.experimental.pallas import tpu as pltpu
from jax.sharding import PartitionSpec as P

CLU_OWN = 16


EPS = 1e-06

GROUP = ("gx", "gy", "gz")


def normalised(block):
    vecs = block.astype(jnp.float32)
    return (vecs * lax.rsqrt(jnp.sum(vecs * vecs, axis=1, keepdims=True) + EPS)).astype(
        jnp.bfloat16
    )


LANES = 128
LABEL_ROWS = 16
VMEM_BYTES = 32 * 2**20
NEAR_COST = 1
FIRST_COST = 200
BACK_COST = 2
LAST_COST = 5


def put_unit(unit, chunk, at, size):
    count, width = unit.shape
    for j in range(width // LANES):
        chunk[j * size + at : j * size + at + count, :] = unit[:, j * LANES : (j + 1) * LANES]


def pack_first_kernel(embeds, label, first, raw, line, sems):
    rows, width = embeds.shape
    half = rows // 2
    copies = [
        pltpu.make_async_copy(label, line, sems.at[0]),
        pltpu.make_async_copy(embeds.at[pl.ds(0, half)], raw, sems.at[1]),
    ]
    for copy in copies:
        copy.start()
    copies[0].wait()
    row = lax.broadcasted_iota(jnp.int32, (LABEL_ROWS, LANES), 0)
    lines = jnp.zeros((LABEL_ROWS, LANES), jnp.float32)
    for i in range(rows // LANES):
        piece = line[:, i * LANES : (i + 1) * LANES].astype(jnp.float32)
        lines = jnp.where(row == i, piece, lines)
    first[half * width // LANES :, :] = lines.astype(jnp.bfloat16)
    copies[1].wait()
    put_unit(normalised(raw[...]), first, 0, half)


def pack_second_kernel(embeds, first, second, both):
    rows, width = embeds.shape
    half = rows // 2
    unit = normalised(embeds[half:, :])
    put_unit(unit, second, 0, half)
    put_chunks(first, second, both, rows)


def put_chunks(first, second, both, rows):
    size = second.shape[0]
    half = rows // 2
    for at in range(0, size, half):
        both[2 * at : 2 * at + half, :] = first[at : at + half, :]
        both[2 * at + half : 2 * (at + half), :] = second[at : at + half, :]
    both[2 * size :, :] = first[size:, :]


class Block:
    def __init__(self, unit, label):
        self.unit = unit
        self.label = label
        self.rows = unit.shape[0]
        self.along_rows = None

    def column(self):
        if self.along_rows is None:
            self.along_rows = jnp.transpose(jnp.broadcast_to(self.label, (LANES, self.rows)))
        return self.along_rows


def unit_in(chunk, rows, end):
    return jnp.concatenate([chunk[at : at + rows, :] for at in range(0, end, rows)], axis=1)


def labels_in(first, rows):
    lines = first[first.shape[0] - LABEL_ROWS :, :].astype(jnp.float32)
    return jnp.concatenate([lines[i : i + 1] for i in range(rows // LANES)], axis=1)


def packed(both, rows):
    return Block(unit_in(both, rows, both.shape[0] - LABEL_ROWS), labels_in(both, rows))


def first_half(first, rows):
    half = rows // 2
    unit = unit_in(first, half, first.shape[0] - LABEL_ROWS)
    return Block(unit, labels_in(first, rows)[:, :half])


def second_half(first, second, rows):
    half = rows // 2
    return Block(unit_in(second, half, second.shape[0]), labels_in(first, rows)[:, half:])


def whole(first, second, rows):
    return joined(first_half(first, rows), second_half(first, second, rows))


def joined(*blocks):
    return Block(
        jnp.concatenate([block.unit for block in blocks], axis=0),
        jnp.concatenate([block.label for block in blocks], axis=1),
    )


def best_of(queries, *all_keys):
    best = None
    for keys in all_keys:
        sims = lax.dot_general(
            keys.unit, queries.unit, (((1,), (1,)), ((), ())), preferred_element_type=jnp.float32
        )
        pieces = []
        for start in range(0, queries.rows, LANES):
            keep = keys.column() == queries.label[:, start : start + LANES]
            if keys is queries:
                row = lax.broadcasted_iota(jnp.int32, keep.shape, 0)
                column = lax.broadcasted_iota(jnp.int32, keep.shape, 1) + start
                keep = keep & (row != column)
            found = jnp.where(keep, sims[:, start : start + LANES], -1.0)
            pieces.append(jnp.max(found, axis=0, keepdims=True))
        found = jnp.concatenate(pieces, axis=1)
        best = found if best is None else jnp.maximum(best, found)
    return best


def near_kernel(own, prev_a, prev_b, succ_a, succ_b, mine, bundle):
    rows = mine.shape[1]
    put_chunks(prev_a, prev_b, bundle.at[0], rows)
    put_chunks(succ_a, succ_b, bundle.at[1], rows)
    bundle[2] = own[...]
    own = packed(own, rows)
    mine[...] = best_of(own, own, whole(prev_a, prev_b, rows), whole(succ_a, succ_b, rows))


def far_first_kernel(own, prev_a, prev_b, succ_a, succ_b, back_a, ahead_a, found):
    rows = found.shape[1]
    near = packed(own, rows), whole(prev_a, prev_b, rows), whole(succ_a, succ_b, rows)
    queries = joined(first_half(back_a, rows), first_half(ahead_a, rows))
    found[...] = best_of(queries, queries, *near)


def far_back_kernel(own, others, succ_a, succ_b, back_a, ahead_a, back_b, found, back, ahead):
    rows = found.shape[1]
    half = rows // 2
    prev_other, succ_other = packed(others.at[0], rows), packed(others.at[1], rows)
    first, rest = first_half(back_a, rows), second_half(back_a, back_b, rows)
    first_ahead = first_half(ahead_a, rows)
    keys = packed(own, rows), whole(succ_a, succ_b, rows), first_ahead
    both = best_of(joined(first, rest), succ_other)
    back[:, :half] = jnp.maximum(found[:, :half], both[:, :half])
    back[:, half:] = jnp.maximum(best_of(rest, *keys), both[:, half:])
    ahead[...] = jnp.maximum(found[:, half:], best_of(first_ahead, rest, prev_other))


def far_last_kernel(own, others, prev_a, prev_b, back_a, ahead_a, back_b, ahead_b, *refs):
    back_found, ahead_found, to_back, to_ahead = refs
    rows = to_back.shape[1]
    half = rows // 2
    back, rest = whole(back_a, back_b, rows), second_half(ahead_a, ahead_b, rows)
    keys = packed(own, rows), whole(prev_a, prev_b, rows), packed(others.at[0], rows), back
    to_back[...] = jnp.maximum(back_found[...], best_of(back, rest))
    to_ahead[:, :half] = ahead_found[...]
    to_ahead[:, half:] = best_of(rest, *keys)


def own_kernel(own, others, back_a, ahead_a, back_b, ahead_b, near, mine):
    rows = mine.shape[1]
    keys = [packed(others.at[at], rows) for at in range(3)]
    keys += [whole(back_a, back_b, rows), whole(ahead_a, ahead_b, rows)]
    mine[...] = jnp.maximum(near[...], best_of(packed(own, rows), *keys))


def ring_perms(size_x, size_y, size_z):
    chips = size_x * size_y

    def device(place, core):
        place = place % chips
        x, y = (place, 0) if place < size_x else (chips - 1 - place, 1)
        return (x * size_y + y) * size_z + core

    def perm(to):
        return [
            (device(p, k), device(*to(p, k))) for p in range(chips) for k in range(size_z)
        ]

    def from_prev(place, core):
        return core ^ (place % chips in (0, chips - 1))

    def from_next(place, core):
        return core ^ (place % chips not in (0, chips - 1))

    return {
        "sibling": perm(lambda p, k: (p, 1 - k)),
        "next": perm(lambda p, k: (p + 1, from_prev(p + 1, k))),
        "prev": perm(lambda p, k: (p - 1, from_next(p - 1, k))),
        "on_next": perm(lambda p, k: (p + 1, k)),
        "on_prev": perm(lambda p, k: (p - 1, k)),
        "home_back": perm(lambda p, k: (p - 2, from_prev(p - 1, k))),
        "home_ahead": perm(lambda p, k: (p + 2, from_next(p + 1, k))),
    }


def kernel_call(kernel, inputs, outputs, matmuls):
    vmem = pl.BlockSpec(memory_space=pltpu.VMEM)
    return pl.pallas_call(
        kernel,
        out_shape=outputs,
        in_specs=[vmem] * len(inputs),
        out_specs=[vmem] * len(outputs),
        compiler_params=pltpu.CompilerParams(vmem_limit_bytes=VMEM_BYTES),
        cost_estimate=pl.CostEstimate(
            flops=matmuls * 2**26, bytes_accessed=2**20, transcendentals=0
        ),
        name=kernel.__name__,
    )(*inputs)


def on_ring(embeds, cluster):
    rows, width = embeds.shape
    half = rows // 2
    perms = ring_perms(*(lax.axis_size(a) for a in GROUP))

    def send(value, name):
        return lax.ppermute(value, GROUP, perms[name])

    line = jax.ShapeDtypeStruct((1, rows), jnp.float32)
    half_line = jax.ShapeDtypeStruct((1, half), jnp.float32)

    def chunk(count, labels):
        size = count * width // LANES + labels * LABEL_ROWS
        return jax.ShapeDtypeStruct((size, LANES), jnp.bfloat16)

    anywhere = pl.BlockSpec(memory_space=pl.ANY)
    vmem = pl.BlockSpec(memory_space=pltpu.VMEM)
    own_a = pl.pallas_call(
        pack_first_kernel,
        out_shape=chunk(half, True),
        in_specs=[anywhere] * 2,
        out_specs=vmem,
        scratch_shapes=[
            pltpu.VMEM((half, width), jnp.bfloat16),
            pltpu.VMEM((1, rows), jnp.int32),
            pltpu.SemaphoreType.DMA((2,)),
        ],
        compiler_params=pltpu.CompilerParams(vmem_limit_bytes=VMEM_BYTES),
        name="pack_first",
    )(
        pltpu.with_memory_space_constraint(embeds, pltpu.HBM),
        pltpu.with_memory_space_constraint(cluster.reshape(1, rows), pltpu.HBM),
    )
    own_b, own = kernel_call(
        pack_second_kernel, [embeds, own_a], [chunk(half, False), chunk(rows, True)], 1
    )
    prev_a, succ_a = send(own_a, "next"), send(own_a, "prev")
    prev_b, succ_b = send(own_b, "next"), send(own_b, "prev")
    back_a, ahead_a = send(prev_a, "on_next"), send(succ_a, "on_prev")
    back_b, ahead_b = send(prev_b, "on_next"), send(succ_b, "on_prev")
    prev, succ, far = [prev_a, prev_b], [succ_a, succ_b], [back_a, ahead_a, back_b, ahead_b]
    bundle_shape = jax.ShapeDtypeStruct((3, *chunk(rows, True).shape), jnp.bfloat16)
    mine, bundle = kernel_call(near_kernel, [own, *prev, *succ], [line, bundle_shape], NEAR_COST)
    others = send(bundle, "sibling")
    (found,) = kernel_call(
        far_first_kernel, [own, *prev, *succ, back_a, ahead_a], [line], FIRST_COST
    )
    found = kernel_call(
        far_back_kernel,
        [own, others, *succ, back_a, ahead_a, back_b, found],
        [line, half_line],
        BACK_COST,
    )
    to_back, to_ahead = kernel_call(
        far_last_kernel, [own, others, *prev, *far, *found], [line] * 2, LAST_COST
    )
    (mine,) = kernel_call(own_kernel, [own, others, *far, mine], [line], 5)
    best = jnp.maximum(
        mine, jnp.maximum(send(to_back, "home_back"), send(to_ahead, "home_ahead"))
    )
    return best.reshape(rows)


def masked_sims(queries, query_labels, query_ids, keys, key_labels, key_ids):
    sims = jnp.einsum("qd,kd->qk", queries, keys, preferred_element_type=jnp.float32)
    keep = (
        (query_labels[:, None] == key_labels[None, :])
        & (query_labels[:, None] >= 0)
        & (query_ids[:, None] != key_ids[None, :])
    )
    return jnp.where(keep, sims, -1.0)


def by_owner(embeds, cluster):
    rows, width = embeds.shape
    size_x = lax.axis_size("gx")
    size_y = lax.axis_size("gy")
    owners = size_x * size_y
    cap = 2 * rows // owners
    total = owners * cap
    unit = normalised(embeds)
    target = cluster // CLU_OWN
    onehot = (target[:, None] == jnp.arange(owners, dtype=jnp.int32)[None, :]).astype(jnp.int32)
    before = jnp.cumsum(onehot, axis=0) - onehot
    slot = jnp.sum(before * onehot, axis=1)
    place = target * cap + slot
    outgoing = jnp.zeros((total, width), jnp.bfloat16).at[place].set(unit)
    out_labels = jnp.full((total,), -1, jnp.int32).at[place].set(cluster)
    got, got_labels = (
        lax.all_to_all(
            outgoing.reshape(owners, cap, width),
            ("gx", "gy"),
            split_axis=0,
            concat_axis=0,
            tiled=True,
        ),
        lax.all_to_all(
            out_labels.reshape(owners, cap), ("gx", "gy"), split_axis=0, concat_axis=0, tiled=True
        ),
    )
    members = got.reshape(total, width)
    labels = got_labels.reshape(total)
    core = lax.axis_index("gz")
    query_ids = core * total + jnp.arange(total, dtype=jnp.int32)
    keys = lax.all_gather(members, "gz", axis=0, tiled=True)
    key_labels = lax.all_gather(labels, "gz", axis=0, tiled=True)
    key_ids = jnp.arange(keys.shape[0], dtype=jnp.int32)
    best = jnp.maximum(
        jnp.full((total,), -1.0, jnp.float32),
        jnp.max(masked_sims(members, labels, query_ids, keys, key_labels, key_ids), axis=1),
    )
    back = lax.all_to_all(
        best.reshape(owners, cap), ("gx", "gy"), split_axis=0, concat_axis=0, tiled=True
    )
    return back.reshape(total)[place]


def solution(mesh):
    shape = mesh.shape
    ring = shape["gx"] * shape["gy"] == 8 and shape["gy"] == 2 and shape["gz"] == 2
    placed = (P(("parts", "gx", "gy", "gz"), None), P(("parts", "gx", "gy", "gz")))
    return jax.shard_map(
        on_ring if ring else by_owner,
        mesh=mesh,
        in_specs=placed,
        out_specs=P(("parts", "gx", "gy", "gz")),
        check_vma=False,
    )
```

```python
import jax
import jax.numpy as jnp
from jax import lax
from jax.experimental import pallas as pl
from jax.experimental.pallas import tpu as pltpu
from jax.sharding import PartitionSpec as P

CLU_OWN = 16


EPS = 1e-06

GROUP = ("gx", "gy", "gz")


def normalised(block):
    vecs = block.astype(jnp.float32)
    return (vecs * lax.rsqrt(jnp.sum(vecs * vecs, axis=1, keepdims=True) + EPS)).astype(
        jnp.bfloat16
    )


LABEL_ROWS = 16
LANES = 128
VMEM_BYTES = 32 * 2**20
NEAR_COST = 2
OWN_COST = 200
ROWS_COST = 6


def pack_kernel(embeds, label, packed, raw, line, sems):
    rows, width = embeds.shape
    half = rows // 2
    copies = [pltpu.make_async_copy(label, line, sems.at[0])]
    for i in range(2):
        part = pl.ds(i * half, half)
        copies.append(pltpu.make_async_copy(embeds.at[part], raw.at[part], sems.at[1 + i]))
    for copy in copies:
        copy.start()
    copies[0].wait()
    row = lax.broadcasted_iota(jnp.int32, (LABEL_ROWS, LANES), 0)
    lines = jnp.zeros((LABEL_ROWS, LANES), jnp.float32)
    for i in range(rows // LANES):
        piece = line[:, i * LANES : (i + 1) * LANES].astype(jnp.float32)
        lines = jnp.where(row == i, piece, lines)
    packed[rows * width // LANES :, :] = lines.astype(jnp.bfloat16)
    for i in range(2):
        copies[1 + i].wait()
        unit = normalised(raw[pl.ds(i * half, half), :])
        for j in range(width // LANES):
            packed[pl.ds(j * rows + i * half, half), :] = unit[:, j * LANES : (j + 1) * LANES]


class Block:
    def __init__(self, packed, rows):
        labels_at = packed.shape[0] - LABEL_ROWS
        columns = [packed[at : at + rows, :] for at in range(0, labels_at, rows)]
        self.unit = jnp.concatenate(columns, axis=1)
        lines = packed[labels_at:, :].astype(jnp.float32)
        self.label = jnp.concatenate([lines[i : i + 1] for i in range(rows // LANES)], axis=1)
        self.rows = rows
        self.along_rows = None

    def column(self):
        if self.along_rows is None:
            self.along_rows = jnp.transpose(jnp.broadcast_to(self.label, (LANES, self.rows)))
        return self.along_rows


def best_of(queries, *all_keys):
    best = None
    for keys in all_keys:
        sims = lax.dot_general(
            keys.unit, queries.unit, (((1,), (1,)), ((), ())), preferred_element_type=jnp.float32
        )
        pieces = []
        for start in range(0, queries.rows, LANES):
            keep = keys.column() == queries.label[:, start : start + LANES]
            if keys is queries:
                row = lax.broadcasted_iota(jnp.int32, keep.shape, 0)
                column = lax.broadcasted_iota(jnp.int32, keep.shape, 1) + start
                keep = keep & (row != column)
            found = jnp.where(keep, sims[:, start : start + LANES], -1.0)
            pieces.append(jnp.max(found, axis=0, keepdims=True))
        found = jnp.concatenate(pieces, axis=1)
        best = found if best is None else jnp.maximum(best, found)
    return best


def near_kernel(rows, other, best):
    size = best.shape[1]
    rows = Block(rows, size)
    best[...] = best_of(rows, rows, Block(other, size))


def rows_kernel(rows, *refs):
    *keys, best = refs
    size = best.shape[1]
    best[...] = best_of(Block(rows, size), *(Block(key, size) for key in keys))


def after_kernel(rows, *refs):
    *keys, _, best = refs
    rows_kernel(rows, *keys, best)


def more_kernel(rows, *refs):
    *keys, found, best = refs
    rows_kernel(rows, *keys, best)
    best[...] = jnp.maximum(best[...], found[...])


KEYS_FAR = (3, 6, 5, 0, 7, 2, 1, 4)
KEYS_TWO = (2, 7, 4, 1, 6, 3, 0, 5)


def ring_perms(size_x, size_y, size_z):
    chips = size_x * size_y

    def device(place, core):
        place = place % chips
        x, y = (place, 0) if place < size_x else (chips - 1 - place, 1)
        return (x * size_y + y) * size_z + core

    def perm(source, swap=0):
        return [
            (device(source(p), k), device(p, k ^ swap))
            for p in range(chips)
            for k in range(size_z)
        ]

    return {
        "sibling": perm(lambda p: p, swap=1),
        "next": perm(lambda p: p - 1),
        "prev": perm(lambda p: p + 1),
        "far": perm(lambda p: KEYS_FAR[p]),
        "two": perm(lambda p: KEYS_TWO[p]),
    }


def kernel_call(kernel, rows, blocks, cost, name):
    vmem = pl.BlockSpec(memory_space=pltpu.VMEM)
    return pl.pallas_call(
        kernel,
        out_shape=jax.ShapeDtypeStruct((1, rows), jnp.float32),
        in_specs=[vmem] * len(blocks),
        out_specs=vmem,
        compiler_params=pltpu.CompilerParams(vmem_limit_bytes=VMEM_BYTES),
        cost_estimate=pl.CostEstimate(
            flops=cost * 2**26, bytes_accessed=2**20, transcendentals=0
        ),
        name=name,
    )(*blocks)


def on_ring(embeds, cluster):
    rows, width = embeds.shape
    perms = ring_perms(*(lax.axis_size(a) for a in GROUP))

    def send(value, name):
        return lax.ppermute(value, GROUP, perms[name])

    anywhere = pl.BlockSpec(memory_space=pl.ANY)
    own = pl.pallas_call(
        pack_kernel,
        out_shape=jax.ShapeDtypeStruct((rows * width // LANES + LABEL_ROWS, LANES), jnp.bfloat16),
        in_specs=[anywhere] * 2,
        out_specs=pl.BlockSpec(memory_space=pltpu.VMEM),
        scratch_shapes=[
            pltpu.VMEM((rows, width), jnp.bfloat16),
            pltpu.VMEM((1, rows), jnp.int32),
            pltpu.SemaphoreType.DMA((3,)),
        ],
        compiler_params=pltpu.CompilerParams(vmem_limit_bytes=VMEM_BYTES),
        name="pack",
    )(
        pltpu.with_memory_space_constraint(embeds, pltpu.HBM),
        pltpu.with_memory_space_constraint(cluster.reshape(1, rows), pltpu.HBM),
    )
    other = send(own, "sibling")
    near = kernel_call(near_kernel, rows, [own, other], NEAR_COST, "near")
    far, two = send(own, "far"), send(own, "two")
    own_again, near = lax.optimization_barrier((own, near))
    behind, ahead = send(own_again, "next"), send(own_again, "prev")
    far_other, two_other = send(far, "sibling"), send(two, "sibling")
    mine = kernel_call(more_kernel, rows, [own, far, two, near], OWN_COST, "own")
    keys = [own, other, far, two, far_other, two_other]
    found_behind = kernel_call(after_kernel, rows, [behind, *keys, mine], ROWS_COST, "behind")
    found_ahead = kernel_call(
        after_kernel, rows, [ahead, *keys, found_behind], ROWS_COST, "ahead"
    )
    mine = kernel_call(more_kernel, rows, [own, far_other, two_other, mine], 2, "rest")
    best = jnp.maximum(
        mine, jnp.maximum(send(found_behind, "prev"), send(found_ahead, "next"))
    )
    return best.reshape(rows)


def masked_sims(queries, query_labels, query_ids, keys, key_labels, key_ids):
    sims = jnp.einsum("qd,kd->qk", queries, keys, preferred_element_type=jnp.float32)
    keep = (
        (query_labels[:, None] == key_labels[None, :])
        & (query_labels[:, None] >= 0)
        & (query_ids[:, None] != key_ids[None, :])
    )
    return jnp.where(keep, sims, -1.0)


def by_owner(embeds, cluster):
    rows, width = embeds.shape
    size_x = lax.axis_size("gx")
    size_y = lax.axis_size("gy")
    owners = size_x * size_y
    cap = 2 * rows // owners
    total = owners * cap
    unit = normalised(embeds)
    target = cluster // CLU_OWN
    onehot = (target[:, None] == jnp.arange(owners, dtype=jnp.int32)[None, :]).astype(jnp.int32)
    before = jnp.cumsum(onehot, axis=0) - onehot
    slot = jnp.sum(before * onehot, axis=1)
    place = target * cap + slot
    outgoing = jnp.zeros((total, width), jnp.bfloat16).at[place].set(unit)
    out_labels = jnp.full((total,), -1, jnp.int32).at[place].set(cluster)
    got, got_labels = (
        lax.all_to_all(
            outgoing.reshape(owners, cap, width),
            ("gx", "gy"),
            split_axis=0,
            concat_axis=0,
            tiled=True,
        ),
        lax.all_to_all(
            out_labels.reshape(owners, cap), ("gx", "gy"), split_axis=0, concat_axis=0, tiled=True
        ),
    )
    members = got.reshape(total, width)
    labels = got_labels.reshape(total)
    core = lax.axis_index("gz")
    query_ids = core * total + jnp.arange(total, dtype=jnp.int32)
    keys = lax.all_gather(members, "gz", axis=0, tiled=True)
    key_labels = lax.all_gather(labels, "gz", axis=0, tiled=True)
    key_ids = jnp.arange(keys.shape[0], dtype=jnp.int32)
    best = jnp.maximum(
        jnp.full((total,), -1.0, jnp.float32),
        jnp.max(masked_sims(members, labels, query_ids, keys, key_labels, key_ids), axis=1),
    )
    back = lax.all_to_all(
        best.reshape(owners, cap), ("gx", "gy"), split_axis=0, concat_axis=0, tiled=True
    )
    return back.reshape(total)[place]


def solution(mesh):
    shape = mesh.shape
    ring = shape["gx"] * shape["gy"] == 8 and shape["gy"] == 2 and shape["gz"] == 2
    placed = (P(("parts", "gx", "gy", "gz"), None), P(("parts", "gx", "gy", "gz")))
    return jax.shard_map(
        on_ring if ring else by_owner,
        mesh=mesh,
        in_specs=placed,
        out_specs=P(("parts", "gx", "gy", "gz")),
        check_vma=False,
    )
```

```python
import jax
import jax.numpy as jnp
from jax import lax
from jax.experimental import pallas as pl
from jax.experimental.pallas import tpu as pltpu
from jax.sharding import PartitionSpec as P

CLU_OWN = 16


EPS = 1e-06

GROUP = ("gx", "gy", "gz")


def normalised(block):
    vecs = block.astype(jnp.float32)
    return (vecs * lax.rsqrt(jnp.sum(vecs * vecs, axis=1, keepdims=True) + EPS)).astype(
        jnp.bfloat16
    )


LANES = 128
LABEL_ROWS = 16
VMEM_BYTES = 32 * 2**20
NEAR_COST = 1
FIRST_COST = 200
BACK_COST = 2
LAST_COST = 5


def put_unit(unit, chunk, at, size):
    count, width = unit.shape
    for j in range(width // LANES):
        chunk[j * size + at : j * size + at + count, :] = unit[:, j * LANES : (j + 1) * LANES]


def pack_first_kernel(embeds, label, first, raw, line, sems):
    rows, width = embeds.shape
    half = rows // 2
    rows_copy = pltpu.make_async_copy(embeds.at[pl.ds(0, half)], raw, sems.at[0])
    line_copy = pltpu.make_async_copy(label, line, sems.at[1])
    rows_copy.start()
    line_copy.start()
    line_copy.wait()
    row = lax.broadcasted_iota(jnp.int32, (LABEL_ROWS, LANES), 0)
    lines = jnp.zeros((LABEL_ROWS, LANES), jnp.float32)
    for i in range(rows // LANES):
        piece = line[:, i * LANES : (i + 1) * LANES].astype(jnp.float32)
        lines = jnp.where(row == i, piece, lines)
    first[half * width // LANES :, :] = lines.astype(jnp.bfloat16)
    rows_copy.wait()
    put_unit(normalised(raw[...]), first, 0, half)


def pack_second_kernel(embeds, first, second, both):
    rows, width = embeds.shape
    half = rows // 2
    unit = normalised(embeds[half:, :])
    put_unit(unit, second, 0, half)
    put_chunks(first, second, both, rows)


def put_chunks(first, second, both, rows):
    size = second.shape[0]
    half = rows // 2
    for at in range(0, size, half):
        both[2 * at : 2 * at + half, :] = first[at : at + half, :]
        both[2 * at + half : 2 * (at + half), :] = second[at : at + half, :]
    both[2 * size :, :] = first[size:, :]


class Block:
    def __init__(self, unit, label):
        self.unit = unit
        self.label = label
        self.rows = unit.shape[0]
        self.along_rows = None

    def column(self):
        if self.along_rows is None:
            self.along_rows = jnp.transpose(jnp.broadcast_to(self.label, (LANES, self.rows)))
        return self.along_rows


def unit_in(chunk, rows, end):
    return jnp.concatenate([chunk[at : at + rows, :] for at in range(0, end, rows)], axis=1)


def labels_in(first, rows):
    lines = first[first.shape[0] - LABEL_ROWS :, :].astype(jnp.float32)
    return jnp.concatenate([lines[i : i + 1] for i in range(rows // LANES)], axis=1)


def packed(both, rows):
    return Block(unit_in(both, rows, both.shape[0] - LABEL_ROWS), labels_in(both, rows))


def first_half(first, rows):
    half = rows // 2
    unit = unit_in(first, half, first.shape[0] - LABEL_ROWS)
    return Block(unit, labels_in(first, rows)[:, :half])


def second_half(first, second, rows):
    half = rows // 2
    return Block(unit_in(second, half, second.shape[0]), labels_in(first, rows)[:, half:])


def whole(first, second, rows):
    return joined(first_half(first, rows), second_half(first, second, rows))


def joined(*blocks):
    return Block(
        jnp.concatenate([block.unit for block in blocks], axis=0),
        jnp.concatenate([block.label for block in blocks], axis=1),
    )


def best_of(queries, *all_keys):
    best = None
    for keys in all_keys:
        sims = lax.dot_general(
            keys.unit, queries.unit, (((1,), (1,)), ((), ())), preferred_element_type=jnp.float32
        )
        pieces = []
        for start in range(0, queries.rows, LANES):
            keep = keys.column() == queries.label[:, start : start + LANES]
            if keys is queries:
                row = lax.broadcasted_iota(jnp.int32, keep.shape, 0)
                column = lax.broadcasted_iota(jnp.int32, keep.shape, 1) + start
                keep = keep & (row != column)
            found = jnp.where(keep, sims[:, start : start + LANES], -1.0)
            pieces.append(jnp.max(found, axis=0, keepdims=True))
        found = jnp.concatenate(pieces, axis=1)
        best = found if best is None else jnp.maximum(best, found)
    return best


def near_kernel(own, prev_a, prev_b, succ_a, succ_b, mine, bundle):
    rows = mine.shape[1]
    put_chunks(prev_a, prev_b, bundle.at[0], rows)
    put_chunks(succ_a, succ_b, bundle.at[1], rows)
    bundle[2] = own[...]
    own = packed(own, rows)
    mine[...] = best_of(own, own, whole(prev_a, prev_b, rows), whole(succ_a, succ_b, rows))


def far_first_kernel(own, prev_a, prev_b, succ_a, succ_b, back_a, ahead_a, found):
    rows = found.shape[1]
    near = packed(own, rows), whole(prev_a, prev_b, rows), whole(succ_a, succ_b, rows)
    queries = joined(first_half(back_a, rows), first_half(ahead_a, rows))
    found[...] = best_of(queries, queries, *near)


def far_back_kernel(own, others, succ_a, succ_b, back_a, ahead_a, back_b, found, back, ahead):
    rows = found.shape[1]
    half = rows // 2
    prev_other, succ_other = packed(others.at[0], rows), packed(others.at[1], rows)
    first, rest = first_half(back_a, rows), second_half(back_a, back_b, rows)
    first_ahead = first_half(ahead_a, rows)
    keys = packed(own, rows), whole(succ_a, succ_b, rows), first_ahead
    both = best_of(joined(first, rest), succ_other)
    back[:, :half] = jnp.maximum(found[:, :half], both[:, :half])
    back[:, half:] = jnp.maximum(best_of(rest, *keys), both[:, half:])
    ahead[...] = jnp.maximum(found[:, half:], best_of(first_ahead, rest, prev_other))


def far_last_kernel(own, others, prev_a, prev_b, back_a, ahead_a, back_b, ahead_b, *refs):
    back_found, ahead_found, to_back, to_ahead = refs
    rows = to_back.shape[1]
    half = rows // 2
    back, rest = whole(back_a, back_b, rows), second_half(ahead_a, ahead_b, rows)
    keys = packed(own, rows), whole(prev_a, prev_b, rows), packed(others.at[0], rows), back
    to_back[...] = jnp.maximum(back_found[...], best_of(back, rest))
    to_ahead[:, :half] = ahead_found[...]
    to_ahead[:, half:] = best_of(rest, *keys)


def own_kernel(own, others, back_a, ahead_a, back_b, ahead_b, near, mine):
    rows = mine.shape[1]
    keys = [packed(others.at[at], rows) for at in range(3)]
    keys += [whole(back_a, back_b, rows), whole(ahead_a, ahead_b, rows)]
    mine[...] = jnp.maximum(near[...], best_of(packed(own, rows), *keys))


def ring_perms(size_x, size_y, size_z):
    chips = size_x * size_y

    def device(place, core):
        place = place % chips
        x, y = (place, 0) if place < size_x else (chips - 1 - place, 1)
        return (x * size_y + y) * size_z + core

    def perm(to):
        return [
            (device(p, k), device(*to(p, k))) for p in range(chips) for k in range(size_z)
        ]

    def from_prev(place, core):
        return core ^ (place % chips in (chips // 2 - 1, chips // 2))

    def from_next(place, core):
        return core ^ (place % chips not in (chips // 2 - 1, chips // 2))

    return {
        "sibling": perm(lambda p, k: (p, 1 - k)),
        "next": perm(lambda p, k: (p + 1, from_prev(p + 1, k))),
        "prev": perm(lambda p, k: (p - 1, from_next(p - 1, k))),
        "on_next": perm(lambda p, k: (p + 1, k)),
        "on_prev": perm(lambda p, k: (p - 1, k)),
        "home_back": perm(lambda p, k: (p - 2, from_prev(p - 1, k))),
        "home_ahead": perm(lambda p, k: (p + 2, from_next(p + 1, k))),
    }


def kernel_call(kernel, inputs, outputs, matmuls):
    vmem = pl.BlockSpec(memory_space=pltpu.VMEM)
    return pl.pallas_call(
        kernel,
        out_shape=outputs,
        in_specs=[vmem] * len(inputs),
        out_specs=[vmem] * len(outputs),
        compiler_params=pltpu.CompilerParams(vmem_limit_bytes=VMEM_BYTES),
        cost_estimate=pl.CostEstimate(
            flops=matmuls * 2**26, bytes_accessed=2**20, transcendentals=0
        ),
        name=kernel.__name__,
    )(*inputs)


def on_ring(embeds, cluster):
    rows, width = embeds.shape
    half = rows // 2
    perms = ring_perms(*(lax.axis_size(a) for a in GROUP))

    def send(value, name):
        return lax.ppermute(value, GROUP, perms[name])

    line = jax.ShapeDtypeStruct((1, rows), jnp.float32)
    half_line = jax.ShapeDtypeStruct((1, half), jnp.float32)

    def chunk(count, labels):
        size = count * width // LANES + labels * LABEL_ROWS
        return jax.ShapeDtypeStruct((size, LANES), jnp.bfloat16)

    anywhere = pl.BlockSpec(memory_space=pl.ANY)
    vmem = pl.BlockSpec(memory_space=pltpu.VMEM)
    own_a = pl.pallas_call(
        pack_first_kernel,
        out_shape=chunk(half, True),
        in_specs=[anywhere] * 2,
        out_specs=vmem,
        scratch_shapes=[
            pltpu.VMEM((half, width), jnp.bfloat16),
            pltpu.VMEM((1, rows), jnp.int32),
            pltpu.SemaphoreType.DMA((2,)),
        ],
        compiler_params=pltpu.CompilerParams(vmem_limit_bytes=VMEM_BYTES),
        name="pack_first",
    )(
        pltpu.with_memory_space_constraint(embeds, pltpu.HBM),
        pltpu.with_memory_space_constraint(cluster.reshape(1, rows), pltpu.HBM),
    )
    own_b, own = kernel_call(
        pack_second_kernel, [embeds, own_a], [chunk(half, False), chunk(rows, True)], 1
    )
    prev_a, succ_a = send(own_a, "next"), send(own_a, "prev")
    prev_b, succ_b = send(own_b, "next"), send(own_b, "prev")
    back_a, ahead_a = send(prev_a, "on_next"), send(succ_a, "on_prev")
    back_b, ahead_b = send(prev_b, "on_next"), send(succ_b, "on_prev")
    prev, succ, far = [prev_a, prev_b], [succ_a, succ_b], [back_a, ahead_a, back_b, ahead_b]
    bundle_shape = jax.ShapeDtypeStruct((3, *chunk(rows, True).shape), jnp.bfloat16)
    mine, bundle = kernel_call(near_kernel, [own, *prev, *succ], [line, bundle_shape], NEAR_COST)
    others = send(bundle, "sibling")
    (found,) = kernel_call(
        far_first_kernel, [own, *prev, *succ, back_a, ahead_a], [line], FIRST_COST
    )
    found = kernel_call(
        far_back_kernel,
        [own, others, *succ, back_a, ahead_a, back_b, found],
        [line, half_line],
        BACK_COST,
    )
    to_back, to_ahead = kernel_call(
        far_last_kernel, [own, others, *prev, *far, *found], [line] * 2, LAST_COST
    )
    (mine,) = kernel_call(own_kernel, [own, others, *far, mine], [line], 5)
    best = jnp.maximum(
        mine, jnp.maximum(send(to_back, "home_back"), send(to_ahead, "home_ahead"))
    )
    return best.reshape(rows)


def masked_sims(queries, query_labels, query_ids, keys, key_labels, key_ids):
    sims = jnp.einsum("qd,kd->qk", queries, keys, preferred_element_type=jnp.float32)
    keep = (
        (query_labels[:, None] == key_labels[None, :])
        & (query_labels[:, None] >= 0)
        & (query_ids[:, None] != key_ids[None, :])
    )
    return jnp.where(keep, sims, -1.0)


def by_owner(embeds, cluster):
    rows, width = embeds.shape
    size_x = lax.axis_size("gx")
    size_y = lax.axis_size("gy")
    owners = size_x * size_y
    cap = 2 * rows // owners
    total = owners * cap
    unit = normalised(embeds)
    target = cluster // CLU_OWN
    onehot = (target[:, None] == jnp.arange(owners, dtype=jnp.int32)[None, :]).astype(jnp.int32)
    before = jnp.cumsum(onehot, axis=0) - onehot
    slot = jnp.sum(before * onehot, axis=1)
    place = target * cap + slot
    outgoing = jnp.zeros((total, width), jnp.bfloat16).at[place].set(unit)
    out_labels = jnp.full((total,), -1, jnp.int32).at[place].set(cluster)
    got, got_labels = (
        lax.all_to_all(
            outgoing.reshape(owners, cap, width),
            ("gx", "gy"),
            split_axis=0,
            concat_axis=0,
            tiled=True,
        ),
        lax.all_to_all(
            out_labels.reshape(owners, cap), ("gx", "gy"), split_axis=0, concat_axis=0, tiled=True
        ),
    )
    members = got.reshape(total, width)
    labels = got_labels.reshape(total)
    core = lax.axis_index("gz")
    query_ids = core * total + jnp.arange(total, dtype=jnp.int32)
    keys = lax.all_gather(members, "gz", axis=0, tiled=True)
    key_labels = lax.all_gather(labels, "gz", axis=0, tiled=True)
    key_ids = jnp.arange(keys.shape[0], dtype=jnp.int32)
    best = jnp.maximum(
        jnp.full((total,), -1.0, jnp.float32),
        jnp.max(masked_sims(members, labels, query_ids, keys, key_labels, key_ids), axis=1),
    )
    back = lax.all_to_all(
        best.reshape(owners, cap), ("gx", "gy"), split_axis=0, concat_axis=0, tiled=True
    )
    return back.reshape(total)[place]


def solution(mesh):
    shape = mesh.shape
    ring = shape["gx"] * shape["gy"] == 8 and shape["gy"] == 2 and shape["gz"] == 2
    placed = (P(("parts", "gx", "gy", "gz"), None), P(("parts", "gx", "gy", "gz")))
    return jax.shard_map(
        on_ring if ring else by_owner,
        mesh=mesh,
        in_specs=placed,
        out_specs=P(("parts", "gx", "gy", "gz")),
        check_vma=False,
    )
```

```python
import jax
import jax.numpy as jnp
from jax import lax
from jax.experimental import pallas as pl
from jax.experimental.pallas import tpu as pltpu
from jax.sharding import PartitionSpec as P

CLU_OWN = 16


EPS = 1e-06

GROUP = ("gx", "gy", "gz")


def normalised(block):
    vecs = block.astype(jnp.float32)
    return (vecs * lax.rsqrt(jnp.sum(vecs * vecs, axis=1, keepdims=True) + EPS)).astype(
        jnp.bfloat16
    )


LANES = 128
LABEL_ROWS = 16
VMEM_BYTES = 32 * 2**20
NEAR_COST = 1
FIRST_COST = 200
BACK_COST = 2
LAST_COST = 5


def put_unit(unit, chunk, at, size):
    count, width = unit.shape
    for j in range(width // LANES):
        chunk[j * size + at : j * size + at + count, :] = unit[:, j * LANES : (j + 1) * LANES]


def pack_first_kernel(embeds, label, first, raw, line, sems):
    rows, width = embeds.shape
    half = rows // 2
    copies = [
        pltpu.make_async_copy(label, line, sems.at[0]),
        pltpu.make_async_copy(embeds.at[pl.ds(0, half)], raw, sems.at[1]),
    ]
    for copy in copies:
        copy.start()
    copies[0].wait()
    row = lax.broadcasted_iota(jnp.int32, (LABEL_ROWS, LANES), 0)
    lines = jnp.zeros((LABEL_ROWS, LANES), jnp.float32)
    for i in range(rows // LANES):
        piece = line[:, i * LANES : (i + 1) * LANES].astype(jnp.float32)
        lines = jnp.where(row == i, piece, lines)
    first[half * width // LANES :, :] = lines.astype(jnp.bfloat16)
    copies[1].wait()
    put_unit(normalised(raw[...]), first, 0, half)


def pack_second_kernel(embeds, first, second, both):
    rows, width = embeds.shape
    half = rows // 2
    unit = normalised(embeds[half:, :])
    put_unit(unit, second, 0, half)
    put_chunks(first, second, both, rows)


def put_chunks(first, second, both, rows):
    size = second.shape[0]
    half = rows // 2
    for at in range(0, size, half):
        both[2 * at : 2 * at + half, :] = first[at : at + half, :]
        both[2 * at + half : 2 * (at + half), :] = second[at : at + half, :]
    both[2 * size :, :] = first[size:, :]


class Block:
    def __init__(self, unit, label):
        self.unit = unit
        self.label = label
        self.rows = unit.shape[0]
        self.along_rows = None

    def column(self):
        if self.along_rows is None:
            self.along_rows = jnp.transpose(jnp.broadcast_to(self.label, (LANES, self.rows)))
        return self.along_rows


def unit_in(chunk, rows, end):
    return jnp.concatenate([chunk[at : at + rows, :] for at in range(0, end, rows)], axis=1)


def labels_in(first, rows):
    lines = first[first.shape[0] - LABEL_ROWS :, :].astype(jnp.float32)
    return jnp.concatenate([lines[i : i + 1] for i in range(rows // LANES)], axis=1)


def packed(both, rows):
    return Block(unit_in(both, rows, both.shape[0] - LABEL_ROWS), labels_in(both, rows))


def first_half(first, rows):
    half = rows // 2
    unit = unit_in(first, half, first.shape[0] - LABEL_ROWS)
    return Block(unit, labels_in(first, rows)[:, :half])


def second_half(first, second, rows):
    half = rows // 2
    return Block(unit_in(second, half, second.shape[0]), labels_in(first, rows)[:, half:])


def whole(first, second, rows):
    return joined(first_half(first, rows), second_half(first, second, rows))


def joined(*blocks):
    return Block(
        jnp.concatenate([block.unit for block in blocks], axis=0),
        jnp.concatenate([block.label for block in blocks], axis=1),
    )


def best_of(queries, *all_keys):
    best = None
    for keys in all_keys:
        sims = lax.dot_general(
            keys.unit, queries.unit, (((1,), (1,)), ((), ())), preferred_element_type=jnp.float32
        )
        pieces = []
        for start in range(0, queries.rows, LANES):
            keep = keys.column() == queries.label[:, start : start + LANES]
            if keys is queries:
                row = lax.broadcasted_iota(jnp.int32, keep.shape, 0)
                column = lax.broadcasted_iota(jnp.int32, keep.shape, 1) + start
                keep = keep & (row != column)
            found = jnp.where(keep, sims[:, start : start + LANES], -1.0)
            pieces.append(jnp.max(found, axis=0, keepdims=True))
        found = jnp.concatenate(pieces, axis=1)
        best = found if best is None else jnp.maximum(best, found)
    return best


def near_kernel(own, prev_a, prev_b, succ_a, succ_b, mine, bundle):
    rows = mine.shape[1]
    put_chunks(prev_a, prev_b, bundle.at[0], rows)
    put_chunks(succ_a, succ_b, bundle.at[1], rows)
    bundle[2] = own[...]
    own = packed(own, rows)
    mine[...] = best_of(own, own, whole(prev_a, prev_b, rows), whole(succ_a, succ_b, rows))


def far_first_kernel(own, prev_a, prev_b, succ_a, succ_b, back_a, ahead_a, found):
    rows = found.shape[1]
    near = packed(own, rows), whole(prev_a, prev_b, rows), whole(succ_a, succ_b, rows)
    queries = joined(first_half(back_a, rows), first_half(ahead_a, rows))
    found[...] = best_of(queries, queries, *near)


def far_back_kernel(own, others, succ_a, succ_b, back_a, ahead_a, back_b, found, back, ahead):
    rows = found.shape[1]
    half = rows // 2
    prev_other, succ_other = packed(others.at[0], rows), packed(others.at[1], rows)
    first, rest = first_half(back_a, rows), second_half(back_a, back_b, rows)
    first_ahead = first_half(ahead_a, rows)
    keys = packed(own, rows), whole(succ_a, succ_b, rows), first_ahead
    both = best_of(joined(first, rest), succ_other)
    back[:, :half] = jnp.maximum(found[:, :half], both[:, :half])
    back[:, half:] = jnp.maximum(best_of(rest, *keys), both[:, half:])
    ahead[...] = jnp.maximum(found[:, half:], best_of(first_ahead, rest, prev_other))


def place_and_core():
    x, y = lax.axis_index("gx"), lax.axis_index("gy")
    chips = lax.axis_size("gx") * lax.axis_size("gy")
    return jnp.where(y == 0, x, chips - 1 - x), lax.axis_index("gz")


def line_of(place, core):
    return place % (lax.axis_size("gx") * lax.axis_size("gy")) * lax.axis_size("gz") + core


def far_last_kernel(own, others, prev_a, prev_b, back_a, ahead_a, back_b, ahead_b, *refs):
    back_found, ahead_found, table = refs
    rows = table.shape[1]
    half = rows // 2
    back, rest = whole(back_a, back_b, rows), second_half(ahead_a, ahead_b, rows)
    keys = packed(own, rows), whole(prev_a, prev_b, rows), packed(others.at[0], rows), back
    place, core = place_and_core()
    chips = lax.axis_size("gx") * lax.axis_size("gy")
    to_back = line_of(place + chips - 2, core ^ changes((place + chips - 1) % chips))
    to_ahead = line_of(place + 2, core ^ 1 ^ changes((place + 1) % chips))
    back_best = jnp.maximum(back_found[...], best_of(back, rest))
    ahead_best = jnp.concatenate([ahead_found[...], best_of(rest, *keys)], axis=1)
    line = lax.broadcasted_iota(jnp.int32, table.shape, 0)
    others_best = jnp.where(line == to_ahead, ahead_best, -1.0)
    table[...] = jnp.where(line == to_back, back_best, others_best)


def last_kernel(table, mine, best):
    line = lax.broadcasted_iota(jnp.int32, table.shape, 0)
    found = jnp.where(line == line_of(*place_and_core()), table[...], -1.0)
    best[...] = jnp.maximum(mine[...], jnp.max(found, axis=0, keepdims=True))


def own_kernel(own, others, back_a, ahead_a, back_b, ahead_b, near, mine):
    rows = mine.shape[1]
    keys = [packed(others.at[at], rows) for at in range(3)]
    keys += [whole(back_a, back_b, rows), whole(ahead_a, ahead_b, rows)]
    mine[...] = jnp.maximum(near[...], best_of(packed(own, rows), *keys))


def changes(place):
    return jnp.int32(place < 2)


def ring_perms(size_x, size_y, size_z):
    chips = size_x * size_y

    def device(place, core):
        place = place % chips
        x, y = (place, 0) if place < size_x else (chips - 1 - place, 1)
        return (x * size_y + y) * size_z + core

    def perm(to):
        return [
            (device(p, k), device(*to(p, k))) for p in range(chips) for k in range(size_z)
        ]

    def from_prev(place, core):
        return core ^ (place % chips in (0, 1))

    def from_next(place, core):
        return core ^ (place % chips not in (0, 1))

    return {
        "sibling": perm(lambda p, k: (p, 1 - k)),
        "next": perm(lambda p, k: (p + 1, from_prev(p + 1, k))),
        "prev": perm(lambda p, k: (p - 1, from_next(p - 1, k))),
        "on_next": perm(lambda p, k: (p + 1, k)),
        "on_prev": perm(lambda p, k: (p - 1, k)),
        "home_back": perm(lambda p, k: (p - 2, from_prev(p - 1, k))),
        "home_ahead": perm(lambda p, k: (p + 2, from_next(p + 1, k))),
    }


def kernel_call(kernel, inputs, outputs, matmuls):
    vmem = pl.BlockSpec(memory_space=pltpu.VMEM)
    return pl.pallas_call(
        kernel,
        out_shape=outputs,
        in_specs=[vmem] * len(inputs),
        out_specs=[vmem] * len(outputs),
        compiler_params=pltpu.CompilerParams(vmem_limit_bytes=VMEM_BYTES),
        cost_estimate=pl.CostEstimate(
            flops=matmuls * 2**26, bytes_accessed=2**20, transcendentals=0
        ),
        name=kernel.__name__,
    )(*inputs)


def on_ring(embeds, cluster):
    rows, width = embeds.shape
    half = rows // 2
    perms = ring_perms(*(lax.axis_size(a) for a in GROUP))

    def send(value, name):
        return lax.ppermute(value, GROUP, perms[name])

    line = jax.ShapeDtypeStruct((1, rows), jnp.float32)
    half_line = jax.ShapeDtypeStruct((1, half), jnp.float32)

    def chunk(count, labels):
        size = count * width // LANES + labels * LABEL_ROWS
        return jax.ShapeDtypeStruct((size, LANES), jnp.bfloat16)

    anywhere = pl.BlockSpec(memory_space=pl.ANY)
    vmem = pl.BlockSpec(memory_space=pltpu.VMEM)
    own_a = pl.pallas_call(
        pack_first_kernel,
        out_shape=chunk(half, True),
        in_specs=[anywhere] * 2,
        out_specs=vmem,
        scratch_shapes=[
            pltpu.VMEM((half, width), jnp.bfloat16),
            pltpu.VMEM((1, rows), jnp.int32),
            pltpu.SemaphoreType.DMA((2,)),
        ],
        compiler_params=pltpu.CompilerParams(vmem_limit_bytes=VMEM_BYTES),
        name="pack_first",
    )(
        pltpu.with_memory_space_constraint(embeds, pltpu.HBM),
        pltpu.with_memory_space_constraint(cluster.reshape(1, rows), pltpu.HBM),
    )
    own_b, own = kernel_call(
        pack_second_kernel, [embeds, own_a], [chunk(half, False), chunk(rows, True)], 1
    )
    prev_a, succ_a = send(own_a, "next"), send(own_a, "prev")
    prev_b, succ_b = send(own_b, "next"), send(own_b, "prev")
    back_a, ahead_a = send(prev_a, "on_next"), send(succ_a, "on_prev")
    back_b, ahead_b = send(prev_b, "on_next"), send(succ_b, "on_prev")
    prev, succ, far = [prev_a, prev_b], [succ_a, succ_b], [back_a, ahead_a, back_b, ahead_b]
    bundle_shape = jax.ShapeDtypeStruct((3, *chunk(rows, True).shape), jnp.bfloat16)
    mine, bundle = kernel_call(near_kernel, [own, *prev, *succ], [line, bundle_shape], NEAR_COST)
    others = send(bundle, "sibling")
    (found,) = kernel_call(
        far_first_kernel, [own, *prev, *succ, back_a, ahead_a], [line], FIRST_COST
    )
    found = kernel_call(
        far_back_kernel,
        [own, others, *succ, back_a, ahead_a, back_b, found],
        [line, half_line],
        BACK_COST,
    )
    devices = lax.axis_size(GROUP)
    (table,) = kernel_call(
        far_last_kernel,
        [own, others, *prev, *far, *found],
        [jax.ShapeDtypeStruct((devices, rows), jnp.float32)],
        LAST_COST,
    )
    (mine,) = kernel_call(own_kernel, [own, others, *far, mine], [line], 5)
    (best,) = kernel_call(last_kernel, [lax.pmax(table, GROUP), mine], [line], 1)
    return best.reshape(rows)


def masked_sims(queries, query_labels, query_ids, keys, key_labels, key_ids):
    sims = jnp.einsum("qd,kd->qk", queries, keys, preferred_element_type=jnp.float32)
    keep = (
        (query_labels[:, None] == key_labels[None, :])
        & (query_labels[:, None] >= 0)
        & (query_ids[:, None] != key_ids[None, :])
    )
    return jnp.where(keep, sims, -1.0)


def by_owner(embeds, cluster):
    rows, width = embeds.shape
    size_x = lax.axis_size("gx")
    size_y = lax.axis_size("gy")
    owners = size_x * size_y
    cap = 2 * rows // owners
    total = owners * cap
    unit = normalised(embeds)
    target = cluster // CLU_OWN
    onehot = (target[:, None] == jnp.arange(owners, dtype=jnp.int32)[None, :]).astype(jnp.int32)
    before = jnp.cumsum(onehot, axis=0) - onehot
    slot = jnp.sum(before * onehot, axis=1)
    place = target * cap + slot
    outgoing = jnp.zeros((total, width), jnp.bfloat16).at[place].set(unit)
    out_labels = jnp.full((total,), -1, jnp.int32).at[place].set(cluster)
    got, got_labels = (
        lax.all_to_all(
            outgoing.reshape(owners, cap, width),
            ("gx", "gy"),
            split_axis=0,
            concat_axis=0,
            tiled=True,
        ),
        lax.all_to_all(
            out_labels.reshape(owners, cap), ("gx", "gy"), split_axis=0, concat_axis=0, tiled=True
        ),
    )
    members = got.reshape(total, width)
    labels = got_labels.reshape(total)
    core = lax.axis_index("gz")
    query_ids = core * total + jnp.arange(total, dtype=jnp.int32)
    keys = lax.all_gather(members, "gz", axis=0, tiled=True)
    key_labels = lax.all_gather(labels, "gz", axis=0, tiled=True)
    key_ids = jnp.arange(keys.shape[0], dtype=jnp.int32)
    best = jnp.maximum(
        jnp.full((total,), -1.0, jnp.float32),
        jnp.max(masked_sims(members, labels, query_ids, keys, key_labels, key_ids), axis=1),
    )
    back = lax.all_to_all(
        best.reshape(owners, cap), ("gx", "gy"), split_axis=0, concat_axis=0, tiled=True
    )
    return back.reshape(total)[place]


def solution(mesh):
    shape = mesh.shape
    ring = shape["gx"] * shape["gy"] == 8 and shape["gy"] == 2 and shape["gz"] == 2
    placed = (P(("parts", "gx", "gy", "gz"), None), P(("parts", "gx", "gy", "gz")))
    return jax.shard_map(
        on_ring if ring else by_owner,
        mesh=mesh,
        in_specs=placed,
        out_specs=P(("parts", "gx", "gy", "gz")),
        check_vma=False,
    )
```

```python
import jax
import jax.numpy as jnp
from jax import lax
from jax.experimental import pallas as pl
from jax.experimental.pallas import tpu as pltpu
from jax.sharding import PartitionSpec as P

CLU_OWN = 16


EPS = 1e-06

GROUP = ("gx", "gy", "gz")


def normalised(block):
    vecs = block.astype(jnp.float32)
    return (vecs * lax.rsqrt(jnp.sum(vecs * vecs, axis=1, keepdims=True) + EPS)).astype(
        jnp.bfloat16
    )


LANES = 128
LABEL_ROWS = 16
VMEM_BYTES = 32 * 2**20
NEAR_COST = 1
FIRST_COST = 200
BACK_COST = 2
LAST_COST = 5


def put_unit(unit, chunk, at, size):
    count, width = unit.shape
    for j in range(width // LANES):
        chunk[j * size + at : j * size + at + count, :] = unit[:, j * LANES : (j + 1) * LANES]


def pack_first_kernel(embeds, label, first, raw, line, sems):
    rows, width = embeds.shape
    half = rows // 2
    copies = [
        pltpu.make_async_copy(label, line, sems.at[0]),
        pltpu.make_async_copy(embeds.at[pl.ds(0, half)], raw, sems.at[1]),
    ]
    for copy in copies:
        copy.start()
    copies[0].wait()
    row = lax.broadcasted_iota(jnp.int32, (LABEL_ROWS, LANES), 0)
    lines = jnp.zeros((LABEL_ROWS, LANES), jnp.float32)
    for i in range(rows // LANES):
        piece = line[:, i * LANES : (i + 1) * LANES].astype(jnp.float32)
        lines = jnp.where(row == i, piece, lines)
    first[half * width // LANES :, :] = lines.astype(jnp.bfloat16)
    copies[1].wait()
    put_unit(normalised(raw[...]), first, 0, half)


def pack_second_kernel(embeds, first, second, both):
    rows, width = embeds.shape
    half = rows // 2
    unit = normalised(embeds[half:, :])
    put_unit(unit, second, 0, half)
    put_chunks(first, second, both, rows)


def put_chunks(first, second, both, rows):
    size = second.shape[0]
    half = rows // 2
    for at in range(0, size, half):
        both[2 * at : 2 * at + half, :] = first[at : at + half, :]
        both[2 * at + half : 2 * (at + half), :] = second[at : at + half, :]
    both[2 * size :, :] = first[size:, :]


class Block:
    def __init__(self, unit, label):
        self.unit = unit
        self.label = label
        self.rows = unit.shape[0]
        self.along_rows = None

    def column(self):
        if self.along_rows is None:
            self.along_rows = jnp.transpose(jnp.broadcast_to(self.label, (LANES, self.rows)))
        return self.along_rows


def unit_in(chunk, rows, end):
    return jnp.concatenate([chunk[at : at + rows, :] for at in range(0, end, rows)], axis=1)


def labels_in(first, rows):
    lines = first[first.shape[0] - LABEL_ROWS :, :].astype(jnp.float32)
    return jnp.concatenate([lines[i : i + 1] for i in range(rows // LANES)], axis=1)


def packed(both, rows):
    return Block(unit_in(both, rows, both.shape[0] - LABEL_ROWS), labels_in(both, rows))


def first_half(first, rows):
    half = rows // 2
    unit = unit_in(first, half, first.shape[0] - LABEL_ROWS)
    return Block(unit, labels_in(first, rows)[:, :half])


def second_half(first, second, rows):
    half = rows // 2
    return Block(unit_in(second, half, second.shape[0]), labels_in(first, rows)[:, half:])


def whole(first, second, rows):
    return joined(first_half(first, rows), second_half(first, second, rows))


def joined(*blocks):
    return Block(
        jnp.concatenate([block.unit for block in blocks], axis=0),
        jnp.concatenate([block.label for block in blocks], axis=1),
    )


def best_of(queries, *all_keys):
    best = None
    for keys in all_keys:
        sims = lax.dot_general(
            keys.unit, queries.unit, (((1,), (1,)), ((), ())), preferred_element_type=jnp.float32
        )
        pieces = []
        for start in range(0, queries.rows, LANES):
            keep = keys.column() == queries.label[:, start : start + LANES]
            if keys is queries:
                row = lax.broadcasted_iota(jnp.int32, keep.shape, 0)
                column = lax.broadcasted_iota(jnp.int32, keep.shape, 1) + start
                keep = keep & (row != column)
            found = jnp.where(keep, sims[:, start : start + LANES], -1.0)
            pieces.append(jnp.max(found, axis=0, keepdims=True))
        found = jnp.concatenate(pieces, axis=1)
        best = found if best is None else jnp.maximum(best, found)
    return best


def near_kernel(own, prev_a, prev_b, succ_a, succ_b, mine, bundle):
    rows = mine.shape[1]
    put_chunks(prev_a, prev_b, bundle.at[0], rows)
    put_chunks(succ_a, succ_b, bundle.at[1], rows)
    bundle[2] = own[...]
    own = packed(own, rows)
    mine[...] = best_of(own, own, whole(prev_a, prev_b, rows), whole(succ_a, succ_b, rows))


def far_first_kernel(own, prev_a, prev_b, succ_a, succ_b, back_a, ahead_a, found):
    rows = found.shape[1]
    near = packed(own, rows), whole(prev_a, prev_b, rows), whole(succ_a, succ_b, rows)
    queries = joined(first_half(back_a, rows), first_half(ahead_a, rows))
    found[...] = best_of(queries, queries, *near)


def far_back_kernel(own, others, succ_a, succ_b, back_a, ahead_a, back_b, found, back, ahead):
    rows = found.shape[1]
    half = rows // 2
    prev_other, succ_other = packed(others.at[0], rows), packed(others.at[1], rows)
    first, rest = first_half(back_a, rows), second_half(back_a, back_b, rows)
    first_ahead = first_half(ahead_a, rows)
    keys = packed(own, rows), whole(succ_a, succ_b, rows), first_ahead
    both = best_of(joined(first, rest), succ_other)
    back[:, :half] = jnp.maximum(found[:, :half], both[:, :half])
    back[:, half:] = jnp.maximum(best_of(rest, *keys), both[:, half:])
    ahead[...] = jnp.maximum(found[:, half:], best_of(first_ahead, rest, prev_other))


def far_last_kernel(own, others, prev_a, prev_b, back_a, ahead_a, back_b, ahead_b, *refs):
    back_found, ahead_found, to_back, to_ahead = refs
    rows = to_back.shape[1]
    half = rows // 2
    back, rest = whole(back_a, back_b, rows), second_half(ahead_a, ahead_b, rows)
    keys = packed(own, rows), whole(prev_a, prev_b, rows), packed(others.at[0], rows), back
    to_back[...] = jnp.maximum(back_found[...], best_of(back, rest))
    to_ahead[:, :half] = ahead_found[...]
    to_ahead[:, half:] = best_of(rest, *keys)


def own_kernel(own, others, back_a, ahead_a, back_b, ahead_b, near, mine):
    rows = mine.shape[1]
    keys = [packed(others.at[at], rows) for at in range(3)]
    keys += [whole(back_a, back_b, rows), whole(ahead_a, ahead_b, rows)]
    mine[...] = jnp.maximum(near[...], best_of(packed(own, rows), *keys))


def ring_perms(size_x, size_y, size_z):
    chips = size_x * size_y

    def device(place, core):
        place = place % chips
        x, y = (place, 1) if place < size_x else (chips - 1 - place, 0)
        return (x * size_y + y) * size_z + core

    def perm(to):
        return [
            (device(p, k), device(*to(p, k))) for p in range(chips) for k in range(size_z)
        ]

    def from_prev(place, core):
        return core ^ (place % chips in (0, 1))

    def from_next(place, core):
        return core ^ (place % chips not in (0, 1))

    return {
        "sibling": perm(lambda p, k: (p, 1 - k)),
        "next": perm(lambda p, k: (p + 1, from_prev(p + 1, k))),
        "prev": perm(lambda p, k: (p - 1, from_next(p - 1, k))),
        "on_next": perm(lambda p, k: (p + 1, k)),
        "on_prev": perm(lambda p, k: (p - 1, k)),
        "home_back": perm(lambda p, k: (p - 2, from_prev(p - 1, k))),
        "home_ahead": perm(lambda p, k: (p + 2, from_next(p + 1, k))),
    }


def kernel_call(kernel, inputs, outputs, matmuls):
    vmem = pl.BlockSpec(memory_space=pltpu.VMEM)
    return pl.pallas_call(
        kernel,
        out_shape=outputs,
        in_specs=[vmem] * len(inputs),
        out_specs=[vmem] * len(outputs),
        compiler_params=pltpu.CompilerParams(vmem_limit_bytes=VMEM_BYTES),
        cost_estimate=pl.CostEstimate(
            flops=matmuls * 2**26, bytes_accessed=2**20, transcendentals=0
        ),
        name=kernel.__name__,
    )(*inputs)


def on_ring(embeds, cluster):
    rows, width = embeds.shape
    half = rows // 2
    perms = ring_perms(*(lax.axis_size(a) for a in GROUP))

    def send(value, name):
        return lax.ppermute(value, GROUP, perms[name])

    line = jax.ShapeDtypeStruct((1, rows), jnp.float32)
    half_line = jax.ShapeDtypeStruct((1, half), jnp.float32)

    def chunk(count, labels):
        size = count * width // LANES + labels * LABEL_ROWS
        return jax.ShapeDtypeStruct((size, LANES), jnp.bfloat16)

    anywhere = pl.BlockSpec(memory_space=pl.ANY)
    vmem = pl.BlockSpec(memory_space=pltpu.VMEM)
    own_a = pl.pallas_call(
        pack_first_kernel,
        out_shape=chunk(half, True),
        in_specs=[anywhere] * 2,
        out_specs=vmem,
        scratch_shapes=[
            pltpu.VMEM((half, width), jnp.bfloat16),
            pltpu.VMEM((1, rows), jnp.int32),
            pltpu.SemaphoreType.DMA((2,)),
        ],
        compiler_params=pltpu.CompilerParams(vmem_limit_bytes=VMEM_BYTES),
        name="pack_first",
    )(
        pltpu.with_memory_space_constraint(embeds, pltpu.HBM),
        pltpu.with_memory_space_constraint(cluster.reshape(1, rows), pltpu.HBM),
    )
    own_b, own = kernel_call(
        pack_second_kernel, [embeds, own_a], [chunk(half, False), chunk(rows, True)], 1
    )
    prev_a, succ_a = send(own_a, "next"), send(own_a, "prev")
    prev_b, succ_b = send(own_b, "next"), send(own_b, "prev")
    back_a, ahead_a = send(prev_a, "on_next"), send(succ_a, "on_prev")
    back_b, ahead_b = send(prev_b, "on_next"), send(succ_b, "on_prev")
    prev, succ, far = [prev_a, prev_b], [succ_a, succ_b], [back_a, ahead_a, back_b, ahead_b]
    bundle_shape = jax.ShapeDtypeStruct((3, *chunk(rows, True).shape), jnp.bfloat16)
    mine, bundle = kernel_call(near_kernel, [own, *prev, *succ], [line, bundle_shape], NEAR_COST)
    others = send(bundle, "sibling")
    (found,) = kernel_call(
        far_first_kernel, [own, *prev, *succ, back_a, ahead_a], [line], FIRST_COST
    )
    found = kernel_call(
        far_back_kernel,
        [own, others, *succ, back_a, ahead_a, back_b, found],
        [line, half_line],
        BACK_COST,
    )
    to_back, to_ahead = kernel_call(
        far_last_kernel, [own, others, *prev, *far, *found], [line] * 2, LAST_COST
    )
    (mine,) = kernel_call(own_kernel, [own, others, *far, mine], [line], 5)
    best = jnp.maximum(
        mine, jnp.maximum(send(to_back, "home_back"), send(to_ahead, "home_ahead"))
    )
    return best.reshape(rows)


def masked_sims(queries, query_labels, query_ids, keys, key_labels, key_ids):
    sims = jnp.einsum("qd,kd->qk", queries, keys, preferred_element_type=jnp.float32)
    keep = (
        (query_labels[:, None] == key_labels[None, :])
        & (query_labels[:, None] >= 0)
        & (query_ids[:, None] != key_ids[None, :])
    )
    return jnp.where(keep, sims, -1.0)


def by_owner(embeds, cluster):
    rows, width = embeds.shape
    size_x = lax.axis_size("gx")
    size_y = lax.axis_size("gy")
    owners = size_x * size_y
    cap = 2 * rows // owners
    total = owners * cap
    unit = normalised(embeds)
    target = cluster // CLU_OWN
    onehot = (target[:, None] == jnp.arange(owners, dtype=jnp.int32)[None, :]).astype(jnp.int32)
    before = jnp.cumsum(onehot, axis=0) - onehot
    slot = jnp.sum(before * onehot, axis=1)
    place = target * cap + slot
    outgoing = jnp.zeros((total, width), jnp.bfloat16).at[place].set(unit)
    out_labels = jnp.full((total,), -1, jnp.int32).at[place].set(cluster)
    got, got_labels = (
        lax.all_to_all(
            outgoing.reshape(owners, cap, width),
            ("gx", "gy"),
            split_axis=0,
            concat_axis=0,
            tiled=True,
        ),
        lax.all_to_all(
            out_labels.reshape(owners, cap), ("gx", "gy"), split_axis=0, concat_axis=0, tiled=True
        ),
    )
    members = got.reshape(total, width)
    labels = got_labels.reshape(total)
    core = lax.axis_index("gz")
    query_ids = core * total + jnp.arange(total, dtype=jnp.int32)
    keys = lax.all_gather(members, "gz", axis=0, tiled=True)
    key_labels = lax.all_gather(labels, "gz", axis=0, tiled=True)
    key_ids = jnp.arange(keys.shape[0], dtype=jnp.int32)
    best = jnp.maximum(
        jnp.full((total,), -1.0, jnp.float32),
        jnp.max(masked_sims(members, labels, query_ids, keys, key_labels, key_ids), axis=1),
    )
    back = lax.all_to_all(
        best.reshape(owners, cap), ("gx", "gy"), split_axis=0, concat_axis=0, tiled=True
    )
    return back.reshape(total)[place]


def solution(mesh):
    shape = mesh.shape
    ring = shape["gx"] * shape["gy"] == 8 and shape["gy"] == 2 and shape["gz"] == 2
    placed = (P(("parts", "gx", "gy", "gz"), None), P(("parts", "gx", "gy", "gz")))
    return jax.shard_map(
        on_ring if ring else by_owner,
        mesh=mesh,
        in_specs=placed,
        out_specs=P(("parts", "gx", "gy", "gz")),
        check_vma=False,
    )
```

```python
import jax
import jax.numpy as jnp
from jax import lax
from jax.experimental import pallas as pl
from jax.experimental.pallas import tpu as pltpu
from jax.sharding import PartitionSpec as P

CLU_OWN = 16


EPS = 1e-06

GROUP = ("gx", "gy", "gz")


def normalised(block):
    vecs = block.astype(jnp.float32)
    return (vecs * lax.rsqrt(jnp.sum(vecs * vecs, axis=1, keepdims=True) + EPS)).astype(
        jnp.bfloat16
    )


LANES = 128
LABEL_ROWS = 16
VMEM_BYTES = 32 * 2**20
NEAR_COST = 1
FIRST_COST = 200
BACK_COST = 2
LAST_COST = 5


def put_unit(unit, chunk):
    count, width = unit.shape
    for j in range(width // LANES):
        chunk[j * count : (j + 1) * count, :] = unit[:, j * LANES : (j + 1) * LANES]


def pack_first_kernel(embeds, label, first, line, sems):
    rows, width = embeds.shape
    half = rows // 2
    copies = []
    for j in range(width // LANES):
        part = embeds.at[pl.ds(0, half), pl.ds(j * LANES, LANES)]
        copies.append(pltpu.make_async_copy(part, first.at[pl.ds(j * half, half)], sems.at[j]))
    copies.append(pltpu.make_async_copy(label, line, sems.at[width // LANES]))
    for copy in copies:
        copy.start()
    copies[-1].wait()
    row = lax.broadcasted_iota(jnp.int32, (LABEL_ROWS, LANES), 0)
    lines = jnp.zeros((LABEL_ROWS, LANES), jnp.float32)
    for i in range(rows // LANES):
        piece = line[:, i * LANES : (i + 1) * LANES].astype(jnp.float32)
        lines = jnp.where(row == i, piece, lines)
    first[half * width // LANES :, :] = lines.astype(jnp.bfloat16)
    for copy in copies[:-1]:
        copy.wait()


def pack_second_kernel(embeds, first, second, both):
    rows, width = embeds.shape
    unit = normalised(embeds[...])
    put_unit(unit[rows // 2 :, :], second)
    put_unit(unit, both)
    put_labels(first, both)


def put_labels(source, both):
    both[both.shape[0] - LABEL_ROWS :, :] = source[source.shape[0] - LABEL_ROWS :, :]


class Block:
    def __init__(self, unit, label):
        self.unit = unit
        self.label = label
        self.rows = unit.shape[0]
        self.along_rows = None

    def column(self):
        if self.along_rows is None:
            self.along_rows = jnp.transpose(jnp.broadcast_to(self.label, (LANES, self.rows)))
        return self.along_rows


def unit_in(chunk, rows, end):
    return jnp.concatenate([chunk[at : at + rows, :] for at in range(0, end, rows)], axis=1)


def labels_in(first, rows):
    lines = first[first.shape[0] - LABEL_ROWS :, :].astype(jnp.float32)
    return jnp.concatenate([lines[i : i + 1] for i in range(rows // LANES)], axis=1)


def packed(both, rows):
    return Block(unit_in(both, rows, both.shape[0] - LABEL_ROWS), labels_in(both, rows))


def first_half(first, rows):
    half = rows // 2
    unit = normalised(unit_in(first, half, first.shape[0] - LABEL_ROWS))
    return Block(unit, labels_in(first, rows)[:, :half])


def second_half(first, second, rows):
    half = rows // 2
    return Block(unit_in(second, half, second.shape[0]), labels_in(first, rows)[:, half:])


def whole(first, second, rows):
    return joined(first_half(first, rows), second_half(first, second, rows))


def joined(*blocks):
    return Block(
        jnp.concatenate([block.unit for block in blocks], axis=0),
        jnp.concatenate([block.label for block in blocks], axis=1),
    )


def best_of(queries, *all_keys):
    best = None
    for keys in all_keys:
        sims = lax.dot_general(
            keys.unit, queries.unit, (((1,), (1,)), ((), ())), preferred_element_type=jnp.float32
        )
        pieces = []
        for start in range(0, queries.rows, LANES):
            keep = keys.column() == queries.label[:, start : start + LANES]
            if keys is queries:
                row = lax.broadcasted_iota(jnp.int32, keep.shape, 0)
                column = lax.broadcasted_iota(jnp.int32, keep.shape, 1) + start
                keep = keep & (row != column)
            found = jnp.where(keep, sims[:, start : start + LANES], -1.0)
            pieces.append(jnp.max(found, axis=0, keepdims=True))
        found = jnp.concatenate(pieces, axis=1)
        best = found if best is None else jnp.maximum(best, found)
    return best


def near_kernel(own, succ_a, succ_b, prev_a, prev_b, mine, bundle):
    rows = mine.shape[1]
    prev, succ = whole(prev_a, prev_b, rows), whole(succ_a, succ_b, rows)
    for at, block, first in ((0, prev, prev_a), (1, succ, succ_a)):
        put_unit(block.unit, bundle.at[at])
        put_labels(first, bundle.at[at])
    bundle[2] = own[...]
    own = packed(own, rows)
    mine[...] = best_of(own, own, prev, succ)


def far_first_kernel(bundle, back_a, ahead_a, found):
    rows = found.shape[1]
    queries = joined(first_half(back_a, rows), first_half(ahead_a, rows))
    found[...] = best_of(queries, queries, *(packed(bundle.at[at], rows) for at in range(3)))


def far_back_kernel(bundle, others, back_a, ahead_a, back_b, found, *refs):
    back_found, ahead_found, back_packed = refs
    rows = found.shape[1]
    half = rows // 2
    succ, own = packed(bundle.at[1], rows), packed(bundle.at[2], rows)
    prev_other, succ_other = packed(others.at[0], rows), packed(others.at[1], rows)
    first, rest = first_half(back_a, rows), second_half(back_a, back_b, rows)
    first_ahead = first_half(ahead_a, rows)
    back = joined(first, rest)
    put_unit(back.unit, back_packed)
    put_labels(back_a, back_packed)
    both = best_of(back, succ_other)
    back_found[:, :half] = jnp.maximum(found[:, :half], both[:, :half])
    back_found[:, half:] = jnp.maximum(best_of(rest, own, succ, first_ahead), both[:, half:])
    ahead_found[...] = jnp.maximum(found[:, half:], best_of(first_ahead, rest, prev_other))


def far_last_kernel(bundle, others, back, ahead_a, ahead_b, *refs):
    back_found, ahead_found, to_back, to_ahead = refs
    rows = to_back.shape[1]
    half = rows // 2
    back, rest = packed(back, rows), second_half(ahead_a, ahead_b, rows)
    keys = (packed(ref, rows) for ref in (bundle.at[2], bundle.at[0], others.at[0]))
    to_back[...] = jnp.maximum(back_found[...], best_of(back, rest))
    to_ahead[:, :half] = ahead_found[...]
    to_ahead[:, half:] = best_of(rest, *keys, back)


def own_kernel(own, others, back, ahead_a, ahead_b, near, mine):
    rows = mine.shape[1]
    keys = [packed(others.at[at], rows) for at in range(3)]
    keys += [packed(back, rows), whole(ahead_a, ahead_b, rows)]
    mine[...] = jnp.maximum(near[...], best_of(packed(own, rows), *keys))


def ring_perms(size_x, size_y, size_z):
    chips = size_x * size_y

    def device(place, core):
        place = place % chips
        x, y = (place, 0) if place < size_x else (chips - 1 - place, 1)
        return (x * size_y + y) * size_z + core

    def perm(to):
        return [
            (device(p, k), device(*to(p, k))) for p in range(chips) for k in range(size_z)
        ]

    def from_prev(place, core):
        return core ^ (place % chips in (0, 1))

    def from_next(place, core):
        return core ^ (place % chips not in (0, 1))

    return {
        "sibling": perm(lambda p, k: (p, 1 - k)),
        "next": perm(lambda p, k: (p + 1, from_prev(p + 1, k))),
        "prev": perm(lambda p, k: (p - 1, from_next(p - 1, k))),
        "on_next": perm(lambda p, k: (p + 1, k)),
        "on_prev": perm(lambda p, k: (p - 1, k)),
        "home_back": perm(lambda p, k: (p - 2, from_prev(p - 1, k))),
        "home_ahead": perm(lambda p, k: (p + 2, from_next(p + 1, k))),
    }


def kernel_call(kernel, inputs, outputs, matmuls):
    vmem = pl.BlockSpec(memory_space=pltpu.VMEM)
    return pl.pallas_call(
        kernel,
        out_shape=outputs,
        in_specs=[vmem] * len(inputs),
        out_specs=[vmem] * len(outputs),
        compiler_params=pltpu.CompilerParams(vmem_limit_bytes=VMEM_BYTES),
        cost_estimate=pl.CostEstimate(
            flops=matmuls * 2**26, bytes_accessed=2**20, transcendentals=0
        ),
        name=kernel.__name__,
    )(*inputs)


def on_ring(embeds, cluster):
    rows, width = embeds.shape
    half = rows // 2
    perms = ring_perms(*(lax.axis_size(a) for a in GROUP))

    def send(value, name):
        return lax.ppermute(value, GROUP, perms[name])

    line = jax.ShapeDtypeStruct((1, rows), jnp.float32)
    half_line = jax.ShapeDtypeStruct((1, half), jnp.float32)

    def chunk(count, labels):
        size = count * width // LANES + labels * LABEL_ROWS
        return jax.ShapeDtypeStruct((size, LANES), jnp.bfloat16)

    anywhere = pl.BlockSpec(memory_space=pl.ANY)
    vmem = pl.BlockSpec(memory_space=pltpu.VMEM)
    own_a = pl.pallas_call(
        pack_first_kernel,
        out_shape=chunk(half, True),
        in_specs=[anywhere] * 2,
        out_specs=vmem,
        scratch_shapes=[
            pltpu.VMEM((1, rows), jnp.int32),
            pltpu.SemaphoreType.DMA((width // LANES + 1,)),
        ],
        compiler_params=pltpu.CompilerParams(vmem_limit_bytes=VMEM_BYTES),
        name="pack_first",
    )(
        pltpu.with_memory_space_constraint(embeds, pltpu.HBM),
        pltpu.with_memory_space_constraint(cluster.reshape(1, rows), pltpu.HBM),
    )
    own_b, own = kernel_call(
        pack_second_kernel, [embeds, own_a], [chunk(half, False), chunk(rows, True)], 1
    )
    prev_a, succ_a = send(own_a, "next"), send(own_a, "prev")
    prev_b, succ_b = send(own_b, "next"), send(own_b, "prev")
    back_a, ahead_a = send(prev_a, "on_next"), send(succ_a, "on_prev")
    back_b, ahead_b = send(prev_b, "on_next"), send(succ_b, "on_prev")
    block = chunk(rows, True)
    bundle_shape = jax.ShapeDtypeStruct((3, *block.shape), jnp.bfloat16)
    mine, bundle = kernel_call(
        near_kernel, [own, succ_a, succ_b, prev_a, prev_b], [line, bundle_shape], NEAR_COST
    )
    others = send(bundle, "sibling")
    (found,) = kernel_call(far_first_kernel, [bundle, back_a, ahead_a], [line], FIRST_COST)
    *found, back = kernel_call(
        far_back_kernel,
        [bundle, others, back_a, ahead_a, back_b, found],
        [line, half_line, block],
        BACK_COST,
    )
    far = [back, ahead_a, ahead_b]
    to_back, to_ahead = kernel_call(
        far_last_kernel, [bundle, others, *far, *found], [line] * 2, LAST_COST
    )
    (mine,) = kernel_call(own_kernel, [own, others, *far, mine], [line], 5)
    best = jnp.maximum(
        mine, jnp.maximum(send(to_back, "home_back"), send(to_ahead, "home_ahead"))
    )
    return best.reshape(rows)


def masked_sims(queries, query_labels, query_ids, keys, key_labels, key_ids):
    sims = jnp.einsum("qd,kd->qk", queries, keys, preferred_element_type=jnp.float32)
    keep = (
        (query_labels[:, None] == key_labels[None, :])
        & (query_labels[:, None] >= 0)
        & (query_ids[:, None] != key_ids[None, :])
    )
    return jnp.where(keep, sims, -1.0)


def by_owner(embeds, cluster):
    rows, width = embeds.shape
    size_x = lax.axis_size("gx")
    size_y = lax.axis_size("gy")
    owners = size_x * size_y
    cap = 2 * rows // owners
    total = owners * cap
    unit = normalised(embeds)
    target = cluster // CLU_OWN
    onehot = (target[:, None] == jnp.arange(owners, dtype=jnp.int32)[None, :]).astype(jnp.int32)
    before = jnp.cumsum(onehot, axis=0) - onehot
    slot = jnp.sum(before * onehot, axis=1)
    place = target * cap + slot
    outgoing = jnp.zeros((total, width), jnp.bfloat16).at[place].set(unit)
    out_labels = jnp.full((total,), -1, jnp.int32).at[place].set(cluster)
    got, got_labels = (
        lax.all_to_all(
            outgoing.reshape(owners, cap, width),
            ("gx", "gy"),
            split_axis=0,
            concat_axis=0,
            tiled=True,
        ),
        lax.all_to_all(
            out_labels.reshape(owners, cap), ("gx", "gy"), split_axis=0, concat_axis=0, tiled=True
        ),
    )
    members = got.reshape(total, width)
    labels = got_labels.reshape(total)
    core = lax.axis_index("gz")
    query_ids = core * total + jnp.arange(total, dtype=jnp.int32)
    keys = lax.all_gather(members, "gz", axis=0, tiled=True)
    key_labels = lax.all_gather(labels, "gz", axis=0, tiled=True)
    key_ids = jnp.arange(keys.shape[0], dtype=jnp.int32)
    best = jnp.maximum(
        jnp.full((total,), -1.0, jnp.float32),
        jnp.max(masked_sims(members, labels, query_ids, keys, key_labels, key_ids), axis=1),
    )
    back = lax.all_to_all(
        best.reshape(owners, cap), ("gx", "gy"), split_axis=0, concat_axis=0, tiled=True
    )
    return back.reshape(total)[place]


def solution(mesh):
    shape = mesh.shape
    ring = shape["gx"] * shape["gy"] == 8 and shape["gy"] == 2 and shape["gz"] == 2
    placed = (P(("parts", "gx", "gy", "gz"), None), P(("parts", "gx", "gy", "gz")))
    return jax.shard_map(
        on_ring if ring else by_owner,
        mesh=mesh,
        in_specs=placed,
        out_specs=P(("parts", "gx", "gy", "gz")),
        check_vma=False,
    )
```

```python
import jax
import jax.numpy as jnp
from jax import lax
from jax.experimental import pallas as pl
from jax.experimental.pallas import tpu as pltpu
from jax.sharding import PartitionSpec as P

CLU_OWN = 16


EPS = 1e-06

GROUP = ("gx", "gy", "gz")


def normalised(block):
    vecs = block.astype(jnp.float32)
    return (vecs * lax.rsqrt(jnp.sum(vecs * vecs, axis=1, keepdims=True) + EPS)).astype(
        jnp.bfloat16
    )


LANES = 128
LABEL_ROWS = 16
VMEM_BYTES = 32 * 2**20
NEAR_COST = 1
FIRST_COST = 200
BACK_COST = 2
LAST_COST = 5


def put_unit(unit, chunk):
    count, width = unit.shape
    for j in range(width // LANES):
        chunk[j * count : (j + 1) * count, :] = unit[:, j * LANES : (j + 1) * LANES]


def pack_first_kernel(embeds, label, first, line, sems):
    rows, width = embeds.shape
    half = rows // 2
    copies = []
    for j in range(width // LANES):
        part = embeds.at[pl.ds(0, half), pl.ds(j * LANES, LANES)]
        copies.append(pltpu.make_async_copy(part, first.at[pl.ds(j * half, half)], sems.at[j]))
    copies.append(pltpu.make_async_copy(label, line, sems.at[width // LANES]))
    for copy in copies:
        copy.start()
    copies[-1].wait()
    row = lax.broadcasted_iota(jnp.int32, (LABEL_ROWS, LANES), 0)
    lines = jnp.zeros((LABEL_ROWS, LANES), jnp.float32)
    for i in range(rows // LANES):
        piece = line[:, i * LANES : (i + 1) * LANES].astype(jnp.float32)
        lines = jnp.where(row == i, piece, lines)
    first[half * width // LANES :, :] = lines.astype(jnp.bfloat16)
    for copy in copies[:-1]:
        copy.wait()


def pack_second_kernel(embeds, first, second, both):
    rows, width = embeds.shape
    unit = normalised(embeds[...])
    put_unit(unit[rows // 2 :, :], second)
    put_unit(unit, both)
    put_labels(first, both)


def put_labels(source, both):
    both[both.shape[0] - LABEL_ROWS :, :] = source[source.shape[0] - LABEL_ROWS :, :]


class Block:
    def __init__(self, unit, label):
        self.unit = unit
        self.label = label
        self.rows = unit.shape[0]
        self.along_rows = None

    def column(self):
        if self.along_rows is None:
            self.along_rows = jnp.transpose(jnp.broadcast_to(self.label, (LANES, self.rows)))
        return self.along_rows


def unit_in(chunk, rows, end):
    return jnp.concatenate([chunk[at : at + rows, :] for at in range(0, end, rows)], axis=1)


def labels_in(first, rows):
    lines = first[first.shape[0] - LABEL_ROWS :, :].astype(jnp.float32)
    return jnp.concatenate([lines[i : i + 1] for i in range(rows // LANES)], axis=1)


def packed(both, rows):
    return Block(unit_in(both, rows, both.shape[0] - LABEL_ROWS), labels_in(both, rows))


def first_half(first, rows):
    half = rows // 2
    unit = normalised(unit_in(first, half, first.shape[0] - LABEL_ROWS))
    return Block(unit, labels_in(first, rows)[:, :half])


def second_half(first, second, rows):
    half = rows // 2
    return Block(unit_in(second, half, second.shape[0]), labels_in(first, rows)[:, half:])


def whole(first, second, rows):
    return joined(first_half(first, rows), second_half(first, second, rows))


def joined(*blocks):
    return Block(
        jnp.concatenate([block.unit for block in blocks], axis=0),
        jnp.concatenate([block.label for block in blocks], axis=1),
    )


def best_of(queries, *all_keys):
    keys_unit = jnp.concatenate([keys.unit for keys in all_keys], axis=0)
    sims = lax.dot_general(
        keys_unit, queries.unit, (((1,), (1,)), ((), ())), preferred_element_type=jnp.float32
    )
    pieces = []
    for start in range(0, queries.rows, LANES):
        best, at = None, 0
        for keys in all_keys:
            keep = keys.column() == queries.label[:, start : start + LANES]
            if keys is queries:
                row = lax.broadcasted_iota(jnp.int32, keep.shape, 0)
                column = lax.broadcasted_iota(jnp.int32, keep.shape, 1) + start
                keep = keep & (row != column)
            found = jnp.where(keep, sims[at : at + keys.rows, start : start + LANES], -1.0)
            found = jnp.max(found, axis=0, keepdims=True)
            best = found if best is None else jnp.maximum(best, found)
            at += keys.rows
        pieces.append(best)
    return jnp.concatenate(pieces, axis=1)


def near_kernel(own, succ_a, succ_b, prev_a, prev_b, mine, bundle):
    rows = mine.shape[1]
    prev, succ = whole(prev_a, prev_b, rows), whole(succ_a, succ_b, rows)
    for at, block, first in ((0, prev, prev_a), (1, succ, succ_a)):
        put_unit(block.unit, bundle.at[at])
        put_labels(first, bundle.at[at])
    bundle[2] = own[...]
    own = packed(own, rows)
    mine[...] = best_of(own, own, prev, succ)


def far_first_kernel(bundle, back_a, ahead_a, found):
    rows = found.shape[1]
    queries = joined(first_half(back_a, rows), first_half(ahead_a, rows))
    found[...] = best_of(queries, queries, *(packed(bundle.at[at], rows) for at in range(3)))


def far_back_kernel(bundle, others, back_a, ahead_a, back_b, found, *refs):
    back_found, ahead_found, back_packed = refs
    rows = found.shape[1]
    half = rows // 2
    succ, own = packed(bundle.at[1], rows), packed(bundle.at[2], rows)
    prev_other, succ_other = packed(others.at[0], rows), packed(others.at[1], rows)
    first, rest = first_half(back_a, rows), second_half(back_a, back_b, rows)
    first_ahead = first_half(ahead_a, rows)
    back = joined(first, rest)
    put_unit(back.unit, back_packed)
    put_labels(back_a, back_packed)
    both = best_of(back, succ_other)
    back_found[:, :half] = jnp.maximum(found[:, :half], both[:, :half])
    back_found[:, half:] = jnp.maximum(best_of(rest, own, succ, first_ahead), both[:, half:])
    ahead_found[...] = jnp.maximum(found[:, half:], best_of(first_ahead, rest, prev_other))


def far_last_kernel(bundle, others, back, ahead_a, ahead_b, *refs):
    back_found, ahead_found, to_back, to_ahead = refs
    rows = to_back.shape[1]
    half = rows // 2
    back, rest = packed(back, rows), second_half(ahead_a, ahead_b, rows)
    keys = (packed(ref, rows) for ref in (bundle.at[2], bundle.at[0], others.at[0]))
    to_back[...] = jnp.maximum(back_found[...], best_of(back, rest))
    to_ahead[:, :half] = ahead_found[...]
    to_ahead[:, half:] = best_of(rest, *keys, back)


def own_kernel(own, others, back, ahead_a, ahead_b, near, mine):
    rows = mine.shape[1]
    keys = [packed(others.at[at], rows) for at in range(3)]
    keys += [packed(back, rows), whole(ahead_a, ahead_b, rows)]
    mine[...] = jnp.maximum(near[...], best_of(packed(own, rows), *keys))


def ring_perms(size_x, size_y, size_z):
    chips = size_x * size_y

    def device(place, core):
        place = place % chips
        x, y = (place, 0) if place < size_x else (chips - 1 - place, 1)
        return (x * size_y + y) * size_z + core

    def perm(to):
        return [
            (device(p, k), device(*to(p, k))) for p in range(chips) for k in range(size_z)
        ]

    def from_prev(place, core):
        return core ^ (place % chips in (0, 1))

    def from_next(place, core):
        return core ^ (place % chips not in (0, 1))

    return {
        "sibling": perm(lambda p, k: (p, 1 - k)),
        "next": perm(lambda p, k: (p + 1, from_prev(p + 1, k))),
        "prev": perm(lambda p, k: (p - 1, from_next(p - 1, k))),
        "on_next": perm(lambda p, k: (p + 1, k)),
        "on_prev": perm(lambda p, k: (p - 1, k)),
        "home_back": perm(lambda p, k: (p - 2, from_prev(p - 1, k))),
        "home_ahead": perm(lambda p, k: (p + 2, from_next(p + 1, k))),
    }


def kernel_call(kernel, inputs, outputs, matmuls):
    vmem = pl.BlockSpec(memory_space=pltpu.VMEM)
    return pl.pallas_call(
        kernel,
        out_shape=outputs,
        in_specs=[vmem] * len(inputs),
        out_specs=[vmem] * len(outputs),
        compiler_params=pltpu.CompilerParams(vmem_limit_bytes=VMEM_BYTES),
        cost_estimate=pl.CostEstimate(
            flops=matmuls * 2**26, bytes_accessed=2**20, transcendentals=0
        ),
        name=kernel.__name__,
    )(*inputs)


def on_ring(embeds, cluster):
    rows, width = embeds.shape
    half = rows // 2
    perms = ring_perms(*(lax.axis_size(a) for a in GROUP))

    def send(value, name):
        return lax.ppermute(value, GROUP, perms[name])

    line = jax.ShapeDtypeStruct((1, rows), jnp.float32)
    half_line = jax.ShapeDtypeStruct((1, half), jnp.float32)

    def chunk(count, labels):
        size = count * width // LANES + labels * LABEL_ROWS
        return jax.ShapeDtypeStruct((size, LANES), jnp.bfloat16)

    anywhere = pl.BlockSpec(memory_space=pl.ANY)
    vmem = pl.BlockSpec(memory_space=pltpu.VMEM)
    own_a = pl.pallas_call(
        pack_first_kernel,
        out_shape=chunk(half, True),
        in_specs=[anywhere] * 2,
        out_specs=vmem,
        scratch_shapes=[
            pltpu.VMEM((1, rows), jnp.int32),
            pltpu.SemaphoreType.DMA((width // LANES + 1,)),
        ],
        compiler_params=pltpu.CompilerParams(vmem_limit_bytes=VMEM_BYTES),
        name="pack_first",
    )(
        pltpu.with_memory_space_constraint(embeds, pltpu.HBM),
        pltpu.with_memory_space_constraint(cluster.reshape(1, rows), pltpu.HBM),
    )
    own_b, own = kernel_call(
        pack_second_kernel, [embeds, own_a], [chunk(half, False), chunk(rows, True)], 1
    )
    prev_a, succ_a = send(own_a, "next"), send(own_a, "prev")
    prev_b, succ_b = send(own_b, "next"), send(own_b, "prev")
    back_a, ahead_a = send(prev_a, "on_next"), send(succ_a, "on_prev")
    back_b, ahead_b = send(prev_b, "on_next"), send(succ_b, "on_prev")
    block = chunk(rows, True)
    bundle_shape = jax.ShapeDtypeStruct((3, *block.shape), jnp.bfloat16)
    mine, bundle = kernel_call(
        near_kernel, [own, succ_a, succ_b, prev_a, prev_b], [line, bundle_shape], NEAR_COST
    )
    others = send(bundle, "sibling")
    (found,) = kernel_call(far_first_kernel, [bundle, back_a, ahead_a], [line], FIRST_COST)
    *found, back = kernel_call(
        far_back_kernel,
        [bundle, others, back_a, ahead_a, back_b, found],
        [line, half_line, block],
        BACK_COST,
    )
    far = [back, ahead_a, ahead_b]
    to_back, to_ahead = kernel_call(
        far_last_kernel, [bundle, others, *far, *found], [line] * 2, LAST_COST
    )
    (mine,) = kernel_call(own_kernel, [own, others, *far, mine], [line], 5)
    best = jnp.maximum(
        mine, jnp.maximum(send(to_back, "home_back"), send(to_ahead, "home_ahead"))
    )
    return best.reshape(rows)


def masked_sims(queries, query_labels, query_ids, keys, key_labels, key_ids):
    sims = jnp.einsum("qd,kd->qk", queries, keys, preferred_element_type=jnp.float32)
    keep = (
        (query_labels[:, None] == key_labels[None, :])
        & (query_labels[:, None] >= 0)
        & (query_ids[:, None] != key_ids[None, :])
    )
    return jnp.where(keep, sims, -1.0)


def by_owner(embeds, cluster):
    rows, width = embeds.shape
    size_x = lax.axis_size("gx")
    size_y = lax.axis_size("gy")
    owners = size_x * size_y
    cap = 2 * rows // owners
    total = owners * cap
    unit = normalised(embeds)
    target = cluster // CLU_OWN
    onehot = (target[:, None] == jnp.arange(owners, dtype=jnp.int32)[None, :]).astype(jnp.int32)
    before = jnp.cumsum(onehot, axis=0) - onehot
    slot = jnp.sum(before * onehot, axis=1)
    place = target * cap + slot
    outgoing = jnp.zeros((total, width), jnp.bfloat16).at[place].set(unit)
    out_labels = jnp.full((total,), -1, jnp.int32).at[place].set(cluster)
    got, got_labels = (
        lax.all_to_all(
            outgoing.reshape(owners, cap, width),
            ("gx", "gy"),
            split_axis=0,
            concat_axis=0,
            tiled=True,
        ),
        lax.all_to_all(
            out_labels.reshape(owners, cap), ("gx", "gy"), split_axis=0, concat_axis=0, tiled=True
        ),
    )
    members = got.reshape(total, width)
    labels = got_labels.reshape(total)
    core = lax.axis_index("gz")
    query_ids = core * total + jnp.arange(total, dtype=jnp.int32)
    keys = lax.all_gather(members, "gz", axis=0, tiled=True)
    key_labels = lax.all_gather(labels, "gz", axis=0, tiled=True)
    key_ids = jnp.arange(keys.shape[0], dtype=jnp.int32)
    best = jnp.maximum(
        jnp.full((total,), -1.0, jnp.float32),
        jnp.max(masked_sims(members, labels, query_ids, keys, key_labels, key_ids), axis=1),
    )
    back = lax.all_to_all(
        best.reshape(owners, cap), ("gx", "gy"), split_axis=0, concat_axis=0, tiled=True
    )
    return back.reshape(total)[place]


def solution(mesh):
    shape = mesh.shape
    ring = shape["gx"] * shape["gy"] == 8 and shape["gy"] == 2 and shape["gz"] == 2
    placed = (P(("parts", "gx", "gy", "gz"), None), P(("parts", "gx", "gy", "gz")))
    return jax.shard_map(
        on_ring if ring else by_owner,
        mesh=mesh,
        in_specs=placed,
        out_specs=P(("parts", "gx", "gy", "gz")),
        check_vma=False,
    )
```

```python
import jax
import jax.numpy as jnp
from jax import lax
from jax.experimental import pallas as pl
from jax.experimental.pallas import tpu as pltpu
from jax.sharding import PartitionSpec as P

CLU_OWN = 16


EPS = 1e-06

GROUP = ("gx", "gy", "gz")


def normalised(block):
    vecs = block.astype(jnp.float32)
    return (vecs * lax.rsqrt(jnp.sum(vecs * vecs, axis=1, keepdims=True) + EPS)).astype(
        jnp.bfloat16
    )


LANES = 128
LABEL_ROWS = 16
VMEM_BYTES = 32 * 2**20
NEAR_COST = 1
FIRST_COST = 200
BACK_COST = 2
LAST_COST = 5


def put_unit(unit, chunk):
    count, width = unit.shape
    for j in range(width // LANES):
        chunk[j * count : (j + 1) * count, :] = unit[:, j * LANES : (j + 1) * LANES]


def pack_first_kernel(embeds, label, first, line, sems):
    rows, width = embeds.shape
    half = rows // 2
    copies = []
    for j in range(width // LANES):
        part = embeds.at[pl.ds(0, half), pl.ds(j * LANES, LANES)]
        copies.append(pltpu.make_async_copy(part, first.at[pl.ds(j * half, half)], sems.at[j]))
    copies.append(pltpu.make_async_copy(label, line, sems.at[width // LANES]))
    for copy in copies:
        copy.start()
    copies[-1].wait()
    row = lax.broadcasted_iota(jnp.int32, (LABEL_ROWS, LANES), 0)
    lines = jnp.zeros((LABEL_ROWS, LANES), jnp.float32)
    for i in range(rows // LANES):
        piece = line[:, i * LANES : (i + 1) * LANES].astype(jnp.float32)
        lines = jnp.where(row == i, piece, lines)
    first[half * width // LANES :, :] = lines.astype(jnp.bfloat16)
    for copy in copies[:-1]:
        copy.wait()


def pack_second_kernel(embeds, first, second, both):
    rows, width = embeds.shape
    unit = normalised(embeds[...])
    put_unit(unit[rows // 2 :, :], second)
    put_unit(unit, both)
    put_labels(first, both)


def put_labels(source, both):
    both[both.shape[0] - LABEL_ROWS :, :] = source[source.shape[0] - LABEL_ROWS :, :]


class Block:
    def __init__(self, unit, label, column=None):
        self.unit = unit
        self.label = label
        self.rows = unit.shape[0]
        self.along_rows = column

    def column(self):
        if self.along_rows is None:
            self.along_rows = jnp.transpose(jnp.broadcast_to(self.label, (LANES, self.rows)))
        return self.along_rows


def unit_in(chunk, rows, end):
    return jnp.concatenate([chunk[at : at + rows, :] for at in range(0, end, rows)], axis=1)


def labels_in(first, rows):
    lines = first[first.shape[0] - LABEL_ROWS :, :].astype(jnp.float32)
    return jnp.concatenate([lines[i : i + 1] for i in range(rows // LANES)], axis=1)


def packed(both, rows, column=None):
    unit = unit_in(both, rows, both.shape[0] - LABEL_ROWS)
    return Block(unit, labels_in(both, rows), None if column is None else column[...])


def first_half(first, rows):
    half = rows // 2
    unit = normalised(unit_in(first, half, first.shape[0] - LABEL_ROWS))
    return Block(unit, labels_in(first, rows)[:, :half])


def second_half(first, second, rows):
    half = rows // 2
    return Block(unit_in(second, half, second.shape[0]), labels_in(first, rows)[:, half:])


def whole(first, second, rows):
    return joined(first_half(first, rows), second_half(first, second, rows))


def joined(*blocks):
    return Block(
        jnp.concatenate([block.unit for block in blocks], axis=0),
        jnp.concatenate([block.label for block in blocks], axis=1),
    )


def best_of(queries, *all_keys):
    keys_unit = jnp.concatenate([keys.unit for keys in all_keys], axis=0)
    sims = lax.dot_general(
        keys_unit, queries.unit, (((1,), (1,)), ((), ())), preferred_element_type=jnp.float32
    )
    pieces = []
    for start in range(0, queries.rows, LANES):
        best, at = None, 0
        for keys in all_keys:
            keep = keys.column() == queries.label[:, start : start + LANES]
            if keys is queries:
                row = lax.broadcasted_iota(jnp.int32, keep.shape, 0)
                column = lax.broadcasted_iota(jnp.int32, keep.shape, 1) + start
                keep = keep & (row != column)
            found = jnp.where(keep, sims[at : at + keys.rows, start : start + LANES], -1.0)
            found = jnp.max(found, axis=0, keepdims=True)
            best = found if best is None else jnp.maximum(best, found)
            at += keys.rows
        pieces.append(best)
    return jnp.concatenate(pieces, axis=1)


def near_kernel(own, succ_a, succ_b, prev_a, prev_b, mine, bundle, columns):
    rows = mine.shape[1]
    prev, succ = whole(prev_a, prev_b, rows), whole(succ_a, succ_b, rows)
    for at, block, first in ((0, prev, prev_a), (1, succ, succ_a)):
        put_unit(block.unit, bundle.at[at])
        put_labels(first, bundle.at[at])
    bundle[2] = own[...]
    own = packed(own, rows)
    mine[...] = best_of(own, own, prev, succ)
    for at, block in enumerate((prev, succ, own)):
        columns[at] = block.column()


def far_first_kernel(bundle, columns, back_a, ahead_a, found):
    rows = found.shape[1]
    queries = joined(first_half(back_a, rows), first_half(ahead_a, rows))
    keys = [packed(bundle.at[at], rows, columns.at[at]) for at in range(3)]
    found[...] = best_of(queries, queries, *keys)


def far_back_kernel(bundle, columns, others, back_a, ahead_a, back_b, found, *refs):
    back_found, ahead_found, back_packed, back_column, other_column = refs
    rows = found.shape[1]
    half = rows // 2
    succ, own = (packed(bundle.at[at], rows, columns.at[at]) for at in (1, 2))
    prev_other, succ_other = packed(others.at[0], rows), packed(others.at[1], rows)
    first, rest = first_half(back_a, rows), second_half(back_a, back_b, rows)
    first_ahead = first_half(ahead_a, rows)
    back = joined(first, rest)
    put_unit(back.unit, back_packed)
    put_labels(back_a, back_packed)
    back_column[:half, :], back_column[half:, :] = first.column(), rest.column()
    other_column[...] = prev_other.column()
    both = best_of(back, succ_other)
    back_found[:, :half] = jnp.maximum(found[:, :half], both[:, :half])
    back_found[:, half:] = jnp.maximum(best_of(rest, own, succ, first_ahead), both[:, half:])
    ahead_found[...] = jnp.maximum(found[:, half:], best_of(first_ahead, rest, prev_other))


def far_last_kernel(bundle, columns, others, back, ahead_a, ahead_b, *refs):
    back_found, ahead_found, back_column, other_column, to_back, to_ahead = refs
    rows = to_back.shape[1]
    half = rows // 2
    back, rest = packed(back, rows, back_column), second_half(ahead_a, ahead_b, rows)
    keys = [packed(bundle.at[at], rows, columns.at[at]) for at in (0, 2)]
    keys.append(packed(others.at[0], rows, other_column))
    to_back[...] = jnp.maximum(back_found[...], best_of(back, rest))
    to_ahead[:, :half] = ahead_found[...]
    to_ahead[:, half:] = best_of(rest, *keys, back)


def own_kernel(own, others, back, ahead_a, ahead_b, near, mine):
    rows = mine.shape[1]
    keys = [packed(others.at[at], rows) for at in range(3)]
    keys += [packed(back, rows), whole(ahead_a, ahead_b, rows)]
    mine[...] = jnp.maximum(near[...], best_of(packed(own, rows), *keys))


def ring_perms(size_x, size_y, size_z):
    chips = size_x * size_y

    def device(place, core):
        place = place % chips
        x, y = (place, 0) if place < size_x else (chips - 1 - place, 1)
        return (x * size_y + y) * size_z + core

    def perm(to):
        return [
            (device(p, k), device(*to(p, k))) for p in range(chips) for k in range(size_z)
        ]

    def from_prev(place, core):
        return core ^ (place % chips in (0, 1))

    def from_next(place, core):
        return core ^ (place % chips not in (0, 1))

    return {
        "sibling": perm(lambda p, k: (p, 1 - k)),
        "next": perm(lambda p, k: (p + 1, from_prev(p + 1, k))),
        "prev": perm(lambda p, k: (p - 1, from_next(p - 1, k))),
        "on_next": perm(lambda p, k: (p + 1, k)),
        "on_prev": perm(lambda p, k: (p - 1, k)),
        "home_back": perm(lambda p, k: (p - 2, from_prev(p - 1, k))),
        "home_ahead": perm(lambda p, k: (p + 2, from_next(p + 1, k))),
    }


def kernel_call(kernel, inputs, outputs, matmuls):
    vmem = pl.BlockSpec(memory_space=pltpu.VMEM)
    return pl.pallas_call(
        kernel,
        out_shape=outputs,
        in_specs=[vmem] * len(inputs),
        out_specs=[vmem] * len(outputs),
        compiler_params=pltpu.CompilerParams(vmem_limit_bytes=VMEM_BYTES),
        cost_estimate=pl.CostEstimate(
            flops=matmuls * 2**26, bytes_accessed=2**20, transcendentals=0
        ),
        name=kernel.__name__,
    )(*inputs)


def on_ring(embeds, cluster):
    rows, width = embeds.shape
    half = rows // 2
    perms = ring_perms(*(lax.axis_size(a) for a in GROUP))

    def send(value, name):
        return lax.ppermute(value, GROUP, perms[name])

    line = jax.ShapeDtypeStruct((1, rows), jnp.float32)
    half_line = jax.ShapeDtypeStruct((1, half), jnp.float32)

    def chunk(count, labels):
        size = count * width // LANES + labels * LABEL_ROWS
        return jax.ShapeDtypeStruct((size, LANES), jnp.bfloat16)

    anywhere = pl.BlockSpec(memory_space=pl.ANY)
    vmem = pl.BlockSpec(memory_space=pltpu.VMEM)
    own_a = pl.pallas_call(
        pack_first_kernel,
        out_shape=chunk(half, True),
        in_specs=[anywhere] * 2,
        out_specs=vmem,
        scratch_shapes=[
            pltpu.VMEM((1, rows), jnp.int32),
            pltpu.SemaphoreType.DMA((width // LANES + 1,)),
        ],
        compiler_params=pltpu.CompilerParams(vmem_limit_bytes=VMEM_BYTES),
        name="pack_first",
    )(
        pltpu.with_memory_space_constraint(embeds, pltpu.HBM),
        pltpu.with_memory_space_constraint(cluster.reshape(1, rows), pltpu.HBM),
    )
    own_b, own = kernel_call(
        pack_second_kernel, [embeds, own_a], [chunk(half, False), chunk(rows, True)], 1
    )
    prev_a, succ_a = send(own_a, "next"), send(own_a, "prev")
    prev_b, succ_b = send(own_b, "next"), send(own_b, "prev")
    back_a, ahead_a = send(prev_a, "on_next"), send(succ_a, "on_prev")
    back_b, ahead_b = send(prev_b, "on_next"), send(succ_b, "on_prev")
    block = chunk(rows, True)
    bundle_shape = jax.ShapeDtypeStruct((3, *block.shape), jnp.bfloat16)
    column = jax.ShapeDtypeStruct((rows, LANES), jnp.float32)
    mine, bundle, columns = kernel_call(
        near_kernel,
        [own, succ_a, succ_b, prev_a, prev_b],
        [line, bundle_shape, jax.ShapeDtypeStruct((3, *column.shape), jnp.float32)],
        NEAR_COST,
    )
    others = send(bundle, "sibling")
    (found,) = kernel_call(far_first_kernel, [bundle, columns, back_a, ahead_a], [line], FIRST_COST)
    back_found, ahead_found, back, *turned = kernel_call(
        far_back_kernel,
        [bundle, columns, others, back_a, ahead_a, back_b, found],
        [line, half_line, block, column, column],
        BACK_COST,
    )
    far = [back, ahead_a, ahead_b]
    to_back, to_ahead = kernel_call(
        far_last_kernel,
        [bundle, columns, others, *far, back_found, ahead_found, *turned],
        [line] * 2,
        LAST_COST,
    )
    (mine,) = kernel_call(own_kernel, [own, others, *far, mine], [line], 5)
    best = jnp.maximum(
        mine, jnp.maximum(send(to_back, "home_back"), send(to_ahead, "home_ahead"))
    )
    return best.reshape(rows)


def masked_sims(queries, query_labels, query_ids, keys, key_labels, key_ids):
    sims = jnp.einsum("qd,kd->qk", queries, keys, preferred_element_type=jnp.float32)
    keep = (
        (query_labels[:, None] == key_labels[None, :])
        & (query_labels[:, None] >= 0)
        & (query_ids[:, None] != key_ids[None, :])
    )
    return jnp.where(keep, sims, -1.0)


def by_owner(embeds, cluster):
    rows, width = embeds.shape
    size_x = lax.axis_size("gx")
    size_y = lax.axis_size("gy")
    owners = size_x * size_y
    cap = 2 * rows // owners
    total = owners * cap
    unit = normalised(embeds)
    target = cluster // CLU_OWN
    onehot = (target[:, None] == jnp.arange(owners, dtype=jnp.int32)[None, :]).astype(jnp.int32)
    before = jnp.cumsum(onehot, axis=0) - onehot
    slot = jnp.sum(before * onehot, axis=1)
    place = target * cap + slot
    outgoing = jnp.zeros((total, width), jnp.bfloat16).at[place].set(unit)
    out_labels = jnp.full((total,), -1, jnp.int32).at[place].set(cluster)
    got, got_labels = (
        lax.all_to_all(
            outgoing.reshape(owners, cap, width),
            ("gx", "gy"),
            split_axis=0,
            concat_axis=0,
            tiled=True,
        ),
        lax.all_to_all(
            out_labels.reshape(owners, cap), ("gx", "gy"), split_axis=0, concat_axis=0, tiled=True
        ),
    )
    members = got.reshape(total, width)
    labels = got_labels.reshape(total)
    core = lax.axis_index("gz")
    query_ids = core * total + jnp.arange(total, dtype=jnp.int32)
    keys = lax.all_gather(members, "gz", axis=0, tiled=True)
    key_labels = lax.all_gather(labels, "gz", axis=0, tiled=True)
    key_ids = jnp.arange(keys.shape[0], dtype=jnp.int32)
    best = jnp.maximum(
        jnp.full((total,), -1.0, jnp.float32),
        jnp.max(masked_sims(members, labels, query_ids, keys, key_labels, key_ids), axis=1),
    )
    back = lax.all_to_all(
        best.reshape(owners, cap), ("gx", "gy"), split_axis=0, concat_axis=0, tiled=True
    )
    return back.reshape(total)[place]


def solution(mesh):
    shape = mesh.shape
    ring = shape["gx"] * shape["gy"] == 8 and shape["gy"] == 2 and shape["gz"] == 2
    placed = (P(("parts", "gx", "gy", "gz"), None), P(("parts", "gx", "gy", "gz")))
    return jax.shard_map(
        on_ring if ring else by_owner,
        mesh=mesh,
        in_specs=placed,
        out_specs=P(("parts", "gx", "gy", "gz")),
        check_vma=False,
    )
```

```python
import functools

import jax
import jax.numpy as jnp
from jax import lax
from jax.experimental import pallas as pl
from jax.experimental.pallas import tpu as pltpu
from jax.sharding import PartitionSpec as P

CLU_OWN = 16


EPS = 1e-06

GROUP = ("gx", "gy", "gz")


def normalised(block):
    vecs = block.astype(jnp.float32)
    return (vecs * lax.rsqrt(jnp.sum(vecs * vecs, axis=1, keepdims=True) + EPS)).astype(
        jnp.bfloat16
    )


LANES = 128
LABEL_ROWS = 16
VMEM_BYTES = 32 * 2**20
NEAR_COST = 1
FIRST_COST = 200
BACK_COST = 2
LAST_COST = 5


def put_unit(unit, chunk):
    count, width = unit.shape
    for j in range(width // LANES):
        chunk[j * count : (j + 1) * count, :] = unit[:, j * LANES : (j + 1) * LANES]


def pack_first_kernel(embeds, label, first, line, sems):
    rows, width = embeds.shape
    half = rows // 2
    copies = []
    for j in range(width // LANES):
        part = embeds.at[pl.ds(0, half), pl.ds(j * LANES, LANES)]
        copies.append(pltpu.make_async_copy(part, first.at[pl.ds(j * half, half)], sems.at[j]))
    copies.append(pltpu.make_async_copy(label, line, sems.at[width // LANES]))
    for copy in copies:
        copy.start()
    copies[-1].wait()
    row = lax.broadcasted_iota(jnp.int32, (LABEL_ROWS, LANES), 0)
    lines = jnp.zeros((LABEL_ROWS, LANES), jnp.float32)
    for i in range(rows // LANES):
        piece = line[:, i * LANES : (i + 1) * LANES].astype(jnp.float32)
        lines = jnp.where(row == i, piece, lines)
    first[half * width // LANES :, :] = lines.astype(jnp.bfloat16)
    for copy in copies[:-1]:
        copy.wait()


def pack_second_kernel(embeds, first, second, both):
    rows, width = embeds.shape
    unit = normalised(embeds[...])
    put_unit(unit[rows // 2 :, :], second)
    put_unit(unit, both)
    put_labels(first, both)


def put_labels(source, both):
    both[both.shape[0] - LABEL_ROWS :, :] = source[source.shape[0] - LABEL_ROWS :, :]


class Block:
    def __init__(self, unit, label):
        self.unit = unit
        self.label = label
        self.rows = unit.shape[0]
        self.along_rows = None

    def column(self):
        if self.along_rows is None:
            self.along_rows = jnp.transpose(jnp.broadcast_to(self.label, (LANES, self.rows)))
        return self.along_rows


def unit_in(chunk, rows, end):
    return jnp.concatenate([chunk[at : at + rows, :] for at in range(0, end, rows)], axis=1)


def labels_in(first, rows):
    lines = first[first.shape[0] - LABEL_ROWS :, :].astype(jnp.float32)
    return jnp.concatenate([lines[i : i + 1] for i in range(rows // LANES)], axis=1)


def packed(both, rows):
    return Block(unit_in(both, rows, both.shape[0] - LABEL_ROWS), labels_in(both, rows))


def first_half(first, rows):
    half = rows // 2
    unit = normalised(unit_in(first, half, first.shape[0] - LABEL_ROWS))
    return Block(unit, labels_in(first, rows)[:, :half])


def second_half(first, second, rows):
    half = rows // 2
    return Block(unit_in(second, half, second.shape[0]), labels_in(first, rows)[:, half:])


def whole(first, second, rows):
    return joined(first_half(first, rows), second_half(first, second, rows))


def joined(*blocks):
    return Block(
        jnp.concatenate([block.unit for block in blocks], axis=0),
        jnp.concatenate([block.label for block in blocks], axis=1),
    )


def best_of(queries, *all_keys):
    keys_unit = jnp.concatenate([keys.unit for keys in all_keys], axis=0)
    sims = lax.dot_general(
        keys_unit, queries.unit, (((1,), (1,)), ((), ())), preferred_element_type=jnp.float32
    )
    pieces = []
    for start in range(0, queries.rows, LANES):
        best, at = None, 0
        for keys in all_keys:
            keep = keys.column() == queries.label[:, start : start + LANES]
            if keys is queries:
                row = lax.broadcasted_iota(jnp.int32, keep.shape, 0)
                column = lax.broadcasted_iota(jnp.int32, keep.shape, 1) + start
                keep = keep & (row != column)
            found = jnp.where(keep, sims[at : at + keys.rows, start : start + LANES], -1.0)
            found = jnp.max(found, axis=0, keepdims=True)
            best = found if best is None else jnp.maximum(best, found)
            at += keys.rows
        pieces.append(best)
    return jnp.concatenate(pieces, axis=1)


def masked(queries, first, *others):
    all_keys = (first, *others)
    sims = lax.dot_general(
        jnp.concatenate([keys.unit for keys in all_keys], axis=0),
        queries.unit,
        (((1,), (1,)), ((), ())),
        preferred_element_type=jnp.float32,
    )
    found, at = [], 0
    for keys in all_keys:
        keep = keys.column() == queries.label
        found.append(jnp.where(keep, sims[at : at + keys.rows, :], -1.0))
        at += keys.rows
    best = [jnp.max(block, axis=0, keepdims=True) for block in found]
    return found[0], functools.reduce(jnp.maximum, best)


def near_kernel(own, succ_a, succ_b, prev_a, prev_b, mine, bundle):
    rows = mine.shape[1]
    prev, succ = whole(prev_a, prev_b, rows), whole(succ_a, succ_b, rows)
    for at, block, first in ((0, prev, prev_a), (1, succ, succ_a)):
        put_unit(block.unit, bundle.at[at])
        put_labels(first, bundle.at[at])
    bundle[2] = own[...]
    own = packed(own, rows)
    mine[...] = best_of(own, own, prev, succ)


def far_first_kernel(bundle, back_a, ahead_a, found):
    rows = found.shape[1]
    queries = joined(first_half(back_a, rows), first_half(ahead_a, rows))
    found[...] = best_of(queries, queries, *(packed(bundle.at[at], rows) for at in range(3)))


def far_back_kernel(bundle, others, back_a, ahead_a, back_b, found, *refs):
    back_found, ahead_found, back_packed = refs
    rows = found.shape[1]
    half = rows // 2
    succ, own = packed(bundle.at[1], rows), packed(bundle.at[2], rows)
    prev_other, succ_other = packed(others.at[0], rows), packed(others.at[1], rows)
    first, rest = first_half(back_a, rows), second_half(back_a, back_b, rows)
    first_ahead = first_half(ahead_a, rows)
    back = joined(first, rest)
    put_unit(back.unit, back_packed)
    put_labels(back_a, back_packed)
    both = best_of(back, succ_other)
    back_found[:, :half] = jnp.maximum(found[:, :half], both[:, :half])
    back_found[:, half:] = jnp.maximum(best_of(rest, own, succ, first_ahead), both[:, half:])
    ahead_found[...] = jnp.maximum(found[:, half:], best_of(first_ahead, rest, prev_other))


def far_last_kernel(bundle, others, back, ahead_a, ahead_b, *refs):
    back_found, ahead_found, to_back, to_ahead = refs
    rows = to_back.shape[1]
    half = rows // 2
    back, rest = packed(back, rows), second_half(ahead_a, ahead_b, rows)
    keys = [packed(ref, rows) for ref in (bundle.at[2], bundle.at[0], others.at[0])]
    sims, found = masked(rest, back, *keys)
    to_ahead[:, :half] = ahead_found[...]
    to_ahead[:, half:] = found
    best = jnp.max(jnp.transpose(sims), axis=0, keepdims=True)
    to_back[...] = jnp.maximum(back_found[...], best)


def own_kernel(own, others, back, ahead_a, ahead_b, near, mine):
    rows = mine.shape[1]
    keys = [packed(others.at[at], rows) for at in range(3)]
    keys += [packed(back, rows), whole(ahead_a, ahead_b, rows)]
    mine[...] = jnp.maximum(near[...], best_of(packed(own, rows), *keys))


def ring_perms(size_x, size_y, size_z):
    chips = size_x * size_y

    def device(place, core):
        place = place % chips
        x, y = (place, 0) if place < size_x else (chips - 1 - place, 1)
        return (x * size_y + y) * size_z + core

    def perm(to):
        return [
            (device(p, k), device(*to(p, k))) for p in range(chips) for k in range(size_z)
        ]

    def from_prev(place, core):
        return core ^ (place % chips in (0, 1))

    def from_next(place, core):
        return core ^ (place % chips not in (0, 1))

    return {
        "sibling": perm(lambda p, k: (p, 1 - k)),
        "next": perm(lambda p, k: (p + 1, from_prev(p + 1, k))),
        "prev": perm(lambda p, k: (p - 1, from_next(p - 1, k))),
        "on_next": perm(lambda p, k: (p + 1, k)),
        "on_prev": perm(lambda p, k: (p - 1, k)),
        "home_back": perm(lambda p, k: (p - 2, from_prev(p - 1, k))),
        "home_ahead": perm(lambda p, k: (p + 2, from_next(p + 1, k))),
    }


def kernel_call(kernel, inputs, outputs, matmuls):
    vmem = pl.BlockSpec(memory_space=pltpu.VMEM)
    return pl.pallas_call(
        kernel,
        out_shape=outputs,
        in_specs=[vmem] * len(inputs),
        out_specs=[vmem] * len(outputs),
        compiler_params=pltpu.CompilerParams(vmem_limit_bytes=VMEM_BYTES),
        cost_estimate=pl.CostEstimate(
            flops=matmuls * 2**26, bytes_accessed=2**20, transcendentals=0
        ),
        name=kernel.__name__,
    )(*inputs)


def on_ring(embeds, cluster):
    rows, width = embeds.shape
    half = rows // 2
    perms = ring_perms(*(lax.axis_size(a) for a in GROUP))

    def send(value, name):
        return lax.ppermute(value, GROUP, perms[name])

    line = jax.ShapeDtypeStruct((1, rows), jnp.float32)
    half_line = jax.ShapeDtypeStruct((1, half), jnp.float32)

    def chunk(count, labels):
        size = count * width // LANES + labels * LABEL_ROWS
        return jax.ShapeDtypeStruct((size, LANES), jnp.bfloat16)

    anywhere = pl.BlockSpec(memory_space=pl.ANY)
    vmem = pl.BlockSpec(memory_space=pltpu.VMEM)
    own_a = pl.pallas_call(
        pack_first_kernel,
        out_shape=chunk(half, True),
        in_specs=[anywhere] * 2,
        out_specs=vmem,
        scratch_shapes=[
            pltpu.VMEM((1, rows), jnp.int32),
            pltpu.SemaphoreType.DMA((width // LANES + 1,)),
        ],
        compiler_params=pltpu.CompilerParams(vmem_limit_bytes=VMEM_BYTES),
        name="pack_first",
    )(
        pltpu.with_memory_space_constraint(embeds, pltpu.HBM),
        pltpu.with_memory_space_constraint(cluster.reshape(1, rows), pltpu.HBM),
    )
    own_b, own = kernel_call(
        pack_second_kernel, [embeds, own_a], [chunk(half, False), chunk(rows, True)], 1
    )
    prev_a, succ_a = send(own_a, "next"), send(own_a, "prev")
    prev_b, succ_b = send(own_b, "next"), send(own_b, "prev")
    back_a, ahead_a = send(prev_a, "on_next"), send(succ_a, "on_prev")
    back_b, ahead_b = send(prev_b, "on_next"), send(succ_b, "on_prev")
    block = chunk(rows, True)
    bundle_shape = jax.ShapeDtypeStruct((3, *block.shape), jnp.bfloat16)
    mine, bundle = kernel_call(
        near_kernel, [own, succ_a, succ_b, prev_a, prev_b], [line, bundle_shape], NEAR_COST
    )
    others = send(bundle, "sibling")
    (found,) = kernel_call(far_first_kernel, [bundle, back_a, ahead_a], [line], FIRST_COST)
    *found, back = kernel_call(
        far_back_kernel,
        [bundle, others, back_a, ahead_a, back_b, found],
        [line, half_line, block],
        BACK_COST,
    )
    far = [back, ahead_a, ahead_b]
    to_back, to_ahead = kernel_call(
        far_last_kernel, [bundle, others, *far, *found], [line] * 2, LAST_COST
    )
    (mine,) = kernel_call(own_kernel, [own, others, *far, mine], [line], 5)
    best = jnp.maximum(
        mine, jnp.maximum(send(to_back, "home_back"), send(to_ahead, "home_ahead"))
    )
    return best.reshape(rows)


def masked_sims(queries, query_labels, query_ids, keys, key_labels, key_ids):
    sims = jnp.einsum("qd,kd->qk", queries, keys, preferred_element_type=jnp.float32)
    keep = (
        (query_labels[:, None] == key_labels[None, :])
        & (query_labels[:, None] >= 0)
        & (query_ids[:, None] != key_ids[None, :])
    )
    return jnp.where(keep, sims, -1.0)


def by_owner(embeds, cluster):
    rows, width = embeds.shape
    size_x = lax.axis_size("gx")
    size_y = lax.axis_size("gy")
    owners = size_x * size_y
    cap = 2 * rows // owners
    total = owners * cap
    unit = normalised(embeds)
    target = cluster // CLU_OWN
    onehot = (target[:, None] == jnp.arange(owners, dtype=jnp.int32)[None, :]).astype(jnp.int32)
    before = jnp.cumsum(onehot, axis=0) - onehot
    slot = jnp.sum(before * onehot, axis=1)
    place = target * cap + slot
    outgoing = jnp.zeros((total, width), jnp.bfloat16).at[place].set(unit)
    out_labels = jnp.full((total,), -1, jnp.int32).at[place].set(cluster)
    got, got_labels = (
        lax.all_to_all(
            outgoing.reshape(owners, cap, width),
            ("gx", "gy"),
            split_axis=0,
            concat_axis=0,
            tiled=True,
        ),
        lax.all_to_all(
            out_labels.reshape(owners, cap), ("gx", "gy"), split_axis=0, concat_axis=0, tiled=True
        ),
    )
    members = got.reshape(total, width)
    labels = got_labels.reshape(total)
    core = lax.axis_index("gz")
    query_ids = core * total + jnp.arange(total, dtype=jnp.int32)
    keys = lax.all_gather(members, "gz", axis=0, tiled=True)
    key_labels = lax.all_gather(labels, "gz", axis=0, tiled=True)
    key_ids = jnp.arange(keys.shape[0], dtype=jnp.int32)
    best = jnp.maximum(
        jnp.full((total,), -1.0, jnp.float32),
        jnp.max(masked_sims(members, labels, query_ids, keys, key_labels, key_ids), axis=1),
    )
    back = lax.all_to_all(
        best.reshape(owners, cap), ("gx", "gy"), split_axis=0, concat_axis=0, tiled=True
    )
    return back.reshape(total)[place]


def solution(mesh):
    shape = mesh.shape
    ring = shape["gx"] * shape["gy"] == 8 and shape["gy"] == 2 and shape["gz"] == 2
    placed = (P(("parts", "gx", "gy", "gz"), None), P(("parts", "gx", "gy", "gz")))
    return jax.shard_map(
        on_ring if ring else by_owner,
        mesh=mesh,
        in_specs=placed,
        out_specs=P(("parts", "gx", "gy", "gz")),
        check_vma=False,
    )
```

```python
import functools

import jax
import jax.numpy as jnp
from jax import lax
from jax.experimental import pallas as pl
from jax.experimental.pallas import tpu as pltpu
from jax.sharding import PartitionSpec as P

CLU_OWN = 16


EPS = 1e-06

GROUP = ("gx", "gy", "gz")


def normalised(block):
    vecs = block.astype(jnp.float32)
    return (vecs * lax.rsqrt(jnp.sum(vecs * vecs, axis=1, keepdims=True) + EPS)).astype(
        jnp.bfloat16
    )


LANES = 128
LABEL_ROWS = 16
VMEM_BYTES = 32 * 2**20
BUNDLE_COST = 1
FIRST_COST = 200
BACK_COST = 2
LAST_COST = 5


def put_unit(unit, chunk):
    count, width = unit.shape
    for j in range(width // LANES):
        chunk[j * count : (j + 1) * count, :] = unit[:, j * LANES : (j + 1) * LANES]


def pack_first_kernel(embeds, label, first, line, sems):
    rows, width = embeds.shape
    half = rows // 2
    copies = []
    for j in range(width // LANES):
        part = embeds.at[pl.ds(0, half), pl.ds(j * LANES, LANES)]
        copies.append(pltpu.make_async_copy(part, first.at[pl.ds(j * half, half)], sems.at[j]))
    copies.append(pltpu.make_async_copy(label, line, sems.at[width // LANES]))
    for copy in copies:
        copy.start()
    copies[-1].wait()
    row = lax.broadcasted_iota(jnp.int32, (LABEL_ROWS, LANES), 0)
    lines = jnp.zeros((LABEL_ROWS, LANES), jnp.float32)
    for i in range(rows // LANES):
        piece = line[:, i * LANES : (i + 1) * LANES].astype(jnp.float32)
        lines = jnp.where(row == i, piece, lines)
    first[half * width // LANES :, :] = lines.astype(jnp.bfloat16)
    for copy in copies[:-1]:
        copy.wait()


def pack_second_kernel(embeds, first, second, both):
    rows, width = embeds.shape
    unit = normalised(embeds[...])
    put_unit(unit[rows // 2 :, :], second)
    put_unit(unit, both)
    put_labels(first, both)


def put_labels(source, both):
    both[both.shape[0] - LABEL_ROWS :, :] = source[source.shape[0] - LABEL_ROWS :, :]


class Block:
    def __init__(self, unit, label):
        self.unit = unit
        self.label = label
        self.rows = unit.shape[0]
        self.along_rows = None

    def column(self):
        if self.along_rows is None:
            self.along_rows = jnp.transpose(jnp.broadcast_to(self.label, (LANES, self.rows)))
        return self.along_rows


def unit_in(chunk, rows, end):
    return jnp.concatenate([chunk[at : at + rows, :] for at in range(0, end, rows)], axis=1)


def labels_in(first, rows):
    lines = first[first.shape[0] - LABEL_ROWS :, :].astype(jnp.float32)
    return jnp.concatenate([lines[i : i + 1] for i in range(rows // LANES)], axis=1)


def packed(both, rows):
    return Block(unit_in(both, rows, both.shape[0] - LABEL_ROWS), labels_in(both, rows))


def first_half(first, rows):
    half = rows // 2
    unit = normalised(unit_in(first, half, first.shape[0] - LABEL_ROWS))
    return Block(unit, labels_in(first, rows)[:, :half])


def second_half(first, second, rows):
    half = rows // 2
    return Block(unit_in(second, half, second.shape[0]), labels_in(first, rows)[:, half:])


def whole(first, second, rows):
    return joined(first_half(first, rows), second_half(first, second, rows))


def joined(*blocks):
    return Block(
        jnp.concatenate([block.unit for block in blocks], axis=0),
        jnp.concatenate([block.label for block in blocks], axis=1),
    )


def best_of(queries, *all_keys):
    keys_unit = jnp.concatenate([keys.unit for keys in all_keys], axis=0)
    sims = lax.dot_general(
        keys_unit, queries.unit, (((1,), (1,)), ((), ())), preferred_element_type=jnp.float32
    )
    pieces = []
    for start in range(0, queries.rows, LANES):
        best, at = None, 0
        for keys in all_keys:
            keep = keys.column() == queries.label[:, start : start + LANES]
            if keys is queries:
                row = lax.broadcasted_iota(jnp.int32, keep.shape, 0)
                column = lax.broadcasted_iota(jnp.int32, keep.shape, 1) + start
                keep = keep & (row != column)
            found = jnp.where(keep, sims[at : at + keys.rows, start : start + LANES], -1.0)
            found = jnp.max(found, axis=0, keepdims=True)
            best = found if best is None else jnp.maximum(best, found)
            at += keys.rows
        pieces.append(best)
    return jnp.concatenate(pieces, axis=1)


def masked(queries, first, *others):
    all_keys = (first, *others)
    sims = lax.dot_general(
        jnp.concatenate([keys.unit for keys in all_keys], axis=0),
        queries.unit,
        (((1,), (1,)), ((), ())),
        preferred_element_type=jnp.float32,
    )
    found, at = [], 0
    for keys in all_keys:
        keep = keys.column() == queries.label
        found.append(jnp.where(keep, sims[at : at + keys.rows, :], -1.0))
        at += keys.rows
    best = [jnp.max(block, axis=0, keepdims=True) for block in found]
    return found[0], functools.reduce(jnp.maximum, best)


def put_bundle(rows, own, succ_a, succ_b, prev_a, prev_b, bundle):
    for at, first, second in ((0, prev_a, prev_b), (1, succ_a, succ_b)):
        put_unit(whole(first, second, rows).unit, bundle.at[at])
        put_labels(first, bundle.at[at])
    bundle[2] = own[...]


def far_first_kernel(own, bundle, back_a, ahead_a, found, mine):
    rows = found.shape[1]
    queries = joined(first_half(back_a, rows), first_half(ahead_a, rows))
    own = packed(own, rows)
    near = [packed(bundle.at[at], rows) for at in range(2)]
    found[...] = best_of(queries, queries, *near, own)
    mine[...] = best_of(own, own, *near)


def far_back_kernel(own, bundle, others, back_a, ahead_a, back_b, found, *refs):
    back_found, ahead_found, back_packed = refs
    rows = found.shape[1]
    half = rows // 2
    succ, own = packed(bundle.at[1], rows), packed(own, rows)
    prev_other, succ_other = packed(others.at[0], rows), packed(others.at[1], rows)
    first, rest = first_half(back_a, rows), second_half(back_a, back_b, rows)
    first_ahead = first_half(ahead_a, rows)
    back = joined(first, rest)
    put_unit(back.unit, back_packed)
    put_labels(back_a, back_packed)
    both = best_of(back, succ_other)
    back_found[:, :half] = jnp.maximum(found[:, :half], both[:, :half])
    back_found[:, half:] = jnp.maximum(best_of(rest, own, succ, first_ahead), both[:, half:])
    ahead_found[...] = jnp.maximum(found[:, half:], best_of(first_ahead, rest, prev_other))


def far_last_kernel(own, bundle, others, back, ahead_a, ahead_b, *refs):
    back_found, ahead_found, to_back, to_ahead = refs
    rows = to_back.shape[1]
    half = rows // 2
    back, rest = packed(back, rows), second_half(ahead_a, ahead_b, rows)
    keys = [packed(ref, rows) for ref in (own, bundle.at[0], others.at[0])]
    sims, found = masked(rest, back, *keys)
    to_ahead[:, :half] = ahead_found[...]
    to_ahead[:, half:] = found
    best = jnp.max(jnp.transpose(sims), axis=0, keepdims=True)
    to_back[...] = jnp.maximum(back_found[...], best)


def own_kernel(own, others, back, ahead_a, ahead_b, near, mine):
    rows = mine.shape[1]
    keys = [packed(ref, rows) for ref in (others.at[at] for at in range(3))]
    keys += [packed(back, rows), whole(ahead_a, ahead_b, rows)]
    mine[...] = jnp.maximum(near[...], best_of(packed(own, rows), *keys))


def ring_perms(size_x, size_y, size_z):
    chips = size_x * size_y

    def device(place, core):
        place = place % chips
        x, y = (place, 0) if place < size_x else (chips - 1 - place, 1)
        return (x * size_y + y) * size_z + core

    def perm(to):
        return [
            (device(p, k), device(*to(p, k))) for p in range(chips) for k in range(size_z)
        ]

    def from_prev(place, core):
        return core ^ (place % chips in (0, 1))

    def from_next(place, core):
        return core ^ (place % chips not in (0, 1))

    return {
        "sibling": perm(lambda p, k: (p, 1 - k)),
        "next": perm(lambda p, k: (p + 1, from_prev(p + 1, k))),
        "prev": perm(lambda p, k: (p - 1, from_next(p - 1, k))),
        "on_next": perm(lambda p, k: (p + 1, k)),
        "on_prev": perm(lambda p, k: (p - 1, k)),
        "home_back": perm(lambda p, k: (p - 2, from_prev(p - 1, k))),
        "home_ahead": perm(lambda p, k: (p + 2, from_next(p + 1, k))),
    }


def kernel_call(kernel, inputs, outputs, matmuls):
    vmem = pl.BlockSpec(memory_space=pltpu.VMEM)
    return pl.pallas_call(
        kernel,
        out_shape=outputs,
        in_specs=[vmem] * len(inputs),
        out_specs=[vmem] * len(outputs),
        compiler_params=pltpu.CompilerParams(vmem_limit_bytes=VMEM_BYTES),
        cost_estimate=pl.CostEstimate(
            flops=matmuls * 2**26, bytes_accessed=2**20, transcendentals=0
        ),
        name=kernel.__name__,
    )(*inputs)


def on_ring(embeds, cluster):
    rows, width = embeds.shape
    half = rows // 2
    perms = ring_perms(*(lax.axis_size(a) for a in GROUP))

    def send(value, name):
        return lax.ppermute(value, GROUP, perms[name])

    line = jax.ShapeDtypeStruct((1, rows), jnp.float32)
    half_line = jax.ShapeDtypeStruct((1, half), jnp.float32)

    def chunk(count, labels):
        size = count * width // LANES + labels * LABEL_ROWS
        return jax.ShapeDtypeStruct((size, LANES), jnp.bfloat16)

    anywhere = pl.BlockSpec(memory_space=pl.ANY)
    vmem = pl.BlockSpec(memory_space=pltpu.VMEM)
    own_a = pl.pallas_call(
        pack_first_kernel,
        out_shape=chunk(half, True),
        in_specs=[anywhere] * 2,
        out_specs=vmem,
        scratch_shapes=[
            pltpu.VMEM((1, rows), jnp.int32),
            pltpu.SemaphoreType.DMA((width // LANES + 1,)),
        ],
        compiler_params=pltpu.CompilerParams(vmem_limit_bytes=VMEM_BYTES),
        name="pack_first",
    )(
        pltpu.with_memory_space_constraint(embeds, pltpu.HBM),
        pltpu.with_memory_space_constraint(cluster.reshape(1, rows), pltpu.HBM),
    )
    own_b, own = kernel_call(
        pack_second_kernel, [embeds, own_a], [chunk(half, False), chunk(rows, True)], 1
    )
    prev_a, succ_a = send(own_a, "next"), send(own_a, "prev")
    prev_b, succ_b = send(own_b, "next"), send(own_b, "prev")
    back_a, ahead_a = send(prev_a, "on_next"), send(succ_a, "on_prev")
    back_b, ahead_b = send(prev_b, "on_next"), send(succ_b, "on_prev")
    block = chunk(rows, True)
    bundle_shape = jax.ShapeDtypeStruct((3, *block.shape), jnp.bfloat16)

    def bundle_kernel(*refs):
        put_bundle(rows, *refs)

    (bundle,) = kernel_call(
        bundle_kernel, [own, succ_a, succ_b, prev_a, prev_b], [bundle_shape], BUNDLE_COST
    )
    others = send(bundle, "sibling")
    found, mine = kernel_call(
        far_first_kernel, [own, bundle, back_a, ahead_a], [line] * 2, FIRST_COST
    )
    *found, back = kernel_call(
        far_back_kernel,
        [own, bundle, others, back_a, ahead_a, back_b, found],
        [line, half_line, block],
        BACK_COST,
    )
    far = [back, ahead_a, ahead_b]
    to_back, to_ahead = kernel_call(
        far_last_kernel, [own, bundle, others, *far, *found], [line] * 2, LAST_COST
    )
    (mine,) = kernel_call(own_kernel, [own, others, *far, mine], [line], 5)
    best = jnp.maximum(
        mine, jnp.maximum(send(to_back, "home_back"), send(to_ahead, "home_ahead"))
    )
    return best.reshape(rows)


def masked_sims(queries, query_labels, query_ids, keys, key_labels, key_ids):
    sims = jnp.einsum("qd,kd->qk", queries, keys, preferred_element_type=jnp.float32)
    keep = (
        (query_labels[:, None] == key_labels[None, :])
        & (query_labels[:, None] >= 0)
        & (query_ids[:, None] != key_ids[None, :])
    )
    return jnp.where(keep, sims, -1.0)


def by_owner(embeds, cluster):
    rows, width = embeds.shape
    size_x = lax.axis_size("gx")
    size_y = lax.axis_size("gy")
    owners = size_x * size_y
    cap = 2 * rows // owners
    total = owners * cap
    unit = normalised(embeds)
    target = cluster // CLU_OWN
    onehot = (target[:, None] == jnp.arange(owners, dtype=jnp.int32)[None, :]).astype(jnp.int32)
    before = jnp.cumsum(onehot, axis=0) - onehot
    slot = jnp.sum(before * onehot, axis=1)
    place = target * cap + slot
    outgoing = jnp.zeros((total, width), jnp.bfloat16).at[place].set(unit)
    out_labels = jnp.full((total,), -1, jnp.int32).at[place].set(cluster)
    got, got_labels = (
        lax.all_to_all(
            outgoing.reshape(owners, cap, width),
            ("gx", "gy"),
            split_axis=0,
            concat_axis=0,
            tiled=True,
        ),
        lax.all_to_all(
            out_labels.reshape(owners, cap), ("gx", "gy"), split_axis=0, concat_axis=0, tiled=True
        ),
    )
    members = got.reshape(total, width)
    labels = got_labels.reshape(total)
    core = lax.axis_index("gz")
    query_ids = core * total + jnp.arange(total, dtype=jnp.int32)
    keys = lax.all_gather(members, "gz", axis=0, tiled=True)
    key_labels = lax.all_gather(labels, "gz", axis=0, tiled=True)
    key_ids = jnp.arange(keys.shape[0], dtype=jnp.int32)
    best = jnp.maximum(
        jnp.full((total,), -1.0, jnp.float32),
        jnp.max(masked_sims(members, labels, query_ids, keys, key_labels, key_ids), axis=1),
    )
    back = lax.all_to_all(
        best.reshape(owners, cap), ("gx", "gy"), split_axis=0, concat_axis=0, tiled=True
    )
    return back.reshape(total)[place]


def solution(mesh):
    shape = mesh.shape
    ring = shape["gx"] * shape["gy"] == 8 and shape["gy"] == 2 and shape["gz"] == 2
    placed = (P(("parts", "gx", "gy", "gz"), None), P(("parts", "gx", "gy", "gz")))
    return jax.shard_map(
        on_ring if ring else by_owner,
        mesh=mesh,
        in_specs=placed,
        out_specs=P(("parts", "gx", "gy", "gz")),
        check_vma=False,
    )
```

```python
import functools

import jax
import jax.numpy as jnp
from jax import lax
from jax.experimental import pallas as pl
from jax.experimental.pallas import tpu as pltpu
from jax.sharding import PartitionSpec as P

CLU_OWN = 16


EPS = 1e-06

GROUP = ("gx", "gy", "gz")


def normalised(block):
    vecs = block.astype(jnp.float32)
    return (vecs * lax.rsqrt(jnp.sum(vecs * vecs, axis=1, keepdims=True) + EPS)).astype(
        jnp.bfloat16
    )


LANES = 128
LABEL_ROWS = 16
VMEM_BYTES = 32 * 2**20
BUNDLE_COST = 1
FIRST_COST = 200
BACK_COST = 2
LAST_COST = 5


def put_unit(unit, chunk):
    count, width = unit.shape
    for j in range(width // LANES):
        chunk[j * count : (j + 1) * count, :] = unit[:, j * LANES : (j + 1) * LANES]


def pack_first_kernel(embeds, label, first, line, sems):
    rows, width = embeds.shape
    half = rows // 2
    copies = []
    for j in range(width // LANES):
        part = embeds.at[pl.ds(0, half), pl.ds(j * LANES, LANES)]
        copies.append(pltpu.make_async_copy(part, first.at[pl.ds(j * half, half)], sems.at[j]))
    copies.append(pltpu.make_async_copy(label, line, sems.at[width // LANES]))
    for copy in copies:
        copy.start()
    copies[-1].wait()
    row = lax.broadcasted_iota(jnp.int32, (LABEL_ROWS, LANES), 0)
    lines = jnp.zeros((LABEL_ROWS, LANES), jnp.float32)
    for i in range(rows // LANES):
        piece = line[:, i * LANES : (i + 1) * LANES].astype(jnp.float32)
        lines = jnp.where(row == i, piece, lines)
    first[half * width // LANES :, :] = lines.astype(jnp.bfloat16)
    for copy in copies[:-1]:
        copy.wait()


def pack_second_kernel(embeds, first, second, both):
    rows, width = embeds.shape
    unit = normalised(embeds[...])
    put_unit(unit[rows // 2 :, :], second)
    put_unit(unit, both)
    put_labels(first, both)


def put_labels(source, both):
    both[both.shape[0] - LABEL_ROWS :, :] = source[source.shape[0] - LABEL_ROWS :, :]


class Block:
    def __init__(self, unit, label):
        self.unit = unit
        self.label = label
        self.rows = unit.shape[0]
        self.along_rows = None

    def column(self):
        if self.along_rows is None:
            self.along_rows = jnp.transpose(jnp.broadcast_to(self.label, (LANES, self.rows)))
        return self.along_rows


def unit_in(chunk, rows, end):
    return jnp.concatenate([chunk[at : at + rows, :] for at in range(0, end, rows)], axis=1)


def labels_in(first, rows):
    lines = first[first.shape[0] - LABEL_ROWS :, :].astype(jnp.float32)
    return jnp.concatenate([lines[i : i + 1] for i in range(rows // LANES)], axis=1)


def packed(both, rows):
    return Block(unit_in(both, rows, both.shape[0] - LABEL_ROWS), labels_in(both, rows))


def first_half(first, rows):
    half = rows // 2
    unit = normalised(unit_in(first, half, first.shape[0] - LABEL_ROWS))
    return Block(unit, labels_in(first, rows)[:, :half])


def second_half(first, second, rows):
    half = rows // 2
    return Block(unit_in(second, half, second.shape[0]), labels_in(first, rows)[:, half:])


def whole(first, second, rows):
    return joined(first_half(first, rows), second_half(first, second, rows))


def joined(*blocks):
    return Block(
        jnp.concatenate([block.unit for block in blocks], axis=0),
        jnp.concatenate([block.label for block in blocks], axis=1),
    )


def best_of(queries, *all_keys):
    keys_unit = jnp.concatenate([keys.unit for keys in all_keys], axis=0)
    sims = lax.dot_general(
        keys_unit, queries.unit, (((1,), (1,)), ((), ())), preferred_element_type=jnp.float32
    )
    pieces = []
    for start in range(0, queries.rows, LANES):
        best, at = None, 0
        for keys in all_keys:
            keep = keys.column() == queries.label[:, start : start + LANES]
            if keys is queries:
                row = lax.broadcasted_iota(jnp.int32, keep.shape, 0)
                column = lax.broadcasted_iota(jnp.int32, keep.shape, 1) + start
                keep = keep & (row != column)
            found = jnp.where(keep, sims[at : at + keys.rows, start : start + LANES], -1.0)
            found = jnp.max(found, axis=0, keepdims=True)
            best = found if best is None else jnp.maximum(best, found)
            at += keys.rows
        pieces.append(best)
    return jnp.concatenate(pieces, axis=1)


def masked(queries, first, *others):
    all_keys = (first, *others)
    sims = lax.dot_general(
        jnp.concatenate([keys.unit for keys in all_keys], axis=0),
        queries.unit,
        (((1,), (1,)), ((), ())),
        preferred_element_type=jnp.float32,
    )
    found, at = [], 0
    for keys in all_keys:
        keep = keys.column() == queries.label
        found.append(jnp.where(keep, sims[at : at + keys.rows, :], -1.0))
        at += keys.rows
    best = [jnp.max(block, axis=0, keepdims=True) for block in found]
    return found[0], functools.reduce(jnp.maximum, best)


def put_bundle(rows, own, succ_a, succ_b, prev_a, prev_b, bundle):
    for at, first, second in ((0, prev_a, prev_b), (1, succ_a, succ_b)):
        put_unit(whole(first, second, rows).unit, bundle.at[at])
        put_labels(first, bundle.at[at])
    bundle[2] = own[...]


def far_first_kernel(own, bundle, back_a, ahead_a, found, mine):
    rows = found.shape[1]
    queries = joined(first_half(back_a, rows), first_half(ahead_a, rows))
    own = packed(own, rows)
    near = [packed(bundle.at[at], rows) for at in range(2)]
    found[...] = best_of(queries, queries, *near, own)
    mine[...] = best_of(own, own, *near)


def far_back_kernel(own, bundle, others, back_a, ahead_a, back_b, found, *refs):
    back_found, ahead_found, back_packed = refs
    rows = found.shape[1]
    half = rows // 2
    succ, own = packed(bundle.at[1], rows), packed(own, rows)
    prev_other, succ_other = packed(others.at[0], rows), packed(others.at[1], rows)
    first, rest = first_half(back_a, rows), second_half(back_a, back_b, rows)
    first_ahead = first_half(ahead_a, rows)
    back = joined(first, rest)
    put_unit(back.unit, back_packed)
    put_labels(back_a, back_packed)
    both = best_of(back, succ_other)
    back_found[:, :half] = jnp.maximum(found[:, :half], both[:, :half])
    back_found[:, half:] = jnp.maximum(best_of(rest, own, succ, first_ahead), both[:, half:])
    ahead_found[...] = jnp.maximum(found[:, half:], best_of(first_ahead, rest, prev_other))


def far_last_kernel(own, bundle, others, back, ahead_a, ahead_b, *refs):
    back_found, ahead_found, to_back, to_ahead = refs
    rows = to_back.shape[1]
    half = rows // 2
    back, rest = packed(back, rows), second_half(ahead_a, ahead_b, rows)
    keys = [packed(ref, rows) for ref in (own, bundle.at[0], others.at[0])]
    sims, found = masked(rest, back, *keys)
    to_ahead[:, :half] = ahead_found[...]
    to_ahead[:, half:] = found
    best = jnp.max(jnp.transpose(sims), axis=0, keepdims=True)
    to_back[...] = jnp.maximum(back_found[...], best)


def own_kernel(own, others, back, ahead_a, ahead_b, near, mine):
    rows = mine.shape[1]
    keys = [packed(ref, rows) for ref in (others.at[at] for at in range(3))]
    keys += [packed(back, rows), whole(ahead_a, ahead_b, rows)]
    mine[...] = jnp.maximum(near[...], best_of(packed(own, rows), *keys))


def ring_perms(size_x, size_y, size_z):
    chips = size_x * size_y

    def device(place, core):
        place = place % chips
        x, y = (place, 0) if place < size_x else (chips - 1 - place, 1)
        return (x * size_y + y) * size_z + core

    def perm(to):
        return [
            (device(p, k), device(*to(p, k))) for p in range(chips) for k in range(size_z)
        ]

    def from_prev(place, core):
        return core ^ (place % chips in (0, 1))

    def from_next(place, core):
        return core ^ (place % chips not in (0, 1))

    return {
        "sibling": perm(lambda p, k: (p, 1 - k)),
        "next": perm(lambda p, k: (p + 1, from_prev(p + 1, k))),
        "prev": perm(lambda p, k: (p - 1, from_next(p - 1, k))),
        "on_next": perm(lambda p, k: (p + 1, k)),
        "on_prev": perm(lambda p, k: (p - 1, k)),
        "home_back": perm(lambda p, k: (p - 2, from_prev(p - 1, k))),
        "home_ahead": perm(lambda p, k: (p + 2, from_next(p + 1, k))),
    }


def kernel_call(kernel, inputs, outputs, matmuls):
    vmem = pl.BlockSpec(memory_space=pltpu.VMEM)
    return pl.pallas_call(
        kernel,
        out_shape=outputs,
        in_specs=[vmem] * len(inputs),
        out_specs=[vmem] * len(outputs),
        compiler_params=pltpu.CompilerParams(vmem_limit_bytes=VMEM_BYTES),
        cost_estimate=pl.CostEstimate(
            flops=matmuls * 2**26, bytes_accessed=2**20, transcendentals=0
        ),
        name=kernel.__name__,
    )(*inputs)


def on_ring(embeds, cluster):
    rows, width = embeds.shape
    half = rows // 2
    perms = ring_perms(*(lax.axis_size(a) for a in GROUP))

    def send(value, name):
        return lax.ppermute(value, GROUP, perms[name])

    line = jax.ShapeDtypeStruct((1, rows), jnp.float32)
    half_line = jax.ShapeDtypeStruct((1, half), jnp.float32)

    def chunk(count, labels):
        size = count * width // LANES + labels * LABEL_ROWS
        return jax.ShapeDtypeStruct((size, LANES), jnp.bfloat16)

    anywhere = pl.BlockSpec(memory_space=pl.ANY)
    vmem = pl.BlockSpec(memory_space=pltpu.VMEM)
    own_a = pl.pallas_call(
        pack_first_kernel,
        out_shape=chunk(half, True),
        in_specs=[anywhere] * 2,
        out_specs=vmem,
        scratch_shapes=[
            pltpu.VMEM((1, rows), jnp.int32),
            pltpu.SemaphoreType.DMA((width // LANES + 1,)),
        ],
        compiler_params=pltpu.CompilerParams(vmem_limit_bytes=VMEM_BYTES),
        name="pack_first",
    )(
        pltpu.with_memory_space_constraint(embeds, pltpu.HBM),
        pltpu.with_memory_space_constraint(cluster.reshape(1, rows), pltpu.HBM),
    )
    own_b, own = kernel_call(
        pack_second_kernel, [embeds, own_a], [chunk(half, False), chunk(rows, True)], 1
    )
    prev_a, succ_a = send(own_a, "next"), send(own_a, "prev")
    prev_b, succ_b = send(own_b, "next"), send(own_b, "prev")
    back_a, ahead_a = send(prev_a, "on_next"), send(succ_a, "on_prev")
    back_b, ahead_b = send(prev_b, "on_next"), send(succ_b, "on_prev")
    block = chunk(rows, True)
    bundle_shape = jax.ShapeDtypeStruct((3, *block.shape), jnp.bfloat16)

    def bundle_kernel(*refs):
        put_bundle(rows, *refs)

    (bundle,) = kernel_call(
        bundle_kernel, [own, succ_a, succ_b, prev_a, prev_b], [bundle_shape], BUNDLE_COST
    )
    others = send(bundle, "sibling")
    found, mine = kernel_call(
        far_first_kernel, [own, bundle, back_a, ahead_a], [line] * 2, FIRST_COST
    )
    *found, back = kernel_call(
        far_back_kernel,
        [own, bundle, others, back_a, ahead_a, back_b, found],
        [line, half_line, block],
        BACK_COST,
    )
    far = [back, ahead_a, ahead_b]
    to_back, to_ahead = kernel_call(
        far_last_kernel, [own, bundle, others, *far, *found], [line] * 2, LAST_COST
    )
    (mine,) = kernel_call(own_kernel, [own, others, *far, mine], [line], 5)
    best = jnp.maximum(
        mine, jnp.maximum(send(to_ahead, "home_ahead"), send(to_back, "home_back"))
    )
    return best.reshape(rows)


def masked_sims(queries, query_labels, query_ids, keys, key_labels, key_ids):
    sims = jnp.einsum("qd,kd->qk", queries, keys, preferred_element_type=jnp.float32)
    keep = (
        (query_labels[:, None] == key_labels[None, :])
        & (query_labels[:, None] >= 0)
        & (query_ids[:, None] != key_ids[None, :])
    )
    return jnp.where(keep, sims, -1.0)


def by_owner(embeds, cluster):
    rows, width = embeds.shape
    size_x = lax.axis_size("gx")
    size_y = lax.axis_size("gy")
    owners = size_x * size_y
    cap = 2 * rows // owners
    total = owners * cap
    unit = normalised(embeds)
    target = cluster // CLU_OWN
    onehot = (target[:, None] == jnp.arange(owners, dtype=jnp.int32)[None, :]).astype(jnp.int32)
    before = jnp.cumsum(onehot, axis=0) - onehot
    slot = jnp.sum(before * onehot, axis=1)
    place = target * cap + slot
    outgoing = jnp.zeros((total, width), jnp.bfloat16).at[place].set(unit)
    out_labels = jnp.full((total,), -1, jnp.int32).at[place].set(cluster)
    got, got_labels = (
        lax.all_to_all(
            outgoing.reshape(owners, cap, width),
            ("gx", "gy"),
            split_axis=0,
            concat_axis=0,
            tiled=True,
        ),
        lax.all_to_all(
            out_labels.reshape(owners, cap), ("gx", "gy"), split_axis=0, concat_axis=0, tiled=True
        ),
    )
    members = got.reshape(total, width)
    labels = got_labels.reshape(total)
    core = lax.axis_index("gz")
    query_ids = core * total + jnp.arange(total, dtype=jnp.int32)
    keys = lax.all_gather(members, "gz", axis=0, tiled=True)
    key_labels = lax.all_gather(labels, "gz", axis=0, tiled=True)
    key_ids = jnp.arange(keys.shape[0], dtype=jnp.int32)
    best = jnp.maximum(
        jnp.full((total,), -1.0, jnp.float32),
        jnp.max(masked_sims(members, labels, query_ids, keys, key_labels, key_ids), axis=1),
    )
    back = lax.all_to_all(
        best.reshape(owners, cap), ("gx", "gy"), split_axis=0, concat_axis=0, tiled=True
    )
    return back.reshape(total)[place]


def solution(mesh):
    shape = mesh.shape
    ring = shape["gx"] * shape["gy"] == 8 and shape["gy"] == 2 and shape["gz"] == 2
    placed = (P(("parts", "gx", "gy", "gz"), None), P(("parts", "gx", "gy", "gz")))
    return jax.shard_map(
        on_ring if ring else by_owner,
        mesh=mesh,
        in_specs=placed,
        out_specs=P(("parts", "gx", "gy", "gz")),
        check_vma=False,
    )
```

```python
import functools

import jax
import jax.numpy as jnp
from jax import lax
from jax.experimental import pallas as pl
from jax.experimental.pallas import tpu as pltpu
from jax.sharding import PartitionSpec as P

CLU_OWN = 16


EPS = 1e-06

GROUP = ("gx", "gy", "gz")


def normalised(block):
    vecs = block.astype(jnp.float32)
    return (vecs * lax.rsqrt(jnp.sum(vecs * vecs, axis=1, keepdims=True) + EPS)).astype(
        jnp.bfloat16
    )


LANES = 128
LABEL_ROWS = 16
VMEM_BYTES = 32 * 2**20
BUNDLE_COST = 1
FIRST_COST = 200
BACK_COST = 2
LAST_COST = 5


def put_unit(unit, chunk):
    count, width = unit.shape
    for j in range(width // LANES):
        chunk[j * count : (j + 1) * count, :] = unit[:, j * LANES : (j + 1) * LANES]


def pack_first_kernel(embeds, label, first, line, sems):
    rows, width = embeds.shape
    half = rows // 2
    copies = []
    for j in range(width // LANES):
        part = embeds.at[pl.ds(0, half), pl.ds(j * LANES, LANES)]
        copies.append(pltpu.make_async_copy(part, first.at[pl.ds(j * half, half)], sems.at[j]))
    copies.append(pltpu.make_async_copy(label, line, sems.at[width // LANES]))
    for copy in copies:
        copy.start()
    copies[-1].wait()
    row = lax.broadcasted_iota(jnp.int32, (LABEL_ROWS, LANES), 0)
    lines = jnp.zeros((LABEL_ROWS, LANES), jnp.float32)
    for i in range(rows // LANES):
        piece = line[:, i * LANES : (i + 1) * LANES].astype(jnp.float32)
        lines = jnp.where(row == i, piece, lines)
    first[half * width // LANES :, :] = lines.astype(jnp.bfloat16)
    for copy in copies[:-1]:
        copy.wait()


def pack_second_kernel(embeds, first, second, both):
    rows, width = embeds.shape
    unit = normalised(embeds[...])
    put_unit(unit[rows // 2 :, :], second)
    put_unit(unit, both)
    put_labels(first, both)


def put_labels(source, both):
    both[both.shape[0] - LABEL_ROWS :, :] = source[source.shape[0] - LABEL_ROWS :, :]


class Block:
    def __init__(self, unit, label):
        self.unit = unit
        self.label = label
        self.rows = unit.shape[0]
        self.along_rows = None

    def column(self):
        if self.along_rows is None:
            self.along_rows = jnp.transpose(jnp.broadcast_to(self.label, (LANES, self.rows)))
        return self.along_rows


def unit_in(chunk, rows, end):
    return jnp.concatenate([chunk[at : at + rows, :] for at in range(0, end, rows)], axis=1)


def labels_in(first, rows):
    lines = first[first.shape[0] - LABEL_ROWS :, :].astype(jnp.float32)
    return jnp.concatenate([lines[i : i + 1] for i in range(rows // LANES)], axis=1)


def packed(both, rows):
    return Block(unit_in(both, rows, both.shape[0] - LABEL_ROWS), labels_in(both, rows))


def first_half(first, rows):
    half = rows // 2
    unit = normalised(unit_in(first, half, first.shape[0] - LABEL_ROWS))
    return Block(unit, labels_in(first, rows)[:, :half])


def second_half(first, second, rows):
    half = rows // 2
    return Block(unit_in(second, half, second.shape[0]), labels_in(first, rows)[:, half:])


def whole(first, second, rows):
    return joined(first_half(first, rows), second_half(first, second, rows))


def joined(*blocks):
    return Block(
        jnp.concatenate([block.unit for block in blocks], axis=0),
        jnp.concatenate([block.label for block in blocks], axis=1),
    )


def best_of(queries, *all_keys):
    keys_unit = jnp.concatenate([keys.unit for keys in all_keys], axis=0)
    sims = lax.dot_general(
        keys_unit, queries.unit, (((1,), (1,)), ((), ())), preferred_element_type=jnp.float32
    )
    pieces = []
    for start in range(0, queries.rows, LANES):
        best, at = None, 0
        for keys in all_keys:
            keep = keys.column() == queries.label[:, start : start + LANES]
            if keys is queries:
                row = lax.broadcasted_iota(jnp.int32, keep.shape, 0)
                column = lax.broadcasted_iota(jnp.int32, keep.shape, 1) + start
                keep = keep & (row != column)
            found = jnp.where(keep, sims[at : at + keys.rows, start : start + LANES], -1.0)
            found = jnp.max(found, axis=0, keepdims=True)
            best = found if best is None else jnp.maximum(best, found)
            at += keys.rows
        pieces.append(best)
    return jnp.concatenate(pieces, axis=1)


def masked(queries, first, *others):
    all_keys = (first, *others)
    sims = lax.dot_general(
        jnp.concatenate([keys.unit for keys in all_keys], axis=0),
        queries.unit,
        (((1,), (1,)), ((), ())),
        preferred_element_type=jnp.float32,
    )
    found, at = [], 0
    for keys in all_keys:
        keep = keys.column() == queries.label
        found.append(jnp.where(keep, sims[at : at + keys.rows, :], -1.0))
        at += keys.rows
    best = [jnp.max(block, axis=0, keepdims=True) for block in found]
    return found[0], functools.reduce(jnp.maximum, best)


def put_bundle(rows, own, succ_a, succ_b, prev_a, prev_b, bundle):
    for at, first, second in ((0, prev_a, prev_b), (1, succ_a, succ_b)):
        put_unit(whole(first, second, rows).unit, bundle.at[at])
        put_labels(first, bundle.at[at])
    bundle[2] = own[...]


def far_first_kernel(own, bundle, back_a, ahead_a, found, mine):
    rows = found.shape[1]
    queries = joined(first_half(back_a, rows), first_half(ahead_a, rows))
    own = packed(own, rows)
    near = [packed(bundle.at[at], rows) for at in range(2)]
    found[...] = best_of(queries, queries, *near, own)
    mine[...] = best_of(own, own, *near)


def far_back_kernel(own, bundle, others, back_a, ahead_a, back_b, found, *refs):
    back_found, ahead_found, back_packed = refs
    rows = found.shape[1]
    half = rows // 2
    succ, own = packed(bundle.at[1], rows), packed(own, rows)
    prev_other, succ_other = packed(others.at[0], rows), packed(others.at[1], rows)
    first, rest = first_half(back_a, rows), second_half(back_a, back_b, rows)
    first_ahead = first_half(ahead_a, rows)
    back = joined(first, rest)
    put_unit(back.unit, back_packed)
    put_labels(back_a, back_packed)
    both = best_of(back, succ_other)
    back_found[:, :half] = jnp.maximum(found[:, :half], both[:, :half])
    back_found[:, half:] = jnp.maximum(best_of(rest, own, succ, first_ahead), both[:, half:])
    ahead_found[...] = jnp.maximum(found[:, half:], best_of(first_ahead, rest, prev_other))


def far_last_kernel(own, bundle, others, back, ahead_a, ahead_b, *refs):
    back_found, ahead_found, along, across = refs
    rows = along.shape[1]
    half = rows // 2
    back, rest = packed(back, rows), second_half(ahead_a, ahead_b, rows)
    keys = [packed(ref, rows) for ref in (own, bundle.at[0], others.at[0])]
    sims, found = masked(rest, back, *keys)
    to_ahead = jnp.concatenate([ahead_found[...], found], axis=1)
    best = jnp.max(jnp.transpose(sims), axis=0, keepdims=True)
    to_back = jnp.maximum(back_found[...], best)
    low = lax.axis_index("gx") < lax.axis_size("gx") // 2
    ahead_along = low == (lax.axis_index("gy") == 0)
    along[...] = jnp.where(ahead_along, to_ahead, to_back)
    across[...] = jnp.where(ahead_along, to_back, to_ahead)


def own_kernel(own, others, back, ahead_a, ahead_b, near, mine):
    rows = mine.shape[1]
    keys = [packed(ref, rows) for ref in (others.at[at] for at in range(3))]
    keys += [packed(back, rows), whole(ahead_a, ahead_b, rows)]
    mine[...] = jnp.maximum(near[...], best_of(packed(own, rows), *keys))


def ring_perms(size_x, size_y, size_z):
    chips = size_x * size_y

    def device(place, core):
        place = place % chips
        x, y = (place, 0) if place < size_x else (chips - 1 - place, 1)
        return (x * size_y + y) * size_z + core

    def perm(to, places=range(chips)):
        return [(device(p, k), device(*to(p, k))) for p in places for k in range(size_z)]

    def from_prev(place, core):
        return core ^ (place % chips in (0, 1))

    def from_next(place, core):
        return core ^ (place % chips not in (0, 1))

    def back(place, core):
        return place - 2, from_prev(place - 1, core)

    def ahead(place, core):
        return place + 2, from_next(place + 1, core)

    def low(place):
        return device(place, 0) // (size_y * size_z) < size_x // 2

    def ahead_along(place):
        return low(place) == (place < size_x)

    def along(place, core):
        return (ahead if ahead_along(place) else back)(place, core)

    def across(place, core):
        return (back if ahead_along(place) else ahead)(place, core)

    return {
        "sibling": perm(lambda p, k: (p, 1 - k)),
        "next": perm(lambda p, k: (p + 1, from_prev(p + 1, k))),
        "prev": perm(lambda p, k: (p - 1, from_next(p - 1, k))),
        "on_next": perm(lambda p, k: (p + 1, k)),
        "on_prev": perm(lambda p, k: (p - 1, k)),
        "home_low": perm(along, [p for p in range(chips) if not low(p)]),
        "home_high": perm(along, [p for p in range(chips) if low(p)]),
        "home_across": perm(across),
    }


def kernel_call(kernel, inputs, outputs, matmuls):
    vmem = pl.BlockSpec(memory_space=pltpu.VMEM)
    return pl.pallas_call(
        kernel,
        out_shape=outputs,
        in_specs=[vmem] * len(inputs),
        out_specs=[vmem] * len(outputs),
        compiler_params=pltpu.CompilerParams(vmem_limit_bytes=VMEM_BYTES),
        cost_estimate=pl.CostEstimate(
            flops=matmuls * 2**26, bytes_accessed=2**20, transcendentals=0
        ),
        name=kernel.__name__,
    )(*inputs)


def on_ring(embeds, cluster):
    rows, width = embeds.shape
    half = rows // 2
    perms = ring_perms(*(lax.axis_size(a) for a in GROUP))

    def send(value, name):
        return lax.ppermute(value, GROUP, perms[name])

    line = jax.ShapeDtypeStruct((1, rows), jnp.float32)
    half_line = jax.ShapeDtypeStruct((1, half), jnp.float32)

    def chunk(count, labels):
        size = count * width // LANES + labels * LABEL_ROWS
        return jax.ShapeDtypeStruct((size, LANES), jnp.bfloat16)

    anywhere = pl.BlockSpec(memory_space=pl.ANY)
    vmem = pl.BlockSpec(memory_space=pltpu.VMEM)
    own_a = pl.pallas_call(
        pack_first_kernel,
        out_shape=chunk(half, True),
        in_specs=[anywhere] * 2,
        out_specs=vmem,
        scratch_shapes=[
            pltpu.VMEM((1, rows), jnp.int32),
            pltpu.SemaphoreType.DMA((width // LANES + 1,)),
        ],
        compiler_params=pltpu.CompilerParams(vmem_limit_bytes=VMEM_BYTES),
        name="pack_first",
    )(
        pltpu.with_memory_space_constraint(embeds, pltpu.HBM),
        pltpu.with_memory_space_constraint(cluster.reshape(1, rows), pltpu.HBM),
    )
    own_b, own = kernel_call(
        pack_second_kernel, [embeds, own_a], [chunk(half, False), chunk(rows, True)], 1
    )
    prev_a, succ_a = send(own_a, "next"), send(own_a, "prev")
    prev_b, succ_b = send(own_b, "next"), send(own_b, "prev")
    back_a, ahead_a = send(prev_a, "on_next"), send(succ_a, "on_prev")
    back_b, ahead_b = send(prev_b, "on_next"), send(succ_b, "on_prev")
    block = chunk(rows, True)
    bundle_shape = jax.ShapeDtypeStruct((3, *block.shape), jnp.bfloat16)

    def bundle_kernel(*refs):
        put_bundle(rows, *refs)

    (bundle,) = kernel_call(
        bundle_kernel, [own, succ_a, succ_b, prev_a, prev_b], [bundle_shape], BUNDLE_COST
    )
    others = send(bundle, "sibling")
    found, mine = kernel_call(
        far_first_kernel, [own, bundle, back_a, ahead_a], [line] * 2, FIRST_COST
    )
    *found, back = kernel_call(
        far_back_kernel,
        [own, bundle, others, back_a, ahead_a, back_b, found],
        [line, half_line, block],
        BACK_COST,
    )
    far = [back, ahead_a, ahead_b]
    along, across = kernel_call(
        far_last_kernel, [own, bundle, others, *far, *found], [line] * 2, LAST_COST
    )
    (mine,) = kernel_call(own_kernel, [own, others, *far, mine], [line], 5)
    found_low = send(along, "home_low")
    found_across = send(across, "home_across")
    along, found_low = lax.optimization_barrier((along, found_low))
    received = found_low + send(along, "home_high")
    best = jnp.maximum(mine, jnp.maximum(found_across, received))
    return best.reshape(rows)


def masked_sims(queries, query_labels, query_ids, keys, key_labels, key_ids):
    sims = jnp.einsum("qd,kd->qk", queries, keys, preferred_element_type=jnp.float32)
    keep = (
        (query_labels[:, None] == key_labels[None, :])
        & (query_labels[:, None] >= 0)
        & (query_ids[:, None] != key_ids[None, :])
    )
    return jnp.where(keep, sims, -1.0)


def by_owner(embeds, cluster):
    rows, width = embeds.shape
    size_x = lax.axis_size("gx")
    size_y = lax.axis_size("gy")
    owners = size_x * size_y
    cap = 2 * rows // owners
    total = owners * cap
    unit = normalised(embeds)
    target = cluster // CLU_OWN
    onehot = (target[:, None] == jnp.arange(owners, dtype=jnp.int32)[None, :]).astype(jnp.int32)
    before = jnp.cumsum(onehot, axis=0) - onehot
    slot = jnp.sum(before * onehot, axis=1)
    place = target * cap + slot
    outgoing = jnp.zeros((total, width), jnp.bfloat16).at[place].set(unit)
    out_labels = jnp.full((total,), -1, jnp.int32).at[place].set(cluster)
    got, got_labels = (
        lax.all_to_all(
            outgoing.reshape(owners, cap, width),
            ("gx", "gy"),
            split_axis=0,
            concat_axis=0,
            tiled=True,
        ),
        lax.all_to_all(
            out_labels.reshape(owners, cap), ("gx", "gy"), split_axis=0, concat_axis=0, tiled=True
        ),
    )
    members = got.reshape(total, width)
    labels = got_labels.reshape(total)
    core = lax.axis_index("gz")
    query_ids = core * total + jnp.arange(total, dtype=jnp.int32)
    keys = lax.all_gather(members, "gz", axis=0, tiled=True)
    key_labels = lax.all_gather(labels, "gz", axis=0, tiled=True)
    key_ids = jnp.arange(keys.shape[0], dtype=jnp.int32)
    best = jnp.maximum(
        jnp.full((total,), -1.0, jnp.float32),
        jnp.max(masked_sims(members, labels, query_ids, keys, key_labels, key_ids), axis=1),
    )
    back = lax.all_to_all(
        best.reshape(owners, cap), ("gx", "gy"), split_axis=0, concat_axis=0, tiled=True
    )
    return back.reshape(total)[place]


def solution(mesh):
    shape = mesh.shape
    ring = shape["gx"] * shape["gy"] == 8 and shape["gy"] == 2 and shape["gz"] == 2
    placed = (P(("parts", "gx", "gy", "gz"), None), P(("parts", "gx", "gy", "gz")))
    return jax.shard_map(
        on_ring if ring else by_owner,
        mesh=mesh,
        in_specs=placed,
        out_specs=P(("parts", "gx", "gy", "gz")),
        check_vma=False,
    )
```

```python
import functools

import jax
import jax.numpy as jnp
from jax import lax
from jax.experimental import pallas as pl
from jax.experimental.pallas import tpu as pltpu
from jax.sharding import PartitionSpec as P

CLU_OWN = 16


EPS = 1e-06

GROUP = ("gx", "gy", "gz")


def normalised(block):
    vecs = block.astype(jnp.float32)
    return (vecs * lax.rsqrt(jnp.sum(vecs * vecs, axis=1, keepdims=True) + EPS)).astype(
        jnp.bfloat16
    )


LANES = 128
LABEL_ROWS = 16
VMEM_BYTES = 32 * 2**20
BUNDLE_COST = 1
FIRST_COST = 200
BACK_COST = 2
LAST_COST = 5


def put_unit(unit, chunk):
    count, width = unit.shape
    for j in range(width // LANES):
        chunk[j * count : (j + 1) * count, :] = unit[:, j * LANES : (j + 1) * LANES]


def pack_first_kernel(embeds, label, first, line, sems):
    rows, width = embeds.shape
    half = rows // 2
    copies = []
    for j in range(width // LANES):
        part = embeds.at[pl.ds(0, half), pl.ds(j * LANES, LANES)]
        copies.append(pltpu.make_async_copy(part, first.at[pl.ds(j * half, half)], sems.at[j]))
    copies.append(pltpu.make_async_copy(label, line, sems.at[width // LANES]))
    for copy in copies:
        copy.start()
    copies[-1].wait()
    row = lax.broadcasted_iota(jnp.int32, (LABEL_ROWS, LANES), 0)
    lines = jnp.zeros((LABEL_ROWS, LANES), jnp.float32)
    for i in range(rows // LANES):
        piece = line[:, i * LANES : (i + 1) * LANES].astype(jnp.float32)
        lines = jnp.where(row == i, piece, lines)
    first[half * width // LANES :, :] = lines.astype(jnp.bfloat16)
    for copy in copies[:-1]:
        copy.wait()


def pack_second_kernel(embeds, first, second, both, mine):
    rows, width = embeds.shape
    unit = normalised(embeds[...])
    put_unit(unit[rows // 2 :, :], second)
    put_unit(unit, both)
    put_labels(first, both)
    own = Block(unit, labels_in(first, rows))
    mine[...] = best_of(own, own)


def put_labels(source, both):
    both[both.shape[0] - LABEL_ROWS :, :] = source[source.shape[0] - LABEL_ROWS :, :]


class Block:
    def __init__(self, unit, label):
        self.unit = unit
        self.label = label
        self.rows = unit.shape[0]
        self.along_rows = None

    def column(self):
        if self.along_rows is None:
            self.along_rows = jnp.transpose(jnp.broadcast_to(self.label, (LANES, self.rows)))
        return self.along_rows


def unit_in(chunk, rows, end):
    return jnp.concatenate([chunk[at : at + rows, :] for at in range(0, end, rows)], axis=1)


def labels_in(first, rows):
    lines = first[first.shape[0] - LABEL_ROWS :, :].astype(jnp.float32)
    return jnp.concatenate([lines[i : i + 1] for i in range(rows // LANES)], axis=1)


def packed(both, rows):
    return Block(unit_in(both, rows, both.shape[0] - LABEL_ROWS), labels_in(both, rows))


def first_half(first, rows):
    half = rows // 2
    unit = normalised(unit_in(first, half, first.shape[0] - LABEL_ROWS))
    return Block(unit, labels_in(first, rows)[:, :half])


def second_half(first, second, rows):
    half = rows // 2
    return Block(unit_in(second, half, second.shape[0]), labels_in(first, rows)[:, half:])


def whole(first, second, rows):
    return joined(first_half(first, rows), second_half(first, second, rows))


def joined(*blocks):
    return Block(
        jnp.concatenate([block.unit for block in blocks], axis=0),
        jnp.concatenate([block.label for block in blocks], axis=1),
    )


def best_of(queries, *all_keys):
    keys_unit = jnp.concatenate([keys.unit for keys in all_keys], axis=0)
    sims = lax.dot_general(
        keys_unit, queries.unit, (((1,), (1,)), ((), ())), preferred_element_type=jnp.float32
    )
    pieces = []
    for start in range(0, queries.rows, LANES):
        best, at = None, 0
        for keys in all_keys:
            keep = keys.column() == queries.label[:, start : start + LANES]
            if keys is queries:
                row = lax.broadcasted_iota(jnp.int32, keep.shape, 0)
                column = lax.broadcasted_iota(jnp.int32, keep.shape, 1) + start
                keep = keep & (row != column)
            found = jnp.where(keep, sims[at : at + keys.rows, start : start + LANES], -1.0)
            found = jnp.max(found, axis=0, keepdims=True)
            best = found if best is None else jnp.maximum(best, found)
            at += keys.rows
        pieces.append(best)
    return jnp.concatenate(pieces, axis=1)


def masked(queries, first, *others):
    all_keys = (first, *others)
    sims = lax.dot_general(
        jnp.concatenate([keys.unit for keys in all_keys], axis=0),
        queries.unit,
        (((1,), (1,)), ((), ())),
        preferred_element_type=jnp.float32,
    )
    found, at = [], 0
    for keys in all_keys:
        keep = keys.column() == queries.label
        found.append(jnp.where(keep, sims[at : at + keys.rows, :], -1.0))
        at += keys.rows
    best = [jnp.max(block, axis=0, keepdims=True) for block in found]
    return found[0], functools.reduce(jnp.maximum, best)


def put_bundle(rows, own, succ_a, succ_b, prev_a, prev_b, bundle):
    for at, first, second in ((0, prev_a, prev_b), (1, succ_a, succ_b)):
        put_unit(whole(first, second, rows).unit, bundle.at[at])
        put_labels(first, bundle.at[at])
    bundle[2] = own[...]


def far_first_kernel(own, bundle, back_a, ahead_a, self_best, found, mine):
    rows = found.shape[1]
    queries = joined(first_half(back_a, rows), first_half(ahead_a, rows))
    own = packed(own, rows)
    near = [packed(bundle.at[at], rows) for at in range(2)]
    found[...] = best_of(queries, queries, *near, own)
    mine[...] = jnp.maximum(self_best[...], best_of(own, *near))


def far_back_kernel(own, bundle, others, back_a, ahead_a, back_b, found, *refs):
    back_found, ahead_found, back_packed = refs
    rows = found.shape[1]
    half = rows // 2
    succ, own = packed(bundle.at[1], rows), packed(own, rows)
    prev_other, succ_other = packed(others.at[0], rows), packed(others.at[1], rows)
    first, rest = first_half(back_a, rows), second_half(back_a, back_b, rows)
    first_ahead = first_half(ahead_a, rows)
    back = joined(first, rest)
    put_unit(back.unit, back_packed)
    put_labels(back_a, back_packed)
    both = best_of(back, succ_other)
    back_found[:, :half] = jnp.maximum(found[:, :half], both[:, :half])
    back_found[:, half:] = jnp.maximum(best_of(rest, own, succ, first_ahead), both[:, half:])
    ahead_found[...] = jnp.maximum(found[:, half:], best_of(first_ahead, rest, prev_other))


def far_last_kernel(own, bundle, others, back, ahead_a, ahead_b, *refs):
    back_found, ahead_found, to_back, to_ahead = refs
    rows = to_back.shape[1]
    half = rows // 2
    back, rest = packed(back, rows), second_half(ahead_a, ahead_b, rows)
    keys = [packed(ref, rows) for ref in (own, bundle.at[0], others.at[0])]
    sims, found = masked(rest, back, *keys)
    to_ahead[:, :half] = ahead_found[...]
    to_ahead[:, half:] = found
    best = jnp.max(jnp.transpose(sims), axis=0, keepdims=True)
    to_back[...] = jnp.maximum(back_found[...], best)


def own_kernel(own, others, back, ahead_a, ahead_b, near, mine):
    rows = mine.shape[1]
    keys = [packed(ref, rows) for ref in (others.at[at] for at in range(3))]
    keys += [packed(back, rows), whole(ahead_a, ahead_b, rows)]
    mine[...] = jnp.maximum(near[...], best_of(packed(own, rows), *keys))


def ring_perms(size_x, size_y, size_z):
    chips = size_x * size_y

    def device(place, core):
        place = place % chips
        x, y = (place, 0) if place < size_x else (chips - 1 - place, 1)
        return (x * size_y + y) * size_z + core

    def perm(to):
        return [
            (device(p, k), device(*to(p, k))) for p in range(chips) for k in range(size_z)
        ]

    def from_prev(place, core):
        return core ^ (place % chips in (0, 1))

    def from_next(place, core):
        return core ^ (place % chips not in (0, 1))

    return {
        "sibling": perm(lambda p, k: (p, 1 - k)),
        "next": perm(lambda p, k: (p + 1, from_prev(p + 1, k))),
        "prev": perm(lambda p, k: (p - 1, from_next(p - 1, k))),
        "on_next": perm(lambda p, k: (p + 1, k)),
        "on_prev": perm(lambda p, k: (p - 1, k)),
        "home_back": perm(lambda p, k: (p - 2, from_prev(p - 1, k))),
        "home_ahead": perm(lambda p, k: (p + 2, from_next(p + 1, k))),
    }


def kernel_call(kernel, inputs, outputs, matmuls):
    vmem = pl.BlockSpec(memory_space=pltpu.VMEM)
    return pl.pallas_call(
        kernel,
        out_shape=outputs,
        in_specs=[vmem] * len(inputs),
        out_specs=[vmem] * len(outputs),
        compiler_params=pltpu.CompilerParams(vmem_limit_bytes=VMEM_BYTES),
        cost_estimate=pl.CostEstimate(
            flops=matmuls * 2**26, bytes_accessed=2**20, transcendentals=0
        ),
        name=kernel.__name__,
    )(*inputs)


def on_ring(embeds, cluster):
    rows, width = embeds.shape
    half = rows // 2
    perms = ring_perms(*(lax.axis_size(a) for a in GROUP))

    def send(value, name):
        return lax.ppermute(value, GROUP, perms[name])

    line = jax.ShapeDtypeStruct((1, rows), jnp.float32)
    half_line = jax.ShapeDtypeStruct((1, half), jnp.float32)

    def chunk(count, labels):
        size = count * width // LANES + labels * LABEL_ROWS
        return jax.ShapeDtypeStruct((size, LANES), jnp.bfloat16)

    anywhere = pl.BlockSpec(memory_space=pl.ANY)
    vmem = pl.BlockSpec(memory_space=pltpu.VMEM)
    own_a = pl.pallas_call(
        pack_first_kernel,
        out_shape=chunk(half, True),
        in_specs=[anywhere] * 2,
        out_specs=vmem,
        scratch_shapes=[
            pltpu.VMEM((1, rows), jnp.int32),
            pltpu.SemaphoreType.DMA((width // LANES + 1,)),
        ],
        compiler_params=pltpu.CompilerParams(vmem_limit_bytes=VMEM_BYTES),
        name="pack_first",
    )(
        pltpu.with_memory_space_constraint(embeds, pltpu.HBM),
        pltpu.with_memory_space_constraint(cluster.reshape(1, rows), pltpu.HBM),
    )
    own_b, own, mine = kernel_call(
        pack_second_kernel, [embeds, own_a], [chunk(half, False), chunk(rows, True), line], 1
    )
    prev_a, succ_a = send(own_a, "next"), send(own_a, "prev")
    prev_b, succ_b = send(own_b, "next"), send(own_b, "prev")
    back_a, ahead_a = send(prev_a, "on_next"), send(succ_a, "on_prev")
    back_b, ahead_b = send(prev_b, "on_next"), send(succ_b, "on_prev")
    block = chunk(rows, True)
    bundle_shape = jax.ShapeDtypeStruct((3, *block.shape), jnp.bfloat16)

    def bundle_kernel(*refs):
        put_bundle(rows, *refs)

    (bundle,) = kernel_call(
        bundle_kernel, [own, succ_a, succ_b, prev_a, prev_b], [bundle_shape], BUNDLE_COST
    )
    others = send(bundle, "sibling")
    found, mine = kernel_call(
        far_first_kernel, [own, bundle, back_a, ahead_a, mine], [line] * 2, FIRST_COST
    )
    *found, back = kernel_call(
        far_back_kernel,
        [own, bundle, others, back_a, ahead_a, back_b, found],
        [line, half_line, block],
        BACK_COST,
    )
    far = [back, ahead_a, ahead_b]
    to_back, to_ahead = kernel_call(
        far_last_kernel, [own, bundle, others, *far, *found], [line] * 2, LAST_COST
    )
    (mine,) = kernel_call(own_kernel, [own, others, *far, mine], [line], 5)
    best = jnp.maximum(
        mine, jnp.maximum(send(to_back, "home_back"), send(to_ahead, "home_ahead"))
    )
    return best.reshape(rows)


def masked_sims(queries, query_labels, query_ids, keys, key_labels, key_ids):
    sims = jnp.einsum("qd,kd->qk", queries, keys, preferred_element_type=jnp.float32)
    keep = (
        (query_labels[:, None] == key_labels[None, :])
        & (query_labels[:, None] >= 0)
        & (query_ids[:, None] != key_ids[None, :])
    )
    return jnp.where(keep, sims, -1.0)


def by_owner(embeds, cluster):
    rows, width = embeds.shape
    size_x = lax.axis_size("gx")
    size_y = lax.axis_size("gy")
    owners = size_x * size_y
    cap = 2 * rows // owners
    total = owners * cap
    unit = normalised(embeds)
    target = cluster // CLU_OWN
    onehot = (target[:, None] == jnp.arange(owners, dtype=jnp.int32)[None, :]).astype(jnp.int32)
    before = jnp.cumsum(onehot, axis=0) - onehot
    slot = jnp.sum(before * onehot, axis=1)
    place = target * cap + slot
    outgoing = jnp.zeros((total, width), jnp.bfloat16).at[place].set(unit)
    out_labels = jnp.full((total,), -1, jnp.int32).at[place].set(cluster)
    got, got_labels = (
        lax.all_to_all(
            outgoing.reshape(owners, cap, width),
            ("gx", "gy"),
            split_axis=0,
            concat_axis=0,
            tiled=True,
        ),
        lax.all_to_all(
            out_labels.reshape(owners, cap), ("gx", "gy"), split_axis=0, concat_axis=0, tiled=True
        ),
    )
    members = got.reshape(total, width)
    labels = got_labels.reshape(total)
    core = lax.axis_index("gz")
    query_ids = core * total + jnp.arange(total, dtype=jnp.int32)
    keys = lax.all_gather(members, "gz", axis=0, tiled=True)
    key_labels = lax.all_gather(labels, "gz", axis=0, tiled=True)
    key_ids = jnp.arange(keys.shape[0], dtype=jnp.int32)
    best = jnp.maximum(
        jnp.full((total,), -1.0, jnp.float32),
        jnp.max(masked_sims(members, labels, query_ids, keys, key_labels, key_ids), axis=1),
    )
    back = lax.all_to_all(
        best.reshape(owners, cap), ("gx", "gy"), split_axis=0, concat_axis=0, tiled=True
    )
    return back.reshape(total)[place]


def solution(mesh):
    shape = mesh.shape
    ring = shape["gx"] * shape["gy"] == 8 and shape["gy"] == 2 and shape["gz"] == 2
    placed = (P(("parts", "gx", "gy", "gz"), None), P(("parts", "gx", "gy", "gz")))
    return jax.shard_map(
        on_ring if ring else by_owner,
        mesh=mesh,
        in_specs=placed,
        out_specs=P(("parts", "gx", "gy", "gz")),
        check_vma=False,
    )
```

```python
import functools

import jax
import jax.numpy as jnp
from jax import lax
from jax.experimental import pallas as pl
from jax.experimental.pallas import tpu as pltpu
from jax.sharding import PartitionSpec as P

CLU_OWN = 16


EPS = 1e-06

GROUP = ("gx", "gy", "gz")


def normalised(block):
    vecs = block.astype(jnp.float32)
    return (vecs * lax.rsqrt(jnp.sum(vecs * vecs, axis=1, keepdims=True) + EPS)).astype(
        jnp.bfloat16
    )


LANES = 128
LABEL_ROWS = 16
VMEM_BYTES = 32 * 2**20
BUNDLE_COST = 1
FIRST_COST = 200
BACK_COST = 2
LAST_COST = 5


def put_unit(unit, chunk):
    count, width = unit.shape
    for j in range(width // LANES):
        chunk[j * count : (j + 1) * count, :] = unit[:, j * LANES : (j + 1) * LANES]


def pack_first_kernel(embeds, label, first, line, sems):
    rows, width = embeds.shape
    half = rows // 2
    copies = []
    for j in range(width // LANES):
        part = embeds.at[pl.ds(0, half), pl.ds(j * LANES, LANES)]
        copies.append(pltpu.make_async_copy(part, first.at[pl.ds(j * half, half)], sems.at[j]))
    copies.append(pltpu.make_async_copy(label, line, sems.at[width // LANES]))
    for copy in copies:
        copy.start()
    copies[-1].wait()
    row = lax.broadcasted_iota(jnp.int32, (LABEL_ROWS, LANES), 0)
    lines = jnp.zeros((LABEL_ROWS, LANES), jnp.float32)
    for i in range(rows // LANES):
        piece = line[:, i * LANES : (i + 1) * LANES].astype(jnp.float32)
        lines = jnp.where(row == i, piece, lines)
    first[half * width // LANES :, :] = lines.astype(jnp.bfloat16)
    for copy in copies[:-1]:
        copy.wait()


def pack_second_kernel(embeds, first, second, both, mine):
    rows, width = embeds.shape
    unit = normalised(embeds[...])
    put_unit(unit[rows // 2 :, :], second)
    put_unit(unit, both)
    put_labels(first, both)
    own = Block(unit, labels_in(first, rows))
    mine[...] = best_of(own, own)


def put_labels(source, both):
    both[both.shape[0] - LABEL_ROWS :, :] = source[source.shape[0] - LABEL_ROWS :, :]


class Block:
    def __init__(self, unit, label):
        self.unit = unit
        self.label = label
        self.rows = unit.shape[0]
        self.along_rows = None

    def column(self):
        if self.along_rows is None:
            self.along_rows = jnp.transpose(jnp.broadcast_to(self.label, (LANES, self.rows)))
        return self.along_rows


def unit_in(chunk, rows, end):
    return jnp.concatenate([chunk[at : at + rows, :] for at in range(0, end, rows)], axis=1)


def labels_in(first, rows):
    lines = first[first.shape[0] - LABEL_ROWS :, :].astype(jnp.float32)
    return jnp.concatenate([lines[i : i + 1] for i in range(rows // LANES)], axis=1)


def packed(both, rows):
    return Block(unit_in(both, rows, both.shape[0] - LABEL_ROWS), labels_in(both, rows))


def first_half(first, rows):
    half = rows // 2
    unit = normalised(unit_in(first, half, first.shape[0] - LABEL_ROWS))
    return Block(unit, labels_in(first, rows)[:, :half])


def second_half(first, second, rows):
    half = rows // 2
    return Block(unit_in(second, half, second.shape[0]), labels_in(first, rows)[:, half:])


def whole(first, second, rows):
    return joined(first_half(first, rows), second_half(first, second, rows))


def joined(*blocks):
    return Block(
        jnp.concatenate([block.unit for block in blocks], axis=0),
        jnp.concatenate([block.label for block in blocks], axis=1),
    )


def best_of(queries, *all_keys):
    keys_unit = jnp.concatenate([keys.unit for keys in all_keys], axis=0)
    sims = lax.dot_general(
        keys_unit, queries.unit, (((1,), (1,)), ((), ())), preferred_element_type=jnp.float32
    )
    pieces = []
    for start in range(0, queries.rows, LANES):
        best, at = None, 0
        for keys in all_keys:
            keep = keys.column() == queries.label[:, start : start + LANES]
            if keys is queries:
                row = lax.broadcasted_iota(jnp.int32, keep.shape, 0)
                column = lax.broadcasted_iota(jnp.int32, keep.shape, 1) + start
                keep = keep & (row != column)
            found = jnp.where(keep, sims[at : at + keys.rows, start : start + LANES], -1.0)
            found = jnp.max(found, axis=0, keepdims=True)
            best = found if best is None else jnp.maximum(best, found)
            at += keys.rows
        pieces.append(best)
    return jnp.concatenate(pieces, axis=1)


def masked(queries, first, *others):
    all_keys = (first, *others)
    sims = lax.dot_general(
        jnp.concatenate([keys.unit for keys in all_keys], axis=0),
        queries.unit,
        (((1,), (1,)), ((), ())),
        preferred_element_type=jnp.float32,
    )
    found, at = [], 0
    for keys in all_keys:
        keep = keys.column() == queries.label
        found.append(jnp.where(keep, sims[at : at + keys.rows, :], -1.0))
        at += keys.rows
    best = [jnp.max(block, axis=0, keepdims=True) for block in found]
    return found[0], functools.reduce(jnp.maximum, best)


def put_bundle(rows, own, succ_a, succ_b, prev_a, prev_b, bundle):
    for at, first, second in ((0, prev_a, prev_b), (1, succ_a, succ_b)):
        put_unit(whole(first, second, rows).unit, bundle.at[at])
        put_labels(first, bundle.at[at])
    bundle[2] = own[...]


def far_first_kernel(own, bundle, back_a, ahead_a, self_best, found, mine):
    rows = found.shape[1]
    queries = joined(first_half(back_a, rows), first_half(ahead_a, rows))
    own = packed(own, rows)
    near = [packed(bundle.at[at], rows) for at in range(2)]
    found[...] = best_of(queries, queries, *near, own)
    mine[...] = jnp.maximum(self_best[...], best_of(own, *near))


def far_back_kernel(own, bundle, others, back_a, ahead_a, back_b, found, *refs):
    back_found, ahead_found, back_packed = refs
    rows = found.shape[1]
    half = rows // 2
    succ, own = packed(bundle.at[1], rows), packed(own, rows)
    prev_other, succ_other = packed(others.at[0], rows), packed(others.at[1], rows)
    first, rest = first_half(back_a, rows), second_half(back_a, back_b, rows)
    first_ahead = first_half(ahead_a, rows)
    back = joined(first, rest)
    put_unit(back.unit, back_packed)
    put_labels(back_a, back_packed)
    both = best_of(back, succ_other)
    back_found[:, :half] = jnp.maximum(found[:, :half], both[:, :half])
    back_found[:, half:] = jnp.maximum(best_of(rest, own, succ, first_ahead), both[:, half:])
    ahead_found[...] = jnp.maximum(found[:, half:], best_of(first_ahead, rest, prev_other))


def far_last_kernel(own, bundle, others, back, ahead_a, ahead_b, *refs):
    back_found, ahead_found, to_back, to_ahead = refs
    rows = to_back.shape[1]
    half = rows // 2
    back, rest = packed(back, rows), second_half(ahead_a, ahead_b, rows)
    keys = [packed(ref, rows) for ref in (own, bundle.at[0], others.at[0])]
    sims, found = masked(rest, back, *keys)
    to_ahead[:, :half] = ahead_found[...]
    to_ahead[:, half:] = found
    best = jnp.max(jnp.transpose(sims), axis=0, keepdims=True)
    to_back[...] = jnp.maximum(back_found[...], best)


def own_kernel(own, others, back, ahead_a, ahead_b, near, mine):
    rows = mine.shape[1]
    keys = [packed(ref, rows) for ref in (others.at[at] for at in range(3))]
    keys += [packed(back, rows), whole(ahead_a, ahead_b, rows)]
    mine[...] = jnp.maximum(near[...], best_of(packed(own, rows), *keys))


def ring_perms(size_x, size_y, size_z):
    chips = size_x * size_y

    def device(place, core):
        place = place % chips
        x, y = (place, 0) if place < size_x else (chips - 1 - place, 1)
        return (x * size_y + y) * size_z + core

    def perm(to):
        return [
            (device(p, k), device(*to(p, k))) for p in range(chips) for k in range(size_z)
        ]

    def from_prev(place, core):
        return core ^ (place % chips in (0, 1, 2, 4))

    def from_next(place, core):
        return core ^ (place % chips not in (0, 1, 2, 4))

    return {
        "sibling": perm(lambda p, k: (p, 1 - k)),
        "next": perm(lambda p, k: (p + 1, from_prev(p + 1, k))),
        "prev": perm(lambda p, k: (p - 1, from_next(p - 1, k))),
        "on_next": perm(lambda p, k: (p + 1, k)),
        "on_prev": perm(lambda p, k: (p - 1, k)),
        "home_back": perm(lambda p, k: (p - 2, from_prev(p - 1, k))),
        "home_ahead": perm(lambda p, k: (p + 2, from_next(p + 1, k))),
    }


def kernel_call(kernel, inputs, outputs, matmuls):
    vmem = pl.BlockSpec(memory_space=pltpu.VMEM)
    return pl.pallas_call(
        kernel,
        out_shape=outputs,
        in_specs=[vmem] * len(inputs),
        out_specs=[vmem] * len(outputs),
        compiler_params=pltpu.CompilerParams(vmem_limit_bytes=VMEM_BYTES),
        cost_estimate=pl.CostEstimate(
            flops=matmuls * 2**26, bytes_accessed=2**20, transcendentals=0
        ),
        name=kernel.__name__,
    )(*inputs)


def on_ring(embeds, cluster):
    rows, width = embeds.shape
    half = rows // 2
    perms = ring_perms(*(lax.axis_size(a) for a in GROUP))

    def send(value, name):
        return lax.ppermute(value, GROUP, perms[name])

    line = jax.ShapeDtypeStruct((1, rows), jnp.float32)
    half_line = jax.ShapeDtypeStruct((1, half), jnp.float32)

    def chunk(count, labels):
        size = count * width // LANES + labels * LABEL_ROWS
        return jax.ShapeDtypeStruct((size, LANES), jnp.bfloat16)

    anywhere = pl.BlockSpec(memory_space=pl.ANY)
    vmem = pl.BlockSpec(memory_space=pltpu.VMEM)
    own_a = pl.pallas_call(
        pack_first_kernel,
        out_shape=chunk(half, True),
        in_specs=[anywhere] * 2,
        out_specs=vmem,
        scratch_shapes=[
            pltpu.VMEM((1, rows), jnp.int32),
            pltpu.SemaphoreType.DMA((width // LANES + 1,)),
        ],
        compiler_params=pltpu.CompilerParams(vmem_limit_bytes=VMEM_BYTES),
        name="pack_first",
    )(
        pltpu.with_memory_space_constraint(embeds, pltpu.HBM),
        pltpu.with_memory_space_constraint(cluster.reshape(1, rows), pltpu.HBM),
    )
    own_b, own, mine = kernel_call(
        pack_second_kernel, [embeds, own_a], [chunk(half, False), chunk(rows, True), line], 1
    )
    prev_a, succ_a = send(own_a, "next"), send(own_a, "prev")
    prev_b, succ_b = send(own_b, "next"), send(own_b, "prev")
    back_a, ahead_a = send(prev_a, "on_next"), send(succ_a, "on_prev")
    back_b, ahead_b = send(prev_b, "on_next"), send(succ_b, "on_prev")
    block = chunk(rows, True)
    bundle_shape = jax.ShapeDtypeStruct((3, *block.shape), jnp.bfloat16)

    def bundle_kernel(*refs):
        put_bundle(rows, *refs)

    (bundle,) = kernel_call(
        bundle_kernel, [own, succ_a, succ_b, prev_a, prev_b], [bundle_shape], BUNDLE_COST
    )
    others = send(bundle, "sibling")
    found, mine = kernel_call(
        far_first_kernel, [own, bundle, back_a, ahead_a, mine], [line] * 2, FIRST_COST
    )
    *found, back = kernel_call(
        far_back_kernel,
        [own, bundle, others, back_a, ahead_a, back_b, found],
        [line, half_line, block],
        BACK_COST,
    )
    far = [back, ahead_a, ahead_b]
    to_back, to_ahead = kernel_call(
        far_last_kernel, [own, bundle, others, *far, *found], [line] * 2, LAST_COST
    )
    (mine,) = kernel_call(own_kernel, [own, others, *far, mine], [line], 5)
    best = jnp.maximum(
        mine, jnp.maximum(send(to_back, "home_back"), send(to_ahead, "home_ahead"))
    )
    return best.reshape(rows)


def masked_sims(queries, query_labels, query_ids, keys, key_labels, key_ids):
    sims = jnp.einsum("qd,kd->qk", queries, keys, preferred_element_type=jnp.float32)
    keep = (
        (query_labels[:, None] == key_labels[None, :])
        & (query_labels[:, None] >= 0)
        & (query_ids[:, None] != key_ids[None, :])
    )
    return jnp.where(keep, sims, -1.0)


def by_owner(embeds, cluster):
    rows, width = embeds.shape
    size_x = lax.axis_size("gx")
    size_y = lax.axis_size("gy")
    owners = size_x * size_y
    cap = 2 * rows // owners
    total = owners * cap
    unit = normalised(embeds)
    target = cluster // CLU_OWN
    onehot = (target[:, None] == jnp.arange(owners, dtype=jnp.int32)[None, :]).astype(jnp.int32)
    before = jnp.cumsum(onehot, axis=0) - onehot
    slot = jnp.sum(before * onehot, axis=1)
    place = target * cap + slot
    outgoing = jnp.zeros((total, width), jnp.bfloat16).at[place].set(unit)
    out_labels = jnp.full((total,), -1, jnp.int32).at[place].set(cluster)
    got, got_labels = (
        lax.all_to_all(
            outgoing.reshape(owners, cap, width),
            ("gx", "gy"),
            split_axis=0,
            concat_axis=0,
            tiled=True,
        ),
        lax.all_to_all(
            out_labels.reshape(owners, cap), ("gx", "gy"), split_axis=0, concat_axis=0, tiled=True
        ),
    )
    members = got.reshape(total, width)
    labels = got_labels.reshape(total)
    core = lax.axis_index("gz")
    query_ids = core * total + jnp.arange(total, dtype=jnp.int32)
    keys = lax.all_gather(members, "gz", axis=0, tiled=True)
    key_labels = lax.all_gather(labels, "gz", axis=0, tiled=True)
    key_ids = jnp.arange(keys.shape[0], dtype=jnp.int32)
    best = jnp.maximum(
        jnp.full((total,), -1.0, jnp.float32),
        jnp.max(masked_sims(members, labels, query_ids, keys, key_labels, key_ids), axis=1),
    )
    back = lax.all_to_all(
        best.reshape(owners, cap), ("gx", "gy"), split_axis=0, concat_axis=0, tiled=True
    )
    return back.reshape(total)[place]


def solution(mesh):
    shape = mesh.shape
    ring = shape["gx"] * shape["gy"] == 8 and shape["gy"] == 2 and shape["gz"] == 2
    placed = (P(("parts", "gx", "gy", "gz"), None), P(("parts", "gx", "gy", "gz")))
    return jax.shard_map(
        on_ring if ring else by_owner,
        mesh=mesh,
        in_specs=placed,
        out_specs=P(("parts", "gx", "gy", "gz")),
        check_vma=False,
    )
```

```python
import functools

import jax
import jax.numpy as jnp
from jax import lax
from jax.experimental import pallas as pl
from jax.experimental.pallas import tpu as pltpu
from jax.sharding import PartitionSpec as P

CLU_OWN = 16


EPS = 1e-06

GROUP = ("gx", "gy", "gz")


def normalised(block):
    vecs = block.astype(jnp.float32)
    return (vecs * lax.rsqrt(jnp.sum(vecs * vecs, axis=1, keepdims=True) + EPS)).astype(
        jnp.bfloat16
    )


LANES = 128
LABEL_ROWS = 16
VMEM_BYTES = 32 * 2**20
BUNDLE_COST = 1
FIRST_COST = 200
BACK_COST = 2
LAST_COST = 5


def put_unit(unit, chunk):
    count, width = unit.shape
    for j in range(width // LANES):
        chunk[j * count : (j + 1) * count, :] = unit[:, j * LANES : (j + 1) * LANES]


def pack_first_kernel(embeds, label, first, line, sems):
    rows, width = embeds.shape
    half = rows // 2
    copies = []
    for j in range(width // LANES):
        part = embeds.at[pl.ds(0, half), pl.ds(j * LANES, LANES)]
        copies.append(pltpu.make_async_copy(part, first.at[pl.ds(j * half, half)], sems.at[j]))
    copies.append(pltpu.make_async_copy(label, line, sems.at[width // LANES]))
    for copy in copies:
        copy.start()
    copies[-1].wait()
    row = lax.broadcasted_iota(jnp.int32, (LABEL_ROWS, LANES), 0)
    lines = jnp.zeros((LABEL_ROWS, LANES), jnp.float32)
    for i in range(rows // LANES):
        piece = line[:, i * LANES : (i + 1) * LANES].astype(jnp.float32)
        lines = jnp.where(row == i, piece, lines)
    first[half * width // LANES :, :] = lines.astype(jnp.bfloat16)
    for copy in copies[:-1]:
        copy.wait()


def pack_second_kernel(embeds, first, second, both, mine):
    rows, width = embeds.shape
    unit = normalised(embeds[...])
    put_unit(unit[rows // 2 :, :], second)
    put_unit(unit, both)
    put_labels(first, both)
    own = Block(unit, labels_in(first, rows))
    mine[...] = best_of(own, own)


def put_labels(source, both):
    both[both.shape[0] - LABEL_ROWS :, :] = source[source.shape[0] - LABEL_ROWS :, :]


class Block:
    def __init__(self, unit, label, column=None):
        self.unit = unit
        self.label = label
        self.rows = unit.shape[0]
        self.along_rows = column

    def column(self):
        if self.along_rows is None:
            self.along_rows = jnp.transpose(jnp.broadcast_to(self.label, (LANES, self.rows)))
        return self.along_rows


def unit_in(chunk, rows, end):
    return jnp.concatenate([chunk[at : at + rows, :] for at in range(0, end, rows)], axis=1)


def labels_in(first, rows):
    lines = first[first.shape[0] - LABEL_ROWS :, :].astype(jnp.float32)
    return jnp.concatenate([lines[i : i + 1] for i in range(rows // LANES)], axis=1)


def packed(both, rows, column=None):
    unit = unit_in(both, rows, both.shape[0] - LABEL_ROWS)
    return Block(unit, labels_in(both, rows), None if column is None else column[...])


def first_half(first, rows):
    half = rows // 2
    unit = normalised(unit_in(first, half, first.shape[0] - LABEL_ROWS))
    return Block(unit, labels_in(first, rows)[:, :half])


def second_half(first, second, rows):
    half = rows // 2
    return Block(unit_in(second, half, second.shape[0]), labels_in(first, rows)[:, half:])


def whole(first, second, rows):
    return joined(first_half(first, rows), second_half(first, second, rows))


def joined(*blocks):
    return Block(
        jnp.concatenate([block.unit for block in blocks], axis=0),
        jnp.concatenate([block.label for block in blocks], axis=1),
    )


def best_of(queries, *all_keys):
    keys_unit = jnp.concatenate([keys.unit for keys in all_keys], axis=0)
    sims = lax.dot_general(
        keys_unit, queries.unit, (((1,), (1,)), ((), ())), preferred_element_type=jnp.float32
    )
    pieces = []
    for start in range(0, queries.rows, LANES):
        best, at = None, 0
        for keys in all_keys:
            keep = keys.column() == queries.label[:, start : start + LANES]
            if keys is queries:
                row = lax.broadcasted_iota(jnp.int32, keep.shape, 0)
                column = lax.broadcasted_iota(jnp.int32, keep.shape, 1) + start
                keep = keep & (row != column)
            found = jnp.where(keep, sims[at : at + keys.rows, start : start + LANES], -1.0)
            found = jnp.max(found, axis=0, keepdims=True)
            best = found if best is None else jnp.maximum(best, found)
            at += keys.rows
        pieces.append(best)
    return jnp.concatenate(pieces, axis=1)


def masked(queries, first, *others):
    all_keys = (first, *others)
    sims = lax.dot_general(
        jnp.concatenate([keys.unit for keys in all_keys], axis=0),
        queries.unit,
        (((1,), (1,)), ((), ())),
        preferred_element_type=jnp.float32,
    )
    found, at = [], 0
    for keys in all_keys:
        keep = keys.column() == queries.label
        found.append(jnp.where(keep, sims[at : at + keys.rows, :], -1.0))
        at += keys.rows
    best = [jnp.max(block, axis=0, keepdims=True) for block in found]
    return found[0], functools.reduce(jnp.maximum, best)


def put_bundle(rows, own, succ_a, succ_b, prev_a, prev_b, bundle):
    for at, first, second in ((0, prev_a, prev_b), (1, succ_a, succ_b)):
        put_unit(whole(first, second, rows).unit, bundle.at[at])
        put_labels(first, bundle.at[at])
    bundle[2] = own[...]


def far_first_kernel(own, bundle, back_a, ahead_a, self_best, found, mine, columns):
    rows = found.shape[1]
    queries = joined(first_half(back_a, rows), first_half(ahead_a, rows))
    own = packed(own, rows)
    near = [packed(bundle.at[at], rows) for at in range(2)]
    found[...] = best_of(queries, queries, *near, own)
    mine[...] = jnp.maximum(self_best[...], best_of(own, *near))
    columns[0], columns[1] = near[0].column(), own.column()


def far_back_kernel(own, bundle, others, back_a, ahead_a, back_b, found, *refs):
    back_found, ahead_found, back_packed, columns = refs
    rows = found.shape[1]
    half = rows // 2
    succ, own = packed(bundle.at[1], rows), packed(own, rows)
    prev_other, succ_other = packed(others.at[0], rows), packed(others.at[1], rows)
    first, rest = first_half(back_a, rows), second_half(back_a, back_b, rows)
    first_ahead = first_half(ahead_a, rows)
    back = joined(first, rest)
    put_unit(back.unit, back_packed)
    put_labels(back_a, back_packed)
    columns[0, :half, :], columns[0, half:, :] = first.column(), rest.column()
    columns[1] = prev_other.column()
    both = best_of(back, succ_other)
    back_found[:, :half] = jnp.maximum(found[:, :half], both[:, :half])
    back_found[:, half:] = jnp.maximum(best_of(rest, own, succ, first_ahead), both[:, half:])
    ahead_found[...] = jnp.maximum(found[:, half:], best_of(first_ahead, rest, prev_other))


def far_last_kernel(own, bundle, others, back, ahead_a, ahead_b, *refs):
    back_found, ahead_found, near_columns, far_columns, to_back, to_ahead = refs
    rows = to_back.shape[1]
    half = rows // 2
    rest = second_half(ahead_a, ahead_b, rows)
    back = packed(back, rows, far_columns.at[0])
    keys = [
        packed(own, rows, near_columns.at[1]),
        packed(bundle.at[0], rows, near_columns.at[0]),
        packed(others.at[0], rows, far_columns.at[1]),
    ]
    sims, found = masked(rest, back, *keys)
    to_ahead[:, :half] = ahead_found[...]
    to_ahead[:, half:] = found
    best = jnp.max(jnp.transpose(sims), axis=0, keepdims=True)
    to_back[...] = jnp.maximum(back_found[...], best)


def own_kernel(own, others, back, ahead_a, ahead_b, near, mine):
    rows = mine.shape[1]
    keys = [packed(ref, rows) for ref in (others.at[at] for at in range(3))]
    keys += [packed(back, rows), whole(ahead_a, ahead_b, rows)]
    mine[...] = jnp.maximum(near[...], best_of(packed(own, rows), *keys))


def ring_perms(size_x, size_y, size_z):
    chips = size_x * size_y

    def device(place, core):
        place = place % chips
        x, y = (place, 0) if place < size_x else (chips - 1 - place, 1)
        return (x * size_y + y) * size_z + core

    def perm(to):
        return [
            (device(p, k), device(*to(p, k))) for p in range(chips) for k in range(size_z)
        ]

    def from_prev(place, core):
        return core ^ (place % chips in (0, 1))

    def from_next(place, core):
        return core ^ (place % chips not in (0, 1))

    return {
        "sibling": perm(lambda p, k: (p, 1 - k)),
        "next": perm(lambda p, k: (p + 1, from_prev(p + 1, k))),
        "prev": perm(lambda p, k: (p - 1, from_next(p - 1, k))),
        "on_next": perm(lambda p, k: (p + 1, k)),
        "on_prev": perm(lambda p, k: (p - 1, k)),
        "home_back": perm(lambda p, k: (p - 2, from_prev(p - 1, k))),
        "home_ahead": perm(lambda p, k: (p + 2, from_next(p + 1, k))),
    }


def kernel_call(kernel, inputs, outputs, matmuls):
    vmem = pl.BlockSpec(memory_space=pltpu.VMEM)
    return pl.pallas_call(
        kernel,
        out_shape=outputs,
        in_specs=[vmem] * len(inputs),
        out_specs=[vmem] * len(outputs),
        compiler_params=pltpu.CompilerParams(vmem_limit_bytes=VMEM_BYTES),
        cost_estimate=pl.CostEstimate(
            flops=matmuls * 2**26, bytes_accessed=2**20, transcendentals=0
        ),
        name=kernel.__name__,
    )(*inputs)


def on_ring(embeds, cluster):
    rows, width = embeds.shape
    half = rows // 2
    perms = ring_perms(*(lax.axis_size(a) for a in GROUP))

    def send(value, name):
        return lax.ppermute(value, GROUP, perms[name])

    line = jax.ShapeDtypeStruct((1, rows), jnp.float32)
    half_line = jax.ShapeDtypeStruct((1, half), jnp.float32)

    def chunk(count, labels):
        size = count * width // LANES + labels * LABEL_ROWS
        return jax.ShapeDtypeStruct((size, LANES), jnp.bfloat16)

    anywhere = pl.BlockSpec(memory_space=pl.ANY)
    vmem = pl.BlockSpec(memory_space=pltpu.VMEM)
    own_a = pl.pallas_call(
        pack_first_kernel,
        out_shape=chunk(half, True),
        in_specs=[anywhere] * 2,
        out_specs=vmem,
        scratch_shapes=[
            pltpu.VMEM((1, rows), jnp.int32),
            pltpu.SemaphoreType.DMA((width // LANES + 1,)),
        ],
        compiler_params=pltpu.CompilerParams(vmem_limit_bytes=VMEM_BYTES),
        name="pack_first",
    )(
        pltpu.with_memory_space_constraint(embeds, pltpu.HBM),
        pltpu.with_memory_space_constraint(cluster.reshape(1, rows), pltpu.HBM),
    )
    own_b, own, mine = kernel_call(
        pack_second_kernel, [embeds, own_a], [chunk(half, False), chunk(rows, True), line], 1
    )
    prev_a, succ_a = send(own_a, "next"), send(own_a, "prev")
    prev_b, succ_b = send(own_b, "next"), send(own_b, "prev")
    back_a, ahead_a = send(prev_a, "on_next"), send(succ_a, "on_prev")
    back_b, ahead_b = send(prev_b, "on_next"), send(succ_b, "on_prev")
    block = chunk(rows, True)
    bundle_shape = jax.ShapeDtypeStruct((3, *block.shape), jnp.bfloat16)

    def bundle_kernel(*refs):
        put_bundle(rows, *refs)

    (bundle,) = kernel_call(
        bundle_kernel, [own, succ_a, succ_b, prev_a, prev_b], [bundle_shape], BUNDLE_COST
    )
    others = send(bundle, "sibling")
    columns = jax.ShapeDtypeStruct((2, rows, LANES), jnp.float32)
    found, mine, near_columns = kernel_call(
        far_first_kernel, [own, bundle, back_a, ahead_a, mine], [line, line, columns], FIRST_COST
    )
    *found, back, far_columns = kernel_call(
        far_back_kernel,
        [own, bundle, others, back_a, ahead_a, back_b, found],
        [line, half_line, block, columns],
        BACK_COST,
    )
    far = [back, ahead_a, ahead_b]
    to_back, to_ahead = kernel_call(
        far_last_kernel,
        [own, bundle, others, *far, *found, near_columns, far_columns],
        [line] * 2,
        LAST_COST,
    )
    (mine,) = kernel_call(own_kernel, [own, others, *far, mine], [line], 5)
    best = jnp.maximum(
        mine, jnp.maximum(send(to_back, "home_back"), send(to_ahead, "home_ahead"))
    )
    return best.reshape(rows)


def masked_sims(queries, query_labels, query_ids, keys, key_labels, key_ids):
    sims = jnp.einsum("qd,kd->qk", queries, keys, preferred_element_type=jnp.float32)
    keep = (
        (query_labels[:, None] == key_labels[None, :])
        & (query_labels[:, None] >= 0)
        & (query_ids[:, None] != key_ids[None, :])
    )
    return jnp.where(keep, sims, -1.0)


def by_owner(embeds, cluster):
    rows, width = embeds.shape
    size_x = lax.axis_size("gx")
    size_y = lax.axis_size("gy")
    owners = size_x * size_y
    cap = 2 * rows // owners
    total = owners * cap
    unit = normalised(embeds)
    target = cluster // CLU_OWN
    onehot = (target[:, None] == jnp.arange(owners, dtype=jnp.int32)[None, :]).astype(jnp.int32)
    before = jnp.cumsum(onehot, axis=0) - onehot
    slot = jnp.sum(before * onehot, axis=1)
    place = target * cap + slot
    outgoing = jnp.zeros((total, width), jnp.bfloat16).at[place].set(unit)
    out_labels = jnp.full((total,), -1, jnp.int32).at[place].set(cluster)
    got, got_labels = (
        lax.all_to_all(
            outgoing.reshape(owners, cap, width),
            ("gx", "gy"),
            split_axis=0,
            concat_axis=0,
            tiled=True,
        ),
        lax.all_to_all(
            out_labels.reshape(owners, cap), ("gx", "gy"), split_axis=0, concat_axis=0, tiled=True
        ),
    )
    members = got.reshape(total, width)
    labels = got_labels.reshape(total)
    core = lax.axis_index("gz")
    query_ids = core * total + jnp.arange(total, dtype=jnp.int32)
    keys = lax.all_gather(members, "gz", axis=0, tiled=True)
    key_labels = lax.all_gather(labels, "gz", axis=0, tiled=True)
    key_ids = jnp.arange(keys.shape[0], dtype=jnp.int32)
    best = jnp.maximum(
        jnp.full((total,), -1.0, jnp.float32),
        jnp.max(masked_sims(members, labels, query_ids, keys, key_labels, key_ids), axis=1),
    )
    back = lax.all_to_all(
        best.reshape(owners, cap), ("gx", "gy"), split_axis=0, concat_axis=0, tiled=True
    )
    return back.reshape(total)[place]


def solution(mesh):
    shape = mesh.shape
    ring = shape["gx"] * shape["gy"] == 8 and shape["gy"] == 2 and shape["gz"] == 2
    placed = (P(("parts", "gx", "gy", "gz"), None), P(("parts", "gx", "gy", "gz")))
    return jax.shard_map(
        on_ring if ring else by_owner,
        mesh=mesh,
        in_specs=placed,
        out_specs=P(("parts", "gx", "gy", "gz")),
        check_vma=False,
    )
```

```python
import functools

import jax
import jax.numpy as jnp
from jax import lax
from jax.experimental import pallas as pl
from jax.experimental.pallas import tpu as pltpu
from jax.sharding import PartitionSpec as P

CLU_OWN = 16


EPS = 1e-06

GROUP = ("gx", "gy", "gz")


def normalised(block):
    vecs = block.astype(jnp.float32)
    return (vecs * lax.rsqrt(jnp.sum(vecs * vecs, axis=1, keepdims=True) + EPS)).astype(
        jnp.bfloat16
    )


LANES = 128
LABEL_ROWS = 16
VMEM_BYTES = 32 * 2**20
BUNDLE_COST = 1
FIRST_COST = 200
BACK_COST = 2
LAST_COST = 5


def put_unit(unit, chunk):
    count, width = unit.shape
    for j in range(width // LANES):
        chunk[j * count : (j + 1) * count, :] = unit[:, j * LANES : (j + 1) * LANES]


def pack_first_kernel(embeds, label, first, line, sems):
    rows, width = embeds.shape
    half = rows // 2
    copies = []
    for j in range(width // LANES):
        part = embeds.at[pl.ds(0, half), pl.ds(j * LANES, LANES)]
        copies.append(pltpu.make_async_copy(part, first.at[pl.ds(j * half, half)], sems.at[j]))
    copies.append(pltpu.make_async_copy(label, line, sems.at[width // LANES]))
    for copy in copies:
        copy.start()
    copies[-1].wait()
    row = lax.broadcasted_iota(jnp.int32, (LABEL_ROWS, LANES), 0)
    lines = jnp.zeros((LABEL_ROWS, LANES), jnp.float32)
    for i in range(rows // LANES):
        piece = line[:, i * LANES : (i + 1) * LANES].astype(jnp.float32)
        lines = jnp.where(row == i, piece, lines)
    first[half * width // LANES :, :] = lines.astype(jnp.bfloat16)
    for copy in copies[:-1]:
        copy.wait()


def pack_second_kernel(embeds, first, second, both, mine):
    rows, width = embeds.shape
    unit = normalised(embeds[...])
    put_unit(unit[rows // 2 :, :], second)
    put_unit(unit, both)
    put_labels(first, both)
    own = Block(unit, labels_in(first, rows))
    mine[...] = best_of(own, own)


def put_labels(source, both):
    both[both.shape[0] - LABEL_ROWS :, :] = source[source.shape[0] - LABEL_ROWS :, :]


class Block:
    def __init__(self, unit, label):
        self.unit = unit
        self.label = label
        self.rows = unit.shape[0]
        self.along_rows = None

    def column(self):
        if self.along_rows is None:
            self.along_rows = jnp.transpose(jnp.broadcast_to(self.label, (LANES, self.rows)))
        return self.along_rows


def unit_in(chunk, rows, end):
    return jnp.concatenate([chunk[at : at + rows, :] for at in range(0, end, rows)], axis=1)


def labels_in(first, rows):
    lines = first[first.shape[0] - LABEL_ROWS :, :].astype(jnp.float32)
    return jnp.concatenate([lines[i : i + 1] for i in range(rows // LANES)], axis=1)


def packed(both, rows):
    return Block(unit_in(both, rows, both.shape[0] - LABEL_ROWS), labels_in(both, rows))


def first_half(first, rows):
    half = rows // 2
    unit = normalised(unit_in(first, half, first.shape[0] - LABEL_ROWS))
    return Block(unit, labels_in(first, rows)[:, :half])


def second_half(first, second, rows):
    half = rows // 2
    return Block(unit_in(second, half, second.shape[0]), labels_in(first, rows)[:, half:])


def whole(first, second, rows):
    return joined(first_half(first, rows), second_half(first, second, rows))


def joined(*blocks):
    return Block(
        jnp.concatenate([block.unit for block in blocks], axis=0),
        jnp.concatenate([block.label for block in blocks], axis=1),
    )


def best_of(queries, *all_keys):
    keys_unit = jnp.concatenate([keys.unit for keys in all_keys], axis=0)
    sims = lax.dot_general(
        keys_unit, queries.unit, (((1,), (1,)), ((), ())), preferred_element_type=jnp.float32
    )
    pieces = []
    for start in range(0, queries.rows, LANES):
        best, at = None, 0
        for keys in all_keys:
            keep = keys.column() == queries.label[:, start : start + LANES]
            if keys is queries:
                row = lax.broadcasted_iota(jnp.int32, keep.shape, 0)
                column = lax.broadcasted_iota(jnp.int32, keep.shape, 1) + start
                keep = keep & (row != column)
            found = jnp.where(keep, sims[at : at + keys.rows, start : start + LANES], -1.0)
            found = jnp.max(found, axis=0, keepdims=True)
            best = found if best is None else jnp.maximum(best, found)
            at += keys.rows
        pieces.append(best)
    return jnp.concatenate(pieces, axis=1)


def masked(queries, first, *others):
    all_keys = (first, *others)
    sims = lax.dot_general(
        jnp.concatenate([keys.unit for keys in all_keys], axis=0),
        queries.unit,
        (((1,), (1,)), ((), ())),
        preferred_element_type=jnp.float32,
    )
    found, at = [], 0
    for keys in all_keys:
        keep = keys.column() == queries.label
        found.append(jnp.where(keep, sims[at : at + keys.rows, :], -1.0))
        at += keys.rows
    best = [jnp.max(block, axis=0, keepdims=True) for block in found]
    return found[0], functools.reduce(jnp.maximum, best)


def put_bundle(rows, own, succ_a, succ_b, prev_a, prev_b, bundle):
    for at, first, second in ((0, prev_a, prev_b), (1, succ_a, succ_b)):
        put_unit(whole(first, second, rows).unit, bundle.at[at])
        put_labels(first, bundle.at[at])
    bundle[2] = own[...]


def far_first_kernel(own, bundle, back_a, ahead_a, self_best, found, mine):
    rows = found.shape[1]
    queries = joined(first_half(back_a, rows), first_half(ahead_a, rows))
    own = packed(own, rows)
    near = [packed(bundle.at[at], rows) for at in range(2)]
    found[...] = best_of(queries, queries, *near, own)
    mine[...] = jnp.maximum(self_best[...], best_of(own, *near))


def far_back_kernel(own, bundle, others, back_a, ahead_a, back_b, found, *refs):
    back_found, ahead_found, back_packed = refs
    rows = found.shape[1]
    half = rows // 2
    succ, own = packed(bundle.at[1], rows), packed(own, rows)
    prev_other, succ_other = packed(others.at[0], rows), packed(others.at[1], rows)
    first, rest = first_half(back_a, rows), second_half(back_a, back_b, rows)
    first_ahead = first_half(ahead_a, rows)
    back = joined(first, rest)
    put_unit(back.unit, back_packed)
    put_labels(back_a, back_packed)
    both = best_of(back, succ_other)
    back_found[:, :half] = jnp.maximum(found[:, :half], both[:, :half])
    back_found[:, half:] = jnp.maximum(best_of(rest, own, succ, first_ahead), both[:, half:])
    ahead_found[...] = jnp.maximum(found[:, half:], best_of(first_ahead, rest, prev_other))


def far_last_kernel(own, bundle, others, back, ahead_a, ahead_b, *refs):
    back_found, ahead_found, to_back, to_ahead = refs
    rows = to_back.shape[1]
    half = rows // 2
    back, rest = packed(back, rows), second_half(ahead_a, ahead_b, rows)
    keys = [packed(ref, rows) for ref in (own, bundle.at[0], others.at[0])]
    sims, found = masked(rest, back, *keys)
    to_ahead[:, :half] = ahead_found[...]
    to_ahead[:, half:] = found
    best = jnp.max(jnp.transpose(sims), axis=0, keepdims=True)
    to_back[...] = jnp.maximum(back_found[...], best)


def own_kernel(own, others, back, ahead_a, ahead_b, near, mine):
    rows = mine.shape[1]
    keys = [packed(ref, rows) for ref in (others.at[at] for at in range(3))]
    keys += [packed(back, rows), whole(ahead_a, ahead_b, rows)]
    mine[...] = jnp.maximum(near[...], best_of(packed(own, rows), *keys))


def ring_perms(size_x, size_y, size_z):
    chips = size_x * size_y

    def device(place, core):
        place = place % chips
        x, y = (place, 1) if place < size_x else (chips - 1 - place, 0)
        return (x * size_y + y) * size_z + core

    def perm(to):
        return [
            (device(p, k), device(*to(p, k))) for p in range(chips) for k in range(size_z)
        ]

    def from_prev(place, core):
        return core ^ (place % chips in (0, 1))

    def from_next(place, core):
        return core ^ (place % chips not in (0, 1))

    return {
        "sibling": perm(lambda p, k: (p, 1 - k)),
        "next": perm(lambda p, k: (p + 1, from_prev(p + 1, k))),
        "prev": perm(lambda p, k: (p - 1, from_next(p - 1, k))),
        "on_next": perm(lambda p, k: (p + 1, k)),
        "on_prev": perm(lambda p, k: (p - 1, k)),
        "home_back": perm(lambda p, k: (p - 2, from_prev(p - 1, k))),
        "home_ahead": perm(lambda p, k: (p + 2, from_next(p + 1, k))),
    }


def kernel_call(kernel, inputs, outputs, matmuls):
    vmem = pl.BlockSpec(memory_space=pltpu.VMEM)
    return pl.pallas_call(
        kernel,
        out_shape=outputs,
        in_specs=[vmem] * len(inputs),
        out_specs=[vmem] * len(outputs),
        compiler_params=pltpu.CompilerParams(vmem_limit_bytes=VMEM_BYTES),
        cost_estimate=pl.CostEstimate(
            flops=matmuls * 2**26, bytes_accessed=2**20, transcendentals=0
        ),
        name=kernel.__name__,
    )(*inputs)


def on_ring(embeds, cluster):
    rows, width = embeds.shape
    half = rows // 2
    perms = ring_perms(*(lax.axis_size(a) for a in GROUP))

    def send(value, name):
        return lax.ppermute(value, GROUP, perms[name])

    line = jax.ShapeDtypeStruct((1, rows), jnp.float32)
    half_line = jax.ShapeDtypeStruct((1, half), jnp.float32)

    def chunk(count, labels):
        size = count * width // LANES + labels * LABEL_ROWS
        return jax.ShapeDtypeStruct((size, LANES), jnp.bfloat16)

    anywhere = pl.BlockSpec(memory_space=pl.ANY)
    vmem = pl.BlockSpec(memory_space=pltpu.VMEM)
    own_a = pl.pallas_call(
        pack_first_kernel,
        out_shape=chunk(half, True),
        in_specs=[anywhere] * 2,
        out_specs=vmem,
        scratch_shapes=[
            pltpu.VMEM((1, rows), jnp.int32),
            pltpu.SemaphoreType.DMA((width // LANES + 1,)),
        ],
        compiler_params=pltpu.CompilerParams(vmem_limit_bytes=VMEM_BYTES),
        name="pack_first",
    )(
        pltpu.with_memory_space_constraint(embeds, pltpu.HBM),
        pltpu.with_memory_space_constraint(cluster.reshape(1, rows), pltpu.HBM),
    )
    own_b, own, mine = kernel_call(
        pack_second_kernel, [embeds, own_a], [chunk(half, False), chunk(rows, True), line], 1
    )
    prev_a, succ_a = send(own_a, "next"), send(own_a, "prev")
    prev_b, succ_b = send(own_b, "next"), send(own_b, "prev")
    back_a, ahead_a = send(prev_a, "on_next"), send(succ_a, "on_prev")
    back_b, ahead_b = send(prev_b, "on_next"), send(succ_b, "on_prev")
    block = chunk(rows, True)
    bundle_shape = jax.ShapeDtypeStruct((3, *block.shape), jnp.bfloat16)

    def bundle_kernel(*refs):
        put_bundle(rows, *refs)

    (bundle,) = kernel_call(
        bundle_kernel, [own, succ_a, succ_b, prev_a, prev_b], [bundle_shape], BUNDLE_COST
    )
    others = send(bundle, "sibling")
    found, mine = kernel_call(
        far_first_kernel, [own, bundle, back_a, ahead_a, mine], [line] * 2, FIRST_COST
    )
    *found, back = kernel_call(
        far_back_kernel,
        [own, bundle, others, back_a, ahead_a, back_b, found],
        [line, half_line, block],
        BACK_COST,
    )
    far = [back, ahead_a, ahead_b]
    to_back, to_ahead = kernel_call(
        far_last_kernel, [own, bundle, others, *far, *found], [line] * 2, LAST_COST
    )
    (mine,) = kernel_call(own_kernel, [own, others, *far, mine], [line], 5)
    best = jnp.maximum(
        mine, jnp.maximum(send(to_back, "home_back"), send(to_ahead, "home_ahead"))
    )
    return best.reshape(rows)


def masked_sims(queries, query_labels, query_ids, keys, key_labels, key_ids):
    sims = jnp.einsum("qd,kd->qk", queries, keys, preferred_element_type=jnp.float32)
    keep = (
        (query_labels[:, None] == key_labels[None, :])
        & (query_labels[:, None] >= 0)
        & (query_ids[:, None] != key_ids[None, :])
    )
    return jnp.where(keep, sims, -1.0)


def by_owner(embeds, cluster):
    rows, width = embeds.shape
    size_x = lax.axis_size("gx")
    size_y = lax.axis_size("gy")
    owners = size_x * size_y
    cap = 2 * rows // owners
    total = owners * cap
    unit = normalised(embeds)
    target = cluster // CLU_OWN
    onehot = (target[:, None] == jnp.arange(owners, dtype=jnp.int32)[None, :]).astype(jnp.int32)
    before = jnp.cumsum(onehot, axis=0) - onehot
    slot = jnp.sum(before * onehot, axis=1)
    place = target * cap + slot
    outgoing = jnp.zeros((total, width), jnp.bfloat16).at[place].set(unit)
    out_labels = jnp.full((total,), -1, jnp.int32).at[place].set(cluster)
    got, got_labels = (
        lax.all_to_all(
            outgoing.reshape(owners, cap, width),
            ("gx", "gy"),
            split_axis=0,
            concat_axis=0,
            tiled=True,
        ),
        lax.all_to_all(
            out_labels.reshape(owners, cap), ("gx", "gy"), split_axis=0, concat_axis=0, tiled=True
        ),
    )
    members = got.reshape(total, width)
    labels = got_labels.reshape(total)
    core = lax.axis_index("gz")
    query_ids = core * total + jnp.arange(total, dtype=jnp.int32)
    keys = lax.all_gather(members, "gz", axis=0, tiled=True)
    key_labels = lax.all_gather(labels, "gz", axis=0, tiled=True)
    key_ids = jnp.arange(keys.shape[0], dtype=jnp.int32)
    best = jnp.maximum(
        jnp.full((total,), -1.0, jnp.float32),
        jnp.max(masked_sims(members, labels, query_ids, keys, key_labels, key_ids), axis=1),
    )
    back = lax.all_to_all(
        best.reshape(owners, cap), ("gx", "gy"), split_axis=0, concat_axis=0, tiled=True
    )
    return back.reshape(total)[place]


def solution(mesh):
    shape = mesh.shape
    ring = shape["gx"] * shape["gy"] == 8 and shape["gy"] == 2 and shape["gz"] == 2
    placed = (P(("parts", "gx", "gy", "gz"), None), P(("parts", "gx", "gy", "gz")))
    return jax.shard_map(
        on_ring if ring else by_owner,
        mesh=mesh,
        in_specs=placed,
        out_specs=P(("parts", "gx", "gy", "gz")),
        check_vma=False,
    )
```

```python
import functools

import jax
import jax.numpy as jnp
from jax import lax
from jax.experimental import pallas as pl
from jax.experimental.pallas import tpu as pltpu
from jax.sharding import PartitionSpec as P

CLU_OWN = 16


EPS = 1e-06

GROUP = ("gx", "gy", "gz")


def normalised(block):
    vecs = block.astype(jnp.float32)
    return (vecs * lax.rsqrt(jnp.sum(vecs * vecs, axis=1, keepdims=True) + EPS)).astype(
        jnp.bfloat16
    )


LANES = 128
LABEL_ROWS = 16
VMEM_BYTES = 32 * 2**20
BUNDLE_COST = 1
FIRST_COST = 200
BACK_COST = 2
LAST_COST = 5


def put_unit(unit, chunk):
    count, width = unit.shape
    for j in range(width // LANES):
        chunk[j * count : (j + 1) * count, :] = unit[:, j * LANES : (j + 1) * LANES]


def pack_first_kernel(embeds, label, first, line, sems):
    rows, width = embeds.shape
    half = rows // 2
    copies = [pltpu.make_async_copy(label, line, sems.at[width // LANES])]
    for j in range(width // LANES):
        part = embeds.at[pl.ds(0, half), pl.ds(j * LANES, LANES)]
        copies.append(pltpu.make_async_copy(part, first.at[pl.ds(j * half, half)], sems.at[j]))
    for copy in copies:
        copy.start()
    copies[0].wait()
    row = lax.broadcasted_iota(jnp.int32, (LABEL_ROWS, LANES), 0)
    lines = jnp.zeros((LABEL_ROWS, LANES), jnp.float32)
    for i in range(rows // LANES):
        piece = line[:, i * LANES : (i + 1) * LANES].astype(jnp.float32)
        lines = jnp.where(row == i, piece, lines)
    first[half * width // LANES :, :] = lines.astype(jnp.bfloat16)
    for copy in copies[1:]:
        copy.wait()


def pack_second_kernel(embeds, first, second, both, mine):
    rows, width = embeds.shape
    unit = normalised(embeds[...])
    put_unit(unit[rows // 2 :, :], second)
    put_unit(unit, both)
    put_labels(first, both)
    own = Block(unit, labels_in(first, rows))
    mine[...] = best_of(own, own)


def put_labels(source, both):
    both[both.shape[0] - LABEL_ROWS :, :] = source[source.shape[0] - LABEL_ROWS :, :]


class Block:
    def __init__(self, unit, label):
        self.unit = unit
        self.label = label
        self.rows = unit.shape[0]
        self.along_rows = None

    def column(self):
        if self.along_rows is None:
            self.along_rows = jnp.transpose(jnp.broadcast_to(self.label, (LANES, self.rows)))
        return self.along_rows


def unit_in(chunk, rows, end):
    return jnp.concatenate([chunk[at : at + rows, :] for at in range(0, end, rows)], axis=1)


def labels_in(first, rows):
    lines = first[first.shape[0] - LABEL_ROWS :, :].astype(jnp.float32)
    return jnp.concatenate([lines[i : i + 1] for i in range(rows // LANES)], axis=1)


def packed(both, rows):
    return Block(unit_in(both, rows, both.shape[0] - LABEL_ROWS), labels_in(both, rows))


def first_half(first, rows):
    half = rows // 2
    unit = normalised(unit_in(first, half, first.shape[0] - LABEL_ROWS))
    return Block(unit, labels_in(first, rows)[:, :half])


def second_half(first, second, rows):
    half = rows // 2
    return Block(unit_in(second, half, second.shape[0]), labels_in(first, rows)[:, half:])


def whole(first, second, rows):
    return joined(first_half(first, rows), second_half(first, second, rows))


def joined(*blocks):
    return Block(
        jnp.concatenate([block.unit for block in blocks], axis=0),
        jnp.concatenate([block.label for block in blocks], axis=1),
    )


def best_of(queries, *all_keys):
    keys_unit = jnp.concatenate([keys.unit for keys in all_keys], axis=0)
    sims = lax.dot_general(
        keys_unit, queries.unit, (((1,), (1,)), ((), ())), preferred_element_type=jnp.float32
    )
    pieces = []
    for start in range(0, queries.rows, LANES):
        best, at = None, 0
        for keys in all_keys:
            keep = keys.column() == queries.label[:, start : start + LANES]
            if keys is queries:
                row = lax.broadcasted_iota(jnp.int32, keep.shape, 0)
                column = lax.broadcasted_iota(jnp.int32, keep.shape, 1) + start
                keep = keep & (row != column)
            found = jnp.where(keep, sims[at : at + keys.rows, start : start + LANES], -1.0)
            found = jnp.max(found, axis=0, keepdims=True)
            best = found if best is None else jnp.maximum(best, found)
            at += keys.rows
        pieces.append(best)
    return jnp.concatenate(pieces, axis=1)


def masked(queries, first, *others):
    all_keys = (first, *others)
    sims = lax.dot_general(
        jnp.concatenate([keys.unit for keys in all_keys], axis=0),
        queries.unit,
        (((1,), (1,)), ((), ())),
        preferred_element_type=jnp.float32,
    )
    found, at = [], 0
    for keys in all_keys:
        keep = keys.column() == queries.label
        found.append(jnp.where(keep, sims[at : at + keys.rows, :], -1.0))
        at += keys.rows
    best = [jnp.max(block, axis=0, keepdims=True) for block in found]
    return found[0], functools.reduce(jnp.maximum, best)


def put_bundle(rows, own, succ_a, succ_b, prev_a, prev_b, bundle):
    for at, first, second in ((0, prev_a, prev_b), (1, succ_a, succ_b)):
        put_unit(whole(first, second, rows).unit, bundle.at[at])
        put_labels(first, bundle.at[at])
    bundle[2] = own[...]


def far_first_kernel(own, bundle, back_a, ahead_a, self_best, found, mine):
    rows = found.shape[1]
    queries = joined(first_half(back_a, rows), first_half(ahead_a, rows))
    own = packed(own, rows)
    near = [packed(bundle.at[at], rows) for at in range(2)]
    found[...] = best_of(queries, queries, *near, own)
    mine[...] = jnp.maximum(self_best[...], best_of(own, *near))


def far_back_kernel(own, bundle, others, back_a, ahead_a, back_b, found, *refs):
    back_found, ahead_found, back_packed = refs
    rows = found.shape[1]
    half = rows // 2
    succ, own = packed(bundle.at[1], rows), packed(own, rows)
    prev_other, succ_other = packed(others.at[0], rows), packed(others.at[1], rows)
    first, rest = first_half(back_a, rows), second_half(back_a, back_b, rows)
    first_ahead = first_half(ahead_a, rows)
    back = joined(first, rest)
    put_unit(back.unit, back_packed)
    put_labels(back_a, back_packed)
    both = best_of(back, succ_other)
    back_found[:, :half] = jnp.maximum(found[:, :half], both[:, :half])
    back_found[:, half:] = jnp.maximum(best_of(rest, own, succ, first_ahead), both[:, half:])
    ahead_found[...] = jnp.maximum(found[:, half:], best_of(first_ahead, rest, prev_other))


def far_last_kernel(own, bundle, others, back, ahead_a, ahead_b, *refs):
    back_found, ahead_found, to_back, to_ahead = refs
    rows = to_back.shape[1]
    half = rows // 2
    back, rest = packed(back, rows), second_half(ahead_a, ahead_b, rows)
    keys = [packed(ref, rows) for ref in (own, bundle.at[0], others.at[0])]
    sims, found = masked(rest, back, *keys)
    to_ahead[:, :half] = ahead_found[...]
    to_ahead[:, half:] = found
    best = jnp.max(jnp.transpose(sims), axis=0, keepdims=True)
    to_back[...] = jnp.maximum(back_found[...], best)


def own_kernel(own, others, back, ahead_a, ahead_b, near, mine):
    rows = mine.shape[1]
    keys = [packed(ref, rows) for ref in (others.at[at] for at in range(3))]
    keys += [packed(back, rows), whole(ahead_a, ahead_b, rows)]
    mine[...] = jnp.maximum(near[...], best_of(packed(own, rows), *keys))


def ring_perms(size_x, size_y, size_z):
    chips = size_x * size_y

    def device(place, core):
        place = place % chips
        x, y = (place, 0) if place < size_x else (chips - 1 - place, 1)
        return (x * size_y + y) * size_z + core

    def perm(to):
        return [
            (device(p, k), device(*to(p, k))) for p in range(chips) for k in range(size_z)
        ]

    def from_prev(place, core):
        return core ^ (place % chips in (0, 1))

    def from_next(place, core):
        return core ^ (place % chips not in (0, 1))

    return {
        "sibling": perm(lambda p, k: (p, 1 - k)),
        "next": perm(lambda p, k: (p + 1, from_prev(p + 1, k))),
        "prev": perm(lambda p, k: (p - 1, from_next(p - 1, k))),
        "on_next": perm(lambda p, k: (p + 1, k)),
        "on_prev": perm(lambda p, k: (p - 1, k)),
        "home_back": perm(lambda p, k: (p - 2, from_prev(p - 1, k))),
        "home_ahead": perm(lambda p, k: (p + 2, from_next(p + 1, k))),
    }


def kernel_call(kernel, inputs, outputs, matmuls):
    vmem = pl.BlockSpec(memory_space=pltpu.VMEM)
    return pl.pallas_call(
        kernel,
        out_shape=outputs,
        in_specs=[vmem] * len(inputs),
        out_specs=[vmem] * len(outputs),
        compiler_params=pltpu.CompilerParams(vmem_limit_bytes=VMEM_BYTES),
        cost_estimate=pl.CostEstimate(
            flops=matmuls * 2**26, bytes_accessed=2**20, transcendentals=0
        ),
        name=kernel.__name__,
    )(*inputs)


def on_ring(embeds, cluster):
    rows, width = embeds.shape
    half = rows // 2
    perms = ring_perms(*(lax.axis_size(a) for a in GROUP))

    def send(value, name):
        return lax.ppermute(value, GROUP, perms[name])

    line = jax.ShapeDtypeStruct((1, rows), jnp.float32)
    half_line = jax.ShapeDtypeStruct((1, half), jnp.float32)

    def chunk(count, labels):
        size = count * width // LANES + labels * LABEL_ROWS
        return jax.ShapeDtypeStruct((size, LANES), jnp.bfloat16)

    anywhere = pl.BlockSpec(memory_space=pl.ANY)
    vmem = pl.BlockSpec(memory_space=pltpu.VMEM)
    own_a = pl.pallas_call(
        pack_first_kernel,
        out_shape=chunk(half, True),
        in_specs=[anywhere] * 2,
        out_specs=vmem,
        scratch_shapes=[
            pltpu.VMEM((1, rows), jnp.int32),
            pltpu.SemaphoreType.DMA((width // LANES + 1,)),
        ],
        compiler_params=pltpu.CompilerParams(vmem_limit_bytes=VMEM_BYTES),
        name="pack_first",
    )(
        pltpu.with_memory_space_constraint(embeds, pltpu.HBM),
        pltpu.with_memory_space_constraint(cluster.reshape(1, rows), pltpu.HBM),
    )
    own_b, own, mine = kernel_call(
        pack_second_kernel, [embeds, own_a], [chunk(half, False), chunk(rows, True), line], 1
    )
    prev_a, succ_a = send(own_a, "next"), send(own_a, "prev")
    prev_b, succ_b = send(own_b, "next"), send(own_b, "prev")
    back_a, ahead_a = send(prev_a, "on_next"), send(succ_a, "on_prev")
    back_b, ahead_b = send(prev_b, "on_next"), send(succ_b, "on_prev")
    block = chunk(rows, True)
    bundle_shape = jax.ShapeDtypeStruct((3, *block.shape), jnp.bfloat16)

    def bundle_kernel(*refs):
        put_bundle(rows, *refs)

    (bundle,) = kernel_call(
        bundle_kernel, [own, succ_a, succ_b, prev_a, prev_b], [bundle_shape], BUNDLE_COST
    )
    others = send(bundle, "sibling")
    found, mine = kernel_call(
        far_first_kernel, [own, bundle, back_a, ahead_a, mine], [line] * 2, FIRST_COST
    )
    *found, back = kernel_call(
        far_back_kernel,
        [own, bundle, others, back_a, ahead_a, back_b, found],
        [line, half_line, block],
        BACK_COST,
    )
    far = [back, ahead_a, ahead_b]
    to_back, to_ahead = kernel_call(
        far_last_kernel, [own, bundle, others, *far, *found], [line] * 2, LAST_COST
    )
    (mine,) = kernel_call(own_kernel, [own, others, *far, mine], [line], 5)
    best = jnp.maximum(
        mine, jnp.maximum(send(to_back, "home_back"), send(to_ahead, "home_ahead"))
    )
    return best.reshape(rows)


def masked_sims(queries, query_labels, query_ids, keys, key_labels, key_ids):
    sims = jnp.einsum("qd,kd->qk", queries, keys, preferred_element_type=jnp.float32)
    keep = (
        (query_labels[:, None] == key_labels[None, :])
        & (query_labels[:, None] >= 0)
        & (query_ids[:, None] != key_ids[None, :])
    )
    return jnp.where(keep, sims, -1.0)


def by_owner(embeds, cluster):
    rows, width = embeds.shape
    size_x = lax.axis_size("gx")
    size_y = lax.axis_size("gy")
    owners = size_x * size_y
    cap = 2 * rows // owners
    total = owners * cap
    unit = normalised(embeds)
    target = cluster // CLU_OWN
    onehot = (target[:, None] == jnp.arange(owners, dtype=jnp.int32)[None, :]).astype(jnp.int32)
    before = jnp.cumsum(onehot, axis=0) - onehot
    slot = jnp.sum(before * onehot, axis=1)
    place = target * cap + slot
    outgoing = jnp.zeros((total, width), jnp.bfloat16).at[place].set(unit)
    out_labels = jnp.full((total,), -1, jnp.int32).at[place].set(cluster)
    got, got_labels = (
        lax.all_to_all(
            outgoing.reshape(owners, cap, width),
            ("gx", "gy"),
            split_axis=0,
            concat_axis=0,
            tiled=True,
        ),
        lax.all_to_all(
            out_labels.reshape(owners, cap), ("gx", "gy"), split_axis=0, concat_axis=0, tiled=True
        ),
    )
    members = got.reshape(total, width)
    labels = got_labels.reshape(total)
    core = lax.axis_index("gz")
    query_ids = core * total + jnp.arange(total, dtype=jnp.int32)
    keys = lax.all_gather(members, "gz", axis=0, tiled=True)
    key_labels = lax.all_gather(labels, "gz", axis=0, tiled=True)
    key_ids = jnp.arange(keys.shape[0], dtype=jnp.int32)
    best = jnp.maximum(
        jnp.full((total,), -1.0, jnp.float32),
        jnp.max(masked_sims(members, labels, query_ids, keys, key_labels, key_ids), axis=1),
    )
    back = lax.all_to_all(
        best.reshape(owners, cap), ("gx", "gy"), split_axis=0, concat_axis=0, tiled=True
    )
    return back.reshape(total)[place]


def solution(mesh):
    shape = mesh.shape
    ring = shape["gx"] * shape["gy"] == 8 and shape["gy"] == 2 and shape["gz"] == 2
    placed = (P(("parts", "gx", "gy", "gz"), None), P(("parts", "gx", "gy", "gz")))
    return jax.shard_map(
        on_ring if ring else by_owner,
        mesh=mesh,
        in_specs=placed,
        out_specs=P(("parts", "gx", "gy", "gz")),
        check_vma=False,
    )
```

```python
import functools

import jax
import jax.numpy as jnp
from jax import lax
from jax.experimental import pallas as pl
from jax.experimental.pallas import tpu as pltpu
from jax.sharding import PartitionSpec as P

CLU_OWN = 16


EPS = 1e-06

GROUP = ("gx", "gy", "gz")


def normalised(block):
    vecs = block.astype(jnp.float32)
    return (vecs * lax.rsqrt(jnp.sum(vecs * vecs, axis=1, keepdims=True) + EPS)).astype(
        jnp.bfloat16
    )


LANES = 128
LABEL_ROWS = 16
VMEM_BYTES = 32 * 2**20
NEAR_COST = 1
FIRST_COST = 200
BACK_COST = 2
LAST_COST = 5


def put_unit(unit, chunk):
    count, width = unit.shape
    for j in range(width // LANES):
        chunk[j * count : (j + 1) * count, :] = unit[:, j * LANES : (j + 1) * LANES]


def pack_first_kernel(embeds, label, first, line, sems):
    rows, width = embeds.shape
    half = rows // 2
    copies = []
    for j in range(width // LANES):
        part = embeds.at[pl.ds(0, half), pl.ds(j * LANES, LANES)]
        copies.append(pltpu.make_async_copy(part, first.at[pl.ds(j * half, half)], sems.at[j]))
    copies.append(pltpu.make_async_copy(label, line, sems.at[width // LANES]))
    for copy in copies:
        copy.start()
    copies[-1].wait()
    row = lax.broadcasted_iota(jnp.int32, (LABEL_ROWS, LANES), 0)
    lines = jnp.zeros((LABEL_ROWS, LANES), jnp.float32)
    for i in range(rows // LANES):
        piece = line[:, i * LANES : (i + 1) * LANES].astype(jnp.float32)
        lines = jnp.where(row == i, piece, lines)
    first[half * width // LANES :, :] = lines.astype(jnp.bfloat16)
    for copy in copies[:-1]:
        copy.wait()


def pack_second_kernel(embeds, first, second, both, mine):
    rows, width = embeds.shape
    unit = normalised(embeds[...])
    put_unit(unit[rows // 2 :, :], second)
    put_unit(unit, both)
    put_labels(first, both)
    own = Block(unit, labels_in(first, rows))
    mine[...] = best_of(own, own)


def put_labels(source, both):
    both[both.shape[0] - LABEL_ROWS :, :] = source[source.shape[0] - LABEL_ROWS :, :]


class Block:
    def __init__(self, unit, label):
        self.unit = unit
        self.label = label
        self.rows = unit.shape[0]
        self.along_rows = None

    def column(self):
        if self.along_rows is None:
            self.along_rows = jnp.transpose(jnp.broadcast_to(self.label, (LANES, self.rows)))
        return self.along_rows


def unit_in(chunk, rows, end):
    return jnp.concatenate([chunk[at : at + rows, :] for at in range(0, end, rows)], axis=1)


def labels_in(first, rows):
    lines = first[first.shape[0] - LABEL_ROWS :, :].astype(jnp.float32)
    return jnp.concatenate([lines[i : i + 1] for i in range(rows // LANES)], axis=1)


def packed(both, rows):
    return Block(unit_in(both, rows, both.shape[0] - LABEL_ROWS), labels_in(both, rows))


def first_half(first, rows):
    half = rows // 2
    unit = normalised(unit_in(first, half, first.shape[0] - LABEL_ROWS))
    return Block(unit, labels_in(first, rows)[:, :half])


def second_half(first, second, rows):
    half = rows // 2
    return Block(unit_in(second, half, second.shape[0]), labels_in(first, rows)[:, half:])


def whole(first, second, rows):
    return joined(first_half(first, rows), second_half(first, second, rows))


def joined(*blocks):
    return Block(
        jnp.concatenate([block.unit for block in blocks], axis=0),
        jnp.concatenate([block.label for block in blocks], axis=1),
    )


def best_of(queries, *all_keys):
    keys_unit = jnp.concatenate([keys.unit for keys in all_keys], axis=0)
    sims = lax.dot_general(
        keys_unit, queries.unit, (((1,), (1,)), ((), ())), preferred_element_type=jnp.float32
    )
    pieces = []
    for start in range(0, queries.rows, LANES):
        best, at = None, 0
        for keys in all_keys:
            keep = keys.column() == queries.label[:, start : start + LANES]
            if keys is queries:
                row = lax.broadcasted_iota(jnp.int32, keep.shape, 0)
                column = lax.broadcasted_iota(jnp.int32, keep.shape, 1) + start
                keep = keep & (row != column)
            found = jnp.where(keep, sims[at : at + keys.rows, start : start + LANES], -1.0)
            found = jnp.max(found, axis=0, keepdims=True)
            best = found if best is None else jnp.maximum(best, found)
            at += keys.rows
        pieces.append(best)
    return jnp.concatenate(pieces, axis=1)


def masked(queries, first, *others):
    all_keys = (first, *others)
    sims = lax.dot_general(
        jnp.concatenate([keys.unit for keys in all_keys], axis=0),
        queries.unit,
        (((1,), (1,)), ((), ())),
        preferred_element_type=jnp.float32,
    )
    found, at = [], 0
    for keys in all_keys:
        keep = keys.column() == queries.label
        found.append(jnp.where(keep, sims[at : at + keys.rows, :], -1.0))
        at += keys.rows
    best = [jnp.max(block, axis=0, keepdims=True) for block in found]
    return found[0], functools.reduce(jnp.maximum, best)


def near_kernel(own, succ_a, succ_b, prev_a, prev_b, self_best, mine, bundle):
    rows = mine.shape[1]
    prev, succ = whole(prev_a, prev_b, rows), whole(succ_a, succ_b, rows)
    for at, block, first in ((0, prev, prev_a), (1, succ, succ_a)):
        put_unit(block.unit, bundle.at[at])
        put_labels(first, bundle.at[at])
    bundle[2] = own[...]
    own = packed(own, rows)
    mine[...] = jnp.maximum(self_best[...], best_of(own, prev, succ))


def far_first_kernel(bundle, back_a, ahead_a, found):
    rows = found.shape[1]
    queries = joined(first_half(back_a, rows), first_half(ahead_a, rows))
    found[...] = best_of(queries, queries, *(packed(bundle.at[at], rows) for at in range(3)))


def far_back_kernel(bundle, others, back_a, ahead_a, back_b, found, *refs):
    back_found, ahead_found, back_packed = refs
    rows = found.shape[1]
    half = rows // 2
    succ, own = packed(bundle.at[1], rows), packed(bundle.at[2], rows)
    prev_other, succ_other = packed(others.at[0], rows), packed(others.at[1], rows)
    first, rest = first_half(back_a, rows), second_half(back_a, back_b, rows)
    first_ahead = first_half(ahead_a, rows)
    back = joined(first, rest)
    put_unit(back.unit, back_packed)
    put_labels(back_a, back_packed)
    both = best_of(back, succ_other)
    back_found[:, :half] = jnp.maximum(found[:, :half], both[:, :half])
    back_found[:, half:] = jnp.maximum(best_of(rest, own, succ, first_ahead), both[:, half:])
    ahead_found[...] = jnp.maximum(found[:, half:], best_of(first_ahead, rest, prev_other))


def far_last_kernel(bundle, others, back, ahead_a, ahead_b, *refs):
    back_found, ahead_found, to_back, to_ahead = refs
    rows = to_back.shape[1]
    half = rows // 2
    back, rest = packed(back, rows), second_half(ahead_a, ahead_b, rows)
    keys = [packed(ref, rows) for ref in (bundle.at[2], bundle.at[0], others.at[0])]
    sims, found = masked(rest, back, *keys)
    to_ahead[:, :half] = ahead_found[...]
    to_ahead[:, half:] = found
    best = jnp.max(jnp.transpose(sims), axis=0, keepdims=True)
    to_back[...] = jnp.maximum(back_found[...], best)


def own_kernel(own, others, back, ahead_a, ahead_b, near, mine):
    rows = mine.shape[1]
    keys = [packed(others.at[at], rows) for at in range(3)]
    keys += [packed(back, rows), whole(ahead_a, ahead_b, rows)]
    mine[...] = jnp.maximum(near[...], best_of(packed(own, rows), *keys))


def ring_perms(size_x, size_y, size_z):
    chips = size_x * size_y

    def device(place, core):
        place = place % chips
        x, y = (place, 0) if place < size_x else (chips - 1 - place, 1)
        return (x * size_y + y) * size_z + core

    def perm(to):
        return [
            (device(p, k), device(*to(p, k))) for p in range(chips) for k in range(size_z)
        ]

    def from_prev(place, core):
        return core ^ (place % chips in (0, 1))

    def from_next(place, core):
        return core ^ (place % chips not in (0, 1))

    return {
        "sibling": perm(lambda p, k: (p, 1 - k)),
        "next": perm(lambda p, k: (p + 1, from_prev(p + 1, k))),
        "prev": perm(lambda p, k: (p - 1, from_next(p - 1, k))),
        "on_next": perm(lambda p, k: (p + 1, k)),
        "on_prev": perm(lambda p, k: (p - 1, k)),
        "home_back": perm(lambda p, k: (p - 2, from_prev(p - 1, k))),
        "home_ahead": perm(lambda p, k: (p + 2, from_next(p + 1, k))),
    }


def kernel_call(kernel, inputs, outputs, matmuls):
    vmem = pl.BlockSpec(memory_space=pltpu.VMEM)
    return pl.pallas_call(
        kernel,
        out_shape=outputs,
        in_specs=[vmem] * len(inputs),
        out_specs=[vmem] * len(outputs),
        compiler_params=pltpu.CompilerParams(vmem_limit_bytes=VMEM_BYTES),
        cost_estimate=pl.CostEstimate(
            flops=matmuls * 2**26, bytes_accessed=2**20, transcendentals=0
        ),
        name=kernel.__name__,
    )(*inputs)


def on_ring(embeds, cluster):
    rows, width = embeds.shape
    half = rows // 2
    perms = ring_perms(*(lax.axis_size(a) for a in GROUP))

    def send(value, name):
        return lax.ppermute(value, GROUP, perms[name])

    line = jax.ShapeDtypeStruct((1, rows), jnp.float32)
    half_line = jax.ShapeDtypeStruct((1, half), jnp.float32)

    def chunk(count, labels):
        size = count * width // LANES + labels * LABEL_ROWS
        return jax.ShapeDtypeStruct((size, LANES), jnp.bfloat16)

    anywhere = pl.BlockSpec(memory_space=pl.ANY)
    vmem = pl.BlockSpec(memory_space=pltpu.VMEM)
    own_a = pl.pallas_call(
        pack_first_kernel,
        out_shape=chunk(half, True),
        in_specs=[anywhere] * 2,
        out_specs=vmem,
        scratch_shapes=[
            pltpu.VMEM((1, rows), jnp.int32),
            pltpu.SemaphoreType.DMA((width // LANES + 1,)),
        ],
        compiler_params=pltpu.CompilerParams(vmem_limit_bytes=VMEM_BYTES),
        name="pack_first",
    )(
        pltpu.with_memory_space_constraint(embeds, pltpu.HBM),
        pltpu.with_memory_space_constraint(cluster.reshape(1, rows), pltpu.HBM),
    )
    own_b, own, mine = kernel_call(
        pack_second_kernel, [embeds, own_a], [chunk(half, False), chunk(rows, True), line], 1
    )
    prev_a, succ_a = send(own_a, "next"), send(own_a, "prev")
    prev_b, succ_b = send(own_b, "next"), send(own_b, "prev")
    back_a, ahead_a = send(prev_a, "on_next"), send(succ_a, "on_prev")
    back_b, ahead_b = send(prev_b, "on_next"), send(succ_b, "on_prev")
    block = chunk(rows, True)
    bundle_shape = jax.ShapeDtypeStruct((3, *block.shape), jnp.bfloat16)
    mine, bundle = kernel_call(
        near_kernel, [own, succ_a, succ_b, prev_a, prev_b, mine], [line, bundle_shape], NEAR_COST
    )
    others = send(bundle, "sibling")
    (found,) = kernel_call(far_first_kernel, [bundle, back_a, ahead_a], [line], FIRST_COST)
    *found, back = kernel_call(
        far_back_kernel,
        [bundle, others, back_a, ahead_a, back_b, found],
        [line, half_line, block],
        BACK_COST,
    )
    far = [back, ahead_a, ahead_b]
    to_back, to_ahead = kernel_call(
        far_last_kernel, [bundle, others, *far, *found], [line] * 2, LAST_COST
    )
    (mine,) = kernel_call(own_kernel, [own, others, *far, mine], [line], 5)
    best = jnp.maximum(
        mine, jnp.maximum(send(to_back, "home_back"), send(to_ahead, "home_ahead"))
    )
    return best.reshape(rows)


def masked_sims(queries, query_labels, query_ids, keys, key_labels, key_ids):
    sims = jnp.einsum("qd,kd->qk", queries, keys, preferred_element_type=jnp.float32)
    keep = (
        (query_labels[:, None] == key_labels[None, :])
        & (query_labels[:, None] >= 0)
        & (query_ids[:, None] != key_ids[None, :])
    )
    return jnp.where(keep, sims, -1.0)


def by_owner(embeds, cluster):
    rows, width = embeds.shape
    size_x = lax.axis_size("gx")
    size_y = lax.axis_size("gy")
    owners = size_x * size_y
    cap = 2 * rows // owners
    total = owners * cap
    unit = normalised(embeds)
    target = cluster // CLU_OWN
    onehot = (target[:, None] == jnp.arange(owners, dtype=jnp.int32)[None, :]).astype(jnp.int32)
    before = jnp.cumsum(onehot, axis=0) - onehot
    slot = jnp.sum(before * onehot, axis=1)
    place = target * cap + slot
    outgoing = jnp.zeros((total, width), jnp.bfloat16).at[place].set(unit)
    out_labels = jnp.full((total,), -1, jnp.int32).at[place].set(cluster)
    got, got_labels = (
        lax.all_to_all(
            outgoing.reshape(owners, cap, width),
            ("gx", "gy"),
            split_axis=0,
            concat_axis=0,
            tiled=True,
        ),
        lax.all_to_all(
            out_labels.reshape(owners, cap), ("gx", "gy"), split_axis=0, concat_axis=0, tiled=True
        ),
    )
    members = got.reshape(total, width)
    labels = got_labels.reshape(total)
    core = lax.axis_index("gz")
    query_ids = core * total + jnp.arange(total, dtype=jnp.int32)
    keys = lax.all_gather(members, "gz", axis=0, tiled=True)
    key_labels = lax.all_gather(labels, "gz", axis=0, tiled=True)
    key_ids = jnp.arange(keys.shape[0], dtype=jnp.int32)
    best = jnp.maximum(
        jnp.full((total,), -1.0, jnp.float32),
        jnp.max(masked_sims(members, labels, query_ids, keys, key_labels, key_ids), axis=1),
    )
    back = lax.all_to_all(
        best.reshape(owners, cap), ("gx", "gy"), split_axis=0, concat_axis=0, tiled=True
    )
    return back.reshape(total)[place]


def solution(mesh):
    shape = mesh.shape
    ring = shape["gx"] * shape["gy"] == 8 and shape["gy"] == 2 and shape["gz"] == 2
    placed = (P(("parts", "gx", "gy", "gz"), None), P(("parts", "gx", "gy", "gz")))
    return jax.shard_map(
        on_ring if ring else by_owner,
        mesh=mesh,
        in_specs=placed,
        out_specs=P(("parts", "gx", "gy", "gz")),
        check_vma=False,
    )
```

```python
import functools

import jax
import jax.numpy as jnp
from jax import lax
from jax.experimental import pallas as pl
from jax.experimental.pallas import tpu as pltpu
from jax.sharding import PartitionSpec as P

CLU_OWN = 16


EPS = 1e-06

GROUP = ("gx", "gy", "gz")


def normalised(block):
    vecs = block.astype(jnp.float32)
    return (vecs * lax.rsqrt(jnp.sum(vecs * vecs, axis=1, keepdims=True) + EPS)).astype(
        jnp.bfloat16
    )


LANES = 128
LABEL_ROWS = 16
VMEM_BYTES = 32 * 2**20
BUNDLE_COST = 1
FIRST_COST = 200
BACK_COST = 2
LAST_COST = 5


def put_unit(unit, chunk):
    count, width = unit.shape
    for j in range(width // LANES):
        chunk[j * count : (j + 1) * count, :] = unit[:, j * LANES : (j + 1) * LANES]


def pack_first_kernel(embeds, label, first, line, sems):
    rows, width = embeds.shape
    half = rows // 2
    copies = []
    for j in range(width // LANES):
        part = embeds.at[pl.ds(0, half), pl.ds(j * LANES, LANES)]
        copies.append(pltpu.make_async_copy(part, first.at[pl.ds(j * half, half)], sems.at[j]))
    copies.append(pltpu.make_async_copy(label, line, sems.at[width // LANES]))
    for copy in copies:
        copy.start()
    copies[-1].wait()
    row = lax.broadcasted_iota(jnp.int32, (LABEL_ROWS, LANES), 0)
    lines = jnp.zeros((LABEL_ROWS, LANES), jnp.float32)
    for i in range(rows // LANES):
        piece = line[:, i * LANES : (i + 1) * LANES].astype(jnp.float32)
        lines = jnp.where(row == i, piece, lines)
    first[half * width // LANES :, :] = lines.astype(jnp.bfloat16)
    for copy in copies[:-1]:
        copy.wait()


def pack_second_kernel(embeds, first, second, both, mine):
    rows, width = embeds.shape
    unit = normalised(embeds[...])
    put_unit(unit[rows // 2 :, :], second)
    put_unit(unit, both)
    put_labels(first, both)
    own = Block(unit, labels_in(first, rows))
    mine[...] = best_of(own, own)


def put_labels(source, both):
    both[both.shape[0] - LABEL_ROWS :, :] = source[source.shape[0] - LABEL_ROWS :, :]


class Block:
    def __init__(self, unit, label):
        self.unit = unit
        self.label = label
        self.rows = unit.shape[0]
        self.along_rows = None

    def column(self):
        if self.along_rows is None:
            self.along_rows = jnp.transpose(jnp.broadcast_to(self.label, (LANES, self.rows)))
        return self.along_rows


def unit_in(chunk, rows, end):
    return jnp.concatenate([chunk[at : at + rows, :] for at in range(0, end, rows)], axis=1)


def labels_in(first, rows):
    lines = first[first.shape[0] - LABEL_ROWS :, :].astype(jnp.float32)
    return jnp.concatenate([lines[i : i + 1] for i in range(rows // LANES)], axis=1)


def packed(both, rows):
    return Block(unit_in(both, rows, both.shape[0] - LABEL_ROWS), labels_in(both, rows))


def first_half(first, rows):
    half = rows // 2
    unit = normalised(unit_in(first, half, first.shape[0] - LABEL_ROWS))
    return Block(unit, labels_in(first, rows)[:, :half])


def second_half(first, second, rows):
    half = rows // 2
    return Block(unit_in(second, half, second.shape[0]), labels_in(first, rows)[:, half:])


def whole(first, second, rows):
    return joined(first_half(first, rows), second_half(first, second, rows))


def joined(*blocks):
    return Block(
        jnp.concatenate([block.unit for block in blocks], axis=0),
        jnp.concatenate([block.label for block in blocks], axis=1),
    )


def best_of(queries, *all_keys):
    keys_unit = jnp.concatenate([keys.unit for keys in all_keys], axis=0)
    sims = lax.dot_general(
        keys_unit, queries.unit, (((1,), (1,)), ((), ())), preferred_element_type=jnp.float32
    )
    pieces = []
    for start in range(0, queries.rows, LANES):
        best, at = None, 0
        for keys in all_keys:
            keep = keys.column() == queries.label[:, start : start + LANES]
            if keys is queries:
                row = lax.broadcasted_iota(jnp.int32, keep.shape, 0)
                column = lax.broadcasted_iota(jnp.int32, keep.shape, 1) + start
                keep = keep & (row != column)
            found = jnp.where(keep, sims[at : at + keys.rows, start : start + LANES], -1.0)
            found = jnp.max(found, axis=0, keepdims=True)
            best = found if best is None else jnp.maximum(best, found)
            at += keys.rows
        pieces.append(best)
    return jnp.concatenate(pieces, axis=1)


def masked(queries, first, *others):
    all_keys = (first, *others)
    sims = lax.dot_general(
        jnp.concatenate([keys.unit for keys in all_keys], axis=0),
        queries.unit,
        (((1,), (1,)), ((), ())),
        preferred_element_type=jnp.float32,
    )
    found, at = [], 0
    for keys in all_keys:
        keep = keys.column() == queries.label
        found.append(jnp.where(keep, sims[at : at + keys.rows, :], -1.0))
        at += keys.rows
    best = [jnp.max(block, axis=0, keepdims=True) for block in found]
    return found[0], functools.reduce(jnp.maximum, best)


def put_bundle(rows, own, succ_a, succ_b, prev_a, prev_b, bundle):
    for at, first, second in ((0, prev_a, prev_b), (1, succ_a, succ_b)):
        put_unit(whole(first, second, rows).unit, bundle.at[at])
        put_labels(first, bundle.at[at])
    bundle[2] = own[...]


def far_first_kernel(own, bundle, back_a, ahead_a, found):
    rows = found.shape[1]
    queries = joined(first_half(back_a, rows), first_half(ahead_a, rows))
    own = packed(own, rows)
    near = [packed(bundle.at[at], rows) for at in range(2)]
    found[...] = best_of(queries, queries, *near, own)


def far_back_kernel(own, bundle, others, back_a, ahead_a, back_b, found, *refs):
    back_found, ahead_found, back_packed = refs
    rows = found.shape[1]
    half = rows // 2
    succ, own = packed(bundle.at[1], rows), packed(own, rows)
    prev_other, succ_other = packed(others.at[0], rows), packed(others.at[1], rows)
    first, rest = first_half(back_a, rows), second_half(back_a, back_b, rows)
    first_ahead = first_half(ahead_a, rows)
    back = joined(first, rest)
    put_unit(back.unit, back_packed)
    put_labels(back_a, back_packed)
    both = best_of(back, succ_other)
    back_found[:, :half] = jnp.maximum(found[:, :half], both[:, :half])
    back_found[:, half:] = jnp.maximum(best_of(rest, own, succ, first_ahead), both[:, half:])
    ahead_found[...] = jnp.maximum(found[:, half:], best_of(first_ahead, rest, prev_other))


def far_last_kernel(own, bundle, others, back, ahead_a, ahead_b, *refs):
    back_found, ahead_found, to_back, to_ahead = refs
    rows = to_back.shape[1]
    half = rows // 2
    back, rest = packed(back, rows), second_half(ahead_a, ahead_b, rows)
    keys = [packed(ref, rows) for ref in (own, bundle.at[0], others.at[0])]
    sims, found = masked(rest, back, *keys)
    to_ahead[:, :half] = ahead_found[...]
    to_ahead[:, half:] = found
    best = jnp.max(jnp.transpose(sims), axis=0, keepdims=True)
    to_back[...] = jnp.maximum(back_found[...], best)


def own_kernel(own, bundle, others, back, ahead_a, ahead_b, near, mine):
    rows = mine.shape[1]
    keys = [packed(others.at[at], rows) for at in range(3)]
    keys += [packed(bundle.at[at], rows) for at in range(2)]
    keys += [packed(back, rows), whole(ahead_a, ahead_b, rows)]
    mine[...] = jnp.maximum(near[...], best_of(packed(own, rows), *keys))


def ring_perms(size_x, size_y, size_z):
    chips = size_x * size_y

    def device(place, core):
        place = place % chips
        x, y = (place, 0) if place < size_x else (chips - 1 - place, 1)
        return (x * size_y + y) * size_z + core

    def perm(to):
        return [
            (device(p, k), device(*to(p, k))) for p in range(chips) for k in range(size_z)
        ]

    def from_prev(place, core):
        return core ^ (place % chips in (0, 1))

    def from_next(place, core):
        return core ^ (place % chips not in (0, 1))

    return {
        "sibling": perm(lambda p, k: (p, 1 - k)),
        "next": perm(lambda p, k: (p + 1, from_prev(p + 1, k))),
        "prev": perm(lambda p, k: (p - 1, from_next(p - 1, k))),
        "on_next": perm(lambda p, k: (p + 1, k)),
        "on_prev": perm(lambda p, k: (p - 1, k)),
        "home_back": perm(lambda p, k: (p - 2, from_prev(p - 1, k))),
        "home_ahead": perm(lambda p, k: (p + 2, from_next(p + 1, k))),
    }


def kernel_call(kernel, inputs, outputs, matmuls):
    vmem = pl.BlockSpec(memory_space=pltpu.VMEM)
    return pl.pallas_call(
        kernel,
        out_shape=outputs,
        in_specs=[vmem] * len(inputs),
        out_specs=[vmem] * len(outputs),
        compiler_params=pltpu.CompilerParams(vmem_limit_bytes=VMEM_BYTES),
        cost_estimate=pl.CostEstimate(
            flops=matmuls * 2**26, bytes_accessed=2**20, transcendentals=0
        ),
        name=kernel.__name__,
    )(*inputs)


def on_ring(embeds, cluster):
    rows, width = embeds.shape
    half = rows // 2
    perms = ring_perms(*(lax.axis_size(a) for a in GROUP))

    def send(value, name):
        return lax.ppermute(value, GROUP, perms[name])

    line = jax.ShapeDtypeStruct((1, rows), jnp.float32)
    half_line = jax.ShapeDtypeStruct((1, half), jnp.float32)

    def chunk(count, labels):
        size = count * width // LANES + labels * LABEL_ROWS
        return jax.ShapeDtypeStruct((size, LANES), jnp.bfloat16)

    anywhere = pl.BlockSpec(memory_space=pl.ANY)
    vmem = pl.BlockSpec(memory_space=pltpu.VMEM)
    own_a = pl.pallas_call(
        pack_first_kernel,
        out_shape=chunk(half, True),
        in_specs=[anywhere] * 2,
        out_specs=vmem,
        scratch_shapes=[
            pltpu.VMEM((1, rows), jnp.int32),
            pltpu.SemaphoreType.DMA((width // LANES + 1,)),
        ],
        compiler_params=pltpu.CompilerParams(vmem_limit_bytes=VMEM_BYTES),
        name="pack_first",
    )(
        pltpu.with_memory_space_constraint(embeds, pltpu.HBM),
        pltpu.with_memory_space_constraint(cluster.reshape(1, rows), pltpu.HBM),
    )
    own_b, own, mine = kernel_call(
        pack_second_kernel, [embeds, own_a], [chunk(half, False), chunk(rows, True), line], 1
    )
    prev_a, succ_a = send(own_a, "next"), send(own_a, "prev")
    prev_b, succ_b = send(own_b, "next"), send(own_b, "prev")
    back_a, ahead_a = send(prev_a, "on_next"), send(succ_a, "on_prev")
    back_b, ahead_b = send(prev_b, "on_next"), send(succ_b, "on_prev")
    block = chunk(rows, True)
    bundle_shape = jax.ShapeDtypeStruct((3, *block.shape), jnp.bfloat16)

    def bundle_kernel(*refs):
        put_bundle(rows, *refs)

    (bundle,) = kernel_call(
        bundle_kernel, [own, succ_a, succ_b, prev_a, prev_b], [bundle_shape], BUNDLE_COST
    )
    others = send(bundle, "sibling")
    (found,) = kernel_call(far_first_kernel, [own, bundle, back_a, ahead_a], [line], FIRST_COST)
    *found, back = kernel_call(
        far_back_kernel,
        [own, bundle, others, back_a, ahead_a, back_b, found],
        [line, half_line, block],
        BACK_COST,
    )
    far = [back, ahead_a, ahead_b]
    to_back, to_ahead = kernel_call(
        far_last_kernel, [own, bundle, others, *far, *found], [line] * 2, LAST_COST
    )
    (mine,) = kernel_call(own_kernel, [own, bundle, others, *far, mine], [line], 5)
    best = jnp.maximum(
        mine, jnp.maximum(send(to_back, "home_back"), send(to_ahead, "home_ahead"))
    )
    return best.reshape(rows)


def masked_sims(queries, query_labels, query_ids, keys, key_labels, key_ids):
    sims = jnp.einsum("qd,kd->qk", queries, keys, preferred_element_type=jnp.float32)
    keep = (
        (query_labels[:, None] == key_labels[None, :])
        & (query_labels[:, None] >= 0)
        & (query_ids[:, None] != key_ids[None, :])
    )
    return jnp.where(keep, sims, -1.0)


def by_owner(embeds, cluster):
    rows, width = embeds.shape
    size_x = lax.axis_size("gx")
    size_y = lax.axis_size("gy")
    owners = size_x * size_y
    cap = 2 * rows // owners
    total = owners * cap
    unit = normalised(embeds)
    target = cluster // CLU_OWN
    onehot = (target[:, None] == jnp.arange(owners, dtype=jnp.int32)[None, :]).astype(jnp.int32)
    before = jnp.cumsum(onehot, axis=0) - onehot
    slot = jnp.sum(before * onehot, axis=1)
    place = target * cap + slot
    outgoing = jnp.zeros((total, width), jnp.bfloat16).at[place].set(unit)
    out_labels = jnp.full((total,), -1, jnp.int32).at[place].set(cluster)
    got, got_labels = (
        lax.all_to_all(
            outgoing.reshape(owners, cap, width),
            ("gx", "gy"),
            split_axis=0,
            concat_axis=0,
            tiled=True,
        ),
        lax.all_to_all(
            out_labels.reshape(owners, cap), ("gx", "gy"), split_axis=0, concat_axis=0, tiled=True
        ),
    )
    members = got.reshape(total, width)
    labels = got_labels.reshape(total)
    core = lax.axis_index("gz")
    query_ids = core * total + jnp.arange(total, dtype=jnp.int32)
    keys = lax.all_gather(members, "gz", axis=0, tiled=True)
    key_labels = lax.all_gather(labels, "gz", axis=0, tiled=True)
    key_ids = jnp.arange(keys.shape[0], dtype=jnp.int32)
    best = jnp.maximum(
        jnp.full((total,), -1.0, jnp.float32),
        jnp.max(masked_sims(members, labels, query_ids, keys, key_labels, key_ids), axis=1),
    )
    back = lax.all_to_all(
        best.reshape(owners, cap), ("gx", "gy"), split_axis=0, concat_axis=0, tiled=True
    )
    return back.reshape(total)[place]


def solution(mesh):
    shape = mesh.shape
    ring = shape["gx"] * shape["gy"] == 8 and shape["gy"] == 2 and shape["gz"] == 2
    placed = (P(("parts", "gx", "gy", "gz"), None), P(("parts", "gx", "gy", "gz")))
    return jax.shard_map(
        on_ring if ring else by_owner,
        mesh=mesh,
        in_specs=placed,
        out_specs=P(("parts", "gx", "gy", "gz")),
        check_vma=False,
    )
```

```python
import functools

import jax
import jax.numpy as jnp
from jax import lax
from jax.experimental import pallas as pl
from jax.experimental.pallas import tpu as pltpu
from jax.sharding import PartitionSpec as P

CLU_OWN = 16


EPS = 1e-06

GROUP = ("gx", "gy", "gz")


def normalised(block):
    vecs = block.astype(jnp.float32)
    return (vecs * lax.rsqrt(jnp.sum(vecs * vecs, axis=1, keepdims=True) + EPS)).astype(
        jnp.bfloat16
    )


LANES = 128
LABEL_ROWS = 16
VMEM_BYTES = 32 * 2**20
BUNDLE_COST = 1
FIRST_COST = 200
BACK_COST = 2
LAST_COST = 5


def put_unit(unit, chunk):
    count, width = unit.shape
    for j in range(width // LANES):
        chunk[j * count : (j + 1) * count, :] = unit[:, j * LANES : (j + 1) * LANES]


def pack_first_kernel(embeds, label, first, line, sems):
    rows, width = embeds.shape
    half = rows // 2
    copies = []
    for j in range(width // LANES):
        part = embeds.at[pl.ds(0, half), pl.ds(j * LANES, LANES)]
        copies.append(pltpu.make_async_copy(part, first.at[pl.ds(j * half, half)], sems.at[j]))
    copies.append(pltpu.make_async_copy(label, line, sems.at[width // LANES]))
    for copy in copies:
        copy.start()
    copies[-1].wait()
    row = lax.broadcasted_iota(jnp.int32, (LABEL_ROWS, LANES), 0)
    lines = jnp.zeros((LABEL_ROWS, LANES), jnp.float32)
    for i in range(rows // LANES):
        piece = line[:, i * LANES : (i + 1) * LANES].astype(jnp.float32)
        lines = jnp.where(row == i, piece, lines)
    first[half * width // LANES :, :] = lines.astype(jnp.bfloat16)
    for copy in copies[:-1]:
        copy.wait()


def pack_second_kernel(embeds, first, second, both, mine):
    rows, width = embeds.shape
    unit = normalised(embeds[...])
    put_unit(unit[rows // 2 :, :], second)
    put_unit(unit, both)
    put_labels(first, both)
    own = Block(unit, labels_in(first, rows))
    mine[...] = best_of(own, own)


def put_labels(source, both):
    both[both.shape[0] - LABEL_ROWS :, :] = source[source.shape[0] - LABEL_ROWS :, :]


class Block:
    def __init__(self, unit, label):
        self.unit = unit
        self.label = label
        self.rows = unit.shape[0]
        self.along_rows = None

    def column(self):
        if self.along_rows is None:
            self.along_rows = jnp.transpose(jnp.broadcast_to(self.label, (LANES, self.rows)))
        return self.along_rows


def unit_in(chunk, rows, end):
    return jnp.concatenate([chunk[at : at + rows, :] for at in range(0, end, rows)], axis=1)


def labels_in(first, rows):
    lines = first[first.shape[0] - LABEL_ROWS :, :].astype(jnp.float32)
    return jnp.concatenate([lines[i : i + 1] for i in range(rows // LANES)], axis=1)


def packed(both, rows):
    return Block(unit_in(both, rows, both.shape[0] - LABEL_ROWS), labels_in(both, rows))


def first_half(first, rows):
    half = rows // 2
    unit = normalised(unit_in(first, half, first.shape[0] - LABEL_ROWS))
    return Block(unit, labels_in(first, rows)[:, :half])


def second_half(first, second, rows):
    half = rows // 2
    return Block(unit_in(second, half, second.shape[0]), labels_in(first, rows)[:, half:])


def whole(first, second, rows):
    return joined(first_half(first, rows), second_half(first, second, rows))


def joined(*blocks):
    return Block(
        jnp.concatenate([block.unit for block in blocks], axis=0),
        jnp.concatenate([block.label for block in blocks], axis=1),
    )


def best_of(queries, *all_keys):
    keys_unit = jnp.concatenate([keys.unit for keys in all_keys], axis=0)
    sims = lax.dot_general(
        keys_unit, queries.unit, (((1,), (1,)), ((), ())), preferred_element_type=jnp.float32
    )
    pieces = []
    for start in range(0, queries.rows, LANES):
        best, at = None, 0
        for keys in all_keys:
            keep = keys.column() == queries.label[:, start : start + LANES]
            if keys is queries:
                row = lax.broadcasted_iota(jnp.int32, keep.shape, 0)
                column = lax.broadcasted_iota(jnp.int32, keep.shape, 1) + start
                keep = keep & (row != column)
            found = jnp.where(keep, sims[at : at + keys.rows, start : start + LANES], -1.0)
            found = jnp.max(found, axis=0, keepdims=True)
            best = found if best is None else jnp.maximum(best, found)
            at += keys.rows
        pieces.append(best)
    return jnp.concatenate(pieces, axis=1)


def masked(queries, first, *others):
    all_keys = (first, *others)
    sims = lax.dot_general(
        jnp.concatenate([keys.unit for keys in all_keys], axis=0),
        queries.unit,
        (((1,), (1,)), ((), ())),
        preferred_element_type=jnp.float32,
    )
    found, at = [], 0
    for keys in all_keys:
        keep = keys.column() == queries.label
        found.append(jnp.where(keep, sims[at : at + keys.rows, :], -1.0))
        at += keys.rows
    best = [jnp.max(block, axis=0, keepdims=True) for block in found]
    return found[0], functools.reduce(jnp.maximum, best)


def put_bundle(rows, own, succ_a, succ_b, prev_a, prev_b, bundle):
    for at, first, second in ((0, prev_a, prev_b), (1, succ_a, succ_b)):
        put_unit(whole(first, second, rows).unit, bundle.at[at])
        put_labels(first, bundle.at[at])
    bundle[2] = own[...]


def far_first_kernel(own, bundle, back_a, ahead_a, found):
    rows = found.shape[1]
    queries = joined(first_half(back_a, rows), first_half(ahead_a, rows))
    own = packed(own, rows)
    near = [packed(bundle.at[at], rows) for at in range(2)]
    found[...] = best_of(queries, queries, *near, own)


def far_back_kernel(own, bundle, others, back_a, ahead_a, back_b, found, *refs):
    back_found, ahead_found, back_packed = refs
    rows = found.shape[1]
    half = rows // 2
    succ, own = packed(bundle.at[1], rows), packed(own, rows)
    prev_other, succ_other = packed(others.at[0], rows), packed(others.at[1], rows)
    first, rest = first_half(back_a, rows), second_half(back_a, back_b, rows)
    first_ahead = first_half(ahead_a, rows)
    back = joined(first, rest)
    put_unit(back.unit, back_packed)
    put_labels(back_a, back_packed)
    both = best_of(back, succ_other)
    back_found[:, :half] = jnp.maximum(found[:, :half], both[:, :half])
    back_found[:, half:] = jnp.maximum(best_of(rest, own, succ, first_ahead), both[:, half:])
    ahead_found[...] = jnp.maximum(found[:, half:], best_of(first_ahead, rest, prev_other))


def far_last_kernel(own, bundle, others, back, ahead_a, ahead_b, *refs):
    back_found, ahead_found, to_back, to_ahead = refs
    rows = to_back.shape[1]
    half = rows // 2
    back, rest = packed(back, rows), second_half(ahead_a, ahead_b, rows)
    keys = [packed(ref, rows) for ref in (own, bundle.at[0], others.at[0])]
    sims, found = masked(rest, back, *keys)
    to_ahead[:, :half] = ahead_found[...]
    to_ahead[:, half:] = found
    best = jnp.max(jnp.transpose(sims), axis=0, keepdims=True)
    to_back[...] = jnp.maximum(back_found[...], best)


def own_kernel(own, bundle, others, back, ahead_a, ahead_b, near, mine):
    rows = mine.shape[1]
    keys = [packed(others.at[at], rows) for at in range(3)]
    keys += [packed(bundle.at[at], rows) for at in range(2)]
    keys += [packed(back, rows), whole(ahead_a, ahead_b, rows)]
    mine[...] = jnp.maximum(near[...], best_of(packed(own, rows), *keys))


def ring_perms(size_x, size_y, size_z):
    chips = size_x * size_y

    def device(place, core):
        place = place % chips
        x, y = (place, 0) if place < size_x else (chips - 1 - place, 1)
        return (x * size_y + y) * size_z + core

    def perm(to):
        return [
            (device(p, k), device(*to(p, k))) for p in range(chips) for k in range(size_z)
        ]

    def from_prev(place, core):
        return core ^ (place % chips in (0, chips - 1))

    def from_next(place, core):
        return core ^ (place % chips not in (0, chips - 1))

    return {
        "sibling": perm(lambda p, k: (p, 1 - k)),
        "next": perm(lambda p, k: (p + 1, from_prev(p + 1, k))),
        "prev": perm(lambda p, k: (p - 1, from_next(p - 1, k))),
        "on_next": perm(lambda p, k: (p + 1, k)),
        "on_prev": perm(lambda p, k: (p - 1, k)),
        "home_back": perm(lambda p, k: (p - 2, from_prev(p - 1, k))),
        "home_ahead": perm(lambda p, k: (p + 2, from_next(p + 1, k))),
    }


def kernel_call(kernel, inputs, outputs, matmuls):
    vmem = pl.BlockSpec(memory_space=pltpu.VMEM)
    return pl.pallas_call(
        kernel,
        out_shape=outputs,
        in_specs=[vmem] * len(inputs),
        out_specs=[vmem] * len(outputs),
        compiler_params=pltpu.CompilerParams(vmem_limit_bytes=VMEM_BYTES),
        cost_estimate=pl.CostEstimate(
            flops=matmuls * 2**26, bytes_accessed=2**20, transcendentals=0
        ),
        name=kernel.__name__,
    )(*inputs)


def on_ring(embeds, cluster):
    rows, width = embeds.shape
    half = rows // 2
    perms = ring_perms(*(lax.axis_size(a) for a in GROUP))

    def send(value, name):
        return lax.ppermute(value, GROUP, perms[name])

    line = jax.ShapeDtypeStruct((1, rows), jnp.float32)
    half_line = jax.ShapeDtypeStruct((1, half), jnp.float32)

    def chunk(count, labels):
        size = count * width // LANES + labels * LABEL_ROWS
        return jax.ShapeDtypeStruct((size, LANES), jnp.bfloat16)

    anywhere = pl.BlockSpec(memory_space=pl.ANY)
    vmem = pl.BlockSpec(memory_space=pltpu.VMEM)
    own_a = pl.pallas_call(
        pack_first_kernel,
        out_shape=chunk(half, True),
        in_specs=[anywhere] * 2,
        out_specs=vmem,
        scratch_shapes=[
            pltpu.VMEM((1, rows), jnp.int32),
            pltpu.SemaphoreType.DMA((width // LANES + 1,)),
        ],
        compiler_params=pltpu.CompilerParams(vmem_limit_bytes=VMEM_BYTES),
        name="pack_first",
    )(
        pltpu.with_memory_space_constraint(embeds, pltpu.HBM),
        pltpu.with_memory_space_constraint(cluster.reshape(1, rows), pltpu.HBM),
    )
    own_b, own, mine = kernel_call(
        pack_second_kernel, [embeds, own_a], [chunk(half, False), chunk(rows, True), line], 1
    )
    prev_a, succ_a = send(own_a, "next"), send(own_a, "prev")
    prev_b, succ_b = send(own_b, "next"), send(own_b, "prev")
    back_a, ahead_a = send(prev_a, "on_next"), send(succ_a, "on_prev")
    back_b, ahead_b = send(prev_b, "on_next"), send(succ_b, "on_prev")
    block = chunk(rows, True)
    bundle_shape = jax.ShapeDtypeStruct((3, *block.shape), jnp.bfloat16)

    def bundle_kernel(*refs):
        put_bundle(rows, *refs)

    (bundle,) = kernel_call(
        bundle_kernel, [own, succ_a, succ_b, prev_a, prev_b], [bundle_shape], BUNDLE_COST
    )
    others = send(bundle, "sibling")
    (found,) = kernel_call(far_first_kernel, [own, bundle, back_a, ahead_a], [line], FIRST_COST)
    *found, back = kernel_call(
        far_back_kernel,
        [own, bundle, others, back_a, ahead_a, back_b, found],
        [line, half_line, block],
        BACK_COST,
    )
    far = [back, ahead_a, ahead_b]
    to_back, to_ahead = kernel_call(
        far_last_kernel, [own, bundle, others, *far, *found], [line] * 2, LAST_COST
    )
    (mine,) = kernel_call(own_kernel, [own, bundle, others, *far, mine], [line], 5)
    best = jnp.maximum(
        mine, jnp.maximum(send(to_back, "home_back"), send(to_ahead, "home_ahead"))
    )
    return best.reshape(rows)


def masked_sims(queries, query_labels, query_ids, keys, key_labels, key_ids):
    sims = jnp.einsum("qd,kd->qk", queries, keys, preferred_element_type=jnp.float32)
    keep = (
        (query_labels[:, None] == key_labels[None, :])
        & (query_labels[:, None] >= 0)
        & (query_ids[:, None] != key_ids[None, :])
    )
    return jnp.where(keep, sims, -1.0)


def by_owner(embeds, cluster):
    rows, width = embeds.shape
    size_x = lax.axis_size("gx")
    size_y = lax.axis_size("gy")
    owners = size_x * size_y
    cap = 2 * rows // owners
    total = owners * cap
    unit = normalised(embeds)
    target = cluster // CLU_OWN
    onehot = (target[:, None] == jnp.arange(owners, dtype=jnp.int32)[None, :]).astype(jnp.int32)
    before = jnp.cumsum(onehot, axis=0) - onehot
    slot = jnp.sum(before * onehot, axis=1)
    place = target * cap + slot
    outgoing = jnp.zeros((total, width), jnp.bfloat16).at[place].set(unit)
    out_labels = jnp.full((total,), -1, jnp.int32).at[place].set(cluster)
    got, got_labels = (
        lax.all_to_all(
            outgoing.reshape(owners, cap, width),
            ("gx", "gy"),
            split_axis=0,
            concat_axis=0,
            tiled=True,
        ),
        lax.all_to_all(
            out_labels.reshape(owners, cap), ("gx", "gy"), split_axis=0, concat_axis=0, tiled=True
        ),
    )
    members = got.reshape(total, width)
    labels = got_labels.reshape(total)
    core = lax.axis_index("gz")
    query_ids = core * total + jnp.arange(total, dtype=jnp.int32)
    keys = lax.all_gather(members, "gz", axis=0, tiled=True)
    key_labels = lax.all_gather(labels, "gz", axis=0, tiled=True)
    key_ids = jnp.arange(keys.shape[0], dtype=jnp.int32)
    best = jnp.maximum(
        jnp.full((total,), -1.0, jnp.float32),
        jnp.max(masked_sims(members, labels, query_ids, keys, key_labels, key_ids), axis=1),
    )
    back = lax.all_to_all(
        best.reshape(owners, cap), ("gx", "gy"), split_axis=0, concat_axis=0, tiled=True
    )
    return back.reshape(total)[place]


def solution(mesh):
    shape = mesh.shape
    ring = shape["gx"] * shape["gy"] == 8 and shape["gy"] == 2 and shape["gz"] == 2
    placed = (P(("parts", "gx", "gy", "gz"), None), P(("parts", "gx", "gy", "gz")))
    return jax.shard_map(
        on_ring if ring else by_owner,
        mesh=mesh,
        in_specs=placed,
        out_specs=P(("parts", "gx", "gy", "gz")),
        check_vma=False,
    )
```
